32 devices in a mesh: dp: 4 (over z), ctx: 2 (over x), fsdp: 4 (over y, core).
Axes of the slice: x: 2, y: 2, z: 4, core: 2. Of those that a mesh axis runs over, the one named last changes fastest.
Arguments:
- tokens: bfloat16 [32, 1024, 576], P(('dp', 'fsdp'), 'ctx'), may hold values from -6 to 6
- norm1_gain: bfloat16 [576], P('fsdp'), may hold values from 0.5 to 1.5
- w_query: bfloat16 [576, 576], P('fsdp'), may hold values from -0.25 to 0.25
- w_key: bfloat16 [576, 192], P('fsdp'), may hold values from -0.25 to 0.25
- w_value: bfloat16 [576, 192], P('fsdp'), may hold values from -0.25 to 0.25
- w_out: bfloat16 [576, 576], P('fsdp'), may hold values from -2 to 2
- norm2_gain: bfloat16 [576], P('fsdp'), may hold values from 0.5 to 1.5
- w_gate: bfloat16 [576, 1536], P('fsdp'), may hold values from -0.25 to 0.25
- w_up: bfloat16 [576, 1536], P('fsdp'), may hold values from -0.25 to 0.25
- w_down: bfloat16 [1536, 576], P('fsdp'), may hold values from -0.15625 to 0.15625
- out_grad: bfloat16 [32, 1024, 576], P(('dp', 'fsdp'), 'ctx'), may hold values from -6 to 6
Outputs:
- output: bfloat16 [32, 1024, 576], P(('dp', 'fsdp'), 'ctx')
- input_grad: float32 [32, 1024, 576], P(('dp', 'fsdp'), 'ctx')
- norm1_gain_grad: float32 [576], P('fsdp')
- w_query_grad: float32 [576, 576], P('fsdp')
- w_key_grad: float32 [576, 192], P('fsdp')
- w_value_grad: float32 [576, 192], P('fsdp')
- w_out_grad: float32 [576, 576], P('fsdp')
- norm2_gain_grad: float32 [576], P('fsdp')
- w_gate_grad: float32 [576, 1536], P('fsdp')
- w_up_grad: float32 [576, 1536], P('fsdp')
- w_down_grad: float32 [1536, 576], P('fsdp')
The draws below stay inside these ranges and needn't reach their ends.
All inputs are finite; a program needn't handle non-finite values.
Results may differ from the reference program's by a relative error of at most 0.03.
Values may be sent and summed in bfloat16 or wider, within the bound.
No kernel may reach another device: no remote copies, remote signals or barrier semaphores. Data moves between devices by JAX's collectives and lax.ppermute only.
A program may use at most 192 MiB of HBM per device.

```python
import math
import jax
import jax.numpy as jnp
from jax import lax

D = 576
QUERY_HEADS = 9
KEY_VALUE_HEADS = 3
HEAD_SIZE = 64
FF = 1536
QW = 576
KW = 192
SEQUENCE_TOKENS = 1024
SEQS = 32


def shard_levels(own_key, shape, shards, low, largest):
    def one(axis_at, shards_of):
        draws = jax.random.uniform(jax.random.fold_in(jax.random.fold_in(own_key, 6), axis_at), (shards_of,), jnp.float32, low / len(shards), largest / len(shards))
        return jnp.repeat(jnp.exp(draws), shape[axis_at] // shards_of).reshape((-1,) + (1,) * (len(shape) - axis_at - 1))

    factor_of = one(*shards[0])
    for cut in shards[1:]:
        factor_of = factor_of * one(*cut)
    return factor_of


def gaussian(stream_key, shape, scale, limit, cuts=(), kind=jnp.bfloat16):
    entries = scale * jax.random.normal(stream_key, shape, jnp.float32)
    if cuts:
        entries = entries * shard_levels(stream_key, shape, cuts, -0.22, 0.18)
    return jnp.clip(entries, -limit, limit).astype(kind)


def setup_inputs(seed: int = 0) -> dict:
    streams_of = jax.random.split(jax.random.key(seed), 12)
    tokens = gaussian(streams_of[0], (SEQS, SEQUENCE_TOKENS, D), 1.0, 6.0, ((0, 16), (1, 2)))
    norm1_gain = jnp.clip(1.0 + 0.1 * jax.random.normal(streams_of[1], (D,), jnp.float32), 0.5, 1.5).astype(jnp.bfloat16)
    w_query = gaussian(streams_of[2], (D, QW), D ** -0.5, 0.25, ((0, 4),))
    w_key = gaussian(streams_of[3], (D, KW), D ** -0.5, 0.25, ((0, 4),))
    w_value = gaussian(streams_of[4], (D, KW), D ** -0.5, 0.25, ((0, 4),))
    w_out = gaussian(streams_of[5], (QW, D), (QW // 64) ** -0.5, 2.0, ((0, 4),))
    norm2_gain = jnp.clip(1.0 + 0.1 * jax.random.normal(streams_of[6], (D,), jnp.float32), 0.5, 1.5).astype(jnp.bfloat16)
    w_gate = gaussian(streams_of[7], (D, FF), D ** -0.5, 0.25, ((0, 4),))
    w_up = gaussian(streams_of[8], (D, FF), D ** -0.5, 0.25, ((0, 4),))
    w_down = gaussian(streams_of[9], (FF, D), FF ** -0.5, 0.15625, ((0, 4),))
    out_grad = gaussian(streams_of[10], (SEQS, SEQUENCE_TOKENS, D), 1.0, 6.0, ((0, 16), (1, 2)))
    return dict(tokens=tokens, norm1_gain=norm1_gain, w_query=w_query, w_key=w_key, w_value=w_value, w_out=w_out, norm2_gain=norm2_gain, w_gate=w_gate, w_up=w_up, w_down=w_down, out_grad=out_grad)


EPSILON = 1e-05
ROPE_THETA = 100000.0
MASKED = -1e+30
HIGHEST = lax.Precision.HIGHEST

@jax.custom_vjp
def lower_precision(v):
    return lax.optimization_barrier(v.astype(jnp.bfloat16)).astype(jnp.float32)

@jax.custom_vjp
def low_back(v):
    return v

def low_keep(v):
    return (lower_precision(v), None)

def low_pass(kept, grad):
    return (grad,)

def back_keep(v):
    return (v, None)

def back_low(kept, grad):
    return (lower_precision(grad),)
lower_precision.defvjp(low_keep, low_pass)
low_back.defvjp(back_keep, back_low)

def rope_tables(positions):
    half_size = HEAD_SIZE // 2
    inverse = jnp.exp(jnp.arange(half_size, dtype=jnp.float32) * (-2.0 * math.log(ROPE_THETA) / HEAD_SIZE))
    angle = positions.astype(jnp.float32)[:, None] * inverse[None, :]
    return (jnp.cos(angle), jnp.sin(angle))

def rotary_apply(tensor, cosine_table, sine_table):
    half_size = tensor.shape[-1] // 2
    first_half = tensor[..., :half_size]
    second_half = tensor[..., half_size:]
    cosine_table = cosine_table[:, None, :]
    sine_table = sine_table[:, None, :]
    return jnp.concatenate([first_half * cosine_table - second_half * sine_table, second_half * cosine_table + first_half * sine_table], -1)

def rms_scale(tensor):
    return lax.rsqrt(lax.optimization_barrier(jnp.mean(tensor * tensor, axis=-1, keepdims=True)) + EPSILON)

def attend_block(begin, query_block, key_row_block, value_row_block):
    block_extent = query_block.shape[0]
    scores = jnp.einsum('qhrd,khd->hrqk', query_block, key_row_block, precision=HIGHEST) * 0.125
    scores = low_back(scores)
    query_pos = begin + jnp.arange(block_extent, dtype=jnp.int32)
    key_pos = jnp.arange(SEQUENCE_TOKENS, dtype=jnp.int32)
    visible = key_pos[None, :] <= query_pos[:, None]
    scores = jnp.where(visible, scores, MASKED)
    probs = lower_precision(jax.nn.softmax(scores, axis=-1))
    mixed = jnp.einsum('hrqk,khd->qhrd', probs, value_row_block, precision=HIGHEST)
    return lower_precision(low_back(mixed))

def layer(inputs, gain1, w_query, w_key, w_value, w_out, gain2, w_gate, w_up, w_down):
    repeat_heads = QUERY_HEADS // KEY_VALUE_HEADS
    cosine_table, sine_table = rope_tables(jnp.arange(SEQUENCE_TOKENS, dtype=jnp.int32))
    normed1 = lower_precision(inputs * rms_scale(inputs) * gain1)
    query_before_rotation = low_back(jnp.dot(normed1, w_query, precision=HIGHEST))
    key_before_rotation = low_back(jnp.dot(normed1, w_key, precision=HIGHEST))
    value_projected = lower_precision(low_back(jnp.dot(normed1, w_value, precision=HIGHEST)))
    query_matrix = lower_precision(rotary_apply(query_before_rotation.reshape(SEQUENCE_TOKENS, QUERY_HEADS, HEAD_SIZE), cosine_table, sine_table)).reshape(SEQUENCE_TOKENS, KEY_VALUE_HEADS, repeat_heads, HEAD_SIZE)
    key_row_block = lower_precision(rotary_apply(key_before_rotation.reshape(SEQUENCE_TOKENS, KEY_VALUE_HEADS, HEAD_SIZE), cosine_table, sine_table))
    value_row_block = value_projected.reshape(SEQUENCE_TOKENS, KEY_VALUE_HEADS, HEAD_SIZE)
    block_extent = min(SEQUENCE_TOKENS, 512)
    block_list = SEQUENCE_TOKENS // block_extent
    starts = jnp.arange(block_list, dtype=jnp.int32) * block_extent
    query_block_list = query_matrix.reshape(block_list, block_extent, KEY_VALUE_HEADS, repeat_heads, HEAD_SIZE)
    saved_block = jax.checkpoint(attend_block)

    def one_block(item):
        return saved_block(item[0], item[1], key_row_block, value_row_block)
    attended = lax.map(one_block, (starts, query_block_list)).reshape(SEQUENCE_TOKENS, QUERY_HEADS * HEAD_SIZE)
    branch = low_back(jnp.dot(attended, w_out, precision=HIGHEST))
    middle = inputs + branch
    normed2 = lower_precision(middle * rms_scale(middle) * gain2)
    gate_act = low_back(jnp.dot(normed2, w_gate, precision=HIGHEST))
    up_act = low_back(jnp.dot(normed2, w_up, precision=HIGHEST))
    hidden = lower_precision(jax.nn.silu(gate_act) * up_act)
    mlp_out = low_back(jnp.dot(hidden, w_down, precision=HIGHEST))
    return middle + mlp_out

def reference(tokens, norm1_gain, w_query, w_key, w_value, w_out, norm2_gain, w_gate, w_up, w_down, out_grad):
    params = tuple((weight.astype(jnp.float32) for weight in (norm1_gain, w_query, w_key, w_value, w_out, norm2_gain, w_gate, w_up, w_down)))

    def per_sequence(totals, item):
        sequence, cotangent = item
        value, pullback = jax.vjp(layer, sequence.astype(jnp.float32), *params)
        grads = pullback(cotangent.astype(jnp.float32))
        totals = tuple((total + grad for total, grad in zip(totals, grads[1:])))
        return (totals, (value.astype(jnp.bfloat16), grads[0]))
    zero_filled = tuple((jnp.zeros_like(weight) for weight in params))
    totals, results = lax.scan(per_sequence, zero_filled, (tokens, out_grad))
    return (results[0], results[1], totals[0], totals[1], totals[2], totals[3], totals[4], totals[5], totals[6], totals[7], totals[8])
```

```python
import functools
import math

import jax
import jax.numpy as jnp
from jax import lax
from jax.experimental import pallas as pl
from jax.experimental.pallas import tpu as pltpu
from jax.sharding import PartitionSpec as P

QUERY_HEADS = 9
KEY_VALUE_HEADS = 3
HEAD_SIZE = 64


EPSILON = 1e-05
ROPE_THETA = 100000.0
MASKED = -1e30


def rope_tables(positions, head_width):
    half_size = head_width // 2
    inverse = jnp.exp(
        jnp.arange(half_size, dtype=jnp.float32) * (-2.0 * math.log(ROPE_THETA) / head_width)
    )
    angle = positions.astype(jnp.float32)[:, None] * inverse[None, :]
    return (jnp.cos(angle), jnp.sin(angle))


def rotary_apply(tensor, cosine_table, sine_table):
    half_size = tensor.shape[-1] // 2
    first_half = tensor[..., :half_size]
    second_half = tensor[..., half_size:]
    cosine_table = cosine_table[None, :, None, :]
    sine_table = sine_table[None, :, None, :]
    return jnp.concatenate(
        [
            first_half * cosine_table - second_half * sine_table,
            second_half * cosine_table + first_half * sine_table,
        ],
        -1,
    )


def rotate_back(tensor, cosine_table, sine_table):
    half_size = tensor.shape[-1] // 2
    first_half = tensor[..., :half_size]
    second_half = tensor[..., half_size:]
    cosine_table = cosine_table[None, :, None, :]
    sine_table = sine_table[None, :, None, :]
    return jnp.concatenate(
        [
            first_half * cosine_table + second_half * sine_table,
            second_half * cosine_table - first_half * sine_table,
        ],
        -1,
    )


def rms_scale(tensor):
    return lax.rsqrt(jnp.mean(tensor * tensor, axis=-1, keepdims=True) + EPSILON)


def block_scores(query_block, key_block, query_pos, key_pos):
    scores = (
        jnp.einsum("gqhrd,gkhd->ghrqk", query_block, key_block, preferred_element_type=jnp.float32)
        * 0.125
    )
    visible = key_pos[None, :] <= query_pos[:, None]
    return jnp.where(visible, scores, MASKED)


def split_context(
    tokens, norm1_gain, w_query, w_key, w_value, w_out, norm2_gain, w_gate, w_up, w_down, out_grad
):
    gain1, wq_full, wk_full, wv_full, wo_full, gain2, wg_full, wu_full, wd_full = (
        lax.all_gather(norm1_gain, "fsdp", axis=0, tiled=True),
        lax.all_gather(w_query, "fsdp", axis=0, tiled=True),
        lax.all_gather(w_key, "fsdp", axis=0, tiled=True),
        lax.all_gather(w_value, "fsdp", axis=0, tiled=True),
        lax.all_gather(w_out, "fsdp", axis=0, tiled=True),
        lax.all_gather(norm2_gain, "fsdp", axis=0, tiled=True),
        lax.all_gather(w_gate, "fsdp", axis=0, tiled=True),
        lax.all_gather(w_up, "fsdp", axis=0, tiled=True),
        lax.all_gather(w_down, "fsdp", axis=0, tiled=True),
    )
    query_group_count, local_row_count, model_width = tokens.shape
    repeat_heads = QUERY_HEADS // KEY_VALUE_HEADS
    head_width = HEAD_SIZE
    key_value_width = KEY_VALUE_HEADS * HEAD_SIZE
    query_width = QUERY_HEADS * HEAD_SIZE
    first_row = lax.axis_index("ctx") * local_row_count
    last_row = first_row + local_row_count - 1
    positions = first_row + jnp.arange(local_row_count, dtype=jnp.int32)
    cosine_table, sine_table = rope_tables(positions, head_width)
    gain1f = gain1.astype(jnp.float32)
    gain2f = gain2.astype(jnp.float32)
    inputs = tokens.astype(jnp.float32)
    scale1 = rms_scale(inputs)
    normed1 = (inputs * scale1 * gain1f).astype(jnp.bfloat16)
    query_before_rotation = jnp.einsum(
        "gsd,de->gse", normed1, wq_full, preferred_element_type=jnp.float32
    )
    key_before_rotation = jnp.einsum(
        "gsd,de->gse", normed1, wk_full, preferred_element_type=jnp.float32
    )
    value_projected = jnp.einsum(
        "gsd,de->gse", normed1, wv_full, preferred_element_type=jnp.float32
    )
    query_matrix = rotary_apply(
        query_before_rotation.reshape(query_group_count, local_row_count, QUERY_HEADS, head_width),
        cosine_table,
        sine_table,
    ).astype(jnp.bfloat16)
    query_matrix = query_matrix.reshape(
        query_group_count, local_row_count, KEY_VALUE_HEADS, repeat_heads, head_width
    )
    key_local = rotary_apply(
        key_before_rotation.reshape(
            query_group_count, local_row_count, KEY_VALUE_HEADS, head_width
        ),
        cosine_table,
        sine_table,
    ).astype(jnp.bfloat16)
    local_value_rows = value_projected.astype(jnp.bfloat16)
    collected_keys, collected_values = (
        lax.all_gather(
            key_local.reshape(query_group_count, local_row_count, key_value_width),
            "ctx",
            axis=1,
            tiled=True,
        ),
        lax.all_gather(local_value_rows, "ctx", axis=1, tiled=True),
    )
    sequence_length = collected_keys.shape[1]
    every_key_row = collected_keys.reshape(
        query_group_count, sequence_length, KEY_VALUE_HEADS, head_width
    )
    every_value_row = collected_values.reshape(
        query_group_count, sequence_length, KEY_VALUE_HEADS, head_width
    )
    local_value_rows = local_value_rows.reshape(
        query_group_count, local_row_count, KEY_VALUE_HEADS, head_width
    )
    key_span = min(sequence_length, 512)
    block_total = last_row // key_span + 1

    def key_slices(step_index):
        first_key = step_index * key_span
        key_block = lax.dynamic_slice_in_dim(every_key_row, first_key, key_span, 1)
        value_block = lax.dynamic_slice_in_dim(every_value_row, first_key, key_span, 1)
        key_pos = first_key + jnp.arange(key_span, dtype=jnp.int32)
        return (key_block, value_block, key_pos)

    def stats_step(step_index, running):
        row_max, row_sum = running
        key_block, value_block, key_pos = key_slices(step_index)
        scores = block_scores(query_matrix, key_block, positions, key_pos)
        new_max = jnp.maximum(row_max, jnp.max(scores, axis=-1))
        row_sum = row_sum * jnp.exp(row_max - new_max) + jnp.sum(
            jnp.exp(scores - new_max[..., None]), axis=-1
        )
        return (new_max, row_sum)

    statistics_shape = (query_group_count, KEY_VALUE_HEADS, repeat_heads, local_row_count)
    row_max, row_sum = lax.fori_loop(
        0,
        block_total,
        stats_step,
        (jnp.full(statistics_shape, MASKED, jnp.float32), jnp.zeros(statistics_shape, jnp.float32)),
    )
    log_total = row_max + jnp.log(row_sum)

    def mix_step(step_index, running):
        key_block, value_block, key_pos = key_slices(step_index)
        scores = block_scores(query_matrix, key_block, positions, key_pos)
        probs = jnp.exp(scores - log_total[..., None]).astype(jnp.bfloat16)
        return running + jnp.einsum(
            "ghrqk,gkhd->gqhrd", probs, value_block, preferred_element_type=jnp.float32
        )

    attended_full = lax.fori_loop(
        0,
        block_total,
        mix_step,
        jnp.zeros(
            (query_group_count, local_row_count, KEY_VALUE_HEADS, repeat_heads, head_width),
            jnp.float32,
        ),
    )
    attended = attended_full.astype(jnp.bfloat16).reshape(
        query_group_count, local_row_count, query_width
    )
    branch = jnp.einsum("gse,ed->gsd", attended, wo_full, preferred_element_type=jnp.float32)
    middle = inputs + branch
    scale2 = rms_scale(middle)
    normed2 = (middle * scale2 * gain2f).astype(jnp.bfloat16)
    gate_act = jnp.einsum("gsd,df->gsf", normed2, wg_full, preferred_element_type=jnp.float32)
    up_act = jnp.einsum("gsd,df->gsf", normed2, wu_full, preferred_element_type=jnp.float32)
    gate_sig = jax.nn.sigmoid(gate_act)
    gate_silu = gate_act * gate_sig
    hidden = (gate_silu * up_act).astype(jnp.bfloat16)
    mlp_out = jnp.einsum("gsf,fd->gsd", hidden, wd_full, preferred_element_type=jnp.float32)
    output = (middle + mlp_out).astype(jnp.bfloat16)
    out_float = out_grad.astype(jnp.float32)
    grad_down = jnp.einsum("gsf,gsd->fd", hidden, out_grad, preferred_element_type=jnp.float32)
    hidden_grad = jnp.einsum("gsd,fd->gsf", out_grad, wd_full, preferred_element_type=jnp.float32)
    gate_grad = (hidden_grad * up_act * gate_sig * (1.0 + gate_act * (1.0 - gate_sig))).astype(
        jnp.bfloat16
    )
    up_grad = (hidden_grad * gate_silu).astype(jnp.bfloat16)
    grad_gate = jnp.einsum("gsd,gsf->df", normed2, gate_grad, preferred_element_type=jnp.float32)
    grad_up = jnp.einsum("gsd,gsf->df", normed2, up_grad, preferred_element_type=jnp.float32)
    normed2_grad = jnp.einsum("gsf,df->gsd", gate_grad, wg_full, preferred_element_type=jnp.float32)
    normed2_grad = normed2_grad + jnp.einsum(
        "gsf,df->gsd", up_grad, wu_full, preferred_element_type=jnp.float32
    )
    grad_gain2 = jnp.sum(normed2_grad * middle * scale2, axis=(0, 1))
    scaled2 = gain2f * normed2_grad
    middle_grad = (
        out_float
        + scale2 * scaled2
        - middle * scale2**3 * jnp.mean(scaled2 * middle, axis=-1, keepdims=True)
    )
    branch_grad = middle_grad.astype(jnp.bfloat16)
    grad_out = jnp.einsum("gse,gsd->ed", attended, branch_grad, preferred_element_type=jnp.float32)
    attended_output_gradient = jnp.einsum(
        "gsd,ed->gse", branch_grad, wo_full, preferred_element_type=jnp.float32
    ).astype(jnp.bfloat16)
    attention_gradient = attended_output_gradient.reshape(
        query_group_count, local_row_count, KEY_VALUE_HEADS, repeat_heads, head_width
    )
    delta = jnp.sum(attention_gradient.astype(jnp.float32) * attended_full, axis=-1).transpose(
        0, 2, 3, 1
    )

    def query_grad_step(step_index, running):
        key_block, value_block, key_pos = key_slices(step_index)
        scores = block_scores(query_matrix, key_block, positions, key_pos)
        probs = jnp.exp(scores - log_total[..., None])
        dprob = jnp.einsum(
            "gqhrd,gkhd->ghrqk", attention_gradient, value_block, preferred_element_type=jnp.float32
        )
        score_grad = (probs * (dprob - delta[..., None])).astype(jnp.bfloat16)
        return running + jnp.einsum(
            "ghrqk,gkhd->gqhrd", score_grad, key_block, preferred_element_type=jnp.float32
        )

    query_grad = (
        lax.fori_loop(
            0,
            block_total,
            query_grad_step,
            jnp.zeros(
                (query_group_count, local_row_count, KEY_VALUE_HEADS, repeat_heads, head_width),
                jnp.float32,
            ),
        )
        * 0.125
    )
    row_total = local_row_count * lax.axis_size("ctx")
    term_span = math.gcd(row_total, key_span)

    def key_block_term(step_index):
        first_key = step_index * term_span
        key_block = lax.dynamic_slice_in_dim(every_key_row, first_key, term_span, 1)
        value_block = lax.dynamic_slice_in_dim(every_value_row, first_key, term_span, 1)
        key_pos = first_key + jnp.arange(term_span, dtype=jnp.int32)

        def compute_term(unused):
            scores = block_scores(query_matrix, key_block, positions, key_pos)
            probs = jnp.exp(scores - log_total[..., None])
            dprob = jnp.einsum(
                "gqhrd,gkhd->ghrqk",
                attention_gradient,
                value_block,
                preferred_element_type=jnp.float32,
            )
            score_grad = (probs * (dprob - delta[..., None])).astype(jnp.bfloat16)
            key_term = (
                jnp.einsum(
                    "ghrqk,gqhrd->kghd",
                    score_grad,
                    query_matrix,
                    preferred_element_type=jnp.float32,
                )
                * 0.125
            )
            value_term = jnp.einsum(
                "ghrqk,gqhrd->kghd",
                probs.astype(jnp.bfloat16),
                attention_gradient,
                preferred_element_type=jnp.float32,
            )
            return jnp.concatenate(
                [
                    key_term.reshape(term_span, query_group_count, key_value_width),
                    value_term.reshape(term_span, query_group_count, key_value_width),
                ],
                -1,
            )

        def empty_term(unused):
            return jnp.zeros((term_span, query_group_count, 2 * key_value_width), jnp.float32)

        return lax.cond(first_key <= last_row, compute_term, empty_term, 0)

    terms = lax.map(key_block_term, jnp.arange(row_total // term_span, dtype=jnp.int32))
    paired_gradients = (
        lax.psum_scatter(
            terms.reshape(row_total, query_group_count, 2 * key_value_width).astype(jnp.bfloat16),
            "ctx",
            scatter_dimension=0,
            tiled=True,
        )
        .astype(jnp.float32)
        .transpose(1, 0, 2)
    )
    key_gradient = paired_gradients[..., :key_value_width].reshape(
        query_group_count, local_row_count, KEY_VALUE_HEADS, head_width
    )
    value_gradient = paired_gradients[..., key_value_width:].reshape(
        query_group_count, local_row_count, KEY_VALUE_HEADS, head_width
    )
    query_pre_grad = rotate_back(
        query_grad.reshape(query_group_count, local_row_count, QUERY_HEADS, head_width),
        cosine_table,
        sine_table,
    )
    query_pre_grad = query_pre_grad.astype(jnp.bfloat16).reshape(
        query_group_count, local_row_count, query_width
    )
    key_pre_grad = (
        rotate_back(key_gradient, cosine_table, sine_table)
        .astype(jnp.bfloat16)
        .reshape(query_group_count, local_row_count, key_value_width)
    )
    value_pre_grad = value_gradient.astype(jnp.bfloat16).reshape(
        query_group_count, local_row_count, key_value_width
    )
    grad_query = jnp.einsum(
        "gsd,gse->de", normed1, query_pre_grad, preferred_element_type=jnp.float32
    )
    grad_key = jnp.einsum("gsd,gse->de", normed1, key_pre_grad, preferred_element_type=jnp.float32)
    grad_value = jnp.einsum(
        "gsd,gse->de", normed1, value_pre_grad, preferred_element_type=jnp.float32
    )
    normed1_grad = jnp.einsum(
        "gse,de->gsd", query_pre_grad, wq_full, preferred_element_type=jnp.float32
    )
    normed1_grad = normed1_grad + jnp.einsum(
        "gse,de->gsd", key_pre_grad, wk_full, preferred_element_type=jnp.float32
    )
    normed1_grad = normed1_grad + jnp.einsum(
        "gse,de->gsd", value_pre_grad, wv_full, preferred_element_type=jnp.float32
    )
    grad_gain1 = jnp.sum(normed1_grad * inputs * scale1, axis=(0, 1))
    scaled1 = gain1f * normed1_grad
    input_grad = (
        middle_grad
        + scale1 * scaled1
        - inputs * scale1**3 * jnp.mean(scaled1 * inputs, axis=-1, keepdims=True)
    )
    totals = lax.psum(
        (
            grad_gain1,
            grad_query,
            grad_key,
            grad_value,
            grad_out,
            grad_gain2,
            grad_gate,
            grad_up,
            grad_down,
        ),
        ("dp", "ctx", "fsdp"),
    )
    owner = lax.axis_index("fsdp")
    shards = (norm1_gain, w_query, w_key, w_value, w_out, norm2_gain, w_gate, w_up, w_down)
    shares = tuple(
        (
            lax.dynamic_slice_in_dim(summed, owner * shard.shape[0], shard.shape[0], 0)
            for summed, shard in zip(totals, shards)
        )
    )
    return (
        output,
        input_grad,
        shares[0],
        shares[1],
        shares[2],
        shares[3],
        shares[4],
        shares[5],
        shares[6],
        shares[7],
        shares[8],
    )


WIDTH = 576
QUERY_WIDTH = QUERY_HEADS * HEAD_SIZE
KEY_WIDTH = KEY_VALUE_HEADS * HEAD_SIZE
ROTATED = QUERY_HEADS + KEY_VALUE_HEADS
REPEAT = QUERY_HEADS // KEY_VALUE_HEADS
HALF = HEAD_SIZE // 2
PACKED = QUERY_WIDTH + 2 * KEY_WIDTH + 64
GAIN_AT = QUERY_WIDTH + 2 * KEY_WIDTH - (PACKED - 128)
TILE = 256
VMEM_LIMIT = 52 * 1024 * 1024
F32 = jnp.float32
BF16 = jnp.bfloat16


def mm(a, b):
    return jnp.dot(a, b, preferred_element_type=F32)


def mm_nt(a, b):
    return lax.dot_general(a, b, (((1,), (1,)), ((), ())), preferred_element_type=F32)


def flip(tensor):
    return tensor.astype(F32).T


def rows_at(index, size):
    return pl.ds(pl.multiple_of(index * size, size), size)


def attend_kernel(
    place,
    mine,
    theirs,
    w_own,
    w_y,
    w_core,
    w_both,
    cosine,
    sine,
    x_seq,
    normed,
    packed,
    gains,
    qkv_t,
    log_total,
    attended_t,
    key_rows,
):
    me, shard = place[0], place[1]
    half_rows = mine.shape[0]
    sequence = 2 * half_rows
    x_seq[rows_at(me, half_rows), :] = mine[...]
    x_seq[rows_at(1 - me, half_rows), :] = theirs[...]
    rows = w_own.shape[0]
    for bits, piece in ((0, w_own), (2, w_y), (1, w_core), (3, w_both)):
        packed[rows_at(shard ^ bits, rows), :] = piece[...]
    gain_rows = flip(packed[:, PACKED - 128 :])
    gains[...] = gain_rows[GAIN_AT : GAIN_AT + 8, :]
    gain1 = gain_rows[GAIN_AT : GAIN_AT + 1, :]

    def project(tile, carry):
        at = rows_at(tile, TILE)
        x = x_seq[at, :].astype(F32)
        scale = lax.rsqrt(jnp.mean(x * x, axis=-1, keepdims=True) + EPSILON)
        normed_tile = (x * scale * gain1).astype(BF16)
        normed[at, :] = normed_tile
        turned = mm(normed_tile, packed[...]).T
        cos, sin = cosine[:, at], sine[:, at]
        for head in range(ROTATED):
            a = turned[head * HEAD_SIZE : head * HEAD_SIZE + HALF, :]
            b = turned[head * HEAD_SIZE + HALF : (head + 1) * HEAD_SIZE, :]
            both = jnp.concatenate([a * cos - b * sin, b * cos + a * sin], 0)
            if head < QUERY_HEADS:
                both = both * 0.125
            else:
                key_rows[head - QUERY_HEADS, at, :] = both.T.astype(BF16)
            qkv_t[head * HEAD_SIZE : (head + 1) * HEAD_SIZE, at] = both.astype(BF16)
        values = turned[ROTATED * HEAD_SIZE : ROTATED * HEAD_SIZE + KEY_WIDTH, :]
        qkv_t[ROTATED * HEAD_SIZE :, at] = values.astype(BF16)
        return carry

    lax.fori_loop(0, sequence // TILE, project, 0)

    def one_head(head, carry):
        group = head // REPEAT
        head_rows = rows_at(head, HEAD_SIZE)
        value_rows = rows_at(ROTATED + group, HEAD_SIZE)
        for tile in range(sequence // TILE):
            extent = (tile + 1) * TILE
            cols = slice(tile * TILE, extent)
            queries = qkv_t[head_rows, cols]
            scores = mm(key_rows[group, :extent, :], queries)
            visible = lax.broadcasted_iota(jnp.int32, (TILE, TILE), 0) <= lax.broadcasted_iota(
                jnp.int32, (TILE, TILE), 1
            )
            last = jnp.where(visible, scores[tile * TILE :, :], MASKED)
            scores = last if tile == 0 else jnp.concatenate([scores[: tile * TILE, :], last], 0)
            top = jnp.max(scores, axis=0, keepdims=True)
            weights = jnp.exp(scores - top)
            total = jnp.sum(weights, axis=0, keepdims=True)
            mixed = mm(qkv_t[value_rows, :extent], weights.astype(BF16))
            attended_t[head_rows, cols] = (mixed * (1.0 / total)).astype(BF16)
            log_total[group, pl.ds(head - group * REPEAT, 1), cols] = top + jnp.log(total)
        return carry

    lax.fori_loop(0, QUERY_HEADS, one_head, 0)


def feed_forward_kernel(
    place,
    x_seq,
    attended_t,
    dy_mine,
    dy_theirs,
    gains,
    a_own,
    a_y,
    a_core,
    a_both,
    b_own,
    b_y,
    b_core,
    b_both,
    out_keep,
    out_send,
    middle_grad_out,
    attended_grad_t,
    keep_b,
    send_b,
    keep_a,
    send_a,
    gain_grad,
    w_out,
    w_down,
    w_gate,
    w_up,
    dy_seq,
    out_seq,
    normed_t,
    hidden,
    gate_grad,
    up_grad,
    branch_grad,
    total,
    total_tall,
):
    me, shard = place[0], place[1]
    half_rows = dy_mine.shape[0]
    sequence = 2 * half_rows
    dy_seq[rows_at(me, half_rows), :] = dy_mine[...]
    dy_seq[rows_at(1 - me, half_rows), :] = dy_theirs[...]
    rows = b_own.shape[0] // 2
    down_rows = a_own.shape[0] - rows
    for bits, a, b in ((0, a_own, b_own), (2, a_y, b_y), (1, a_core, b_core), (3, a_both, b_both)):
        w_out[rows_at(shard ^ bits, rows), :] = a[:rows, :]
        w_down[rows_at(shard ^ bits, down_rows), :] = a[rows:, :]
        w_gate[rows_at(shard ^ bits, rows), :] = b[:rows, :]
        w_up[rows_at(shard ^ bits, rows), :] = b[rows:, :]
    gain2 = gains[1:2, :]
    gain_grad[...] = jnp.zeros_like(gain_grad)

    def one_tile(tile, carry):
        at = rows_at(tile, TILE)
        attended = flip(attended_t[:, at]).astype(BF16)
        middle = x_seq[at, :].astype(F32) + mm(attended, w_out[...])
        scale = lax.rsqrt(jnp.mean(middle * middle, axis=-1, keepdims=True) + EPSILON)
        ready = middle * scale
        normed = ready * gain2
        normed_t[:, at] = normed.T.astype(BF16)
        normed = normed.astype(BF16)
        gate = mm(normed, w_gate[...])
        up = mm(normed, w_up[...])
        sig = 1.0 / (1.0 + jnp.exp(-gate))
        silu = gate * sig
        hidden_tile = (silu * up).astype(BF16)
        hidden[at, :] = hidden_tile
        out_seq[at, :] = (middle + mm(hidden_tile, w_down[...])).astype(BF16)
        dy = dy_seq[at, :]
        hidden_grad = mm_nt(dy, w_down[...])
        gate_tile = (hidden_grad * up * sig * (1.0 + gate * (1.0 - sig))).astype(BF16)
        up_tile = (hidden_grad * silu).astype(BF16)
        gate_grad[at, :] = gate_tile
        up_grad[at, :] = up_tile
        normed_grad = mm_nt(gate_tile, w_gate[...]) + mm_nt(up_tile, w_up[...])
        gain_grad[0:1, :] += jnp.sum(normed_grad * ready, axis=0, keepdims=True)
        scaled = normed_grad * gain2
        middle_grad = (
            dy.astype(F32)
            + scale * scaled
            - middle * (scale * scale * scale) * jnp.mean(scaled * middle, axis=-1, keepdims=True)
        )
        middle_grad_out[at, :] = middle_grad
        branch = middle_grad.astype(BF16)
        branch_grad[at, :] = branch
        attended_grad_t[:, at] = mm_nt(branch, w_out[...]).T.astype(BF16)
        return carry

    lax.fori_loop(0, sequence // TILE, one_tile, 0)
    out_keep[...] = out_seq[rows_at(me, half_rows), :]
    out_send[...] = out_seq[rows_at(1 - me, half_rows), :]
    wide = gate_grad.shape[1]
    for part, grads in ((0, gate_grad), (1, up_grad)):
        for first in range(0, wide, 512):
            cols = slice(first, min(first + 512, wide))
            total[:, cols] = mm(normed_t[...], grads[:, cols]).astype(BF16)
        at = slice(part * rows, (part + 1) * rows)
        for y_bit in range(2):
            keep_b[y_bit, at, :] = total[rows_at(shard ^ (2 * y_bit), rows), :]
            send_b[y_bit, at, :] = total[rows_at(shard ^ (2 * y_bit + 1), rows), :]
    for first in range(0, wide, 512):
        cols = slice(first, min(first + 512, wide))
        total_tall[cols, :] = mm(flip(hidden[:, cols]).astype(BF16), dy_seq[...]).astype(BF16)
    for y_bit in range(2):
        keep_a[y_bit, rows:, :] = total_tall[rows_at(shard ^ (2 * y_bit), down_rows), :]
        send_a[y_bit, rows:, :] = total_tall[rows_at(shard ^ (2 * y_bit + 1), down_rows), :]
    total[:, :QUERY_WIDTH] = mm(attended_t[...], branch_grad[...]).astype(BF16)
    for y_bit in range(2):
        keep_a[y_bit, :rows, :] = total[rows_at(shard ^ (2 * y_bit), rows), :QUERY_WIDTH]
        send_a[y_bit, :rows, :] = total[rows_at(shard ^ (2 * y_bit + 1), rows), :QUERY_WIDTH]


def attend_back_kernel(
    queries_t,
    keys_t,
    values_t,
    log_total,
    attended_t,
    grad_t,
    cosine,
    sine,
    dq_out,
    dk_out,
    dv_out,
    keys,
    values,
    dk,
    dv,
    dq,
):
    sequence = keys_t.shape[1]
    keys[...] = flip(keys_t[...]).astype(BF16)
    values[...] = flip(values_t[...]).astype(BF16)
    dk[...] = jnp.zeros_like(dk)
    dv[...] = jnp.zeros_like(dv)

    def back(a, b, cos, sin):
        return (a * cos + b * sin).astype(BF16), (b * cos - a * sin).astype(BF16)

    def one_head(head, carry):
        head_rows = rows_at(head, HEAD_SIZE)
        for tile in range(sequence // TILE):
            extent = (tile + 1) * TILE
            cols = slice(tile * TILE, extent)
            q_t = queries_t[head_rows, cols]
            do_t = grad_t[head_rows, cols]
            do_wide = do_t.astype(F32)
            delta = jnp.sum(
                do_wide * attended_t[head_rows, cols].astype(F32), axis=0, keepdims=True
            )
            scores = mm(keys[:extent, :], q_t)
            visible = lax.broadcasted_iota(jnp.int32, (TILE, TILE), 0) <= lax.broadcasted_iota(
                jnp.int32, (TILE, TILE), 1
            )
            last = jnp.where(visible, scores[tile * TILE :, :], MASKED)
            scores = last if tile == 0 else jnp.concatenate([scores[: tile * TILE, :], last], 0)
            probs = jnp.exp(scores - log_total[0, pl.ds(head, 1), cols])
            dprob = mm(values[:extent, :], do_t)
            score_grad = (probs * (dprob - delta)).astype(BF16)
            dv[:extent, :] += mm(probs.astype(BF16), do_wide.T.astype(BF16))
            dk[:extent, :] += mm(score_grad, flip(q_t).astype(BF16))
            dq[:, cols] = mm(keys_t[:, :extent], score_grad) * 0.125
        cos, sin = cosine[...], sine[...]
        a, b = back(dq[:HALF, :], dq[HALF:, :], cos, sin)
        dq_out[pl.ds(pl.multiple_of(head * HEAD_SIZE, HEAD_SIZE), HALF), :] = a
        dq_out[pl.ds(pl.multiple_of(head * HEAD_SIZE + HALF, HALF), HALF), :] = b
        return carry

    lax.fori_loop(0, queries_t.shape[0] // HEAD_SIZE, one_head, 0)
    turned = dk[...].T
    a, b = back(turned[:HALF, :], turned[HALF:, :], cosine[...], sine[...])
    dk_out[:HALF, :] = a
    dk_out[HALF:, :] = b
    dv_out[...] = dv[...].T.astype(BF16)


def input_kernel(
    place,
    x_seq,
    normed,
    packed,
    gains,
    gain2_grad,
    middle_grad,
    *rest,
):
    heads = rest[: 3 * KEY_VALUE_HEADS]
    keep_w, send_w, keep_x, send_x, joined, grad_seq, total = rest[3 * KEY_VALUE_HEADS :]
    me, shard = place[0], place[1]
    half_rows = keep_x.shape[0]
    sequence = 2 * half_rows
    group_width = REPEAT * HEAD_SIZE
    for group in range(KEY_VALUE_HEADS):
        dq, dk, dv = heads[3 * group : 3 * group + 3]
        joined[group * group_width : (group + 1) * group_width, :] = dq[...]
        at = QUERY_WIDTH + group * HEAD_SIZE
        joined[at : at + HEAD_SIZE, :] = dk[...]
        at = QUERY_WIDTH + KEY_WIDTH + group * HEAD_SIZE
        joined[at : at + HEAD_SIZE, :] = dv[...]
    joined[QUERY_WIDTH + 2 * KEY_WIDTH :, :] = jnp.zeros(
        (PACKED - QUERY_WIDTH - 2 * KEY_WIDTH, sequence), BF16
    )
    gain1 = gains[0:1, :]
    gain1_grad = jnp.zeros((1, WIDTH), F32)
    for tile in range(sequence // TILE):
        at = slice(tile * TILE, (tile + 1) * TILE)
        normed_grad = mm(packed[...], joined[:, at]).T
        x = x_seq[at, :].astype(F32)
        scale = lax.rsqrt(jnp.mean(x * x, axis=-1, keepdims=True) + EPSILON)
        gain1_grad += jnp.sum(normed_grad * x * scale, axis=0, keepdims=True)
        scaled = normed_grad * gain1
        grad_seq[at, :] = (
            middle_grad[at, :]
            + scale * scaled
            - x * (scale * scale * scale) * jnp.mean(scaled * x, axis=-1, keepdims=True)
        )
    keep_x[...] = grad_seq[rows_at(me, half_rows), :]
    send_x[...] = grad_seq[rows_at(1 - me, half_rows), :].astype(BF16)
    for first in range(0, PACKED, TILE):
        at = slice(first, first + TILE)
        total[:, at] = mm(joined[at, :], normed[...]).T.astype(BF16)
    row = lax.broadcasted_iota(jnp.int32, (128, WIDTH), 0)
    gain_rows = jnp.where(row == GAIN_AT, gain1_grad, 0.0) + jnp.where(
        row == GAIN_AT + 1, gain2_grad[0:1, :], 0.0
    )
    lane = lax.broadcasted_iota(jnp.int32, (WIDTH, 128), 1)
    last = total[:, PACKED - 128 :].astype(F32)
    total[:, PACKED - 128 :] = jnp.where(lane < GAIN_AT, last, gain_rows.T).astype(BF16)
    rows = keep_w.shape[1]
    for y_bit in range(2):
        keep_w[y_bit] = total[rows_at(shard ^ (2 * y_bit), rows), :]
        send_w[y_bit] = total[rows_at(shard ^ (2 * y_bit + 1), rows), :]


def call(kernel, out, scratch, flops, exps, args, name):
    shapes = [jax.ShapeDtypeStruct(s, d) for s, d in out]
    moved = sum(a.size * a.dtype.itemsize for a in args[1:]) + sum(
        s.size * s.dtype.itemsize for s in shapes
    )
    in_specs = [pl.BlockSpec(memory_space=pltpu.SMEM)] + [
        pl.BlockSpec(memory_space=pltpu.VMEM)
    ] * (len(args) - 1)
    return pl.pallas_call(
        kernel,
        out_shape=shapes,
        in_specs=in_specs,
        out_specs=[pl.BlockSpec(memory_space=pltpu.VMEM)] * len(shapes),
        scratch_shapes=[pltpu.VMEM(s, d) for s, d in scratch],
        compiler_params=pltpu.CompilerParams(vmem_limit_bytes=VMEM_LIMIT),
        cost_estimate=pl.CostEstimate(flops=flops, bytes_accessed=moved, transcendentals=exps),
        name=name,
    )(*args)


def attend_back(group, qkv_t, log_total, attended_t, grad_t, cosine, sine):
    sequence = qkv_t.shape[1]
    group_width = REPEAT * HEAD_SIZE

    def rows_of(size, index):
        return pl.BlockSpec((size, sequence), lambda step: (index, 0))

    flops = 5 * REPEAT * sequence * sequence * HEAD_SIZE * 2
    return pl.pallas_call(
        attend_back_kernel,
        grid=(1,),
        out_shape=[
            jax.ShapeDtypeStruct((group_width, sequence), BF16),
            jax.ShapeDtypeStruct((HEAD_SIZE, sequence), BF16),
            jax.ShapeDtypeStruct((HEAD_SIZE, sequence), BF16),
        ],
        in_specs=[
            rows_of(group_width, group),
            rows_of(HEAD_SIZE, QUERY_HEADS + group),
            rows_of(HEAD_SIZE, ROTATED + group),
            pl.BlockSpec((1, 8, sequence), lambda step: (group, 0, 0)),
            rows_of(group_width, group),
            rows_of(group_width, group),
            rows_of(HALF, 0),
            rows_of(HALF, 0),
        ],
        out_specs=[rows_of(group_width, 0), rows_of(HEAD_SIZE, 0), rows_of(HEAD_SIZE, 0)],
        scratch_shapes=[
            pltpu.VMEM((sequence, HEAD_SIZE), BF16),
            pltpu.VMEM((sequence, HEAD_SIZE), BF16),
            pltpu.VMEM((sequence, HEAD_SIZE), F32),
            pltpu.VMEM((sequence, HEAD_SIZE), F32),
            pltpu.VMEM((HEAD_SIZE, sequence), F32),
        ],
        compiler_params=pltpu.CompilerParams(vmem_limit_bytes=VMEM_LIMIT),
        cost_estimate=pl.CostEstimate(
            flops=flops, bytes_accessed=4_000_000, transcendentals=REPEAT * sequence * sequence
        ),
        name="attend_back",
    )(qkv_t, qkv_t, qkv_t, log_total, attended_t, grad_t, cosine, sine)


def across(tensor, bit):
    return lax.ppermute(tensor, "fsdp", [(i, i ^ bit) for i in range(4)])


def over_context(tensor):
    return lax.ppermute(tensor, "ctx", [(0, 1), (1, 0)])


def after(tensor, *done):
    return lax.optimization_barrier((tensor, *done))[0]


def add(a, b):
    return (a.astype(F32) + b.astype(F32)).astype(BF16)


def sum_line(part):
    size = lax.axis_size("dp")
    at = lax.axis_index("dp")
    middle = size // 2
    for step in range(middle - 1):
        pairs = [(step, step + 1), (size - 1 - step, size - 2 - step)]
        part = add(part, lax.ppermute(part, "dp", pairs))
    part = add(part, lax.ppermute(part, "dp", [(middle - 1, middle), (middle, middle - 1)]))
    for step in range(middle - 2, -1, -1):
        pairs = [(step + 1, step), (size - 2 - step, size - 1 - step)]
        got = lax.ppermute(part, "dp", pairs)
        part = jnp.where((at == step) | (at == size - 1 - step), got, part)
    return part


def reduce_shard(keep, send, axis):
    me = lax.axis_index("ctx")
    pair = add(keep, across(send, 1))
    own = add(pair[0], across(pair[1], 2))
    low, high = jnp.split(own, 2, axis)
    part = add(jnp.where(me == 0, low, high), over_context(jnp.where(me == 0, high, low)))
    part = sum_line(part)
    other = over_context(part)
    return (
        jnp.where(me == 0, part, other).astype(F32),
        jnp.where(me == 0, other, part).astype(F32),
    )


def gather_pieces(own, *done):
    first = after(own, *done) if done else own
    y_piece = across(first, 2)
    return own, y_piece, across(first, 1), across(y_piece, 1)


def whole_sequences(
    tokens, norm1_gain, w_query, w_key, w_value, w_out, norm2_gain, w_gate, w_up, w_down, out_grad
):
    half_rows, width = tokens.shape[1:]
    sequence = 2 * half_rows
    rows = w_query.shape[0]
    down_rows = w_down.shape[0]
    hidden_width = w_gate.shape[1]
    me = lax.axis_index("ctx")
    place = jnp.stack([me, lax.axis_index("fsdp")]).astype(jnp.int32)

    packed = jnp.concatenate(
        [
            w_query,
            w_key,
            w_value,
            norm1_gain[:, None],
            norm2_gain[:, None],
            jnp.zeros((rows, PACKED - QUERY_WIDTH - 2 * KEY_WIDTH - 2), BF16),
        ],
        1,
    )
    packed_pieces = gather_pieces(packed)
    tokens_mine = lax.dynamic_index_in_dim(tokens, me, 0, False)
    tokens_theirs = over_context(lax.dynamic_index_in_dim(tokens, 1 - me, 0, False))
    a_pieces = gather_pieces(jnp.concatenate([w_out, w_down], 0), packed_pieces[1])
    b_pieces = gather_pieces(jnp.concatenate([w_gate, w_up], 0), packed_pieces[1])
    dy_mine = lax.dynamic_index_in_dim(out_grad, me, 0, False)
    dy_theirs = over_context(
        after(lax.dynamic_index_in_dim(out_grad, 1 - me, 0, False), tokens_theirs)
    )

    cosine, sine = rope_tables(jnp.arange(sequence, dtype=jnp.int32), HEAD_SIZE)
    cosine, sine = cosine.T, sine.T

    pairs = sequence * sequence
    x_seq, normed, packed_all, gains, qkv_t, log_total, attended_t = call(
        attend_kernel,
        [
            ((sequence, width), BF16),
            ((sequence, width), BF16),
            ((width, PACKED), BF16),
            ((8, width), F32),
            ((QUERY_WIDTH + 2 * KEY_WIDTH, sequence), BF16),
            ((KEY_VALUE_HEADS, 8, sequence), F32),
            ((QUERY_WIDTH, sequence), BF16),
        ],
        [((KEY_VALUE_HEADS, sequence, HEAD_SIZE), BF16)],
        2 * sequence * width * PACKED + 4 * QUERY_WIDTH * pairs,
        QUERY_HEADS * pairs,
        (place, tokens_mine, tokens_theirs, *packed_pieces, cosine, sine),
        "attend",
    )

    (
        out_keep,
        out_send,
        middle_grad,
        grad_t,
        keep_b,
        send_b,
        keep_a,
        send_a,
        gain2_grad,
    ) = call(
        feed_forward_kernel,
        [
            ((half_rows, width), BF16),
            ((half_rows, width), BF16),
            ((sequence, width), F32),
            ((QUERY_WIDTH, sequence), BF16),
            ((2, 2 * rows, hidden_width), BF16),
            ((2, 2 * rows, hidden_width), BF16),
            ((2, rows + down_rows, width), BF16),
            ((2, rows + down_rows, width), BF16),
            ((8, width), F32),
        ],
        [
            ((QUERY_WIDTH, width), BF16),
            ((hidden_width, width), BF16),
            ((width, hidden_width), BF16),
            ((width, hidden_width), BF16),
            ((sequence, width), BF16),
            ((sequence, width), BF16),
            ((width, sequence), BF16),
            ((sequence, hidden_width), BF16),
            ((sequence, hidden_width), BF16),
            ((sequence, hidden_width), BF16),
            ((sequence, width), BF16),
            ((width, hidden_width), BF16),
            ((hidden_width, width), BF16),
        ],
        2 * sequence * width * (9 * hidden_width + 3 * QUERY_WIDTH),
        sequence * hidden_width,
        (place, x_seq, attended_t, dy_mine, dy_theirs, gains, *a_pieces, *b_pieces),
        "feed_forward",
    )
    out_theirs = over_context(out_send)
    gate_sum, up_sum = reduce_shard(keep_b, send_b, 0)
    a_low, a_high = reduce_shard(keep_a, send_a, 0)
    a_sum = jnp.concatenate([a_low, a_high], 0)

    head_grads = []
    for group in range(KEY_VALUE_HEADS):
        head_grads += attend_back(group, qkv_t, log_total, attended_t, grad_t, cosine, sine)

    keep_w, send_w, keep_x, send_x = call(
        input_kernel,
        [
            ((2, rows, PACKED), BF16),
            ((2, rows, PACKED), BF16),
            ((half_rows, width), F32),
            ((half_rows, width), BF16),
        ],
        [((PACKED, sequence), BF16), ((sequence, width), F32), ((width, PACKED), BF16)],
        4 * sequence * width * PACKED,
        sequence,
        (place, x_seq, normed, packed_all, gains, gain2_grad, middle_grad, *head_grads),
        "input_side",
    )
    x_theirs = over_context(send_x).astype(F32)
    w_sum = jnp.concatenate(reduce_shard(keep_w, send_w, 1), 1)

    def place_halves(keep, got):
        return jnp.where(me == 0, jnp.stack([keep, got]), jnp.stack([got, keep]))

    key_at = QUERY_WIDTH + KEY_WIDTH
    value_at = key_at + KEY_WIDTH
    return (
        place_halves(out_keep, out_theirs),
        place_halves(keep_x, x_theirs),
        w_sum[:, value_at],
        w_sum[:, :QUERY_WIDTH],
        w_sum[:, QUERY_WIDTH:key_at],
        w_sum[:, key_at:value_at],
        a_sum[:rows],
        w_sum[:, value_at + 1],
        gate_sum,
        up_sum,
        a_sum[rows:],
    )


def layer_step(tokens, *rest):
    whole = (
        lax.axis_size("ctx") == 2
        and lax.axis_size("fsdp") == 4
        and lax.axis_size("dp") % 2 == 0
        and tokens.shape[0] == 2
        and tokens.shape[1] % TILE == 0
    )
    return (whole_sequences if whole else split_context)(tokens, *rest)


def solution(mesh):
    return jax.shard_map(
        layer_step,
        mesh=mesh,
        in_specs=(
            P(("dp", "fsdp"), "ctx", None),
            P("fsdp"),
            P("fsdp", None),
            P("fsdp", None),
            P("fsdp", None),
            P("fsdp", None),
            P("fsdp"),
            P("fsdp", None),
            P("fsdp", None),
            P("fsdp", None),
            P(("dp", "fsdp"), "ctx", None),
        ),
        out_specs=(
            P(("dp", "fsdp"), "ctx", None),
            P(("dp", "fsdp"), "ctx", None),
            P("fsdp"),
            P("fsdp", None),
            P("fsdp", None),
            P("fsdp", None),
            P("fsdp", None),
            P("fsdp"),
            P("fsdp", None),
            P("fsdp", None),
            P("fsdp", None),
        ),
        check_vma=False,
    )
```

```python
import functools
import math

import jax
import jax.numpy as jnp
from jax import lax
from jax.experimental import pallas as pl
from jax.experimental.pallas import tpu as pltpu
from jax.sharding import PartitionSpec as P

QUERY_HEADS = 9
KEY_VALUE_HEADS = 3
HEAD_SIZE = 64


EPSILON = 1e-05
ROPE_THETA = 100000.0
MASKED = -1e30


def rope_tables(positions, head_width):
    half_size = head_width // 2
    inverse = jnp.exp(
        jnp.arange(half_size, dtype=jnp.float32) * (-2.0 * math.log(ROPE_THETA) / head_width)
    )
    angle = positions.astype(jnp.float32)[:, None] * inverse[None, :]
    return (jnp.cos(angle), jnp.sin(angle))


def rotary_apply(tensor, cosine_table, sine_table):
    half_size = tensor.shape[-1] // 2
    first_half = tensor[..., :half_size]
    second_half = tensor[..., half_size:]
    cosine_table = cosine_table[None, :, None, :]
    sine_table = sine_table[None, :, None, :]
    return jnp.concatenate(
        [
            first_half * cosine_table - second_half * sine_table,
            second_half * cosine_table + first_half * sine_table,
        ],
        -1,
    )


def rotate_back(tensor, cosine_table, sine_table):
    half_size = tensor.shape[-1] // 2
    first_half = tensor[..., :half_size]
    second_half = tensor[..., half_size:]
    cosine_table = cosine_table[None, :, None, :]
    sine_table = sine_table[None, :, None, :]
    return jnp.concatenate(
        [
            first_half * cosine_table + second_half * sine_table,
            second_half * cosine_table - first_half * sine_table,
        ],
        -1,
    )


def rms_scale(tensor):
    return lax.rsqrt(jnp.mean(tensor * tensor, axis=-1, keepdims=True) + EPSILON)


def block_scores(query_block, key_block, query_pos, key_pos):
    scores = (
        jnp.einsum("gqhrd,gkhd->ghrqk", query_block, key_block, preferred_element_type=jnp.float32)
        * 0.125
    )
    visible = key_pos[None, :] <= query_pos[:, None]
    return jnp.where(visible, scores, MASKED)


def split_context(
    tokens, norm1_gain, w_query, w_key, w_value, w_out, norm2_gain, w_gate, w_up, w_down, out_grad
):
    gain1, wq_full, wk_full, wv_full, wo_full, gain2, wg_full, wu_full, wd_full = (
        lax.all_gather(norm1_gain, "fsdp", axis=0, tiled=True),
        lax.all_gather(w_query, "fsdp", axis=0, tiled=True),
        lax.all_gather(w_key, "fsdp", axis=0, tiled=True),
        lax.all_gather(w_value, "fsdp", axis=0, tiled=True),
        lax.all_gather(w_out, "fsdp", axis=0, tiled=True),
        lax.all_gather(norm2_gain, "fsdp", axis=0, tiled=True),
        lax.all_gather(w_gate, "fsdp", axis=0, tiled=True),
        lax.all_gather(w_up, "fsdp", axis=0, tiled=True),
        lax.all_gather(w_down, "fsdp", axis=0, tiled=True),
    )
    query_group_count, local_row_count, model_width = tokens.shape
    repeat_heads = QUERY_HEADS // KEY_VALUE_HEADS
    head_width = HEAD_SIZE
    key_value_width = KEY_VALUE_HEADS * HEAD_SIZE
    query_width = QUERY_HEADS * HEAD_SIZE
    first_row = lax.axis_index("ctx") * local_row_count
    last_row = first_row + local_row_count - 1
    positions = first_row + jnp.arange(local_row_count, dtype=jnp.int32)
    cosine_table, sine_table = rope_tables(positions, head_width)
    gain1f = gain1.astype(jnp.float32)
    gain2f = gain2.astype(jnp.float32)
    inputs = tokens.astype(jnp.float32)
    scale1 = rms_scale(inputs)
    normed1 = (inputs * scale1 * gain1f).astype(jnp.bfloat16)
    query_before_rotation = jnp.einsum(
        "gsd,de->gse", normed1, wq_full, preferred_element_type=jnp.float32
    )
    key_before_rotation = jnp.einsum(
        "gsd,de->gse", normed1, wk_full, preferred_element_type=jnp.float32
    )
    value_projected = jnp.einsum(
        "gsd,de->gse", normed1, wv_full, preferred_element_type=jnp.float32
    )
    query_matrix = rotary_apply(
        query_before_rotation.reshape(query_group_count, local_row_count, QUERY_HEADS, head_width),
        cosine_table,
        sine_table,
    ).astype(jnp.bfloat16)
    query_matrix = query_matrix.reshape(
        query_group_count, local_row_count, KEY_VALUE_HEADS, repeat_heads, head_width
    )
    key_local = rotary_apply(
        key_before_rotation.reshape(
            query_group_count, local_row_count, KEY_VALUE_HEADS, head_width
        ),
        cosine_table,
        sine_table,
    ).astype(jnp.bfloat16)
    local_value_rows = value_projected.astype(jnp.bfloat16)
    collected_keys, collected_values = (
        lax.all_gather(
            key_local.reshape(query_group_count, local_row_count, key_value_width),
            "ctx",
            axis=1,
            tiled=True,
        ),
        lax.all_gather(local_value_rows, "ctx", axis=1, tiled=True),
    )
    sequence_length = collected_keys.shape[1]
    every_key_row = collected_keys.reshape(
        query_group_count, sequence_length, KEY_VALUE_HEADS, head_width
    )
    every_value_row = collected_values.reshape(
        query_group_count, sequence_length, KEY_VALUE_HEADS, head_width
    )
    local_value_rows = local_value_rows.reshape(
        query_group_count, local_row_count, KEY_VALUE_HEADS, head_width
    )
    key_span = min(sequence_length, 512)
    block_total = last_row // key_span + 1

    def key_slices(step_index):
        first_key = step_index * key_span
        key_block = lax.dynamic_slice_in_dim(every_key_row, first_key, key_span, 1)
        value_block = lax.dynamic_slice_in_dim(every_value_row, first_key, key_span, 1)
        key_pos = first_key + jnp.arange(key_span, dtype=jnp.int32)
        return (key_block, value_block, key_pos)

    def stats_step(step_index, running):
        row_max, row_sum = running
        key_block, value_block, key_pos = key_slices(step_index)
        scores = block_scores(query_matrix, key_block, positions, key_pos)
        new_max = jnp.maximum(row_max, jnp.max(scores, axis=-1))
        row_sum = row_sum * jnp.exp(row_max - new_max) + jnp.sum(
            jnp.exp(scores - new_max[..., None]), axis=-1
        )
        return (new_max, row_sum)

    statistics_shape = (query_group_count, KEY_VALUE_HEADS, repeat_heads, local_row_count)
    row_max, row_sum = lax.fori_loop(
        0,
        block_total,
        stats_step,
        (jnp.full(statistics_shape, MASKED, jnp.float32), jnp.zeros(statistics_shape, jnp.float32)),
    )
    log_total = row_max + jnp.log(row_sum)

    def mix_step(step_index, running):
        key_block, value_block, key_pos = key_slices(step_index)
        scores = block_scores(query_matrix, key_block, positions, key_pos)
        probs = jnp.exp(scores - log_total[..., None]).astype(jnp.bfloat16)
        return running + jnp.einsum(
            "ghrqk,gkhd->gqhrd", probs, value_block, preferred_element_type=jnp.float32
        )

    attended_full = lax.fori_loop(
        0,
        block_total,
        mix_step,
        jnp.zeros(
            (query_group_count, local_row_count, KEY_VALUE_HEADS, repeat_heads, head_width),
            jnp.float32,
        ),
    )
    attended = attended_full.astype(jnp.bfloat16).reshape(
        query_group_count, local_row_count, query_width
    )
    branch = jnp.einsum("gse,ed->gsd", attended, wo_full, preferred_element_type=jnp.float32)
    middle = inputs + branch
    scale2 = rms_scale(middle)
    normed2 = (middle * scale2 * gain2f).astype(jnp.bfloat16)
    gate_act = jnp.einsum("gsd,df->gsf", normed2, wg_full, preferred_element_type=jnp.float32)
    up_act = jnp.einsum("gsd,df->gsf", normed2, wu_full, preferred_element_type=jnp.float32)
    gate_sig = jax.nn.sigmoid(gate_act)
    gate_silu = gate_act * gate_sig
    hidden = (gate_silu * up_act).astype(jnp.bfloat16)
    mlp_out = jnp.einsum("gsf,fd->gsd", hidden, wd_full, preferred_element_type=jnp.float32)
    output = (middle + mlp_out).astype(jnp.bfloat16)
    out_float = out_grad.astype(jnp.float32)
    grad_down = jnp.einsum("gsf,gsd->fd", hidden, out_grad, preferred_element_type=jnp.float32)
    hidden_grad = jnp.einsum("gsd,fd->gsf", out_grad, wd_full, preferred_element_type=jnp.float32)
    gate_grad = (hidden_grad * up_act * gate_sig * (1.0 + gate_act * (1.0 - gate_sig))).astype(
        jnp.bfloat16
    )
    up_grad = (hidden_grad * gate_silu).astype(jnp.bfloat16)
    grad_gate = jnp.einsum("gsd,gsf->df", normed2, gate_grad, preferred_element_type=jnp.float32)
    grad_up = jnp.einsum("gsd,gsf->df", normed2, up_grad, preferred_element_type=jnp.float32)
    normed2_grad = jnp.einsum("gsf,df->gsd", gate_grad, wg_full, preferred_element_type=jnp.float32)
    normed2_grad = normed2_grad + jnp.einsum(
        "gsf,df->gsd", up_grad, wu_full, preferred_element_type=jnp.float32
    )
    grad_gain2 = jnp.sum(normed2_grad * middle * scale2, axis=(0, 1))
    scaled2 = gain2f * normed2_grad
    middle_grad = (
        out_float
        + scale2 * scaled2
        - middle * scale2**3 * jnp.mean(scaled2 * middle, axis=-1, keepdims=True)
    )
    branch_grad = middle_grad.astype(jnp.bfloat16)
    grad_out = jnp.einsum("gse,gsd->ed", attended, branch_grad, preferred_element_type=jnp.float32)
    attended_output_gradient = jnp.einsum(
        "gsd,ed->gse", branch_grad, wo_full, preferred_element_type=jnp.float32
    ).astype(jnp.bfloat16)
    attention_gradient = attended_output_gradient.reshape(
        query_group_count, local_row_count, KEY_VALUE_HEADS, repeat_heads, head_width
    )
    delta = jnp.sum(attention_gradient.astype(jnp.float32) * attended_full, axis=-1).transpose(
        0, 2, 3, 1
    )

    def query_grad_step(step_index, running):
        key_block, value_block, key_pos = key_slices(step_index)
        scores = block_scores(query_matrix, key_block, positions, key_pos)
        probs = jnp.exp(scores - log_total[..., None])
        dprob = jnp.einsum(
            "gqhrd,gkhd->ghrqk", attention_gradient, value_block, preferred_element_type=jnp.float32
        )
        score_grad = (probs * (dprob - delta[..., None])).astype(jnp.bfloat16)
        return running + jnp.einsum(
            "ghrqk,gkhd->gqhrd", score_grad, key_block, preferred_element_type=jnp.float32
        )

    query_grad = (
        lax.fori_loop(
            0,
            block_total,
            query_grad_step,
            jnp.zeros(
                (query_group_count, local_row_count, KEY_VALUE_HEADS, repeat_heads, head_width),
                jnp.float32,
            ),
        )
        * 0.125
    )
    row_total = local_row_count * lax.axis_size("ctx")
    term_span = math.gcd(row_total, key_span)

    def key_block_term(step_index):
        first_key = step_index * term_span
        key_block = lax.dynamic_slice_in_dim(every_key_row, first_key, term_span, 1)
        value_block = lax.dynamic_slice_in_dim(every_value_row, first_key, term_span, 1)
        key_pos = first_key + jnp.arange(term_span, dtype=jnp.int32)

        def compute_term(unused):
            scores = block_scores(query_matrix, key_block, positions, key_pos)
            probs = jnp.exp(scores - log_total[..., None])
            dprob = jnp.einsum(
                "gqhrd,gkhd->ghrqk",
                attention_gradient,
                value_block,
                preferred_element_type=jnp.float32,
            )
            score_grad = (probs * (dprob - delta[..., None])).astype(jnp.bfloat16)
            key_term = (
                jnp.einsum(
                    "ghrqk,gqhrd->kghd",
                    score_grad,
                    query_matrix,
                    preferred_element_type=jnp.float32,
                )
                * 0.125
            )
            value_term = jnp.einsum(
                "ghrqk,gqhrd->kghd",
                probs.astype(jnp.bfloat16),
                attention_gradient,
                preferred_element_type=jnp.float32,
            )
            return jnp.concatenate(
                [
                    key_term.reshape(term_span, query_group_count, key_value_width),
                    value_term.reshape(term_span, query_group_count, key_value_width),
                ],
                -1,
            )

        def empty_term(unused):
            return jnp.zeros((term_span, query_group_count, 2 * key_value_width), jnp.float32)

        return lax.cond(first_key <= last_row, compute_term, empty_term, 0)

    terms = lax.map(key_block_term, jnp.arange(row_total // term_span, dtype=jnp.int32))
    paired_gradients = (
        lax.psum_scatter(
            terms.reshape(row_total, query_group_count, 2 * key_value_width).astype(jnp.bfloat16),
            "ctx",
            scatter_dimension=0,
            tiled=True,
        )
        .astype(jnp.float32)
        .transpose(1, 0, 2)
    )
    key_gradient = paired_gradients[..., :key_value_width].reshape(
        query_group_count, local_row_count, KEY_VALUE_HEADS, head_width
    )
    value_gradient = paired_gradients[..., key_value_width:].reshape(
        query_group_count, local_row_count, KEY_VALUE_HEADS, head_width
    )
    query_pre_grad = rotate_back(
        query_grad.reshape(query_group_count, local_row_count, QUERY_HEADS, head_width),
        cosine_table,
        sine_table,
    )
    query_pre_grad = query_pre_grad.astype(jnp.bfloat16).reshape(
        query_group_count, local_row_count, query_width
    )
    key_pre_grad = (
        rotate_back(key_gradient, cosine_table, sine_table)
        .astype(jnp.bfloat16)
        .reshape(query_group_count, local_row_count, key_value_width)
    )
    value_pre_grad = value_gradient.astype(jnp.bfloat16).reshape(
        query_group_count, local_row_count, key_value_width
    )
    grad_query = jnp.einsum(
        "gsd,gse->de", normed1, query_pre_grad, preferred_element_type=jnp.float32
    )
    grad_key = jnp.einsum("gsd,gse->de", normed1, key_pre_grad, preferred_element_type=jnp.float32)
    grad_value = jnp.einsum(
        "gsd,gse->de", normed1, value_pre_grad, preferred_element_type=jnp.float32
    )
    normed1_grad = jnp.einsum(
        "gse,de->gsd", query_pre_grad, wq_full, preferred_element_type=jnp.float32
    )
    normed1_grad = normed1_grad + jnp.einsum(
        "gse,de->gsd", key_pre_grad, wk_full, preferred_element_type=jnp.float32
    )
    normed1_grad = normed1_grad + jnp.einsum(
        "gse,de->gsd", value_pre_grad, wv_full, preferred_element_type=jnp.float32
    )
    grad_gain1 = jnp.sum(normed1_grad * inputs * scale1, axis=(0, 1))
    scaled1 = gain1f * normed1_grad
    input_grad = (
        middle_grad
        + scale1 * scaled1
        - inputs * scale1**3 * jnp.mean(scaled1 * inputs, axis=-1, keepdims=True)
    )
    totals = lax.psum(
        (
            grad_gain1,
            grad_query,
            grad_key,
            grad_value,
            grad_out,
            grad_gain2,
            grad_gate,
            grad_up,
            grad_down,
        ),
        ("dp", "ctx", "fsdp"),
    )
    owner = lax.axis_index("fsdp")
    shards = (norm1_gain, w_query, w_key, w_value, w_out, norm2_gain, w_gate, w_up, w_down)
    shares = tuple(
        (
            lax.dynamic_slice_in_dim(summed, owner * shard.shape[0], shard.shape[0], 0)
            for summed, shard in zip(totals, shards)
        )
    )
    return (
        output,
        input_grad,
        shares[0],
        shares[1],
        shares[2],
        shares[3],
        shares[4],
        shares[5],
        shares[6],
        shares[7],
        shares[8],
    )


WIDTH = 576
QUERY_WIDTH = QUERY_HEADS * HEAD_SIZE
KEY_WIDTH = KEY_VALUE_HEADS * HEAD_SIZE
ROTATED = QUERY_HEADS + KEY_VALUE_HEADS
REPEAT = QUERY_HEADS // KEY_VALUE_HEADS
HALF = HEAD_SIZE // 2
USED = QUERY_WIDTH + 2 * KEY_WIDTH
PACKED = USED + 64
GAIN_AT = USED - (PACKED - 128)
TILE = 256
VMEM_LIMIT = 60 * 1024 * 1024
F32 = jnp.float32
BF16 = jnp.bfloat16


def mm(a, b):
    return jnp.dot(a, b, preferred_element_type=F32)


def mm_nt(a, b):
    return lax.dot_general(a, b, (((1,), (1,)), ((), ())), preferred_element_type=F32)


def flip(tensor):
    return tensor.astype(F32).T.astype(tensor.dtype)


def span(index, size, step=None):
    step = size if step is None else step
    return pl.ds(pl.multiple_of(index * step, step), size)


def flip_blocks(target, source, block):
    def one(step, carry):
        at = span(step, block)
        target[at, :] = flip(source[:, at])
        return carry

    lax.fori_loop(0, source.shape[1] // block, one, 0)


def column_scale(tensor):
    return lax.rsqrt(jnp.mean(tensor * tensor, axis=0, keepdims=True) + EPSILON)


def sigmoid(tensor):
    return 0.5 * jnp.tanh(0.5 * tensor) + 0.5


def causal_last(scores, tile):
    visible = lax.broadcasted_iota(jnp.int32, (TILE, TILE), 0) <= lax.broadcasted_iota(
        jnp.int32, (TILE, TILE), 1
    )
    last = jnp.where(visible, scores[tile * TILE :, :], MASKED)
    return last if tile == 0 else jnp.concatenate([scores[: tile * TILE, :], last], 0)


def attend_kernel(
    place,
    tokens,
    theirs,
    w_own,
    w_y,
    w_core,
    w_both,
    cosine,
    sine,
    x_seq,
    normed,
    packed,
    gains,
    qkv_t,
    log_total,
    attended_t,
    packed_t,
    key_rows,
):
    me, shard = place[0], place[1]
    half_rows = theirs.shape[1]
    sequence = 2 * half_rows
    x_seq[:, span(me, half_rows)] = tokens[me]
    x_seq[:, span(1 - me, half_rows)] = theirs[...]
    rows = w_own.shape[0]
    for bits, piece in ((0, w_own), (2, w_y), (1, w_core), (3, w_both)):
        packed[span(shard ^ bits, rows), :] = piece[...]
    flip_blocks(packed_t, packed, TILE)
    gains[...] = packed[:, PACKED - 128 :].astype(F32)
    gain1 = gains[:, GAIN_AT : GAIN_AT + 1]

    def project(tile, carry):
        at = span(tile, TILE)
        x = x_seq[:, at].astype(F32)
        normed_tile = (x * column_scale(x) * gain1).astype(BF16)
        normed[:, at] = normed_tile
        turned = mm(packed_t[:USED, :], normed_tile)
        cos, sin = cosine[:, at], sine[:, at]
        for head in range(ROTATED):
            a = turned[head * HEAD_SIZE : head * HEAD_SIZE + HALF, :]
            b = turned[head * HEAD_SIZE + HALF : (head + 1) * HEAD_SIZE, :]
            both = jnp.concatenate([a * cos - b * sin, b * cos + a * sin], 0)
            if head < QUERY_HEADS:
                both = both * 0.125
            else:
                key_rows[head - QUERY_HEADS, at, :] = both.T.astype(BF16)
            qkv_t[head * HEAD_SIZE : (head + 1) * HEAD_SIZE, at] = both.astype(BF16)
        qkv_t[ROTATED * HEAD_SIZE :, at] = turned[ROTATED * HEAD_SIZE :, :].astype(BF16)
        return carry

    lax.fori_loop(0, sequence // TILE, project, 0)

    def one_head(head, carry):
        group = head // REPEAT
        head_rows = span(head, HEAD_SIZE)
        value_rows = span(ROTATED + group, HEAD_SIZE)
        for tile in range(sequence // TILE):
            extent = (tile + 1) * TILE
            cols = slice(tile * TILE, extent)
            scores = causal_last(mm(key_rows[group, :extent, :], qkv_t[head_rows, cols]), tile)
            top = jnp.max(scores, axis=0, keepdims=True)
            weights = jnp.exp(scores - top)
            total = jnp.sum(weights, axis=0, keepdims=True)
            mixed = mm(qkv_t[value_rows, :extent], weights.astype(BF16))
            attended_t[head_rows, cols] = (mixed * (1.0 / total)).astype(BF16)
            log_total[group, pl.ds(head - group * REPEAT, 1), cols] = top + jnp.log(total)
        return carry

    lax.fori_loop(0, QUERY_HEADS, one_head, 0)


def feed_forward_kernel(
    place,
    x_seq,
    attended_t,
    out_grad,
    dy_theirs,
    gains,
    a_own,
    a_y,
    a_core,
    a_both,
    b_own,
    b_y,
    b_core,
    b_both,
    out_keep,
    out_send,
    middle_grad_out,
    attended_grad_t,
    keep_b,
    send_b,
    keep_a,
    send_a,
    gain_grad,
    w_out,
    w_gate,
    w_up,
    w_down,
    w_out_t,
    w_gate_t,
    w_up_t,
    w_down_t,
    dy_seq,
    normed_t,
    hidden,
    gate_grad,
    up_grad,
    branch_grad,
    gain_sum,
    total,
):
    me, shard = place[0], place[1]
    half_rows = dy_theirs.shape[1]
    sequence = 2 * half_rows
    dy_seq[:, span(me, half_rows)] = out_grad[me]
    dy_seq[:, span(1 - me, half_rows)] = dy_theirs[...]
    rows = b_own.shape[0]
    wide = w_gate.shape[1]
    down_rows = a_own.shape[1]
    for bits, a, b in ((0, a_own, b_own), (2, a_y, b_y), (1, a_core, b_core), (3, a_both, b_both)):
        at = span(shard ^ bits, rows)
        w_gate[at, :] = b[:, :wide]
        w_up[at, :] = b[:, wide : 2 * wide]
        w_out[at, :] = b[:, 2 * wide :]
        w_down_t[:, span(shard ^ bits, down_rows)] = a[...]
    flip_blocks(w_gate_t, w_gate, TILE)
    flip_blocks(w_up_t, w_up, TILE)
    w_out_t[...] = flip(w_out[...])
    flip_blocks(w_down, w_down_t, TILE)
    gain2 = gains[:, GAIN_AT + 1 : GAIN_AT + 2]
    gain_sum[...] = jnp.zeros_like(gain_sum)

    def one_tile(tile, carry):
        at = span(tile, TILE)
        middle = x_seq[:, at].astype(F32) + mm(w_out_t[...], attended_t[:, at])
        scale = column_scale(middle)
        ready = middle * scale
        normed = (ready * gain2).astype(BF16)
        normed_t[:, at] = normed
        gate = mm(w_gate_t[...], normed)
        up = mm(w_up_t[...], normed)
        sig = sigmoid(gate)
        silu = gate * sig
        hidden_tile = (silu * up).astype(BF16)
        hidden[:, at] = hidden_tile
        output = (middle + mm(w_down_t[...], hidden_tile)).astype(BF16)
        block = tile // (half_rows // TILE)
        block_cols = span(tile - block * (half_rows // TILE), TILE)

        @pl.when(block == me)
        def _():
            out_keep[:, block_cols] = output

        @pl.when(block != me)
        def _():
            out_send[:, block_cols] = output

        dy = dy_seq[:, at]
        hidden_grad = mm(w_down[...], dy)
        gate_tile = (hidden_grad * up * sig * (1.0 + gate * (1.0 - sig))).astype(BF16)
        up_tile = (hidden_grad * silu).astype(BF16)
        gate_grad[:, at] = gate_tile
        up_grad[:, at] = up_tile
        normed_grad = mm(w_gate[...], gate_tile) + mm(w_up[...], up_tile)
        gain_sum[...] += normed_grad * ready
        scaled = normed_grad * gain2
        middle_grad = (
            dy.astype(F32)
            + scale * scaled
            - middle * (scale * scale * scale) * jnp.mean(scaled * middle, axis=0, keepdims=True)
        )
        middle_grad_out[:, at] = middle_grad
        branch = middle_grad.astype(BF16)
        branch_grad[:, at] = branch
        attended_grad_t[:, at] = mm(w_out[...], branch).astype(BF16)
        return carry

    lax.fori_loop(0, sequence // TILE, one_tile, 0)
    gain_grad[...] = jnp.broadcast_to(
        jnp.sum(gain_sum[...], axis=1, keepdims=True), gain_grad.shape
    )

    half = rows // 2
    for left, right, first in (
        (normed_t, gate_grad, 0),
        (normed_t, up_grad, wide),
        (attended_t, branch_grad, 2 * wide),
    ):
        size = right.shape[0]
        for start in range(0, size, 512):
            count = min(512, size - start)
            total[:, :count] = mm_nt(left[...], right[start : start + count, :])
            cols = slice(first + start, first + start + count)
            for y_bit in range(2):
                for x_bit in range(2):
                    for core_bit, target in ((0, keep_b), (1, send_b)):
                        row = (shard ^ (2 * y_bit + core_bit)) * 2 + (me ^ x_bit)
                        target[y_bit, x_bit, :, cols] = total[span(row, half), :count].astype(BF16)
    half = keep_a.shape[2]
    for y_bit in range(2):
        for core_bit, target in ((0, keep_a), (1, send_a)):
            columns = span(shard ^ (2 * y_bit + core_bit), down_rows)
            total[:, :down_rows] = mm_nt(dy_seq[...], hidden[columns, :])
            for x_bit in range(2):
                target[x_bit, y_bit] = total[span(me ^ x_bit, half), :down_rows].astype(BF16)


def attend_back_kernel(
    queries_t,
    keys_t,
    values_t,
    log_total,
    attended_t,
    grad_t,
    cosine,
    sine,
    dq_out,
    dk_out,
    dv_out,
    keys,
    values,
    dk,
    dv,
    dq,
):
    sequence = keys_t.shape[1]
    keys[...] = flip(keys_t[...])
    values[...] = flip(values_t[...])
    dk[...] = jnp.zeros_like(dk)
    dv[...] = jnp.zeros_like(dv)

    def back(a, b, cos, sin):
        return (a * cos + b * sin).astype(BF16), (b * cos - a * sin).astype(BF16)

    def one_head(head, carry):
        head_rows = span(head, HEAD_SIZE)
        for tile in range(sequence // TILE):
            extent = (tile + 1) * TILE
            cols = slice(tile * TILE, extent)
            q_t = queries_t[head_rows, cols]
            do_t = grad_t[head_rows, cols]
            do_wide = do_t.astype(F32)
            delta = jnp.sum(
                do_wide * attended_t[head_rows, cols].astype(F32), axis=0, keepdims=True
            )
            scores = causal_last(mm(keys[:extent, :], q_t), tile)
            probs = jnp.exp(scores - log_total[0, pl.ds(head, 1), cols])
            dprob = mm(values[:extent, :], do_t)
            score_grad = (probs * (dprob - delta)).astype(BF16)
            dv[:extent, :] += mm(probs.astype(BF16), do_wide.T.astype(BF16))
            dk[:extent, :] += mm(score_grad, flip(q_t))
            dq[:, cols] = mm(keys_t[:, :extent], score_grad) * 0.125
        cos, sin = cosine[...], sine[...]
        a, b = back(dq[:HALF, :], dq[HALF:, :], cos, sin)
        dq_out[span(head, HALF, HEAD_SIZE), :] = a
        dq_out[span(2 * head + 1, HALF), :] = b
        return carry

    lax.fori_loop(0, queries_t.shape[0] // HEAD_SIZE, one_head, 0)
    turned = dk[...].T
    a, b = back(turned[:HALF, :], turned[HALF:, :], cosine[...], sine[...])
    dk_out[:HALF, :] = a
    dk_out[HALF:, :] = b
    dv_out[...] = dv[...].T.astype(BF16)


def input_kernel(place, x_seq, normed, packed, gains, gain2_grad, middle_grad, *rest):
    heads = rest[: 3 * KEY_VALUE_HEADS]
    keep_w, send_w, keep_x, send_x, joined, grad_seq, total = rest[3 * KEY_VALUE_HEADS :]
    me, shard = place[0], place[1]
    half_rows = keep_x.shape[1]
    sequence = 2 * half_rows
    group_width = REPEAT * HEAD_SIZE
    for group in range(KEY_VALUE_HEADS):
        dq, dk, dv = heads[3 * group : 3 * group + 3]
        joined[group * group_width : (group + 1) * group_width, :] = dq[...]
        at = QUERY_WIDTH + group * HEAD_SIZE
        joined[at : at + HEAD_SIZE, :] = dk[...]
        at = QUERY_WIDTH + KEY_WIDTH + group * HEAD_SIZE
        joined[at : at + HEAD_SIZE, :] = dv[...]
    joined[USED:, :] = jnp.zeros((PACKED - USED, sequence), BF16)
    gain1 = gains[:, GAIN_AT : GAIN_AT + 1]
    gain_sum = jnp.zeros((WIDTH, TILE), F32)
    for tile in range(sequence // TILE):
        at = slice(tile * TILE, (tile + 1) * TILE)
        normed_grad = mm(packed[...], joined[:, at])
        x = x_seq[:, at].astype(F32)
        scale = column_scale(x)
        gain_sum += normed_grad * x * scale
        scaled = normed_grad * gain1
        grad_seq[:, at] = (
            middle_grad[:, at]
            + scale * scaled
            - x * (scale * scale * scale) * jnp.mean(scaled * x, axis=0, keepdims=True)
        )
    keep_x[...] = grad_seq[:, span(me, half_rows)]
    send_x[...] = grad_seq[:, span(1 - me, half_rows)].astype(BF16)
    for first in range(0, PACKED, 512):
        total[:, first : first + 512] = mm_nt(normed[...], joined[first : first + 512, :])
    lane = lax.broadcasted_iota(jnp.int32, (WIDTH, 128), 1)
    last = total[:, PACKED - 128 :]
    last = jnp.where(lane == GAIN_AT, jnp.sum(gain_sum, axis=1, keepdims=True), last)
    total[:, PACKED - 128 :] = jnp.where(lane == GAIN_AT + 1, gain2_grad[...], last)
    half = keep_w.shape[2]
    for y_bit in range(2):
        for x_bit in range(2):
            row = (shard ^ (2 * y_bit)) * 2 + (me ^ x_bit)
            keep_w[y_bit, x_bit] = total[span(row, half), :].astype(BF16)
            row = (shard ^ (2 * y_bit + 1)) * 2 + (me ^ x_bit)
            send_w[y_bit, x_bit] = total[span(row, half), :].astype(BF16)


def call(kernel, out, scratch, flops, exps, args, name):
    shapes = [jax.ShapeDtypeStruct(s, d) for s, d in out]
    moved = sum(a.size * a.dtype.itemsize for a in args[1:]) + sum(
        s.size * s.dtype.itemsize for s in shapes
    )
    in_specs = [pl.BlockSpec(memory_space=pltpu.SMEM)] + [
        pl.BlockSpec(memory_space=pltpu.VMEM)
    ] * (len(args) - 1)
    return pl.pallas_call(
        kernel,
        out_shape=shapes,
        in_specs=in_specs,
        out_specs=[pl.BlockSpec(memory_space=pltpu.VMEM)] * len(shapes),
        scratch_shapes=[pltpu.VMEM(s, d) for s, d in scratch],
        compiler_params=pltpu.CompilerParams(vmem_limit_bytes=VMEM_LIMIT),
        cost_estimate=pl.CostEstimate(flops=flops, bytes_accessed=moved, transcendentals=exps),
        name=name,
    )(*args)


def attend_back(group, qkv_t, log_total, attended_t, grad_t, cosine, sine):
    sequence = qkv_t.shape[1]
    group_width = REPEAT * HEAD_SIZE

    def rows_of(size, index):
        return pl.BlockSpec((size, sequence), lambda step: (index, 0))

    flops = 5 * REPEAT * sequence * sequence * HEAD_SIZE * 2
    return pl.pallas_call(
        attend_back_kernel,
        grid=(1,),
        out_shape=[
            jax.ShapeDtypeStruct((group_width, sequence), BF16),
            jax.ShapeDtypeStruct((HEAD_SIZE, sequence), BF16),
            jax.ShapeDtypeStruct((HEAD_SIZE, sequence), BF16),
        ],
        in_specs=[
            rows_of(group_width, group),
            rows_of(HEAD_SIZE, QUERY_HEADS + group),
            rows_of(HEAD_SIZE, ROTATED + group),
            pl.BlockSpec((1, 8, sequence), lambda step: (group, 0, 0)),
            rows_of(group_width, group),
            rows_of(group_width, group),
            rows_of(HALF, 0),
            rows_of(HALF, 0),
        ],
        out_specs=[rows_of(group_width, 0), rows_of(HEAD_SIZE, 0), rows_of(HEAD_SIZE, 0)],
        scratch_shapes=[
            pltpu.VMEM((sequence, HEAD_SIZE), BF16),
            pltpu.VMEM((sequence, HEAD_SIZE), BF16),
            pltpu.VMEM((sequence, HEAD_SIZE), F32),
            pltpu.VMEM((sequence, HEAD_SIZE), F32),
            pltpu.VMEM((HEAD_SIZE, sequence), F32),
        ],
        compiler_params=pltpu.CompilerParams(vmem_limit_bytes=VMEM_LIMIT),
        cost_estimate=pl.CostEstimate(
            flops=flops, bytes_accessed=4_000_000, transcendentals=REPEAT * sequence * sequence
        ),
        name="attend_back",
    )(qkv_t, qkv_t, qkv_t, log_total, attended_t, grad_t, cosine, sine)


def across(tensor, bit):
    return lax.ppermute(tensor, "fsdp", [(i, i ^ bit) for i in range(4)])


def over_context(tensor):
    return lax.ppermute(tensor, "ctx", [(0, 1), (1, 0)])


def after(tensor, *done):
    return lax.optimization_barrier((tensor, *done))[0]


def together(*values):
    return lax.optimization_barrier(values)


def add(a, b):
    return (a.astype(F32) + b.astype(F32)).astype(BF16)


def sum_line(part):
    size = lax.axis_size("dp")
    at = lax.axis_index("dp")
    middle = size // 2
    for step in range(middle - 1):
        pairs = [(step, step + 1), (size - 1 - step, size - 2 - step)]
        part = add(part, lax.ppermute(part, "dp", pairs))
    part = add(part, lax.ppermute(part, "dp", [(middle - 1, middle), (middle, middle - 1)]))
    for step in range(middle - 2, -1, -1):
        pairs = [(step + 1, step), (size - 2 - step, size - 1 - step)]
        got = lax.ppermute(part, "dp", pairs)
        part = jnp.where((at == step) | (at == size - 1 - step), got, part)
    return part


def whole_sequences(
    tokens, norm1_gain, w_query, w_key, w_value, w_out, norm2_gain, w_gate, w_up, w_down, out_grad
):
    half_rows, width = tokens.shape[1:]
    sequence = 2 * half_rows
    rows = w_query.shape[0]
    down_rows = w_down.shape[0]
    hidden_width = w_gate.shape[1]
    me = lax.axis_index("ctx")
    place = jnp.stack([me, lax.axis_index("fsdp")]).astype(jnp.int32)
    tokens = jnp.swapaxes(tokens, 1, 2)
    out_grad = jnp.swapaxes(out_grad, 1, 2)

    packed = jnp.concatenate(
        [
            w_query,
            w_key,
            w_value,
            norm1_gain[:, None],
            norm2_gain[:, None],
            jnp.zeros((rows, PACKED - USED - 2), BF16),
        ],
        1,
    )
    tokens_theirs = over_context(lax.dynamic_index_in_dim(tokens, 1 - me, 0, False))
    packed_y = across(packed, 2)
    packed_core = across(packed, 1)
    packed_both = across(packed_y, 1)
    b_own = jnp.concatenate([w_gate, w_up, w_out], 1)
    a_own = w_down.T
    b_own, a_own = together(b_own, a_own, packed_y)[:2]
    b_y, a_y = across(b_own, 2), across(a_own, 2)
    b_core, a_core = across(b_own, 1), across(a_own, 1)
    dy_theirs = over_context(
        after(lax.dynamic_index_in_dim(out_grad, 1 - me, 0, False), tokens_theirs)
    )

    cosine, sine = rope_tables(jnp.arange(sequence, dtype=jnp.int32), HEAD_SIZE)
    cosine, sine = cosine.T, sine.T

    pairs = sequence * sequence
    x_seq, normed, packed_all, gains, qkv_t, log_total, attended_t = call(
        attend_kernel,
        [
            ((width, sequence), BF16),
            ((width, sequence), BF16),
            ((width, PACKED), BF16),
            ((width, 128), F32),
            ((USED, sequence), BF16),
            ((KEY_VALUE_HEADS, 8, sequence), F32),
            ((QUERY_WIDTH, sequence), BF16),
        ],
        [((PACKED, width), BF16), ((KEY_VALUE_HEADS, sequence, HEAD_SIZE), BF16)],
        2 * sequence * width * PACKED + 4 * QUERY_WIDTH * pairs,
        QUERY_HEADS * pairs,
        (place, tokens, tokens_theirs, packed, packed_y, packed_core, packed_both, cosine, sine),
        "attend",
    )

    b_y, a_y, b_core, a_core, dy_theirs, attended_t = together(
        b_y, a_y, b_core, a_core, dy_theirs, attended_t
    )
    b_both, a_both = across(b_y, 1), across(a_y, 1)

    b_shape = ((2, 2, rows // 2, b_own.shape[1]), BF16)
    a_shape = ((2, 2, width // 2, down_rows), BF16)
    (
        out_keep,
        out_send,
        middle_grad,
        grad_t,
        keep_b,
        send_b,
        keep_a,
        send_a,
        gain2_grad,
    ) = call(
        feed_forward_kernel,
        [
            ((width, half_rows), BF16),
            ((width, half_rows), BF16),
            ((width, sequence), F32),
            ((QUERY_WIDTH, sequence), BF16),
            b_shape,
            b_shape,
            a_shape,
            a_shape,
            ((width, 128), F32),
        ],
        [
            ((QUERY_WIDTH, width), BF16),
            ((width, hidden_width), BF16),
            ((width, hidden_width), BF16),
            ((hidden_width, width), BF16),
            ((width, QUERY_WIDTH), BF16),
            ((hidden_width, width), BF16),
            ((hidden_width, width), BF16),
            ((width, hidden_width), BF16),
            ((width, sequence), BF16),
            ((width, sequence), BF16),
            ((hidden_width, sequence), BF16),
            ((hidden_width, sequence), BF16),
            ((hidden_width, sequence), BF16),
            ((width, sequence), BF16),
            ((width, TILE), F32),
            ((width, 512), F32),
        ],
        2 * sequence * width * (9 * hidden_width + 3 * QUERY_WIDTH),
        sequence * hidden_width,
        (
            place,
            x_seq,
            attended_t,
            out_grad,
            dy_theirs,
            gains,
            a_own,
            a_y,
            a_core,
            a_both,
            b_own,
            b_y,
            b_core,
            b_both,
        ),
        "feed_forward",
    )

    back_args = (log_total, attended_t, grad_t, cosine, sine)
    out_theirs = over_context(out_send)
    got_b, got_a = across(send_b, 1), across(send_a, 1)
    grads0 = attend_back(0, qkv_t, *back_args)
    got_b, got_a, *grads0 = together(got_b, got_a, *grads0)
    b0, b1 = add(keep_b[0], got_b[0]), add(keep_b[1], got_b[1])
    a0, a1 = add(keep_a[0], got_a[0]), add(keep_a[1], got_a[1])
    b1, a1, qkv_t = together(b1, a1, qkv_t)
    got_b, got_a = across(b1, 2), over_context(a1)
    grads1 = attend_back(1, qkv_t, *back_args)
    grads2 = attend_back(2, qkv_t, *back_args)
    got_b, got_a, out_theirs, *grads2 = together(got_b, got_a, out_theirs, *grads2)
    b0, b1 = add(b0[0], got_b[0]), add(b0[1], got_b[1])
    a0, a1 = add(a0[0], got_a[0]), add(a0[1], got_a[1])
    b1, a1, *grads2 = together(b1, a1, *grads2)
    got_b, got_a = over_context(b1), across(a1, 2)

    keep_w, send_w, keep_x, send_x = call(
        input_kernel,
        [
            ((2, 2, rows // 2, PACKED), BF16),
            ((2, 2, rows // 2, PACKED), BF16),
            ((width, half_rows), F32),
            ((width, half_rows), BF16),
        ],
        [((PACKED, sequence), BF16), ((width, sequence), F32), ((width, PACKED), F32)],
        4 * sequence * width * PACKED,
        sequence,
        (
            place,
            x_seq,
            normed,
            packed_all,
            gains,
            gain2_grad,
            middle_grad,
            *grads0,
            *grads1,
            *grads2,
        ),
        "input_side",
    )
    got_b, got_a, send_w = together(got_b, got_a, send_w)
    w_got = across(send_w, 1)
    x_theirs = over_context(send_x)
    b_part = sum_line(add(b0, got_b))
    a_part = sum_line(add(a0, got_a))
    w0, w1 = add(keep_w[0], w_got[0]), add(keep_w[1], w_got[1])
    w_got = across(w1, 2)
    w0, w1 = add(w0[0], w_got[0]), add(w0[1], w_got[1])
    w_part = sum_line(add(w0, over_context(w1)))

    def both_halves(part, other):
        first = jnp.where(me == 0, part, other)
        second = jnp.where(me == 0, other, part)
        return jnp.concatenate([first, second], 0).astype(F32)

    b_sum = both_halves(b_part, over_context(b_part))
    a_sum = both_halves(a_part, over_context(a_part))
    w_sum = both_halves(w_part, over_context(w_part))

    def place_halves(keep, got):
        got = got.astype(keep.dtype)
        both = jnp.where(me == 0, jnp.stack([keep, got]), jnp.stack([got, keep]))
        return jnp.swapaxes(both, 1, 2)

    key_at = QUERY_WIDTH + KEY_WIDTH
    return (
        place_halves(out_keep, out_theirs),
        place_halves(keep_x, x_theirs),
        w_sum[:, USED],
        w_sum[:, :QUERY_WIDTH],
        w_sum[:, QUERY_WIDTH:key_at],
        w_sum[:, key_at:USED],
        b_sum[:, 2 * hidden_width :],
        w_sum[:, USED + 1],
        b_sum[:, :hidden_width],
        b_sum[:, hidden_width : 2 * hidden_width],
        a_sum.T,
    )


def layer_step(tokens, *rest):
    whole = (
        lax.axis_size("ctx") == 2
        and lax.axis_size("fsdp") == 4
        and lax.axis_size("dp") % 2 == 0
        and tokens.shape[0] == 2
        and tokens.shape[1] % TILE == 0
    )
    return (whole_sequences if whole else split_context)(tokens, *rest)


def solution(mesh):
    return jax.shard_map(
        layer_step,
        mesh=mesh,
        in_specs=(
            P(("dp", "fsdp"), "ctx", None),
            P("fsdp"),
            P("fsdp", None),
            P("fsdp", None),
            P("fsdp", None),
            P("fsdp", None),
            P("fsdp"),
            P("fsdp", None),
            P("fsdp", None),
            P("fsdp", None),
            P(("dp", "fsdp"), "ctx", None),
        ),
        out_specs=(
            P(("dp", "fsdp"), "ctx", None),
            P(("dp", "fsdp"), "ctx", None),
            P("fsdp"),
            P("fsdp", None),
            P("fsdp", None),
            P("fsdp", None),
            P("fsdp", None),
            P("fsdp"),
            P("fsdp", None),
            P("fsdp", None),
            P("fsdp", None),
        ),
        check_vma=False,
    )
```

```python
import functools
import math

import jax
import jax.numpy as jnp
from jax import lax
from jax.experimental import pallas as pl
from jax.experimental.pallas import tpu as pltpu
from jax.sharding import PartitionSpec as P

QUERY_HEADS = 9
KEY_VALUE_HEADS = 3
HEAD_SIZE = 64


EPSILON = 1e-05
ROPE_THETA = 100000.0
MASKED = -1e30


def rope_tables(positions, head_width):
    half_size = head_width // 2
    inverse = jnp.exp(
        jnp.arange(half_size, dtype=jnp.float32) * (-2.0 * math.log(ROPE_THETA) / head_width)
    )
    angle = positions.astype(jnp.float32)[:, None] * inverse[None, :]
    return (jnp.cos(angle), jnp.sin(angle))


def rotary_apply(tensor, cosine_table, sine_table):
    half_size = tensor.shape[-1] // 2
    first_half = tensor[..., :half_size]
    second_half = tensor[..., half_size:]
    cosine_table = cosine_table[None, :, None, :]
    sine_table = sine_table[None, :, None, :]
    return jnp.concatenate(
        [
            first_half * cosine_table - second_half * sine_table,
            second_half * cosine_table + first_half * sine_table,
        ],
        -1,
    )


def rotate_back(tensor, cosine_table, sine_table):
    half_size = tensor.shape[-1] // 2
    first_half = tensor[..., :half_size]
    second_half = tensor[..., half_size:]
    cosine_table = cosine_table[None, :, None, :]
    sine_table = sine_table[None, :, None, :]
    return jnp.concatenate(
        [
            first_half * cosine_table + second_half * sine_table,
            second_half * cosine_table - first_half * sine_table,
        ],
        -1,
    )


def rms_scale(tensor):
    return lax.rsqrt(jnp.mean(tensor * tensor, axis=-1, keepdims=True) + EPSILON)


def block_scores(query_block, key_block, query_pos, key_pos):
    scores = (
        jnp.einsum("gqhrd,gkhd->ghrqk", query_block, key_block, preferred_element_type=jnp.float32)
        * 0.125
    )
    visible = key_pos[None, :] <= query_pos[:, None]
    return jnp.where(visible, scores, MASKED)


def split_context(
    tokens, norm1_gain, w_query, w_key, w_value, w_out, norm2_gain, w_gate, w_up, w_down, out_grad
):
    gain1, wq_full, wk_full, wv_full, wo_full, gain2, wg_full, wu_full, wd_full = (
        lax.all_gather(norm1_gain, "fsdp", axis=0, tiled=True),
        lax.all_gather(w_query, "fsdp", axis=0, tiled=True),
        lax.all_gather(w_key, "fsdp", axis=0, tiled=True),
        lax.all_gather(w_value, "fsdp", axis=0, tiled=True),
        lax.all_gather(w_out, "fsdp", axis=0, tiled=True),
        lax.all_gather(norm2_gain, "fsdp", axis=0, tiled=True),
        lax.all_gather(w_gate, "fsdp", axis=0, tiled=True),
        lax.all_gather(w_up, "fsdp", axis=0, tiled=True),
        lax.all_gather(w_down, "fsdp", axis=0, tiled=True),
    )
    query_group_count, local_row_count, model_width = tokens.shape
    repeat_heads = QUERY_HEADS // KEY_VALUE_HEADS
    head_width = HEAD_SIZE
    key_value_width = KEY_VALUE_HEADS * HEAD_SIZE
    query_width = QUERY_HEADS * HEAD_SIZE
    first_row = lax.axis_index("ctx") * local_row_count
    last_row = first_row + local_row_count - 1
    positions = first_row + jnp.arange(local_row_count, dtype=jnp.int32)
    cosine_table, sine_table = rope_tables(positions, head_width)
    gain1f = gain1.astype(jnp.float32)
    gain2f = gain2.astype(jnp.float32)
    inputs = tokens.astype(jnp.float32)
    scale1 = rms_scale(inputs)
    normed1 = (inputs * scale1 * gain1f).astype(jnp.bfloat16)
    query_before_rotation = jnp.einsum(
        "gsd,de->gse", normed1, wq_full, preferred_element_type=jnp.float32
    )
    key_before_rotation = jnp.einsum(
        "gsd,de->gse", normed1, wk_full, preferred_element_type=jnp.float32
    )
    value_projected = jnp.einsum(
        "gsd,de->gse", normed1, wv_full, preferred_element_type=jnp.float32
    )
    query_matrix = rotary_apply(
        query_before_rotation.reshape(query_group_count, local_row_count, QUERY_HEADS, head_width),
        cosine_table,
        sine_table,
    ).astype(jnp.bfloat16)
    query_matrix = query_matrix.reshape(
        query_group_count, local_row_count, KEY_VALUE_HEADS, repeat_heads, head_width
    )
    key_local = rotary_apply(
        key_before_rotation.reshape(
            query_group_count, local_row_count, KEY_VALUE_HEADS, head_width
        ),
        cosine_table,
        sine_table,
    ).astype(jnp.bfloat16)
    local_value_rows = value_projected.astype(jnp.bfloat16)
    collected_keys, collected_values = (
        lax.all_gather(
            key_local.reshape(query_group_count, local_row_count, key_value_width),
            "ctx",
            axis=1,
            tiled=True,
        ),
        lax.all_gather(local_value_rows, "ctx", axis=1, tiled=True),
    )
    sequence_length = collected_keys.shape[1]
    every_key_row = collected_keys.reshape(
        query_group_count, sequence_length, KEY_VALUE_HEADS, head_width
    )
    every_value_row = collected_values.reshape(
        query_group_count, sequence_length, KEY_VALUE_HEADS, head_width
    )
    local_value_rows = local_value_rows.reshape(
        query_group_count, local_row_count, KEY_VALUE_HEADS, head_width
    )
    key_span = min(sequence_length, 512)
    block_total = last_row // key_span + 1

    def key_slices(step_index):
        first_key = step_index * key_span
        key_block = lax.dynamic_slice_in_dim(every_key_row, first_key, key_span, 1)
        value_block = lax.dynamic_slice_in_dim(every_value_row, first_key, key_span, 1)
        key_pos = first_key + jnp.arange(key_span, dtype=jnp.int32)
        return (key_block, value_block, key_pos)

    def stats_step(step_index, running):
        row_max, row_sum = running
        key_block, value_block, key_pos = key_slices(step_index)
        scores = block_scores(query_matrix, key_block, positions, key_pos)
        new_max = jnp.maximum(row_max, jnp.max(scores, axis=-1))
        row_sum = row_sum * jnp.exp(row_max - new_max) + jnp.sum(
            jnp.exp(scores - new_max[..., None]), axis=-1
        )
        return (new_max, row_sum)

    statistics_shape = (query_group_count, KEY_VALUE_HEADS, repeat_heads, local_row_count)
    row_max, row_sum = lax.fori_loop(
        0,
        block_total,
        stats_step,
        (jnp.full(statistics_shape, MASKED, jnp.float32), jnp.zeros(statistics_shape, jnp.float32)),
    )
    log_total = row_max + jnp.log(row_sum)

    def mix_step(step_index, running):
        key_block, value_block, key_pos = key_slices(step_index)
        scores = block_scores(query_matrix, key_block, positions, key_pos)
        probs = jnp.exp(scores - log_total[..., None]).astype(jnp.bfloat16)
        return running + jnp.einsum(
            "ghrqk,gkhd->gqhrd", probs, value_block, preferred_element_type=jnp.float32
        )

    attended_full = lax.fori_loop(
        0,
        block_total,
        mix_step,
        jnp.zeros(
            (query_group_count, local_row_count, KEY_VALUE_HEADS, repeat_heads, head_width),
            jnp.float32,
        ),
    )
    attended = attended_full.astype(jnp.bfloat16).reshape(
        query_group_count, local_row_count, query_width
    )
    branch = jnp.einsum("gse,ed->gsd", attended, wo_full, preferred_element_type=jnp.float32)
    middle = inputs + branch
    scale2 = rms_scale(middle)
    normed2 = (middle * scale2 * gain2f).astype(jnp.bfloat16)
    gate_act = jnp.einsum("gsd,df->gsf", normed2, wg_full, preferred_element_type=jnp.float32)
    up_act = jnp.einsum("gsd,df->gsf", normed2, wu_full, preferred_element_type=jnp.float32)
    gate_sig = jax.nn.sigmoid(gate_act)
    gate_silu = gate_act * gate_sig
    hidden = (gate_silu * up_act).astype(jnp.bfloat16)
    mlp_out = jnp.einsum("gsf,fd->gsd", hidden, wd_full, preferred_element_type=jnp.float32)
    output = (middle + mlp_out).astype(jnp.bfloat16)
    out_float = out_grad.astype(jnp.float32)
    grad_down = jnp.einsum("gsf,gsd->fd", hidden, out_grad, preferred_element_type=jnp.float32)
    hidden_grad = jnp.einsum("gsd,fd->gsf", out_grad, wd_full, preferred_element_type=jnp.float32)
    gate_grad = (hidden_grad * up_act * gate_sig * (1.0 + gate_act * (1.0 - gate_sig))).astype(
        jnp.bfloat16
    )
    up_grad = (hidden_grad * gate_silu).astype(jnp.bfloat16)
    grad_gate = jnp.einsum("gsd,gsf->df", normed2, gate_grad, preferred_element_type=jnp.float32)
    grad_up = jnp.einsum("gsd,gsf->df", normed2, up_grad, preferred_element_type=jnp.float32)
    normed2_grad = jnp.einsum("gsf,df->gsd", gate_grad, wg_full, preferred_element_type=jnp.float32)
    normed2_grad = normed2_grad + jnp.einsum(
        "gsf,df->gsd", up_grad, wu_full, preferred_element_type=jnp.float32
    )
    grad_gain2 = jnp.sum(normed2_grad * middle * scale2, axis=(0, 1))
    scaled2 = gain2f * normed2_grad
    middle_grad = (
        out_float
        + scale2 * scaled2
        - middle * scale2**3 * jnp.mean(scaled2 * middle, axis=-1, keepdims=True)
    )
    branch_grad = middle_grad.astype(jnp.bfloat16)
    grad_out = jnp.einsum("gse,gsd->ed", attended, branch_grad, preferred_element_type=jnp.float32)
    attended_output_gradient = jnp.einsum(
        "gsd,ed->gse", branch_grad, wo_full, preferred_element_type=jnp.float32
    ).astype(jnp.bfloat16)
    attention_gradient = attended_output_gradient.reshape(
        query_group_count, local_row_count, KEY_VALUE_HEADS, repeat_heads, head_width
    )
    delta = jnp.sum(attention_gradient.astype(jnp.float32) * attended_full, axis=-1).transpose(
        0, 2, 3, 1
    )

    def query_grad_step(step_index, running):
        key_block, value_block, key_pos = key_slices(step_index)
        scores = block_scores(query_matrix, key_block, positions, key_pos)
        probs = jnp.exp(scores - log_total[..., None])
        dprob = jnp.einsum(
            "gqhrd,gkhd->ghrqk", attention_gradient, value_block, preferred_element_type=jnp.float32
        )
        score_grad = (probs * (dprob - delta[..., None])).astype(jnp.bfloat16)
        return running + jnp.einsum(
            "ghrqk,gkhd->gqhrd", score_grad, key_block, preferred_element_type=jnp.float32
        )

    query_grad = (
        lax.fori_loop(
            0,
            block_total,
            query_grad_step,
            jnp.zeros(
                (query_group_count, local_row_count, KEY_VALUE_HEADS, repeat_heads, head_width),
                jnp.float32,
            ),
        )
        * 0.125
    )
    row_total = local_row_count * lax.axis_size("ctx")
    term_span = math.gcd(row_total, key_span)

    def key_block_term(step_index):
        first_key = step_index * term_span
        key_block = lax.dynamic_slice_in_dim(every_key_row, first_key, term_span, 1)
        value_block = lax.dynamic_slice_in_dim(every_value_row, first_key, term_span, 1)
        key_pos = first_key + jnp.arange(term_span, dtype=jnp.int32)

        def compute_term(unused):
            scores = block_scores(query_matrix, key_block, positions, key_pos)
            probs = jnp.exp(scores - log_total[..., None])
            dprob = jnp.einsum(
                "gqhrd,gkhd->ghrqk",
                attention_gradient,
                value_block,
                preferred_element_type=jnp.float32,
            )
            score_grad = (probs * (dprob - delta[..., None])).astype(jnp.bfloat16)
            key_term = (
                jnp.einsum(
                    "ghrqk,gqhrd->kghd",
                    score_grad,
                    query_matrix,
                    preferred_element_type=jnp.float32,
                )
                * 0.125
            )
            value_term = jnp.einsum(
                "ghrqk,gqhrd->kghd",
                probs.astype(jnp.bfloat16),
                attention_gradient,
                preferred_element_type=jnp.float32,
            )
            return jnp.concatenate(
                [
                    key_term.reshape(term_span, query_group_count, key_value_width),
                    value_term.reshape(term_span, query_group_count, key_value_width),
                ],
                -1,
            )

        def empty_term(unused):
            return jnp.zeros((term_span, query_group_count, 2 * key_value_width), jnp.float32)

        return lax.cond(first_key <= last_row, compute_term, empty_term, 0)

    terms = lax.map(key_block_term, jnp.arange(row_total // term_span, dtype=jnp.int32))
    paired_gradients = (
        lax.psum_scatter(
            terms.reshape(row_total, query_group_count, 2 * key_value_width).astype(jnp.bfloat16),
            "ctx",
            scatter_dimension=0,
            tiled=True,
        )
        .astype(jnp.float32)
        .transpose(1, 0, 2)
    )
    key_gradient = paired_gradients[..., :key_value_width].reshape(
        query_group_count, local_row_count, KEY_VALUE_HEADS, head_width
    )
    value_gradient = paired_gradients[..., key_value_width:].reshape(
        query_group_count, local_row_count, KEY_VALUE_HEADS, head_width
    )
    query_pre_grad = rotate_back(
        query_grad.reshape(query_group_count, local_row_count, QUERY_HEADS, head_width),
        cosine_table,
        sine_table,
    )
    query_pre_grad = query_pre_grad.astype(jnp.bfloat16).reshape(
        query_group_count, local_row_count, query_width
    )
    key_pre_grad = (
        rotate_back(key_gradient, cosine_table, sine_table)
        .astype(jnp.bfloat16)
        .reshape(query_group_count, local_row_count, key_value_width)
    )
    value_pre_grad = value_gradient.astype(jnp.bfloat16).reshape(
        query_group_count, local_row_count, key_value_width
    )
    grad_query = jnp.einsum(
        "gsd,gse->de", normed1, query_pre_grad, preferred_element_type=jnp.float32
    )
    grad_key = jnp.einsum("gsd,gse->de", normed1, key_pre_grad, preferred_element_type=jnp.float32)
    grad_value = jnp.einsum(
        "gsd,gse->de", normed1, value_pre_grad, preferred_element_type=jnp.float32
    )
    normed1_grad = jnp.einsum(
        "gse,de->gsd", query_pre_grad, wq_full, preferred_element_type=jnp.float32
    )
    normed1_grad = normed1_grad + jnp.einsum(
        "gse,de->gsd", key_pre_grad, wk_full, preferred_element_type=jnp.float32
    )
    normed1_grad = normed1_grad + jnp.einsum(
        "gse,de->gsd", value_pre_grad, wv_full, preferred_element_type=jnp.float32
    )
    grad_gain1 = jnp.sum(normed1_grad * inputs * scale1, axis=(0, 1))
    scaled1 = gain1f * normed1_grad
    input_grad = (
        middle_grad
        + scale1 * scaled1
        - inputs * scale1**3 * jnp.mean(scaled1 * inputs, axis=-1, keepdims=True)
    )
    totals = lax.psum(
        (
            grad_gain1,
            grad_query,
            grad_key,
            grad_value,
            grad_out,
            grad_gain2,
            grad_gate,
            grad_up,
            grad_down,
        ),
        ("dp", "ctx", "fsdp"),
    )
    owner = lax.axis_index("fsdp")
    shards = (norm1_gain, w_query, w_key, w_value, w_out, norm2_gain, w_gate, w_up, w_down)
    shares = tuple(
        (
            lax.dynamic_slice_in_dim(summed, owner * shard.shape[0], shard.shape[0], 0)
            for summed, shard in zip(totals, shards)
        )
    )
    return (
        output,
        input_grad,
        shares[0],
        shares[1],
        shares[2],
        shares[3],
        shares[4],
        shares[5],
        shares[6],
        shares[7],
        shares[8],
    )


WIDTH = 576
QUERY_WIDTH = QUERY_HEADS * HEAD_SIZE
KEY_WIDTH = KEY_VALUE_HEADS * HEAD_SIZE
ROTATED = QUERY_HEADS + KEY_VALUE_HEADS
REPEAT = QUERY_HEADS // KEY_VALUE_HEADS
HALF = HEAD_SIZE // 2
USED = QUERY_WIDTH + 2 * KEY_WIDTH
PACKED = USED + 64
GAIN_ROWS = 16
TILE = 256
WIDE_TILE = 512
VMEM_LIMIT = 60 * 1024 * 1024
F32 = jnp.float32
BF16 = jnp.bfloat16


def mm(a, b):
    return jnp.dot(a, b, preferred_element_type=F32)


def mm_nt(a, b):
    return lax.dot_general(a, b, (((1,), (1,)), ((), ())), preferred_element_type=F32)


def flip(tensor):
    return tensor.astype(F32).T.astype(tensor.dtype)


def span(index, size, step=None):
    step = size if step is None else step
    return pl.ds(pl.multiple_of(index * step, step), size)


def flip_blocks(target, source, block):
    def one(step, carry):
        at = span(step, block)
        target[at, :] = flip(source[:, at])
        return carry

    lax.fori_loop(0, source.shape[1] // block, one, 0)


def column_scale(tensor):
    return lax.rsqrt(jnp.mean(tensor * tensor, axis=0, keepdims=True) + EPSILON)


def sigmoid(tensor):
    return 0.5 * jnp.tanh(0.5 * tensor) + 0.5


def causal_last(scores, tile):
    shape = (TILE, REPEAT * TILE)
    visible = lax.broadcasted_iota(jnp.int32, shape, 0) <= (
        lax.broadcasted_iota(jnp.int32, shape, 1) & (TILE - 1)
    )
    last = jnp.where(visible, scores[tile * TILE :, :], MASKED)
    return last if tile == 0 else jnp.concatenate([scores[: tile * TILE, :], last], 0)


def attend_kernel(
    place,
    tokens,
    theirs,
    w_own,
    w_y,
    w_core,
    w_both,
    cosine,
    sine,
    x_seq,
    normed,
    packed,
    gains,
    qkv_t,
    log_total,
    attended_t,
    packed_t,
    key_rows,
):
    me, shard = place[0], place[1]
    half_rows = theirs.shape[1]
    sequence = 2 * half_rows
    x_seq[:, span(me, half_rows)] = tokens[me]
    x_seq[:, span(1 - me, half_rows)] = theirs[...]
    rows = packed.shape[0] // 4
    for bits, piece in ((0, w_own), (2, w_y), (1, w_core), (3, w_both)):
        at = span(shard ^ bits, rows)
        packed[at, :] = piece[:rows, :]
        gains[at, :GAIN_ROWS] = piece[rows:, :TILE].astype(F32).T[:rows, :]
    flip_blocks(packed_t, packed, TILE)
    gain1 = gains[:, :1]

    def project(step, carry):
        at = span(step, WIDE_TILE)
        x = x_seq[:, at].astype(F32)
        normed_tile = (x * column_scale(x) * gain1).astype(BF16)
        normed[:, at] = normed_tile
        turned = mm(packed_t[:USED, :], normed_tile)
        cos, sin = cosine[:, at], sine[:, at]
        for head in range(ROTATED):
            a = turned[head * HEAD_SIZE : head * HEAD_SIZE + HALF, :]
            b = turned[head * HEAD_SIZE + HALF : (head + 1) * HEAD_SIZE, :]
            both = jnp.concatenate([a * cos - b * sin, b * cos + a * sin], 0)
            if head < QUERY_HEADS:
                both = both * 0.125
            else:
                key_rows[head - QUERY_HEADS, at, :] = both.T.astype(BF16)
            qkv_t[head * HEAD_SIZE : (head + 1) * HEAD_SIZE, at] = both.astype(BF16)
        qkv_t[ROTATED * HEAD_SIZE :, at] = turned[ROTATED * HEAD_SIZE :, :].astype(BF16)
        return carry

    lax.fori_loop(0, sequence // WIDE_TILE, project, 0)

    def one_group(group, carry):
        value_rows = span(ROTATED + group, HEAD_SIZE)
        for tile in range(sequence // TILE):
            extent = (tile + 1) * TILE
            cols = slice(tile * TILE, extent)
            queries = jnp.concatenate(
                [qkv_t[span(group * REPEAT + r, HEAD_SIZE), cols] for r in range(REPEAT)], 1
            )
            scores = causal_last(mm(key_rows[group, :extent, :], queries), tile)
            top = jnp.max(scores, axis=0, keepdims=True)
            weights = jnp.exp(scores - top)
            total = jnp.sum(weights, axis=0, keepdims=True)
            mixed = mm(qkv_t[value_rows, :extent], weights.astype(BF16))
            mixed = (mixed * (1.0 / total)).astype(BF16)
            logs = top + jnp.log(total)
            for r in range(REPEAT):
                own = slice(r * TILE, (r + 1) * TILE)
                attended_t[span(group * REPEAT + r, HEAD_SIZE), cols] = mixed[:, own]
                log_total[group, r : r + 1, cols] = logs[:, own]
        return carry

    lax.fori_loop(0, KEY_VALUE_HEADS, one_group, 0)


def feed_forward_kernel(
    place,
    x_seq,
    attended_t,
    out_grad,
    dy_theirs,
    gains,
    a_own,
    a_y,
    a_core,
    a_both,
    b_own,
    b_y,
    b_core,
    b_both,
    out_keep,
    out_send,
    middle_grad,
    attended_grad_t,
    keep_g,
    send_g,
    keep_u,
    send_u,
    keep_a,
    send_a,
    w_out,
    w_gate,
    w_up,
    w_down,
    w_out_t,
    w_gate_t,
    w_up_t,
    w_down_t,
    dy_seq,
    normed,
    hidden,
    gate_grad,
    up_grad,
    out_sum,
    grad_sum,
    scales,
    total,
):
    me, shard, level = place[0], place[1], place[2]
    half_rows = dy_theirs.shape[1]
    sequence = 2 * half_rows
    dy_seq[:, span(me, half_rows)] = out_grad[me]
    dy_seq[:, span(1 - me, half_rows)] = dy_theirs[...]
    rows = b_own.shape[0]
    half = rows // 2
    part = w_gate.shape[1] // 4
    down_rows = a_own.shape[1]
    wide = 4 * down_rows
    a_pieces = ((0, a_own), (2, a_y), (1, a_core), (3, a_both))
    b_pieces = ((0, b_own), (2, b_y), (1, b_core), (3, b_both))
    for bits, b in b_pieces:
        w_out[span(shard ^ bits, rows), :] = b[:, 2 * wide :]
    w_out_t[...] = flip(w_out[...])
    gain2 = gains[:, 1:2]
    tiles = [slice(i, i + WIDE_TILE) for i in range(0, sequence, WIDE_TILE)]
    for at in tiles:
        middle = x_seq[:, at].astype(F32) + mm(w_out_t[...], attended_t[:, at])
        middle_grad[:, at] = middle
        scale = column_scale(middle)
        scales[0:1, at] = scale
        normed[:, at] = (middle * scale * gain2).astype(BF16)

    def shard_slices():
        for y_bit in range(2):
            for x_bit in range(2):
                for core_bit in range(2):
                    row = (shard ^ (2 * y_bit + core_bit)) * 2 + (me ^ x_bit)
                    yield y_bit, x_bit, core_bit, span(row, half)

    def one_chunk(chunk, carry):
        for bits, b in b_pieces:
            at = span(shard ^ bits, rows)
            for s in range(4):
                to = slice(s * part, (s + 1) * part)
                first = s * down_rows
                w_gate[at, to] = b[:, pl.ds(pl.multiple_of(first + chunk * part, part), part)]
                first = wide + s * down_rows
                w_up[at, to] = b[:, pl.ds(pl.multiple_of(first + chunk * part, part), part)]
        for bits, a in a_pieces:
            w_down_t[:, span(shard ^ bits, part)] = a[:, span(chunk, part)]
        w_gate_t[...] = flip(w_gate[...])
        w_up_t[...] = flip(w_up[...])
        w_down[...] = flip(w_down_t[...])
        for at in tiles:
            gate = mm(w_gate_t[...], normed[:, at])
            up = mm(w_up_t[...], normed[:, at])
            hidden_grad = mm(w_down[...], dy_seq[:, at])
            sig = sigmoid(gate)
            silu = gate * sig
            hidden_tile = (silu * up).astype(BF16)
            gate_tile = (hidden_grad * up * (sig + silu * (1.0 - sig))).astype(BF16)
            up_tile = (hidden_grad * silu).astype(BF16)
            hidden[:, at] = hidden_tile
            gate_grad[:, at] = gate_tile
            up_grad[:, at] = up_tile
            out_part = mm(w_down_t[...], hidden_tile)
            grad_part = mm(w_gate[...], gate_tile) + mm(w_up[...], up_tile)

            @pl.when(chunk == 0)
            def _():
                out_sum[:, at] = out_part
                grad_sum[:, at] = grad_part

            @pl.when(chunk > 0)
            def _():
                out_sum[:, at] += out_part
                grad_sum[:, at] += grad_part

        total[...] = mm_nt(normed[...], gate_grad[...])
        for y_bit, x_bit, core_bit, at in shard_slices():
            target = send_g if core_bit else keep_g
            for s in range(4):
                half_at, first = divmod(s * down_rows, 2 * down_rows)
                to = pl.ds(pl.multiple_of(first + chunk * part, part), part)
                target[y_bit, x_bit, level ^ half_at, :, to] = total[
                    at, s * part : (s + 1) * part
                ].astype(BF16)
        total[...] = mm_nt(normed[...], up_grad[...])
        for y_bit, x_bit, core_bit, at in shard_slices():
            target = send_u if core_bit else keep_u
            for s in range(4):
                half_at, first = divmod(s * down_rows, 2 * down_rows)
                to = pl.ds(pl.multiple_of(first + chunk * part, part), part)
                target[y_bit, x_bit, level ^ half_at, :, to] = total[
                    at, s * part : (s + 1) * part
                ].astype(BF16)
        total[...] = mm_nt(dy_seq[...], hidden[...])
        for y_bit in range(2):
            for core_bit, target in ((0, keep_a), (1, send_a)):
                columns = span(shard ^ (2 * y_bit + core_bit), part)
                for x_bit in range(2):
                    target[x_bit, y_bit, :, span(chunk, part)] = total[
                        span(me ^ x_bit, keep_a.shape[2]), columns
                    ].astype(BF16)
        return carry

    lax.fori_loop(0, down_rows // part, one_chunk, 0)

    for index, at in enumerate(tiles):
        middle = middle_grad[:, at]
        output = (middle + out_sum[:, at]).astype(BF16)
        block, first = divmod(index * WIDE_TILE, half_rows)
        block_cols = slice(first, first + WIDE_TILE)

        @pl.when(me == block)
        def _():
            out_keep[:, block_cols] = output

        @pl.when(me != block)
        def _():
            out_send[:, block_cols] = output

        scale = scales[0:1, at]
        scaled = grad_sum[:, at] * gain2
        back = (
            dy_seq[:, at].astype(F32)
            + scale * scaled
            - middle * (scale * scale * scale) * jnp.mean(scaled * middle, axis=0, keepdims=True)
        )
        middle_grad[:, at] = back
        branch = back.astype(BF16)
        normed[:, at] = branch
        attended_grad_t[:, at] = mm(w_out[...], branch).astype(BF16)
    columns = QUERY_WIDTH // 2
    for start in (0, TILE, 2 * TILE):
        count = min(TILE, QUERY_WIDTH - start)
        total[:, :count] = mm_nt(attended_t[...], normed[start : start + count, :])
        for y_bit, x_bit, core_bit, at in shard_slices():
            target = send_u if core_bit else keep_u
            for half_at in range(2):
                low = max(start, half_at * columns)
                high = min(start + count, (half_at + 1) * columns)
                if low < high:
                    to = 2 * down_rows + low - half_at * columns
                    target[y_bit, x_bit, level ^ half_at, :, to : to + high - low] = total[
                        at, low - start : high - start
                    ].astype(BF16)


def attend_back_kernel(
    queries_t,
    keys_t,
    values_t,
    log_total,
    attended_t,
    grad_t,
    cosine,
    sine,
    dq_out,
    dk_out,
    dv_out,
    keys,
    values,
    dk,
    dv,
):
    sequence = keys_t.shape[1]
    keys[...] = flip(keys_t[...])
    values[...] = flip(values_t[...])
    dk[...] = jnp.zeros_like(dk)
    dv[...] = jnp.zeros_like(dv)

    def back(a, b, cos, sin):
        return (a * cos + b * sin).astype(BF16), (b * cos - a * sin).astype(BF16)

    for tile in range(sequence // TILE):
        extent = (tile + 1) * TILE
        cols = slice(tile * TILE, extent)
        heads = [slice(r * HEAD_SIZE, (r + 1) * HEAD_SIZE) for r in range(REPEAT)]
        q_t = jnp.concatenate([queries_t[head, cols] for head in heads], 1)
        do_t = jnp.concatenate([grad_t[head, cols] for head in heads], 1)
        mixed = jnp.concatenate([attended_t[head, cols] for head in heads], 1)
        logs = jnp.concatenate([log_total[0, r : r + 1, cols] for r in range(REPEAT)], 1)
        delta = jnp.sum(do_t.astype(F32) * mixed.astype(F32), axis=0, keepdims=True)
        scores = causal_last(mm(keys[:extent, :], q_t), tile)
        probs = jnp.exp(scores - logs)
        dprob = mm(values[:extent, :], do_t)
        score_grad = (probs * (dprob - delta)).astype(BF16)
        dv[:extent, :] += mm(probs.astype(BF16), flip(do_t))
        dk[:extent, :] += mm(score_grad, flip(q_t))
        dq = mm(keys_t[:, :extent], score_grad) * 0.125
        cos, sin = cosine[:, cols], sine[:, cols]
        for r, head in enumerate(heads):
            own = slice(r * TILE, (r + 1) * TILE)
            a, b = back(dq[:HALF, own], dq[HALF:, own], cos, sin)
            dq_out[head.start : head.start + HALF, cols] = a
            dq_out[head.start + HALF : head.stop, cols] = b
    turned = dk[...].T
    a, b = back(turned[:HALF, :], turned[HALF:, :], cosine[...], sine[...])
    dk_out[:HALF, :] = a
    dk_out[HALF:, :] = b
    dv_out[...] = dv[...].T.astype(BF16)


def joined_kernel(place, normed, *rest):
    heads = rest[: 3 * KEY_VALUE_HEADS]
    keep_w, send_w, joined, total = rest[3 * KEY_VALUE_HEADS :]
    me, shard = place[0], place[1]
    group_width = REPEAT * HEAD_SIZE
    for group in range(KEY_VALUE_HEADS):
        dq, dk, dv = heads[3 * group : 3 * group + 3]
        joined[group * group_width : (group + 1) * group_width, :] = dq[...]
        at = QUERY_WIDTH + group * HEAD_SIZE
        joined[at : at + HEAD_SIZE, :] = dk[...]
        at = QUERY_WIDTH + KEY_WIDTH + group * HEAD_SIZE
        joined[at : at + HEAD_SIZE, :] = dv[...]
    half = keep_w.shape[2]
    for first in range(0, USED, 512):
        cols = slice(first, min(first + 512, USED))
        total[:, cols] = mm_nt(normed[...], joined[cols, :])
    for y_bit in range(2):
        for x_bit in range(2):
            for core_bit, target in ((0, keep_w), (1, send_w)):
                row = (shard ^ (2 * y_bit + core_bit)) * 2 + (me ^ x_bit)
                target[y_bit, x_bit] = total[span(row, half), :].astype(BF16)


def input_kernel(place, x_seq, packed, gains, middle_grad, joined, keep_x, send_x, grad_seq):
    me = place[0]
    half_rows = keep_x.shape[1]
    sequence = 2 * half_rows
    gain1 = gains[:, :1]
    for first in range(0, sequence, WIDE_TILE):
        at = slice(first, first + WIDE_TILE)
        scaled = mm(packed[:, :USED], joined[:, at]) * gain1
        x = x_seq[:, at].astype(F32)
        scale = column_scale(x)
        grad_seq[:, at] = (
            middle_grad[:, at]
            + scale * scaled
            - x * (scale * scale * scale) * jnp.mean(scaled * x, axis=0, keepdims=True)
        )
    keep_x[...] = grad_seq[:, span(me, half_rows)]
    send_x[...] = grad_seq[:, span(1 - me, half_rows)].astype(BF16)


def call(kernel, out, scratch, flops, exps, args, name):
    shapes = [jax.ShapeDtypeStruct(s, d) for s, d in out]
    moved = sum(a.size * a.dtype.itemsize for a in args[1:]) + sum(
        s.size * s.dtype.itemsize for s in shapes
    )
    in_specs = [pl.BlockSpec(memory_space=pltpu.SMEM)] + [
        pl.BlockSpec(memory_space=pltpu.VMEM)
    ] * (len(args) - 1)
    return pl.pallas_call(
        kernel,
        out_shape=shapes,
        in_specs=in_specs,
        out_specs=[pl.BlockSpec(memory_space=pltpu.VMEM)] * len(shapes),
        scratch_shapes=[pltpu.VMEM(s, d) for s, d in scratch],
        compiler_params=pltpu.CompilerParams(vmem_limit_bytes=VMEM_LIMIT),
        cost_estimate=pl.CostEstimate(flops=flops, bytes_accessed=moved, transcendentals=exps),
        name=name,
    )(*args)


def attend_back(group, qkv_t, log_total, attended_t, grad_t, cosine, sine):
    sequence = qkv_t.shape[1]
    group_width = REPEAT * HEAD_SIZE

    def rows_of(size, index):
        return pl.BlockSpec((size, sequence), lambda step: (index, 0))

    flops = 5 * REPEAT * sequence * sequence * HEAD_SIZE * 2
    return pl.pallas_call(
        attend_back_kernel,
        grid=(1,),
        out_shape=[
            jax.ShapeDtypeStruct((group_width, sequence), BF16),
            jax.ShapeDtypeStruct((HEAD_SIZE, sequence), BF16),
            jax.ShapeDtypeStruct((HEAD_SIZE, sequence), BF16),
        ],
        in_specs=[
            rows_of(group_width, group),
            rows_of(HEAD_SIZE, QUERY_HEADS + group),
            rows_of(HEAD_SIZE, ROTATED + group),
            pl.BlockSpec((1, 8, sequence), lambda step: (group, 0, 0)),
            rows_of(group_width, group),
            rows_of(group_width, group),
            rows_of(HALF, 0),
            rows_of(HALF, 0),
        ],
        out_specs=[rows_of(group_width, 0), rows_of(HEAD_SIZE, 0), rows_of(HEAD_SIZE, 0)],
        scratch_shapes=[
            pltpu.VMEM((sequence, HEAD_SIZE), BF16),
            pltpu.VMEM((sequence, HEAD_SIZE), BF16),
            pltpu.VMEM((sequence, HEAD_SIZE), F32),
            pltpu.VMEM((sequence, HEAD_SIZE), F32),
        ],
        compiler_params=pltpu.CompilerParams(vmem_limit_bytes=VMEM_LIMIT),
        cost_estimate=pl.CostEstimate(
            flops=flops, bytes_accessed=4_000_000, transcendentals=REPEAT * sequence * sequence
        ),
        name="attend_back",
    )(qkv_t, qkv_t, qkv_t, log_total, attended_t, grad_t, cosine, sine)


def across(tensor, bit):
    return lax.ppermute(tensor, "fsdp", [(i, i ^ bit) for i in range(4)])


def over_context(tensor):
    return lax.ppermute(tensor, "ctx", [(0, 1), (1, 0)])


def after(tensor, *done):
    return lax.optimization_barrier((tensor, *done))[0]


def together(*values):
    return lax.optimization_barrier(values)


def add(a, b):
    return (a.astype(F32) + b.astype(F32)).astype(BF16)


def along(tensor, bit):
    size = lax.axis_size("dp")
    return lax.ppermute(tensor, "dp", [(i, i ^ bit) for i in range(size)])


def sum_along(part, first=1):
    bit = first
    while bit < lax.axis_size("dp"):
        part = add(part, along(part, bit))
        bit *= 2
    return part


def whole_sequences(
    tokens, norm1_gain, w_query, w_key, w_value, w_out, norm2_gain, w_gate, w_up, w_down, out_grad
):
    half_rows, width = tokens.shape[1:]
    sequence = 2 * half_rows
    rows = w_query.shape[0]
    half = rows // 2
    down_rows = w_down.shape[0]
    hidden_width = w_gate.shape[1]
    part = 128
    me = lax.axis_index("ctx")
    place = jnp.stack([me, lax.axis_index("fsdp"), lax.axis_index("dp") & 1]).astype(jnp.int32)
    tokens = jnp.swapaxes(tokens, 1, 2)
    out_grad = jnp.swapaxes(out_grad, 1, 2)

    tokens_send = lax.dynamic_index_in_dim(tokens, 1 - me, 0, False)
    tokens_theirs = over_context(tokens_send)
    qkv_own = after(jnp.concatenate([w_query, w_key, w_value], 1), tokens_send)
    gain_own = jnp.pad(
        jnp.stack([norm1_gain, norm2_gain]), ((0, GAIN_ROWS - 2), (0, PACKED - rows))
    )
    packed = jnp.concatenate([jnp.pad(qkv_own, ((0, 0), (0, PACKED - USED))), gain_own], 0)
    packed_y = across(packed, 2)
    packed_core = across(packed, 1)
    b_own = jnp.concatenate([w_gate, w_up, w_out], 1)
    a_own = w_down.T
    cosine, sine = rope_tables(jnp.arange(sequence, dtype=jnp.int32), HEAD_SIZE)
    b_own, a_own, packed_y, cosine, sine, place = together(
        b_own, a_own, packed_y, cosine.T, sine.T, place
    )
    packed_both = across(packed_y, 1)
    b_y, a_y = across(b_own, 2), across(a_own, 2)
    b_core, a_core = across(b_own, 1), across(a_own, 1)
    dy_theirs = over_context(
        after(lax.dynamic_index_in_dim(out_grad, 1 - me, 0, False), tokens_theirs)
    )

    pairs = sequence * sequence
    x_seq, normed, packed_all, gains, qkv_t, log_total, attended_t = call(
        attend_kernel,
        [
            ((width, sequence), BF16),
            ((width, sequence), BF16),
            ((width, PACKED), BF16),
            ((width, 128), F32),
            ((USED, sequence), BF16),
            ((KEY_VALUE_HEADS, 8, sequence), F32),
            ((QUERY_WIDTH, sequence), BF16),
        ],
        [((PACKED, width), BF16), ((KEY_VALUE_HEADS, sequence, HEAD_SIZE), BF16)],
        2 * sequence * width * PACKED + 4 * QUERY_WIDTH * pairs,
        QUERY_HEADS * pairs,
        (place, tokens, tokens_theirs, packed, packed_y, packed_core, packed_both, cosine, sine),
        "attend",
    )

    b_y, a_y, b_core, a_core, dy_theirs, attended_t = together(
        b_y, a_y, b_core, a_core, dy_theirs, attended_t
    )
    b_both, a_both = across(b_y, 1), across(a_y, 1)

    g_shape = ((2, 2, 2, half, hidden_width // 2), BF16)
    u_shape = ((2, 2, 2, half, (hidden_width + QUERY_WIDTH) // 2), BF16)
    a_shape = ((2, 2, width // 2, down_rows), BF16)
    natural, turned = ((width, 4 * part), BF16), ((4 * part, width), BF16)
    row, wide_row = ((width, sequence), BF16), ((4 * part, sequence), BF16)
    (
        out_keep,
        out_send,
        middle_grad,
        grad_t,
        keep_g,
        send_g,
        keep_u,
        send_u,
        keep_a,
        send_a,
    ) = call(
        feed_forward_kernel,
        [
            ((width, half_rows), BF16),
            ((width, half_rows), BF16),
            ((width, sequence), F32),
            ((QUERY_WIDTH, sequence), BF16),
            g_shape,
            g_shape,
            u_shape,
            u_shape,
            a_shape,
            a_shape,
        ],
        [
            ((QUERY_WIDTH, width), BF16),
            natural,
            natural,
            turned,
            ((width, QUERY_WIDTH), BF16),
            turned,
            turned,
            natural,
            row,
            row,
            wide_row,
            wide_row,
            wide_row,
            ((width, sequence), F32),
            ((width, sequence), F32),
            ((8, sequence), F32),
            ((width, 4 * part), F32),
        ],
        2 * sequence * width * (9 * hidden_width + 3 * QUERY_WIDTH),
        sequence * hidden_width,
        (
            place,
            x_seq,
            attended_t,
            out_grad,
            dy_theirs,
            gains,
            a_own,
            a_y,
            a_core,
            a_both,
            b_own,
            b_y,
            b_core,
            b_both,
        ),
        "feed_forward",
    )

    back_args = (log_total, attended_t, grad_t, cosine, sine)
    out_theirs = over_context(out_send)
    got_g, got_u, got_a = across(send_g, 1), across(send_u, 1), across(send_a, 1)
    grads0 = attend_back(0, qkv_t, *back_args)
    got_g, got_u, got_a, *grads0 = together(got_g, got_u, got_a, *grads0)
    g0, g1 = add(keep_g[0], got_g[0]), add(keep_g[1], got_g[1])
    a0, a1 = add(keep_a[0], got_a[0]), add(keep_a[1], got_a[1])
    u0, u1 = add(keep_u[0], got_u[0]), add(keep_u[1], got_u[1])
    g1, a1, u1, out_theirs, qkv_t = together(g1, a1, u1, out_theirs, qkv_t)

    got_g, got_a, got_u = across(g1, 2), over_context(a1), across(u1, 2)
    grads1 = attend_back(1, qkv_t, *back_args)
    got_g, got_a, *grads1 = together(got_g, got_a, *grads1)
    g0, g1 = add(g0[0], got_g[0]), add(g0[1], got_g[1])
    a0, a1 = add(a0[0], got_a[0]), add(a0[1], got_a[1])
    g1, a1, qkv_t = together(g1, a1, qkv_t)

    got_g, got_a = over_context(g1), across(a1, 2)
    grads2 = attend_back(2, qkv_t, *back_args)
    keep_w, send_w, joined = call(
        joined_kernel,
        [((2, 2, half, USED), BF16), ((2, 2, half, USED), BF16), ((USED, sequence), BF16)],
        [((width, USED), F32)],
        2 * sequence * width * USED,
        0,
        (place, normed, *grads0, *grads1, *grads2),
        "joined",
    )
    got_g, got_u, got_a, send_w, joined = together(got_g, got_u, got_a, send_w, joined)
    got_w = across(send_w, 1)
    u0, u1 = add(u0[0], got_u[0]), add(u0[1], got_u[1])
    g0, g1 = add(g0[0], got_g[0]), add(g0[1], got_g[1])
    a_part = add(a0, got_a)
    u1, g1, a_part, joined = together(u1, g1, a_part, joined)
    got_u, got_g, got_a = over_context(u1), along(g1, 1), along(a_part, 1)

    keep_x, send_x = call(
        input_kernel,
        [((width, half_rows), F32), ((width, half_rows), BF16)],
        [((width, sequence), F32)],
        2 * sequence * width * USED,
        sequence,
        (place, x_seq, packed_all, gains, middle_grad, joined),
        "input_side",
    )
    got_u, got_g, got_a, got_w, send_x = together(got_u, got_g, got_a, got_w, send_x)
    w0, w1 = add(keep_w[0], got_w[0]), add(keep_w[1], got_w[1])
    got_w = across(w1, 2)
    level = lax.axis_index("dp") & 1
    x_theirs = over_context(send_x)

    def finish_halves(own):
        own = sum_along(own, 2)
        other = along(own, 1)
        low = jnp.where(level == 0, own, other)
        high = jnp.where(level == 0, other, own)
        return jnp.stack([low, high])

    g_part = finish_halves(add(g0, got_g))
    a_part = sum_along(add(a_part, got_a), 2)
    w0, w1 = add(w0[0], got_w[0]), add(w0[1], got_w[1])
    w_part = sum_along(add(w0, over_context(w1)))
    u0, u1 = add(u0[0], got_u[0]), add(u0[1], got_u[1])
    u_part = finish_halves(add(u0, along(u1, 1)))

    def both_halves(part, other, axis=0):
        first = jnp.where(me == 0, part, other)
        second = jnp.where(me == 0, other, part)
        return jnp.concatenate([first, second], axis).astype(F32)

    g_sum = both_halves(g_part, over_context(g_part), 1)
    u_sum = both_halves(u_part, over_context(u_part), 1)
    a_sum = both_halves(a_part, over_context(a_part))
    w_sum = both_halves(w_part, over_context(w_part))
    gate_sum = jnp.concatenate([g_sum[0], g_sum[1]], 1)
    up_sum = jnp.concatenate([u_sum[i, :, : hidden_width // 2] for i in range(2)], 1)
    out_sum = jnp.concatenate([u_sum[i, :, hidden_width // 2 :] for i in range(2)], 1)

    def place_halves(keep, got):
        got = got.astype(keep.dtype)
        both = jnp.where(me == 0, jnp.stack([keep, got]), jnp.stack([got, keep]))
        return jnp.swapaxes(both, 1, 2)

    key_at = QUERY_WIDTH + KEY_WIDTH
    query_sum, key_sum, value_sum = (
        w_sum[:, :QUERY_WIDTH],
        w_sum[:, QUERY_WIDTH:key_at],
        w_sum[:, key_at:],
    )

    def gain_sum(gain, *pairs):
        return sum(jnp.sum(w.astype(F32) * g, axis=1) for w, g in pairs) / gain.astype(F32)

    return (
        place_halves(out_keep, out_theirs),
        place_halves(keep_x, x_theirs),
        gain_sum(norm1_gain, (w_query, query_sum), (w_key, key_sum), (w_value, value_sum)),
        query_sum,
        key_sum,
        value_sum,
        out_sum,
        gain_sum(norm2_gain, (w_gate, gate_sum), (w_up, up_sum)),
        gate_sum,
        up_sum,
        a_sum.T,
    )


def layer_step(tokens, *rest):
    whole = (
        lax.axis_size("ctx") == 2
        and lax.axis_size("fsdp") == 4
        and lax.axis_size("dp") % 2 == 0
        and tokens.shape[0] == 2
        and tokens.shape[1] % WIDE_TILE == 0
    )
    return (whole_sequences if whole else split_context)(tokens, *rest)


def solution(mesh):
    return jax.shard_map(
        layer_step,
        mesh=mesh,
        in_specs=(
            P(("dp", "fsdp"), "ctx", None),
            P("fsdp"),
            P("fsdp", None),
            P("fsdp", None),
            P("fsdp", None),
            P("fsdp", None),
            P("fsdp"),
            P("fsdp", None),
            P("fsdp", None),
            P("fsdp", None),
            P(("dp", "fsdp"), "ctx", None),
        ),
        out_specs=(
            P(("dp", "fsdp"), "ctx", None),
            P(("dp", "fsdp"), "ctx", None),
            P("fsdp"),
            P("fsdp", None),
            P("fsdp", None),
            P("fsdp", None),
            P("fsdp", None),
            P("fsdp"),
            P("fsdp", None),
            P("fsdp", None),
            P("fsdp", None),
        ),
        check_vma=False,
    )
```

```python
import functools
import math

import jax
import jax.numpy as jnp
from jax import lax
from jax.experimental import pallas as pl
from jax.experimental.pallas import tpu as pltpu
from jax.sharding import PartitionSpec as P

QUERY_HEADS = 9
KEY_VALUE_HEADS = 3
HEAD_SIZE = 64


EPSILON = 1e-05
ROPE_THETA = 100000.0
MASKED = -1e30


def rope_tables(positions, head_width):
    half_size = head_width // 2
    inverse = jnp.exp(
        jnp.arange(half_size, dtype=jnp.float32) * (-2.0 * math.log(ROPE_THETA) / head_width)
    )
    angle = positions.astype(jnp.float32)[:, None] * inverse[None, :]
    return (jnp.cos(angle), jnp.sin(angle))


def rotary_apply(tensor, cosine_table, sine_table):
    half_size = tensor.shape[-1] // 2
    first_half = tensor[..., :half_size]
    second_half = tensor[..., half_size:]
    cosine_table = cosine_table[None, :, None, :]
    sine_table = sine_table[None, :, None, :]
    return jnp.concatenate(
        [
            first_half * cosine_table - second_half * sine_table,
            second_half * cosine_table + first_half * sine_table,
        ],
        -1,
    )


def rotate_back(tensor, cosine_table, sine_table):
    half_size = tensor.shape[-1] // 2
    first_half = tensor[..., :half_size]
    second_half = tensor[..., half_size:]
    cosine_table = cosine_table[None, :, None, :]
    sine_table = sine_table[None, :, None, :]
    return jnp.concatenate(
        [
            first_half * cosine_table + second_half * sine_table,
            second_half * cosine_table - first_half * sine_table,
        ],
        -1,
    )


def rms_scale(tensor):
    return lax.rsqrt(jnp.mean(tensor * tensor, axis=-1, keepdims=True) + EPSILON)


def block_scores(query_block, key_block, query_pos, key_pos):
    scores = (
        jnp.einsum("gqhrd,gkhd->ghrqk", query_block, key_block, preferred_element_type=jnp.float32)
        * 0.125
    )
    visible = key_pos[None, :] <= query_pos[:, None]
    return jnp.where(visible, scores, MASKED)


def split_context(
    tokens, norm1_gain, w_query, w_key, w_value, w_out, norm2_gain, w_gate, w_up, w_down, out_grad
):
    gain1, wq_full, wk_full, wv_full, wo_full, gain2, wg_full, wu_full, wd_full = (
        lax.all_gather(norm1_gain, "fsdp", axis=0, tiled=True),
        lax.all_gather(w_query, "fsdp", axis=0, tiled=True),
        lax.all_gather(w_key, "fsdp", axis=0, tiled=True),
        lax.all_gather(w_value, "fsdp", axis=0, tiled=True),
        lax.all_gather(w_out, "fsdp", axis=0, tiled=True),
        lax.all_gather(norm2_gain, "fsdp", axis=0, tiled=True),
        lax.all_gather(w_gate, "fsdp", axis=0, tiled=True),
        lax.all_gather(w_up, "fsdp", axis=0, tiled=True),
        lax.all_gather(w_down, "fsdp", axis=0, tiled=True),
    )
    query_group_count, local_row_count, model_width = tokens.shape
    repeat_heads = QUERY_HEADS // KEY_VALUE_HEADS
    head_width = HEAD_SIZE
    key_value_width = KEY_VALUE_HEADS * HEAD_SIZE
    query_width = QUERY_HEADS * HEAD_SIZE
    first_row = lax.axis_index("ctx") * local_row_count
    last_row = first_row + local_row_count - 1
    positions = first_row + jnp.arange(local_row_count, dtype=jnp.int32)
    cosine_table, sine_table = rope_tables(positions, head_width)
    gain1f = gain1.astype(jnp.float32)
    gain2f = gain2.astype(jnp.float32)
    inputs = tokens.astype(jnp.float32)
    scale1 = rms_scale(inputs)
    normed1 = (inputs * scale1 * gain1f).astype(jnp.bfloat16)
    query_before_rotation = jnp.einsum(
        "gsd,de->gse", normed1, wq_full, preferred_element_type=jnp.float32
    )
    key_before_rotation = jnp.einsum(
        "gsd,de->gse", normed1, wk_full, preferred_element_type=jnp.float32
    )
    value_projected = jnp.einsum(
        "gsd,de->gse", normed1, wv_full, preferred_element_type=jnp.float32
    )
    query_matrix = rotary_apply(
        query_before_rotation.reshape(query_group_count, local_row_count, QUERY_HEADS, head_width),
        cosine_table,
        sine_table,
    ).astype(jnp.bfloat16)
    query_matrix = query_matrix.reshape(
        query_group_count, local_row_count, KEY_VALUE_HEADS, repeat_heads, head_width
    )
    key_local = rotary_apply(
        key_before_rotation.reshape(
            query_group_count, local_row_count, KEY_VALUE_HEADS, head_width
        ),
        cosine_table,
        sine_table,
    ).astype(jnp.bfloat16)
    local_value_rows = value_projected.astype(jnp.bfloat16)
    collected_keys, collected_values = (
        lax.all_gather(
            key_local.reshape(query_group_count, local_row_count, key_value_width),
            "ctx",
            axis=1,
            tiled=True,
        ),
        lax.all_gather(local_value_rows, "ctx", axis=1, tiled=True),
    )
    sequence_length = collected_keys.shape[1]
    every_key_row = collected_keys.reshape(
        query_group_count, sequence_length, KEY_VALUE_HEADS, head_width
    )
    every_value_row = collected_values.reshape(
        query_group_count, sequence_length, KEY_VALUE_HEADS, head_width
    )
    local_value_rows = local_value_rows.reshape(
        query_group_count, local_row_count, KEY_VALUE_HEADS, head_width
    )
    key_span = min(sequence_length, 512)
    block_total = last_row // key_span + 1

    def key_slices(step_index):
        first_key = step_index * key_span
        key_block = lax.dynamic_slice_in_dim(every_key_row, first_key, key_span, 1)
        value_block = lax.dynamic_slice_in_dim(every_value_row, first_key, key_span, 1)
        key_pos = first_key + jnp.arange(key_span, dtype=jnp.int32)
        return (key_block, value_block, key_pos)

    def stats_step(step_index, running):
        row_max, row_sum = running
        key_block, value_block, key_pos = key_slices(step_index)
        scores = block_scores(query_matrix, key_block, positions, key_pos)
        new_max = jnp.maximum(row_max, jnp.max(scores, axis=-1))
        row_sum = row_sum * jnp.exp(row_max - new_max) + jnp.sum(
            jnp.exp(scores - new_max[..., None]), axis=-1
        )
        return (new_max, row_sum)

    statistics_shape = (query_group_count, KEY_VALUE_HEADS, repeat_heads, local_row_count)
    row_max, row_sum = lax.fori_loop(
        0,
        block_total,
        stats_step,
        (jnp.full(statistics_shape, MASKED, jnp.float32), jnp.zeros(statistics_shape, jnp.float32)),
    )
    log_total = row_max + jnp.log(row_sum)

    def mix_step(step_index, running):
        key_block, value_block, key_pos = key_slices(step_index)
        scores = block_scores(query_matrix, key_block, positions, key_pos)
        probs = jnp.exp(scores - log_total[..., None]).astype(jnp.bfloat16)
        return running + jnp.einsum(
            "ghrqk,gkhd->gqhrd", probs, value_block, preferred_element_type=jnp.float32
        )

    attended_full = lax.fori_loop(
        0,
        block_total,
        mix_step,
        jnp.zeros(
            (query_group_count, local_row_count, KEY_VALUE_HEADS, repeat_heads, head_width),
            jnp.float32,
        ),
    )
    attended = attended_full.astype(jnp.bfloat16).reshape(
        query_group_count, local_row_count, query_width
    )
    branch = jnp.einsum("gse,ed->gsd", attended, wo_full, preferred_element_type=jnp.float32)
    middle = inputs + branch
    scale2 = rms_scale(middle)
    normed2 = (middle * scale2 * gain2f).astype(jnp.bfloat16)
    gate_act = jnp.einsum("gsd,df->gsf", normed2, wg_full, preferred_element_type=jnp.float32)
    up_act = jnp.einsum("gsd,df->gsf", normed2, wu_full, preferred_element_type=jnp.float32)
    gate_sig = jax.nn.sigmoid(gate_act)
    gate_silu = gate_act * gate_sig
    hidden = (gate_silu * up_act).astype(jnp.bfloat16)
    mlp_out = jnp.einsum("gsf,fd->gsd", hidden, wd_full, preferred_element_type=jnp.float32)
    output = (middle + mlp_out).astype(jnp.bfloat16)
    out_float = out_grad.astype(jnp.float32)
    grad_down = jnp.einsum("gsf,gsd->fd", hidden, out_grad, preferred_element_type=jnp.float32)
    hidden_grad = jnp.einsum("gsd,fd->gsf", out_grad, wd_full, preferred_element_type=jnp.float32)
    gate_grad = (hidden_grad * up_act * gate_sig * (1.0 + gate_act * (1.0 - gate_sig))).astype(
        jnp.bfloat16
    )
    up_grad = (hidden_grad * gate_silu).astype(jnp.bfloat16)
    grad_gate = jnp.einsum("gsd,gsf->df", normed2, gate_grad, preferred_element_type=jnp.float32)
    grad_up = jnp.einsum("gsd,gsf->df", normed2, up_grad, preferred_element_type=jnp.float32)
    normed2_grad = jnp.einsum("gsf,df->gsd", gate_grad, wg_full, preferred_element_type=jnp.float32)
    normed2_grad = normed2_grad + jnp.einsum(
        "gsf,df->gsd", up_grad, wu_full, preferred_element_type=jnp.float32
    )
    grad_gain2 = jnp.sum(normed2_grad * middle * scale2, axis=(0, 1))
    scaled2 = gain2f * normed2_grad
    middle_grad = (
        out_float
        + scale2 * scaled2
        - middle * scale2**3 * jnp.mean(scaled2 * middle, axis=-1, keepdims=True)
    )
    branch_grad = middle_grad.astype(jnp.bfloat16)
    grad_out = jnp.einsum("gse,gsd->ed", attended, branch_grad, preferred_element_type=jnp.float32)
    attended_output_gradient = jnp.einsum(
        "gsd,ed->gse", branch_grad, wo_full, preferred_element_type=jnp.float32
    ).astype(jnp.bfloat16)
    attention_gradient = attended_output_gradient.reshape(
        query_group_count, local_row_count, KEY_VALUE_HEADS, repeat_heads, head_width
    )
    delta = jnp.sum(attention_gradient.astype(jnp.float32) * attended_full, axis=-1).transpose(
        0, 2, 3, 1
    )

    def query_grad_step(step_index, running):
        key_block, value_block, key_pos = key_slices(step_index)
        scores = block_scores(query_matrix, key_block, positions, key_pos)
        probs = jnp.exp(scores - log_total[..., None])
        dprob = jnp.einsum(
            "gqhrd,gkhd->ghrqk", attention_gradient, value_block, preferred_element_type=jnp.float32
        )
        score_grad = (probs * (dprob - delta[..., None])).astype(jnp.bfloat16)
        return running + jnp.einsum(
            "ghrqk,gkhd->gqhrd", score_grad, key_block, preferred_element_type=jnp.float32
        )

    query_grad = (
        lax.fori_loop(
            0,
            block_total,
            query_grad_step,
            jnp.zeros(
                (query_group_count, local_row_count, KEY_VALUE_HEADS, repeat_heads, head_width),
                jnp.float32,
            ),
        )
        * 0.125
    )
    row_total = local_row_count * lax.axis_size("ctx")
    term_span = math.gcd(row_total, key_span)

    def key_block_term(step_index):
        first_key = step_index * term_span
        key_block = lax.dynamic_slice_in_dim(every_key_row, first_key, term_span, 1)
        value_block = lax.dynamic_slice_in_dim(every_value_row, first_key, term_span, 1)
        key_pos = first_key + jnp.arange(term_span, dtype=jnp.int32)

        def compute_term(unused):
            scores = block_scores(query_matrix, key_block, positions, key_pos)
            probs = jnp.exp(scores - log_total[..., None])
            dprob = jnp.einsum(
                "gqhrd,gkhd->ghrqk",
                attention_gradient,
                value_block,
                preferred_element_type=jnp.float32,
            )
            score_grad = (probs * (dprob - delta[..., None])).astype(jnp.bfloat16)
            key_term = (
                jnp.einsum(
                    "ghrqk,gqhrd->kghd",
                    score_grad,
                    query_matrix,
                    preferred_element_type=jnp.float32,
                )
                * 0.125
            )
            value_term = jnp.einsum(
                "ghrqk,gqhrd->kghd",
                probs.astype(jnp.bfloat16),
                attention_gradient,
                preferred_element_type=jnp.float32,
            )
            return jnp.concatenate(
                [
                    key_term.reshape(term_span, query_group_count, key_value_width),
                    value_term.reshape(term_span, query_group_count, key_value_width),
                ],
                -1,
            )

        def empty_term(unused):
            return jnp.zeros((term_span, query_group_count, 2 * key_value_width), jnp.float32)

        return lax.cond(first_key <= last_row, compute_term, empty_term, 0)

    terms = lax.map(key_block_term, jnp.arange(row_total // term_span, dtype=jnp.int32))
    paired_gradients = (
        lax.psum_scatter(
            terms.reshape(row_total, query_group_count, 2 * key_value_width).astype(jnp.bfloat16),
            "ctx",
            scatter_dimension=0,
            tiled=True,
        )
        .astype(jnp.float32)
        .transpose(1, 0, 2)
    )
    key_gradient = paired_gradients[..., :key_value_width].reshape(
        query_group_count, local_row_count, KEY_VALUE_HEADS, head_width
    )
    value_gradient = paired_gradients[..., key_value_width:].reshape(
        query_group_count, local_row_count, KEY_VALUE_HEADS, head_width
    )
    query_pre_grad = rotate_back(
        query_grad.reshape(query_group_count, local_row_count, QUERY_HEADS, head_width),
        cosine_table,
        sine_table,
    )
    query_pre_grad = query_pre_grad.astype(jnp.bfloat16).reshape(
        query_group_count, local_row_count, query_width
    )
    key_pre_grad = (
        rotate_back(key_gradient, cosine_table, sine_table)
        .astype(jnp.bfloat16)
        .reshape(query_group_count, local_row_count, key_value_width)
    )
    value_pre_grad = value_gradient.astype(jnp.bfloat16).reshape(
        query_group_count, local_row_count, key_value_width
    )
    grad_query = jnp.einsum(
        "gsd,gse->de", normed1, query_pre_grad, preferred_element_type=jnp.float32
    )
    grad_key = jnp.einsum("gsd,gse->de", normed1, key_pre_grad, preferred_element_type=jnp.float32)
    grad_value = jnp.einsum(
        "gsd,gse->de", normed1, value_pre_grad, preferred_element_type=jnp.float32
    )
    normed1_grad = jnp.einsum(
        "gse,de->gsd", query_pre_grad, wq_full, preferred_element_type=jnp.float32
    )
    normed1_grad = normed1_grad + jnp.einsum(
        "gse,de->gsd", key_pre_grad, wk_full, preferred_element_type=jnp.float32
    )
    normed1_grad = normed1_grad + jnp.einsum(
        "gse,de->gsd", value_pre_grad, wv_full, preferred_element_type=jnp.float32
    )
    grad_gain1 = jnp.sum(normed1_grad * inputs * scale1, axis=(0, 1))
    scaled1 = gain1f * normed1_grad
    input_grad = (
        middle_grad
        + scale1 * scaled1
        - inputs * scale1**3 * jnp.mean(scaled1 * inputs, axis=-1, keepdims=True)
    )
    totals = lax.psum(
        (
            grad_gain1,
            grad_query,
            grad_key,
            grad_value,
            grad_out,
            grad_gain2,
            grad_gate,
            grad_up,
            grad_down,
        ),
        ("dp", "ctx", "fsdp"),
    )
    owner = lax.axis_index("fsdp")
    shards = (norm1_gain, w_query, w_key, w_value, w_out, norm2_gain, w_gate, w_up, w_down)
    shares = tuple(
        (
            lax.dynamic_slice_in_dim(summed, owner * shard.shape[0], shard.shape[0], 0)
            for summed, shard in zip(totals, shards)
        )
    )
    return (
        output,
        input_grad,
        shares[0],
        shares[1],
        shares[2],
        shares[3],
        shares[4],
        shares[5],
        shares[6],
        shares[7],
        shares[8],
    )


WIDTH = 576
QUERY_WIDTH = QUERY_HEADS * HEAD_SIZE
KEY_WIDTH = KEY_VALUE_HEADS * HEAD_SIZE
ROTATED = QUERY_HEADS + KEY_VALUE_HEADS
REPEAT = QUERY_HEADS // KEY_VALUE_HEADS
HALF = HEAD_SIZE // 2
USED = QUERY_WIDTH + 2 * KEY_WIDTH
PACKED = USED + 64
GAIN_ROWS = 16
TILE = 256
WIDE_TILE = 512
MEBI = 1024 * 1024
F32 = jnp.float32
BF16 = jnp.bfloat16


def mm(a, b):
    return jnp.dot(a, b, preferred_element_type=F32)


def mm_nt(a, b):
    return lax.dot_general(a, b, (((1,), (1,)), ((), ())), preferred_element_type=F32)


def flip(tensor):
    return tensor.astype(F32).T.astype(tensor.dtype)


def span(index, size, step=None):
    step = size if step is None else step
    return pl.ds(pl.multiple_of(index * step, step), size)


def flip_blocks(target, source, block):
    def one(step, carry):
        at = span(step, block)
        target[at, :] = flip(source[:, at])
        return carry

    lax.fori_loop(0, source.shape[1] // block, one, 0)


def column_scale(tensor):
    return lax.rsqrt(jnp.mean(tensor * tensor, axis=0, keepdims=True) + EPSILON)


def sigmoid(tensor):
    return 0.5 * jnp.tanh(0.5 * tensor) + 0.5


def causal_last(scores, tile):
    shape = (TILE, REPEAT * TILE)
    visible = lax.broadcasted_iota(jnp.int32, shape, 0) <= (
        lax.broadcasted_iota(jnp.int32, shape, 1) & (TILE - 1)
    )
    last = jnp.where(visible, scores[tile * TILE :, :], MASKED)
    return last if tile == 0 else jnp.concatenate([scores[: tile * TILE, :], last], 0)


def attend_kernel(
    place,
    tokens,
    theirs,
    w_own,
    w_y,
    w_core,
    w_both,
    cosine,
    sine,
    x_seq,
    normed,
    packed,
    gains,
    qkv_t,
    log_total,
    attended_t,
    packed_t,
    key_rows,
):
    me, shard = place[0], place[1]
    half_rows = theirs.shape[1]
    sequence = 2 * half_rows
    x_seq[:, span(me, half_rows)] = tokens[me]
    x_seq[:, span(1 - me, half_rows)] = theirs[...]
    rows = packed.shape[0] // 4
    for bits, piece in ((0, w_own), (2, w_y), (1, w_core), (3, w_both)):
        at = span(shard ^ bits, rows)
        packed[at, :] = piece[:rows, :]
        gains[at, :GAIN_ROWS] = piece[rows:, :TILE].astype(F32).T[:rows, :]
    flip_blocks(packed_t, packed, TILE)
    gain1 = gains[:, :1]

    def project(step, carry):
        at = span(step, WIDE_TILE)
        x = x_seq[:, at].astype(F32)
        normed_tile = (x * column_scale(x) * gain1).astype(BF16)
        normed[:, at] = normed_tile
        turned = mm(packed_t[:USED, :], normed_tile)
        cos, sin = cosine[:, at], sine[:, at]
        for head in range(ROTATED):
            a = turned[head * HEAD_SIZE : head * HEAD_SIZE + HALF, :]
            b = turned[head * HEAD_SIZE + HALF : (head + 1) * HEAD_SIZE, :]
            both = jnp.concatenate([a * cos - b * sin, b * cos + a * sin], 0)
            if head < QUERY_HEADS:
                both = both * 0.125
            else:
                key_rows[head - QUERY_HEADS, at, :] = both.T.astype(BF16)
            qkv_t[head * HEAD_SIZE : (head + 1) * HEAD_SIZE, at] = both.astype(BF16)
        qkv_t[ROTATED * HEAD_SIZE :, at] = turned[ROTATED * HEAD_SIZE :, :].astype(BF16)
        return carry

    lax.fori_loop(0, sequence // WIDE_TILE, project, 0)

    def one_group(group, carry):
        value_rows = span(ROTATED + group, HEAD_SIZE)
        for tile in range(sequence // TILE):
            extent = (tile + 1) * TILE
            cols = slice(tile * TILE, extent)
            queries = jnp.concatenate(
                [qkv_t[span(group * REPEAT + r, HEAD_SIZE), cols] for r in range(REPEAT)], 1
            )
            scores = causal_last(mm(key_rows[group, :extent, :], queries), tile)
            top = jnp.max(scores, axis=0, keepdims=True)
            weights = jnp.exp(scores - top)
            total = jnp.sum(weights, axis=0, keepdims=True)
            mixed = mm(qkv_t[value_rows, :extent], weights.astype(BF16))
            mixed = (mixed * (1.0 / total)).astype(BF16)
            logs = top + jnp.log(total)
            for r in range(REPEAT):
                own = slice(r * TILE, (r + 1) * TILE)
                attended_t[span(group * REPEAT + r, HEAD_SIZE), cols] = mixed[:, own]
                log_total[group, r : r + 1, cols] = logs[:, own]
        return carry

    lax.fori_loop(0, KEY_VALUE_HEADS, one_group, 0)


def feed_forward_kernel(
    place,
    x_seq,
    attended_t,
    out_grad,
    dy_theirs,
    gains,
    a_own,
    a_y,
    a_core,
    a_both,
    b_own,
    b_y,
    b_core,
    b_both,
    out_keep,
    out_send,
    middle_grad,
    attended_grad_t,
    keep_g,
    send_g,
    keep_u,
    send_u,
    keep_a,
    send_a,
    w_out,
    w_gate,
    w_up,
    w_down,
    w_out_t,
    w_gate_t,
    w_up_t,
    w_down_t,
    dy_seq,
    normed,
    hidden,
    gate_grad,
    up_grad,
    out_sum,
    grad_sum,
    scales,
    total,
):
    me, shard, level = place[0], place[1], place[2]
    half_rows = dy_theirs.shape[1]
    sequence = 2 * half_rows
    dy_seq[:, span(me, half_rows)] = out_grad[me]
    dy_seq[:, span(1 - me, half_rows)] = dy_theirs[...]
    rows = b_own.shape[0]
    half = rows // 2
    part = w_gate.shape[1] // 4
    down_rows = a_own.shape[1]
    wide = 4 * down_rows
    a_pieces = ((0, a_own), (2, a_y), (1, a_core), (3, a_both))
    b_pieces = ((0, b_own), (2, b_y), (1, b_core), (3, b_both))
    for bits, b in b_pieces:
        w_out[span(shard ^ bits, rows), :] = b[:, 2 * wide :]
    w_out_t[...] = flip(w_out[...])
    gain2 = gains[:, 1:2]
    tiles = [slice(i, i + WIDE_TILE) for i in range(0, sequence, WIDE_TILE)]
    for at in tiles:
        middle = x_seq[:, at].astype(F32) + mm(w_out_t[...], attended_t[:, at])
        middle_grad[:, at] = middle
        out_sum[:, at] = middle
        grad_sum[:, at] = jnp.zeros_like(middle)
        scale = column_scale(middle)
        scales[0:1, at] = scale
        normed[:, at] = (middle * scale * gain2).astype(BF16)

    def shard_slices():
        for y_bit in range(2):
            for x_bit in range(2):
                for core_bit in range(2):
                    row = (shard ^ (2 * y_bit + core_bit)) * 2 + (me ^ x_bit)
                    yield y_bit, x_bit, core_bit, span(row, half)

    def one_chunk(chunk, carry):
        for bits, b in b_pieces:
            at = span(shard ^ bits, rows)
            for s in range(4):
                to = slice(s * part, (s + 1) * part)
                first = s * down_rows
                w_gate[at, to] = b[:, pl.ds(pl.multiple_of(first + chunk * part, part), part)]
                first = wide + s * down_rows
                w_up[at, to] = b[:, pl.ds(pl.multiple_of(first + chunk * part, part), part)]
        for bits, a in a_pieces:
            w_down_t[:, span(shard ^ bits, part)] = a[:, span(chunk, part)]
        w_gate_t[...] = flip(w_gate[...])
        w_up_t[...] = flip(w_up[...])
        w_down[...] = flip(w_down_t[...])
        for at in tiles:
            gate = mm(w_gate_t[...], normed[:, at])
            up = mm(w_up_t[...], normed[:, at])
            hidden_grad = mm(w_down[...], dy_seq[:, at])
            sig = sigmoid(gate)
            silu = gate * sig
            hidden_tile = (silu * up).astype(BF16)
            gate_tile = (hidden_grad * up * (sig + silu * (1.0 - sig))).astype(BF16)
            up_tile = (hidden_grad * silu).astype(BF16)
            hidden[:, at] = hidden_tile
            gate_grad[:, at] = gate_tile
            up_grad[:, at] = up_tile
            out_sum[:, at] += mm(w_down_t[...], hidden_tile)
            grad_sum[:, at] += mm(w_gate[...], gate_tile) + mm(w_up[...], up_tile)

        total[...] = mm_nt(normed[...], gate_grad[...])
        for y_bit, x_bit, core_bit, at in shard_slices():
            target = send_g if core_bit else keep_g
            for s in range(4):
                half_at, first = divmod(s * down_rows, 2 * down_rows)
                to = pl.ds(pl.multiple_of(first + chunk * part, part), part)
                target[y_bit, x_bit, level ^ half_at, :, to] = total[
                    at, s * part : (s + 1) * part
                ].astype(BF16)
        total[...] = mm_nt(normed[...], up_grad[...])
        for y_bit, x_bit, core_bit, at in shard_slices():
            target = send_u if core_bit else keep_u
            for s in range(4):
                half_at, first = divmod(s * down_rows, 2 * down_rows)
                to = pl.ds(pl.multiple_of(first + chunk * part, part), part)
                target[y_bit, x_bit, level ^ half_at, :, to] = total[
                    at, s * part : (s + 1) * part
                ].astype(BF16)
        total[...] = mm_nt(dy_seq[...], hidden[...])
        for y_bit in range(2):
            for core_bit, target in ((0, keep_a), (1, send_a)):
                columns = span(shard ^ (2 * y_bit + core_bit), part)
                quarter = keep_a.shape[3]
                for x_bit in range(2):
                    for z_bit in range(2):
                        row = (me ^ x_bit) * 2 + (level ^ z_bit)
                        target[x_bit, y_bit, z_bit, :, span(chunk, part)] = total[
                            span(row, quarter), columns
                        ].astype(BF16)
        return carry

    lax.fori_loop(0, down_rows // part, one_chunk, 0)

    for index, at in enumerate(tiles):
        middle = middle_grad[:, at]
        output = out_sum[:, at].astype(BF16)
        block, first = divmod(index * WIDE_TILE, half_rows)
        block_cols = slice(first, first + WIDE_TILE)

        @pl.when(me == block)
        def _():
            out_keep[:, block_cols] = output

        @pl.when(me != block)
        def _():
            out_send[:, block_cols] = output

        scale = scales[0:1, at]
        scaled = grad_sum[:, at] * gain2
        back = (
            dy_seq[:, at].astype(F32)
            + scale * scaled
            - middle * (scale * scale * scale) * jnp.mean(scaled * middle, axis=0, keepdims=True)
        )
        middle_grad[:, at] = back
        branch = back.astype(BF16)
        normed[:, at] = branch
        attended_grad_t[:, at] = mm(w_out[...], branch).astype(BF16)
    columns = QUERY_WIDTH // 2
    for start in (0, TILE, 2 * TILE):
        count = min(TILE, QUERY_WIDTH - start)
        total[:, :count] = mm_nt(attended_t[...], normed[start : start + count, :])
        for y_bit, x_bit, core_bit, at in shard_slices():
            target = send_u if core_bit else keep_u
            for half_at in range(2):
                low = max(start, half_at * columns)
                high = min(start + count, (half_at + 1) * columns)
                if low < high:
                    to = 2 * down_rows + low - half_at * columns
                    target[y_bit, x_bit, level ^ half_at, :, to : to + high - low] = total[
                        at, low - start : high - start
                    ].astype(BF16)


def attend_back_kernel(
    queries_t,
    keys_t,
    values_t,
    log_total,
    attended_t,
    grad_t,
    cosine,
    sine,
    dq_out,
    dk_out,
    dv_out,
    keys,
    values,
    dk,
    dv,
):
    sequence = keys_t.shape[1]
    keys[...] = flip(keys_t[...])
    values[...] = flip(values_t[...])
    dk[...] = jnp.zeros_like(dk)
    dv[...] = jnp.zeros_like(dv)

    def back(a, b, cos, sin):
        return (a * cos + b * sin).astype(BF16), (b * cos - a * sin).astype(BF16)

    for tile in range(sequence // TILE):
        extent = (tile + 1) * TILE
        cols = slice(tile * TILE, extent)
        heads = [slice(r * HEAD_SIZE, (r + 1) * HEAD_SIZE) for r in range(REPEAT)]
        q_t = jnp.concatenate([queries_t[head, cols] for head in heads], 1)
        do_t = jnp.concatenate([grad_t[head, cols] for head in heads], 1)
        mixed = jnp.concatenate([attended_t[head, cols] for head in heads], 1)
        logs = jnp.concatenate([log_total[0, r : r + 1, cols] for r in range(REPEAT)], 1)
        delta = jnp.sum(do_t.astype(F32) * mixed.astype(F32), axis=0, keepdims=True)
        scores = causal_last(mm(keys[:extent, :], q_t), tile)
        probs = jnp.exp(scores - logs)
        dprob = mm(values[:extent, :], do_t)
        score_grad = (probs * (dprob - delta)).astype(BF16)
        dv[:extent, :] += mm(probs.astype(BF16), flip(do_t))
        dk[:extent, :] += mm(score_grad, flip(q_t))
        dq = mm(keys_t[:, :extent], score_grad) * 0.125
        cos, sin = cosine[:, cols], sine[:, cols]
        for r, head in enumerate(heads):
            own = slice(r * TILE, (r + 1) * TILE)
            a, b = back(dq[:HALF, own], dq[HALF:, own], cos, sin)
            dq_out[head.start : head.start + HALF, cols] = a
            dq_out[head.start + HALF : head.stop, cols] = b
    turned = dk[...].T
    a, b = back(turned[:HALF, :], turned[HALF:, :], cosine[...], sine[...])
    dk_out[:HALF, :] = a
    dk_out[HALF:, :] = b
    dv_out[...] = dv[...].T.astype(BF16)


def joined_kernel(place, normed, *rest):
    heads = rest[: 3 * KEY_VALUE_HEADS]
    keep_w, send_w, joined, total = rest[3 * KEY_VALUE_HEADS :]
    me, shard = place[0], place[1]
    group_width = REPEAT * HEAD_SIZE
    for group in range(KEY_VALUE_HEADS):
        dq, dk, dv = heads[3 * group : 3 * group + 3]
        joined[group * group_width : (group + 1) * group_width, :] = dq[...]
        at = QUERY_WIDTH + group * HEAD_SIZE
        joined[at : at + HEAD_SIZE, :] = dk[...]
        at = QUERY_WIDTH + KEY_WIDTH + group * HEAD_SIZE
        joined[at : at + HEAD_SIZE, :] = dv[...]
    half = keep_w.shape[2]
    for first in range(0, USED, 512):
        cols = slice(first, min(first + 512, USED))
        total[:, cols] = mm_nt(normed[...], joined[cols, :])
    for y_bit in range(2):
        for x_bit in range(2):
            for core_bit, target in ((0, keep_w), (1, send_w)):
                row = (shard ^ (2 * y_bit + core_bit)) * 2 + (me ^ x_bit)
                target[y_bit, x_bit] = total[span(row, half), :].astype(BF16)


def input_kernel(
    place, x_seq, packed, gains, middle_grad, joined, keep_x, send_low, send_high, grad_seq
):
    me = place[0]
    half_rows = keep_x.shape[1]
    sequence = 2 * half_rows
    gain1 = gains[:, :1]
    for first in range(0, sequence, WIDE_TILE):
        at = slice(first, first + WIDE_TILE)
        scaled = mm(packed[:, :USED], joined[:, at]) * gain1
        x = x_seq[:, at].astype(F32)
        scale = column_scale(x)
        grad_seq[:, at] = (
            middle_grad[:, at]
            + scale * scaled
            - x * (scale * scale * scale) * jnp.mean(scaled * x, axis=0, keepdims=True)
        )
    keep_x[...] = grad_seq[:, span(me, half_rows)]
    low = send_low.shape[0]
    send_low[...] = grad_seq[:low, span(1 - me, half_rows)].astype(BF16)
    send_high[...] = grad_seq[low:, span(1 - me, half_rows)].astype(BF16)


def call(kernel, out, scratch, flops, exps, args, name, limit):
    shapes = [jax.ShapeDtypeStruct(s, d) for s, d in out]
    moved = sum(a.size * a.dtype.itemsize for a in args[1:]) + sum(
        s.size * s.dtype.itemsize for s in shapes
    )
    in_specs = [pl.BlockSpec(memory_space=pltpu.SMEM)] + [
        pl.BlockSpec(memory_space=pltpu.VMEM)
    ] * (len(args) - 1)
    return pl.pallas_call(
        kernel,
        out_shape=shapes,
        in_specs=in_specs,
        out_specs=[pl.BlockSpec(memory_space=pltpu.VMEM)] * len(shapes),
        scratch_shapes=[pltpu.VMEM(s, d) for s, d in scratch],
        compiler_params=pltpu.CompilerParams(vmem_limit_bytes=limit * MEBI),
        cost_estimate=pl.CostEstimate(flops=flops, bytes_accessed=moved, transcendentals=exps),
        name=name,
    )(*args)


def attend_back(group, qkv_t, log_total, attended_t, grad_t, cosine, sine):
    sequence = qkv_t.shape[1]
    group_width = REPEAT * HEAD_SIZE

    def rows_of(size, index):
        return pl.BlockSpec((size, sequence), lambda step: (index, 0))

    flops = 5 * REPEAT * sequence * sequence * HEAD_SIZE * 2
    return pl.pallas_call(
        attend_back_kernel,
        grid=(1,),
        out_shape=[
            jax.ShapeDtypeStruct((group_width, sequence), BF16),
            jax.ShapeDtypeStruct((HEAD_SIZE, sequence), BF16),
            jax.ShapeDtypeStruct((HEAD_SIZE, sequence), BF16),
        ],
        in_specs=[
            rows_of(group_width, group),
            rows_of(HEAD_SIZE, QUERY_HEADS + group),
            rows_of(HEAD_SIZE, ROTATED + group),
            pl.BlockSpec((1, 8, sequence), lambda step: (group, 0, 0)),
            rows_of(group_width, group),
            rows_of(group_width, group),
            rows_of(HALF, 0),
            rows_of(HALF, 0),
        ],
        out_specs=[rows_of(group_width, 0), rows_of(HEAD_SIZE, 0), rows_of(HEAD_SIZE, 0)],
        scratch_shapes=[
            pltpu.VMEM((sequence, HEAD_SIZE), BF16),
            pltpu.VMEM((sequence, HEAD_SIZE), BF16),
            pltpu.VMEM((sequence, HEAD_SIZE), F32),
            pltpu.VMEM((sequence, HEAD_SIZE), F32),
        ],
        compiler_params=pltpu.CompilerParams(vmem_limit_bytes=28 * MEBI),
        cost_estimate=pl.CostEstimate(
            flops=flops, bytes_accessed=4_000_000, transcendentals=REPEAT * sequence * sequence
        ),
        name="attend_back",
    )(qkv_t, qkv_t, qkv_t, log_total, attended_t, grad_t, cosine, sine)


def across(tensor, bit):
    return lax.ppermute(tensor, "fsdp", [(i, i ^ bit) for i in range(4)])


def over_context(tensor):
    return lax.ppermute(tensor, "ctx", [(0, 1), (1, 0)])


def after(tensor, *done):
    return lax.optimization_barrier((tensor, *done))[0]


def together(*values):
    return lax.optimization_barrier(values)


def add(a, b):
    return (a.astype(F32) + b.astype(F32)).astype(BF16)


def along(tensor, bit):
    size = lax.axis_size("dp")
    return lax.ppermute(tensor, "dp", [(i, i ^ bit) for i in range(size)])


def whole_sequences(
    tokens, norm1_gain, w_query, w_key, w_value, w_out, norm2_gain, w_gate, w_up, w_down, out_grad
):
    half_rows, width = tokens.shape[1:]
    sequence = 2 * half_rows
    rows = w_query.shape[0]
    half = rows // 2
    down_rows = w_down.shape[0]
    hidden_width = w_gate.shape[1]
    part = 128
    me = lax.axis_index("ctx")
    place = jnp.stack([me, lax.axis_index("fsdp"), lax.axis_index("dp") & 1]).astype(jnp.int32)
    tokens = jnp.swapaxes(tokens, 1, 2)
    out_grad = jnp.swapaxes(out_grad, 1, 2)

    tokens_send = lax.dynamic_index_in_dim(tokens, 1 - me, 0, False)
    tokens_theirs = over_context(tokens_send)
    qkv_own = after(jnp.concatenate([w_query, w_key, w_value], 1), tokens_send)
    gain_own = jnp.pad(
        jnp.stack([norm1_gain, norm2_gain]), ((0, GAIN_ROWS - 2), (0, PACKED - rows))
    )
    packed = jnp.concatenate([jnp.pad(qkv_own, ((0, 0), (0, PACKED - USED))), gain_own], 0)
    packed_y = across(packed, 2)
    packed_core = across(packed, 1)
    b_own = jnp.concatenate([w_gate, w_up, w_out], 1)
    cosine, sine = rope_tables(jnp.arange(sequence, dtype=jnp.int32), HEAD_SIZE)
    b_own, a_own, _, cosine, sine, place = together(
        b_own, w_down.T, packed, cosine.T, sine.T, place
    )
    packed_both = across(packed_y, 1)
    b_y, a_y = across(b_own, 2), across(a_own, 2)
    b_core, a_core = across(b_own, 1), across(a_own, 1)
    dy_theirs = over_context(
        after(lax.dynamic_index_in_dim(out_grad, 1 - me, 0, False), tokens_theirs)
    )

    pairs = sequence * sequence
    x_seq, normed, packed_all, gains, qkv_t, log_total, attended_t = call(
        attend_kernel,
        [
            ((width, sequence), BF16),
            ((width, sequence), BF16),
            ((width, PACKED), BF16),
            ((width, 128), F32),
            ((USED, sequence), BF16),
            ((KEY_VALUE_HEADS, 8, sequence), F32),
            ((QUERY_WIDTH, sequence), BF16),
        ],
        [((PACKED, width), BF16), ((KEY_VALUE_HEADS, sequence, HEAD_SIZE), BF16)],
        2 * sequence * width * PACKED + 4 * QUERY_WIDTH * pairs,
        QUERY_HEADS * pairs,
        (place, tokens, tokens_theirs, packed, packed_y, packed_core, packed_both, cosine, sine),
        "attend",
        30,
    )

    b_y, a_y, b_core, a_core, dy_theirs, attended_t = together(
        b_y, a_y, b_core, a_core, dy_theirs, attended_t
    )
    b_both, a_both = across(b_y, 1), across(a_y, 1)

    g_shape = ((2, 2, 2, half, hidden_width // 2), BF16)
    u_shape = ((2, 2, 2, half, (hidden_width + QUERY_WIDTH) // 2), BF16)
    a_shape = ((2, 2, 2, width // 4, down_rows), BF16)
    natural, turned = ((width, 4 * part), BF16), ((4 * part, width), BF16)
    row, wide_row = ((width, sequence), BF16), ((4 * part, sequence), BF16)
    (
        out_keep,
        out_send,
        middle_grad,
        grad_t,
        keep_g,
        send_g,
        keep_u,
        send_u,
        keep_a,
        send_a,
    ) = call(
        feed_forward_kernel,
        [
            ((width, half_rows), BF16),
            ((width, half_rows), BF16),
            ((width, sequence), F32),
            ((QUERY_WIDTH, sequence), BF16),
            g_shape,
            g_shape,
            u_shape,
            u_shape,
            a_shape,
            a_shape,
        ],
        [
            ((QUERY_WIDTH, width), BF16),
            natural,
            natural,
            turned,
            ((width, QUERY_WIDTH), BF16),
            turned,
            turned,
            natural,
            row,
            row,
            wide_row,
            wide_row,
            wide_row,
            ((width, sequence), F32),
            ((width, sequence), F32),
            ((8, sequence), F32),
            ((width, 4 * part), F32),
        ],
        2 * sequence * width * (9 * hidden_width + 3 * QUERY_WIDTH),
        sequence * hidden_width,
        (
            place,
            x_seq,
            attended_t,
            out_grad,
            dy_theirs,
            gains,
            a_own,
            a_y,
            a_core,
            a_both,
            b_own,
            b_y,
            b_core,
            b_both,
        ),
        "feed_forward",
        46,
    )

    back_args = (log_total, attended_t, grad_t, cosine, sine)
    level = lax.axis_index("dp") & 1

    def in_order(own, other):
        low = jnp.where(level == 0, own, other)
        high = jnp.where(level == 0, other, own)
        return jnp.stack([low, high])

    def add_pair(pair, got):
        return add(pair[0], got[0]), add(pair[1], got[1])

    out_theirs = over_context(out_send)
    got_g, got_u, got_a = across(send_g, 1), across(send_u, 1), across(send_a, 1)
    grads0 = attend_back(0, qkv_t, *back_args)
    got_g, got_u, got_a, *grads0 = together(got_g, got_u, got_a, *grads0)
    g, a, u = add_pair(keep_g, got_g), add_pair(keep_a, got_a), add_pair(keep_u, got_u)
    g1, a1, u1, out_theirs, qkv_t = together(g[1], a[1], u[1], out_theirs, qkv_t)

    got_g, got_a, got_u = across(g1, 2), over_context(a1), across(u1, 2)
    grads1 = attend_back(1, qkv_t, *back_args)
    got_g, got_a, *grads1 = together(got_g, got_a, *grads1)
    g, a = add_pair(g[0], got_g), add_pair(a[0], got_a)
    g1, a1, qkv_t = together(g[1], a[1], qkv_t)

    got_g, got_a = over_context(g1), across(a1, 2)
    grads2 = attend_back(2, qkv_t, *back_args)
    got_g, *grads2 = together(got_g, *grads2)
    g = add_pair(g[0], got_g)
    g1, *grads2 = together(g[1], *grads2)

    got_g = along(g1, 1)
    keep_w, send_w, joined = call(
        joined_kernel,
        [((2, 2, half, USED), BF16), ((2, 2, half, USED), BF16), ((USED, sequence), BF16)],
        [((width, USED), F32)],
        2 * sequence * width * USED,
        0,
        (place, normed, *grads0, *grads1, *grads2),
        "joined",
        16,
    )
    got_g, got_u, got_a, send_w, joined = together(got_g, got_u, got_a, send_w, joined)
    got_w = across(send_w, 1)
    u, a, g = add_pair(u[0], got_u), add_pair(a[0], got_a), add(g[0], got_g)
    u1, a1, g, joined = together(u[1], a[1], g, joined)

    got_u, got_a, got_g = over_context(u1), along(a1, 1), along(g, 2)
    keep_x, *send_x = call(
        input_kernel,
        [((width, half_rows), F32), ((width // 2, half_rows), BF16), ((width // 2, half_rows), BF16)],
        [((width, sequence), F32)],
        2 * sequence * width * USED,
        sequence,
        (place, x_seq, packed_all, gains, middle_grad, joined),
        "input_side",
        24,
    )
    got_w, got_u, got_a, got_g, *send_x = together(got_w, got_u, got_a, got_g, *send_x)
    w = add_pair(keep_w, got_w)
    u, a, g = add_pair(u[0], got_u), add(a[0], got_a), add(g, got_g)
    w1, u1, a, g = together(w[1], u[1], a, g)

    got_w, got_u, got_a, got_g = across(w1, 2), along(u1, 1), along(a, 2), along(g, 1)
    x_first = over_context(after(send_x[0], w1))
    got_w, got_u, got_a, got_g = together(got_w, got_u, got_a, got_g)
    w = add_pair(w[0], got_w)
    u, a, g = add(u[0], got_u), add(a, got_a), in_order(g, got_g)
    w1, u, a, g = together(w[1], u, a, g)

    got_w, got_u, got_a = over_context(w1), along(u, 2), along(a, 1)
    other_g = over_context(after(g, w1))
    x_second = over_context(after(send_x[1], g))
    got_w, got_u, got_a = together(got_w, got_u, got_a)
    w, u, a = add(w[0], got_w), add(u, got_u), in_order(a, got_a)
    w, u, a = together(w, u, a)

    got_w, got_u, other_a = along(w, 1), along(u, 1), over_context(a)
    got_w, got_u = together(got_w, got_u)
    w, u = add(w, got_w), in_order(u, got_u)
    w, u = together(w, u)

    got_w, other_u = along(w, 2), over_context(u)
    w = add(w, got_w)
    other_w = over_context(w)
    x_theirs = jnp.concatenate([x_first, x_second], 0)

    def both_halves(part, other, axis=0):
        first = jnp.where(me == 0, part, other)
        second = jnp.where(me == 0, other, part)
        return jnp.concatenate([first, second], axis).astype(F32)

    g_sum = both_halves(g, other_g, 1)
    u_sum = both_halves(u, other_u, 1)
    a_sum = both_halves(a.reshape(width // 2, down_rows), other_a.reshape(width // 2, down_rows))
    w_sum = both_halves(w, other_w)
    gate_sum = jnp.concatenate([g_sum[0], g_sum[1]], 1)
    up_sum = jnp.concatenate([u_sum[i, :, : hidden_width // 2] for i in range(2)], 1)
    out_sum = jnp.concatenate([u_sum[i, :, hidden_width // 2 :] for i in range(2)], 1)

    def place_halves(keep, got):
        got = got.astype(keep.dtype)
        both = jnp.where(me == 0, jnp.stack([keep, got]), jnp.stack([got, keep]))
        return jnp.swapaxes(both, 1, 2)

    key_at = QUERY_WIDTH + KEY_WIDTH
    query_sum, key_sum, value_sum = (
        w_sum[:, :QUERY_WIDTH],
        w_sum[:, QUERY_WIDTH:key_at],
        w_sum[:, key_at:],
    )

    def gain_sum(gain, *pairs):
        return sum(jnp.sum(w.astype(F32) * g, axis=1) for w, g in pairs) / gain.astype(F32)

    return (
        place_halves(out_keep, out_theirs),
        place_halves(keep_x, x_theirs),
        gain_sum(norm1_gain, (w_query, query_sum), (w_key, key_sum), (w_value, value_sum)),
        query_sum,
        key_sum,
        value_sum,
        out_sum,
        gain_sum(norm2_gain, (w_gate, gate_sum), (w_up, up_sum)),
        gate_sum,
        up_sum,
        a_sum.T,
    )


def layer_step(tokens, *rest):
    whole = (
        lax.axis_size("ctx") == 2
        and lax.axis_size("fsdp") == 4
        and lax.axis_size("dp") % 2 == 0
        and tokens.shape[0] == 2
        and tokens.shape[1] % WIDE_TILE == 0
    )
    return (whole_sequences if whole else split_context)(tokens, *rest)


def solution(mesh):
    return jax.shard_map(
        layer_step,
        mesh=mesh,
        in_specs=(
            P(("dp", "fsdp"), "ctx", None),
            P("fsdp"),
            P("fsdp", None),
            P("fsdp", None),
            P("fsdp", None),
            P("fsdp", None),
            P("fsdp"),
            P("fsdp", None),
            P("fsdp", None),
            P("fsdp", None),
            P(("dp", "fsdp"), "ctx", None),
        ),
        out_specs=(
            P(("dp", "fsdp"), "ctx", None),
            P(("dp", "fsdp"), "ctx", None),
            P("fsdp"),
            P("fsdp", None),
            P("fsdp", None),
            P("fsdp", None),
            P("fsdp", None),
            P("fsdp"),
            P("fsdp", None),
            P("fsdp", None),
            P("fsdp", None),
        ),
        check_vma=False,
    )
```

```python
import functools
import math

import jax
import jax.numpy as jnp
from jax import lax
from jax.experimental import pallas as pl
from jax.experimental.pallas import tpu as pltpu
from jax.sharding import PartitionSpec as P

QUERY_HEADS = 9
KEY_VALUE_HEADS = 3
HEAD_SIZE = 64


EPSILON = 1e-05
ROPE_THETA = 100000.0
MASKED = -1e30


def rope_tables(positions, head_width):
    half_size = head_width // 2
    inverse = jnp.exp(
        jnp.arange(half_size, dtype=jnp.float32) * (-2.0 * math.log(ROPE_THETA) / head_width)
    )
    angle = positions.astype(jnp.float32)[:, None] * inverse[None, :]
    return (jnp.cos(angle), jnp.sin(angle))


def rotary_apply(tensor, cosine_table, sine_table):
    half_size = tensor.shape[-1] // 2
    first_half = tensor[..., :half_size]
    second_half = tensor[..., half_size:]
    cosine_table = cosine_table[None, :, None, :]
    sine_table = sine_table[None, :, None, :]
    return jnp.concatenate(
        [
            first_half * cosine_table - second_half * sine_table,
            second_half * cosine_table + first_half * sine_table,
        ],
        -1,
    )


def rotate_back(tensor, cosine_table, sine_table):
    half_size = tensor.shape[-1] // 2
    first_half = tensor[..., :half_size]
    second_half = tensor[..., half_size:]
    cosine_table = cosine_table[None, :, None, :]
    sine_table = sine_table[None, :, None, :]
    return jnp.concatenate(
        [
            first_half * cosine_table + second_half * sine_table,
            second_half * cosine_table - first_half * sine_table,
        ],
        -1,
    )


def rms_scale(tensor):
    return lax.rsqrt(jnp.mean(tensor * tensor, axis=-1, keepdims=True) + EPSILON)


def block_scores(query_block, key_block, query_pos, key_pos):
    scores = (
        jnp.einsum("gqhrd,gkhd->ghrqk", query_block, key_block, preferred_element_type=jnp.float32)
        * 0.125
    )
    visible = key_pos[None, :] <= query_pos[:, None]
    return jnp.where(visible, scores, MASKED)


def split_context(
    tokens, norm1_gain, w_query, w_key, w_value, w_out, norm2_gain, w_gate, w_up, w_down, out_grad
):
    gain1, wq_full, wk_full, wv_full, wo_full, gain2, wg_full, wu_full, wd_full = (
        lax.all_gather(norm1_gain, "fsdp", axis=0, tiled=True),
        lax.all_gather(w_query, "fsdp", axis=0, tiled=True),
        lax.all_gather(w_key, "fsdp", axis=0, tiled=True),
        lax.all_gather(w_value, "fsdp", axis=0, tiled=True),
        lax.all_gather(w_out, "fsdp", axis=0, tiled=True),
        lax.all_gather(norm2_gain, "fsdp", axis=0, tiled=True),
        lax.all_gather(w_gate, "fsdp", axis=0, tiled=True),
        lax.all_gather(w_up, "fsdp", axis=0, tiled=True),
        lax.all_gather(w_down, "fsdp", axis=0, tiled=True),
    )
    query_group_count, local_row_count, model_width = tokens.shape
    repeat_heads = QUERY_HEADS // KEY_VALUE_HEADS
    head_width = HEAD_SIZE
    key_value_width = KEY_VALUE_HEADS * HEAD_SIZE
    query_width = QUERY_HEADS * HEAD_SIZE
    first_row = lax.axis_index("ctx") * local_row_count
    last_row = first_row + local_row_count - 1
    positions = first_row + jnp.arange(local_row_count, dtype=jnp.int32)
    cosine_table, sine_table = rope_tables(positions, head_width)
    gain1f = gain1.astype(jnp.float32)
    gain2f = gain2.astype(jnp.float32)
    inputs = tokens.astype(jnp.float32)
    scale1 = rms_scale(inputs)
    normed1 = (inputs * scale1 * gain1f).astype(jnp.bfloat16)
    query_before_rotation = jnp.einsum(
        "gsd,de->gse", normed1, wq_full, preferred_element_type=jnp.float32
    )
    key_before_rotation = jnp.einsum(
        "gsd,de->gse", normed1, wk_full, preferred_element_type=jnp.float32
    )
    value_projected = jnp.einsum(
        "gsd,de->gse", normed1, wv_full, preferred_element_type=jnp.float32
    )
    query_matrix = rotary_apply(
        query_before_rotation.reshape(query_group_count, local_row_count, QUERY_HEADS, head_width),
        cosine_table,
        sine_table,
    ).astype(jnp.bfloat16)
    query_matrix = query_matrix.reshape(
        query_group_count, local_row_count, KEY_VALUE_HEADS, repeat_heads, head_width
    )
    key_local = rotary_apply(
        key_before_rotation.reshape(
            query_group_count, local_row_count, KEY_VALUE_HEADS, head_width
        ),
        cosine_table,
        sine_table,
    ).astype(jnp.bfloat16)
    local_value_rows = value_projected.astype(jnp.bfloat16)
    collected_keys, collected_values = (
        lax.all_gather(
            key_local.reshape(query_group_count, local_row_count, key_value_width),
            "ctx",
            axis=1,
            tiled=True,
        ),
        lax.all_gather(local_value_rows, "ctx", axis=1, tiled=True),
    )
    sequence_length = collected_keys.shape[1]
    every_key_row = collected_keys.reshape(
        query_group_count, sequence_length, KEY_VALUE_HEADS, head_width
    )
    every_value_row = collected_values.reshape(
        query_group_count, sequence_length, KEY_VALUE_HEADS, head_width
    )
    local_value_rows = local_value_rows.reshape(
        query_group_count, local_row_count, KEY_VALUE_HEADS, head_width
    )
    key_span = min(sequence_length, 512)
    block_total = last_row // key_span + 1

    def key_slices(step_index):
        first_key = step_index * key_span
        key_block = lax.dynamic_slice_in_dim(every_key_row, first_key, key_span, 1)
        value_block = lax.dynamic_slice_in_dim(every_value_row, first_key, key_span, 1)
        key_pos = first_key + jnp.arange(key_span, dtype=jnp.int32)
        return (key_block, value_block, key_pos)

    def stats_step(step_index, running):
        row_max, row_sum = running
        key_block, value_block, key_pos = key_slices(step_index)
        scores = block_scores(query_matrix, key_block, positions, key_pos)
        new_max = jnp.maximum(row_max, jnp.max(scores, axis=-1))
        row_sum = row_sum * jnp.exp(row_max - new_max) + jnp.sum(
            jnp.exp(scores - new_max[..., None]), axis=-1
        )
        return (new_max, row_sum)

    statistics_shape = (query_group_count, KEY_VALUE_HEADS, repeat_heads, local_row_count)
    row_max, row_sum = lax.fori_loop(
        0,
        block_total,
        stats_step,
        (jnp.full(statistics_shape, MASKED, jnp.float32), jnp.zeros(statistics_shape, jnp.float32)),
    )
    log_total = row_max + jnp.log(row_sum)

    def mix_step(step_index, running):
        key_block, value_block, key_pos = key_slices(step_index)
        scores = block_scores(query_matrix, key_block, positions, key_pos)
        probs = jnp.exp(scores - log_total[..., None]).astype(jnp.bfloat16)
        return running + jnp.einsum(
            "ghrqk,gkhd->gqhrd", probs, value_block, preferred_element_type=jnp.float32
        )

    attended_full = lax.fori_loop(
        0,
        block_total,
        mix_step,
        jnp.zeros(
            (query_group_count, local_row_count, KEY_VALUE_HEADS, repeat_heads, head_width),
            jnp.float32,
        ),
    )
    attended = attended_full.astype(jnp.bfloat16).reshape(
        query_group_count, local_row_count, query_width
    )
    branch = jnp.einsum("gse,ed->gsd", attended, wo_full, preferred_element_type=jnp.float32)
    middle = inputs + branch
    scale2 = rms_scale(middle)
    normed2 = (middle * scale2 * gain2f).astype(jnp.bfloat16)
    gate_act = jnp.einsum("gsd,df->gsf", normed2, wg_full, preferred_element_type=jnp.float32)
    up_act = jnp.einsum("gsd,df->gsf", normed2, wu_full, preferred_element_type=jnp.float32)
    gate_sig = jax.nn.sigmoid(gate_act)
    gate_silu = gate_act * gate_sig
    hidden = (gate_silu * up_act).astype(jnp.bfloat16)
    mlp_out = jnp.einsum("gsf,fd->gsd", hidden, wd_full, preferred_element_type=jnp.float32)
    output = (middle + mlp_out).astype(jnp.bfloat16)
    out_float = out_grad.astype(jnp.float32)
    grad_down = jnp.einsum("gsf,gsd->fd", hidden, out_grad, preferred_element_type=jnp.float32)
    hidden_grad = jnp.einsum("gsd,fd->gsf", out_grad, wd_full, preferred_element_type=jnp.float32)
    gate_grad = (hidden_grad * up_act * gate_sig * (1.0 + gate_act * (1.0 - gate_sig))).astype(
        jnp.bfloat16
    )
    up_grad = (hidden_grad * gate_silu).astype(jnp.bfloat16)
    grad_gate = jnp.einsum("gsd,gsf->df", normed2, gate_grad, preferred_element_type=jnp.float32)
    grad_up = jnp.einsum("gsd,gsf->df", normed2, up_grad, preferred_element_type=jnp.float32)
    normed2_grad = jnp.einsum("gsf,df->gsd", gate_grad, wg_full, preferred_element_type=jnp.float32)
    normed2_grad = normed2_grad + jnp.einsum(
        "gsf,df->gsd", up_grad, wu_full, preferred_element_type=jnp.float32
    )
    grad_gain2 = jnp.sum(normed2_grad * middle * scale2, axis=(0, 1))
    scaled2 = gain2f * normed2_grad
    middle_grad = (
        out_float
        + scale2 * scaled2
        - middle * scale2**3 * jnp.mean(scaled2 * middle, axis=-1, keepdims=True)
    )
    branch_grad = middle_grad.astype(jnp.bfloat16)
    grad_out = jnp.einsum("gse,gsd->ed", attended, branch_grad, preferred_element_type=jnp.float32)
    attended_output_gradient = jnp.einsum(
        "gsd,ed->gse", branch_grad, wo_full, preferred_element_type=jnp.float32
    ).astype(jnp.bfloat16)
    attention_gradient = attended_output_gradient.reshape(
        query_group_count, local_row_count, KEY_VALUE_HEADS, repeat_heads, head_width
    )
    delta = jnp.sum(attention_gradient.astype(jnp.float32) * attended_full, axis=-1).transpose(
        0, 2, 3, 1
    )

    def query_grad_step(step_index, running):
        key_block, value_block, key_pos = key_slices(step_index)
        scores = block_scores(query_matrix, key_block, positions, key_pos)
        probs = jnp.exp(scores - log_total[..., None])
        dprob = jnp.einsum(
            "gqhrd,gkhd->ghrqk", attention_gradient, value_block, preferred_element_type=jnp.float32
        )
        score_grad = (probs * (dprob - delta[..., None])).astype(jnp.bfloat16)
        return running + jnp.einsum(
            "ghrqk,gkhd->gqhrd", score_grad, key_block, preferred_element_type=jnp.float32
        )

    query_grad = (
        lax.fori_loop(
            0,
            block_total,
            query_grad_step,
            jnp.zeros(
                (query_group_count, local_row_count, KEY_VALUE_HEADS, repeat_heads, head_width),
                jnp.float32,
            ),
        )
        * 0.125
    )
    row_total = local_row_count * lax.axis_size("ctx")
    term_span = math.gcd(row_total, key_span)

    def key_block_term(step_index):
        first_key = step_index * term_span
        key_block = lax.dynamic_slice_in_dim(every_key_row, first_key, term_span, 1)
        value_block = lax.dynamic_slice_in_dim(every_value_row, first_key, term_span, 1)
        key_pos = first_key + jnp.arange(term_span, dtype=jnp.int32)

        def compute_term(unused):
            scores = block_scores(query_matrix, key_block, positions, key_pos)
            probs = jnp.exp(scores - log_total[..., None])
            dprob = jnp.einsum(
                "gqhrd,gkhd->ghrqk",
                attention_gradient,
                value_block,
                preferred_element_type=jnp.float32,
            )
            score_grad = (probs * (dprob - delta[..., None])).astype(jnp.bfloat16)
            key_term = (
                jnp.einsum(
                    "ghrqk,gqhrd->kghd",
                    score_grad,
                    query_matrix,
                    preferred_element_type=jnp.float32,
                )
                * 0.125
            )
            value_term = jnp.einsum(
                "ghrqk,gqhrd->kghd",
                probs.astype(jnp.bfloat16),
                attention_gradient,
                preferred_element_type=jnp.float32,
            )
            return jnp.concatenate(
                [
                    key_term.reshape(term_span, query_group_count, key_value_width),
                    value_term.reshape(term_span, query_group_count, key_value_width),
                ],
                -1,
            )

        def empty_term(unused):
            return jnp.zeros((term_span, query_group_count, 2 * key_value_width), jnp.float32)

        return lax.cond(first_key <= last_row, compute_term, empty_term, 0)

    terms = lax.map(key_block_term, jnp.arange(row_total // term_span, dtype=jnp.int32))
    paired_gradients = (
        lax.psum_scatter(
            terms.reshape(row_total, query_group_count, 2 * key_value_width).astype(jnp.bfloat16),
            "ctx",
            scatter_dimension=0,
            tiled=True,
        )
        .astype(jnp.float32)
        .transpose(1, 0, 2)
    )
    key_gradient = paired_gradients[..., :key_value_width].reshape(
        query_group_count, local_row_count, KEY_VALUE_HEADS, head_width
    )
    value_gradient = paired_gradients[..., key_value_width:].reshape(
        query_group_count, local_row_count, KEY_VALUE_HEADS, head_width
    )
    query_pre_grad = rotate_back(
        query_grad.reshape(query_group_count, local_row_count, QUERY_HEADS, head_width),
        cosine_table,
        sine_table,
    )
    query_pre_grad = query_pre_grad.astype(jnp.bfloat16).reshape(
        query_group_count, local_row_count, query_width
    )
    key_pre_grad = (
        rotate_back(key_gradient, cosine_table, sine_table)
        .astype(jnp.bfloat16)
        .reshape(query_group_count, local_row_count, key_value_width)
    )
    value_pre_grad = value_gradient.astype(jnp.bfloat16).reshape(
        query_group_count, local_row_count, key_value_width
    )
    grad_query = jnp.einsum(
        "gsd,gse->de", normed1, query_pre_grad, preferred_element_type=jnp.float32
    )
    grad_key = jnp.einsum("gsd,gse->de", normed1, key_pre_grad, preferred_element_type=jnp.float32)
    grad_value = jnp.einsum(
        "gsd,gse->de", normed1, value_pre_grad, preferred_element_type=jnp.float32
    )
    normed1_grad = jnp.einsum(
        "gse,de->gsd", query_pre_grad, wq_full, preferred_element_type=jnp.float32
    )
    normed1_grad = normed1_grad + jnp.einsum(
        "gse,de->gsd", key_pre_grad, wk_full, preferred_element_type=jnp.float32
    )
    normed1_grad = normed1_grad + jnp.einsum(
        "gse,de->gsd", value_pre_grad, wv_full, preferred_element_type=jnp.float32
    )
    grad_gain1 = jnp.sum(normed1_grad * inputs * scale1, axis=(0, 1))
    scaled1 = gain1f * normed1_grad
    input_grad = (
        middle_grad
        + scale1 * scaled1
        - inputs * scale1**3 * jnp.mean(scaled1 * inputs, axis=-1, keepdims=True)
    )
    totals = lax.psum(
        (
            grad_gain1,
            grad_query,
            grad_key,
            grad_value,
            grad_out,
            grad_gain2,
            grad_gate,
            grad_up,
            grad_down,
        ),
        ("dp", "ctx", "fsdp"),
    )
    owner = lax.axis_index("fsdp")
    shards = (norm1_gain, w_query, w_key, w_value, w_out, norm2_gain, w_gate, w_up, w_down)
    shares = tuple(
        (
            lax.dynamic_slice_in_dim(summed, owner * shard.shape[0], shard.shape[0], 0)
            for summed, shard in zip(totals, shards)
        )
    )
    return (
        output,
        input_grad,
        shares[0],
        shares[1],
        shares[2],
        shares[3],
        shares[4],
        shares[5],
        shares[6],
        shares[7],
        shares[8],
    )


WIDTH = 576
QUERY_WIDTH = QUERY_HEADS * HEAD_SIZE
KEY_WIDTH = KEY_VALUE_HEADS * HEAD_SIZE
ROTATED = QUERY_HEADS + KEY_VALUE_HEADS
REPEAT = QUERY_HEADS // KEY_VALUE_HEADS
HALF = HEAD_SIZE // 2
USED = QUERY_WIDTH + 2 * KEY_WIDTH
PACKED = USED + 64
GAIN_ROWS = 16
TILE = 256
WIDE_TILE = 512
MEBI = 1024 * 1024
F32 = jnp.float32
BF16 = jnp.bfloat16


def mm(a, b):
    return jnp.dot(a, b, preferred_element_type=F32)


def mm_nt(a, b):
    return lax.dot_general(a, b, (((1,), (1,)), ((), ())), preferred_element_type=F32)


def flip(tensor):
    return tensor.astype(F32).T.astype(tensor.dtype)


def span(index, size, step=None):
    step = size if step is None else step
    return pl.ds(pl.multiple_of(index * step, step), size)


def flip_blocks(target, source, block):
    def one(step, carry):
        at = span(step, block)
        target[at, :] = flip(source[:, at])
        return carry

    lax.fori_loop(0, source.shape[1] // block, one, 0)


def column_scale(tensor):
    return lax.rsqrt(jnp.mean(tensor * tensor, axis=0, keepdims=True) + EPSILON)


def sigmoid(tensor):
    return 0.5 * jnp.tanh(0.5 * tensor) + 0.5


def causal_last(scores, tile):
    shape = (TILE, REPEAT * TILE)
    visible = lax.broadcasted_iota(jnp.int32, shape, 0) <= (
        lax.broadcasted_iota(jnp.int32, shape, 1) & (TILE - 1)
    )
    last = jnp.where(visible, scores[tile * TILE :, :], MASKED)
    return last if tile == 0 else jnp.concatenate([scores[: tile * TILE, :], last], 0)


def attend_kernel(
    place,
    tokens,
    theirs,
    w_own,
    w_y,
    w_core,
    w_both,
    cosine,
    sine,
    x_seq,
    normed,
    packed,
    gains,
    qkv_t,
    log_total,
    attended_t,
    packed_t,
    key_rows,
):
    me, shard = place[0], place[1]
    half_rows = theirs.shape[1]
    sequence = 2 * half_rows
    x_seq[:, span(me, half_rows)] = tokens[me]
    x_seq[:, span(1 - me, half_rows)] = theirs[...]
    rows = packed.shape[0] // 4
    for bits, piece in ((0, w_own), (2, w_y), (1, w_core), (3, w_both)):
        at = span(shard ^ bits, rows)
        packed[at, :] = piece[:rows, :]
        gains[at, :GAIN_ROWS] = piece[rows:, :TILE].astype(F32).T[:rows, :]
    flip_blocks(packed_t, packed, TILE)
    gain1 = gains[:, :1]

    def project(step, carry):
        at = span(step, WIDE_TILE)
        x = x_seq[:, at].astype(F32)
        normed_tile = (x * column_scale(x) * gain1).astype(BF16)
        normed[:, at] = normed_tile
        turned = mm(packed_t[:USED, :], normed_tile)
        cos, sin = cosine[:, at], sine[:, at]
        for head in range(ROTATED):
            a = turned[head * HEAD_SIZE : head * HEAD_SIZE + HALF, :]
            b = turned[head * HEAD_SIZE + HALF : (head + 1) * HEAD_SIZE, :]
            both = jnp.concatenate([a * cos - b * sin, b * cos + a * sin], 0)
            if head < QUERY_HEADS:
                both = both * 0.125
            else:
                key_rows[head - QUERY_HEADS, at, :] = both.T.astype(BF16)
            qkv_t[head * HEAD_SIZE : (head + 1) * HEAD_SIZE, at] = both.astype(BF16)
        qkv_t[ROTATED * HEAD_SIZE :, at] = turned[ROTATED * HEAD_SIZE :, :].astype(BF16)
        return carry

    lax.fori_loop(0, sequence // WIDE_TILE, project, 0)

    def one_group(group, carry):
        value_rows = span(ROTATED + group, HEAD_SIZE)
        for tile in range(sequence // TILE):
            extent = (tile + 1) * TILE
            cols = slice(tile * TILE, extent)
            queries = jnp.concatenate(
                [qkv_t[span(group * REPEAT + r, HEAD_SIZE), cols] for r in range(REPEAT)], 1
            )
            scores = causal_last(mm(key_rows[group, :extent, :], queries), tile)
            top = jnp.max(scores, axis=0, keepdims=True)
            weights = jnp.exp(scores - top)
            total = jnp.sum(weights, axis=0, keepdims=True)
            mixed = mm(qkv_t[value_rows, :extent], weights.astype(BF16))
            mixed = (mixed * (1.0 / total)).astype(BF16)
            logs = top + jnp.log(total)
            for r in range(REPEAT):
                own = slice(r * TILE, (r + 1) * TILE)
                attended_t[span(group * REPEAT + r, HEAD_SIZE), cols] = mixed[:, own]
                log_total[group, r : r + 1, cols] = logs[:, own]
        return carry

    lax.fori_loop(0, KEY_VALUE_HEADS, one_group, 0)


def chunk_step(shard, pieces, normed, dy, out_sum, grad_sum, keep, send, scratch):
    w_gate, w_up, w_down_t, w_gate_t, w_up_t, w_down, hidden, gate_grad, up_grad, total = scratch
    rows = pieces[0].shape[0]
    wide = w_gate.shape[1]
    part = wide // 4
    sequence = normed.shape[1]
    for bits, piece in zip((0, 2, 1, 3), pieces):
        at = span(shard ^ bits, rows)
        w_gate[at, :] = piece[:, :wide]
        w_up[at, :] = piece[:, wide : 2 * wide]
        for block in range(4):
            first = 2 * wide + block * part
            w_down_t[block * rows : (block + 1) * rows, span(shard ^ bits, part)] = piece[
                :, first : first + part
            ]
    w_gate_t[...] = flip(w_gate[...])
    w_up_t[...] = flip(w_up[...])
    w_down[...] = flip(w_down_t[...])
    for first in range(0, sequence, WIDE_TILE):
        at = slice(first, first + WIDE_TILE)
        gate = mm(w_gate_t[...], normed[:, at])
        up = mm(w_up_t[...], normed[:, at])
        hidden_grad = mm(w_down[...], dy[:, at])
        sig = sigmoid(gate)
        silu = gate * sig
        hidden_tile = (silu * up).astype(BF16)
        gate_tile = (hidden_grad * up * (sig + silu * (1.0 - sig))).astype(BF16)
        up_tile = (hidden_grad * silu).astype(BF16)
        hidden[:, at] = hidden_tile
        gate_grad[:, at] = gate_tile
        up_grad[:, at] = up_tile
        out_sum[:, at] += mm(w_down_t[...], hidden_tile)
        grad_sum[:, at] += mm(w_gate[...], gate_tile) + mm(w_up[...], up_tile)
    for grads, first in ((gate_grad, 0), (up_grad, wide)):
        total[...] = mm_nt(normed[...], grads[...])
        for y_bit in range(2):
            for core_bit, target in ((0, keep), (1, send)):
                at = span(shard ^ (2 * y_bit + core_bit), rows)
                target[y_bit, :, first : first + wide] = total[at, :].astype(BF16)
    total[...] = mm_nt(dy[...], hidden[...])
    for y_bit in range(2):
        for core_bit, target in ((0, keep), (1, send)):
            columns = span(shard ^ (2 * y_bit + core_bit), part)
            for block in range(4):
                first = 2 * wide + block * part
                target[y_bit, :, first : first + part] = total[
                    block * rows : (block + 1) * rows, columns
                ].astype(BF16)


def first_chunk_kernel(
    place,
    x_seq,
    attended_t,
    out_grad,
    dy_theirs,
    gains,
    p_own,
    p_y,
    p_core,
    p_both,
    middle,
    normed,
    scales,
    dy,
    w_out,
    out_sum,
    grad_sum,
    keep,
    send,
    w_out_t,
    *scratch,
):
    me, shard = place[0], place[1]
    half_rows = dy_theirs.shape[1]
    sequence = 2 * half_rows
    dy[:, span(me, half_rows)] = out_grad[me]
    dy[:, span(1 - me, half_rows)] = dy_theirs[...]
    pieces = (p_own, p_y, p_core, p_both)
    rows = p_own.shape[0]
    packed_width = keep.shape[2]
    for bits, piece in zip((0, 2, 1, 3), pieces):
        w_out[span(shard ^ bits, rows), :] = piece[:, packed_width:]
    w_out_t[...] = flip(w_out[...])
    gain2 = gains[:, 1:2]
    for first in range(0, sequence, WIDE_TILE):
        at = slice(first, first + WIDE_TILE)
        mid = x_seq[:, at].astype(F32) + mm(w_out_t[...], attended_t[:, at])
        middle[:, at] = mid
        out_sum[:, at] = mid
        grad_sum[:, at] = jnp.zeros_like(mid)
        scale = column_scale(mid)
        scales[:, at] = jnp.broadcast_to(scale, (8, WIDE_TILE))
        normed[:, at] = (mid * scale * gain2).astype(BF16)
    chunk_step(shard, pieces, normed, dy, out_sum, grad_sum, keep, send, scratch)


def next_chunk_kernel(
    place, normed, dy, out_in, grad_in, p_own, p_y, p_core, p_both, out_sum, grad_sum, keep, send, *scratch
):
    out_sum[...] = out_in[...]
    grad_sum[...] = grad_in[...]
    pieces = (p_own, p_y, p_core, p_both)
    chunk_step(place[1], pieces, normed, dy, out_sum, grad_sum, keep, send, scratch)


def last_chunk_kernel(
    place,
    normed,
    dy,
    out_in,
    grad_in,
    p_own,
    p_y,
    p_core,
    p_both,
    attended_t,
    gains,
    middle,
    scales,
    w_out,
    out_keep,
    out_send,
    middle_grad,
    attended_grad_t,
    keep,
    send,
    out_sum,
    grad_sum,
    branch_grad,
    *scratch,
):
    me, shard = place[0], place[1]
    half_rows = out_keep.shape[1]
    sequence = 2 * half_rows
    out_sum[...] = out_in[...]
    grad_sum[...] = grad_in[...]
    pieces = (p_own, p_y, p_core, p_both)
    chunk_step(shard, pieces, normed, dy, out_sum, grad_sum, keep, send, scratch)
    gain2 = gains[:, 1:2]
    for first in range(0, sequence, WIDE_TILE):
        at = slice(first, first + WIDE_TILE)
        output = out_sum[:, at].astype(BF16)
        block, start = divmod(first, half_rows)
        block_cols = slice(start, start + WIDE_TILE)

        @pl.when(me == block)
        def _():
            out_keep[:, block_cols] = output

        @pl.when(me != block)
        def _():
            out_send[:, block_cols] = output

        mid = middle[:, at]
        scale = scales[0:1, at]
        scaled = grad_sum[:, at] * gain2
        back = (
            dy[:, at].astype(F32)
            + scale * scaled
            - mid * (scale * scale * scale) * jnp.mean(scaled * mid, axis=0, keepdims=True)
        )
        middle_grad[:, at] = back
        branch = back.astype(BF16)
        branch_grad[:, at] = branch
        attended_grad_t[:, at] = mm(w_out[...], branch).astype(BF16)
    total = scratch[-1]
    rows = p_own.shape[0]
    packed_width = p_own.shape[1]
    for start in range(0, QUERY_WIDTH, 512):
        count = min(512, QUERY_WIDTH - start)
        total[:, :count] = mm_nt(attended_t[...], branch_grad[start : start + count, :])
        cols = slice(packed_width + start, packed_width + start + count)
        for y_bit in range(2):
            for core_bit, target in ((0, keep), (1, send)):
                at = span(shard ^ (2 * y_bit + core_bit), rows)
                target[y_bit, :, cols] = total[at, :count].astype(BF16)


def attend_back_kernel(
    queries_t,
    keys_t,
    values_t,
    log_total,
    attended_t,
    grad_t,
    cosine,
    sine,
    dq_out,
    dk_out,
    dv_out,
    keys,
    values,
    dk,
    dv,
):
    sequence = keys_t.shape[1]
    keys[...] = flip(keys_t[...])
    values[...] = flip(values_t[...])
    dk[...] = jnp.zeros_like(dk)
    dv[...] = jnp.zeros_like(dv)

    def back(a, b, cos, sin):
        return (a * cos + b * sin).astype(BF16), (b * cos - a * sin).astype(BF16)

    for tile in range(sequence // TILE):
        extent = (tile + 1) * TILE
        cols = slice(tile * TILE, extent)
        heads = [slice(r * HEAD_SIZE, (r + 1) * HEAD_SIZE) for r in range(REPEAT)]
        q_t = jnp.concatenate([queries_t[head, cols] for head in heads], 1)
        do_t = jnp.concatenate([grad_t[head, cols] for head in heads], 1)
        mixed = jnp.concatenate([attended_t[head, cols] for head in heads], 1)
        logs = jnp.concatenate([log_total[0, r : r + 1, cols] for r in range(REPEAT)], 1)
        delta = jnp.sum(do_t.astype(F32) * mixed.astype(F32), axis=0, keepdims=True)
        scores = causal_last(mm(keys[:extent, :], q_t), tile)
        probs = jnp.exp(scores - logs)
        dprob = mm(values[:extent, :], do_t)
        score_grad = (probs * (dprob - delta)).astype(BF16)
        dv[:extent, :] += mm(probs.astype(BF16), flip(do_t))
        dk[:extent, :] += mm(score_grad, flip(q_t))
        dq = mm(keys_t[:, :extent], score_grad) * 0.125
        cos, sin = cosine[:, cols], sine[:, cols]
        for r, head in enumerate(heads):
            own = slice(r * TILE, (r + 1) * TILE)
            a, b = back(dq[:HALF, own], dq[HALF:, own], cos, sin)
            dq_out[head.start : head.start + HALF, cols] = a
            dq_out[head.start + HALF : head.stop, cols] = b
    turned = dk[...].T
    a, b = back(turned[:HALF, :], turned[HALF:, :], cosine[...], sine[...])
    dk_out[:HALF, :] = a
    dk_out[HALF:, :] = b
    dv_out[...] = dv[...].T.astype(BF16)


def joined_kernel(place, normed, *rest):
    heads = rest[: 3 * KEY_VALUE_HEADS]
    keep_w, send_w, joined, total = rest[3 * KEY_VALUE_HEADS :]
    shard = place[1]
    group_width = REPEAT * HEAD_SIZE
    for group in range(KEY_VALUE_HEADS):
        dq, dk, dv = heads[3 * group : 3 * group + 3]
        joined[group * group_width : (group + 1) * group_width, :] = dq[...]
        at = QUERY_WIDTH + group * HEAD_SIZE
        joined[at : at + HEAD_SIZE, :] = dk[...]
        at = QUERY_WIDTH + KEY_WIDTH + group * HEAD_SIZE
        joined[at : at + HEAD_SIZE, :] = dv[...]
    rows = keep_w.shape[1]
    for first in range(0, USED, 512):
        cols = slice(first, min(first + 512, USED))
        total[:, cols] = mm_nt(normed[...], joined[cols, :])
    for y_bit in range(2):
        for core_bit, target in ((0, keep_w), (1, send_w)):
            at = span(shard ^ (2 * y_bit + core_bit), rows)
            target[y_bit] = total[at, :].astype(BF16)


def input_kernel(
    place, x_seq, packed, gains, middle_grad, joined, keep_x, send_x, grad_seq
):
    me = place[0]
    half_rows = keep_x.shape[1]
    sequence = 2 * half_rows
    gain1 = gains[:, :1]
    for first in range(0, sequence, WIDE_TILE):
        at = slice(first, first + WIDE_TILE)
        scaled = mm(packed[:, :USED], joined[:, at]) * gain1
        x = x_seq[:, at].astype(F32)
        scale = column_scale(x)
        grad_seq[:, at] = (
            middle_grad[:, at]
            + scale * scaled
            - x * (scale * scale * scale) * jnp.mean(scaled * x, axis=0, keepdims=True)
        )
    keep_x[...] = grad_seq[:, span(me, half_rows)]
    send_x[...] = grad_seq[:, span(1 - me, half_rows)].astype(BF16)


def call(kernel, out, scratch, flops, exps, args, name, limit):
    shapes = [jax.ShapeDtypeStruct(s, d) for s, d in out]
    moved = sum(a.size * a.dtype.itemsize for a in args[1:]) + sum(
        s.size * s.dtype.itemsize for s in shapes
    )
    in_specs = [pl.BlockSpec(memory_space=pltpu.SMEM)] + [
        pl.BlockSpec(memory_space=pltpu.VMEM)
    ] * (len(args) - 1)
    return pl.pallas_call(
        kernel,
        out_shape=shapes,
        in_specs=in_specs,
        out_specs=[pl.BlockSpec(memory_space=pltpu.VMEM)] * len(shapes),
        scratch_shapes=[pltpu.VMEM(s, d) for s, d in scratch],
        compiler_params=pltpu.CompilerParams(vmem_limit_bytes=limit * MEBI),
        cost_estimate=pl.CostEstimate(flops=flops, bytes_accessed=moved, transcendentals=exps),
        name=name,
    )(*args)


def attend_back(group, qkv_t, log_total, attended_t, grad_t, cosine, sine):
    sequence = qkv_t.shape[1]
    group_width = REPEAT * HEAD_SIZE

    def rows_of(size, index):
        return pl.BlockSpec((size, sequence), lambda step: (index, 0))

    flops = 5 * REPEAT * sequence * sequence * HEAD_SIZE * 2
    return pl.pallas_call(
        attend_back_kernel,
        grid=(1,),
        out_shape=[
            jax.ShapeDtypeStruct((group_width, sequence), BF16),
            jax.ShapeDtypeStruct((HEAD_SIZE, sequence), BF16),
            jax.ShapeDtypeStruct((HEAD_SIZE, sequence), BF16),
        ],
        in_specs=[
            rows_of(group_width, group),
            rows_of(HEAD_SIZE, QUERY_HEADS + group),
            rows_of(HEAD_SIZE, ROTATED + group),
            pl.BlockSpec((1, 8, sequence), lambda step: (group, 0, 0)),
            rows_of(group_width, group),
            rows_of(group_width, group),
            rows_of(HALF, 0),
            rows_of(HALF, 0),
        ],
        out_specs=[rows_of(group_width, 0), rows_of(HEAD_SIZE, 0), rows_of(HEAD_SIZE, 0)],
        scratch_shapes=[
            pltpu.VMEM((sequence, HEAD_SIZE), BF16),
            pltpu.VMEM((sequence, HEAD_SIZE), BF16),
            pltpu.VMEM((sequence, HEAD_SIZE), F32),
            pltpu.VMEM((sequence, HEAD_SIZE), F32),
        ],
        compiler_params=pltpu.CompilerParams(vmem_limit_bytes=28 * MEBI),
        cost_estimate=pl.CostEstimate(
            flops=flops, bytes_accessed=4_000_000, transcendentals=REPEAT * sequence * sequence
        ),
        name="attend_back",
    )(qkv_t, qkv_t, qkv_t, log_total, attended_t, grad_t, cosine, sine)


def across(tensor, bit):
    return lax.ppermute(tensor, "fsdp", [(i, i ^ bit) for i in range(4)])


def over_context(tensor):
    return lax.ppermute(tensor, "ctx", [(0, 1), (1, 0)])


def after(tensor, *done):
    return lax.optimization_barrier((tensor, *done))[0]


def together(*values):
    return lax.optimization_barrier(values)


def add(a, b):
    return (a.astype(F32) + b.astype(F32)).astype(BF16)


def whole_sequences(
    tokens, norm1_gain, w_query, w_key, w_value, w_out, norm2_gain, w_gate, w_up, w_down, out_grad
):
    half_rows, width = tokens.shape[1:]
    sequence = 2 * half_rows
    rows = w_query.shape[0]
    down_rows = w_down.shape[0]
    hidden_width = w_gate.shape[1]
    part = 128
    me = lax.axis_index("ctx")
    place = jnp.stack([me, lax.axis_index("fsdp")]).astype(jnp.int32)
    tokens = jnp.swapaxes(tokens, 1, 2)
    out_grad = jnp.swapaxes(out_grad, 1, 2)

    tokens_send = lax.dynamic_index_in_dim(tokens, 1 - me, 0, False)
    tokens_theirs = over_context(tokens_send)
    qkv_own = after(jnp.concatenate([w_query, w_key, w_value], 1), tokens_send)
    gain_own = jnp.pad(
        jnp.stack([norm1_gain, norm2_gain]), ((0, GAIN_ROWS - 2), (0, PACKED - rows))
    )
    packed = jnp.concatenate([jnp.pad(qkv_own, ((0, 0), (0, PACKED - USED))), gain_own], 0)
    packed_y = across(packed, 2)
    packed_core = across(packed, 1)
    dy_theirs = over_context(lax.dynamic_index_in_dim(out_grad, 1 - me, 0, False))
    w_down_t = w_down.T
    chunks = []
    for chunk in range(down_rows // part):
        columns = [slice(i * down_rows + chunk * part, i * down_rows + chunk * part + part) for i in range(4)]
        down = w_down_t[:, chunk * part : (chunk + 1) * part]
        blocks = [w[:, at] for w in (w_gate, w_up) for at in columns]
        blocks += [down[i * rows : (i + 1) * rows] for i in range(4)]
        chunks.append(jnp.concatenate(blocks + ([w_out] if chunk == 0 else []), 1))
    cosine, sine = rope_tables(jnp.arange(sequence, dtype=jnp.int32), HEAD_SIZE)
    *chunks, _, cosine, sine, place = together(*chunks, packed, cosine.T, sine.T, place)
    packed_both = across(packed_y, 1)
    chunks_y = [across(chunk, 2) for chunk in chunks]
    chunks_core = [across(chunk, 1) for chunk in chunks]

    pairs = sequence * sequence
    x_seq, normed, packed_all, gains, qkv_t, log_total, attended_t = call(
        attend_kernel,
        [
            ((width, sequence), BF16),
            ((width, sequence), BF16),
            ((width, PACKED), BF16),
            ((width, 128), F32),
            ((USED, sequence), BF16),
            ((KEY_VALUE_HEADS, 8, sequence), F32),
            ((QUERY_WIDTH, sequence), BF16),
        ],
        [((PACKED, width), BF16), ((KEY_VALUE_HEADS, sequence, HEAD_SIZE), BF16)],
        2 * sequence * width * PACKED + 4 * QUERY_WIDTH * pairs,
        QUERY_HEADS * pairs,
        (place, tokens, tokens_theirs, packed, packed_y, packed_core, packed_both, cosine, sine),
        "attend",
        30,
    )

    natural, turned = ((width, 4 * part), BF16), ((4 * part, width), BF16)
    row, wide_row = ((width, sequence), BF16), ((4 * part, sequence), BF16)
    row_sum = ((width, sequence), F32)
    share = ((2, rows, 12 * part), BF16)
    last_share = ((2, rows, 12 * part + QUERY_WIDTH), BF16)
    chunk_scratch = [
        natural,
        natural,
        natural,
        turned,
        turned,
        turned,
        wide_row,
        wide_row,
        wide_row,
        ((width, 4 * part), F32),
    ]
    flops = 2 * sequence * width * 9 * 4 * part
    exps = sequence * 4 * part

    def pieces_of(chunk, *done):
        y_piece, *done = together(chunks_y[chunk], *done)
        return (chunks[chunk], y_piece, chunks_core[chunk], across(y_piece, 1)), done

    pieces, (attended_t, dy_theirs) = pieces_of(0, attended_t, dy_theirs)
    middle, normed2, scales, dy, w_out_all, out_sum, grad_sum, keep0, send0 = call(
        first_chunk_kernel,
        [
            row_sum,
            row,
            ((8, sequence), F32),
            row,
            ((QUERY_WIDTH, width), BF16),
            row_sum,
            row_sum,
            share,
            share,
        ],
        [((width, QUERY_WIDTH), BF16), *chunk_scratch],
        flops + 2 * sequence * width * QUERY_WIDTH,
        exps,
        (place, x_seq, attended_t, out_grad, dy_theirs, gains, *pieces),
        "first_chunk",
        44,
    )

    def add_pair(pair, got):
        return add(pair[0], got[0]), add(pair[1], got[1])

    got0 = across(send0, 1)
    pieces, (out_sum,) = pieces_of(1, out_sum)
    out_sum, grad_sum, keep1, send1 = call(
        next_chunk_kernel,
        [row_sum, row_sum, share, share],
        chunk_scratch,
        flops,
        exps,
        (place, normed2, dy, out_sum, grad_sum, *pieces),
        "next_chunk",
        40,
    )

    got0, out_sum = together(got0, out_sum)
    own0, part0 = add_pair(keep0, got0)
    pieces, (part0, out_sum) = pieces_of(2, part0, out_sum)
    got0, got1 = across(part0, 2), across(send1, 1)
    out_keep, out_send, middle_grad, grad_t, keep2, send2 = call(
        last_chunk_kernel,
        [
            ((width, half_rows), BF16),
            ((width, half_rows), BF16),
            row_sum,
            ((QUERY_WIDTH, sequence), BF16),
            last_share,
            last_share,
        ],
        [row_sum, row_sum, row, *chunk_scratch],
        flops + 4 * sequence * width * QUERY_WIDTH,
        exps,
        (
            place,
            normed2,
            dy,
            out_sum,
            grad_sum,
            *pieces,
            attended_t,
            gains,
            middle,
            scales,
            w_out_all,
        ),
        "last_chunk",
        44,
    )

    everywhere = ("dp", "ctx")
    got0, got1, grad_t = together(got0, got1, grad_t)
    own1, part1 = add_pair(keep1, got1)
    own0, part1, grad_t = together(add(own0, got0), part1, grad_t)
    sum0 = lax.psum(own0, everywhere)
    got1, got2 = across(part1, 2), across(send2, 1)
    out_theirs = over_context(out_send)

    back_args = (log_total, attended_t, grad_t, cosine, sine)
    grads0 = attend_back(0, qkv_t, *back_args)
    got2, *grads0 = together(got2, *grads0)
    own2, part2 = add_pair(keep2, got2)
    part2, qkv_t = together(part2, qkv_t)

    got2 = across(part2, 2)
    grads1 = attend_back(1, qkv_t, *back_args)
    got1, out_theirs, *grads1 = together(got1, out_theirs, *grads1)
    own1, qkv_t, sum0 = together(add(own1, got1), qkv_t, sum0)
    sum1 = lax.psum(own1, everywhere)

    grads2 = attend_back(2, qkv_t, *back_args)
    keep_w, send_w, joined = call(
        joined_kernel,
        [((2, rows, USED), BF16), ((2, rows, USED), BF16), ((USED, sequence), BF16)],
        [((width, USED), F32)],
        2 * sequence * width * USED,
        0,
        (place, normed, *grads0, *grads1, *grads2),
        "joined",
        16,
    )
    got_w = across(send_w, 1)
    got2, joined = together(got2, joined)
    own2, joined, sum1 = together(add(own2, got2), joined, sum1)
    sum2 = lax.psum(own2, everywhere)

    keep_x, send_x = call(
        input_kernel,
        [((width, half_rows), F32), ((width, half_rows), BF16)],
        [((width, sequence), F32)],
        2 * sequence * width * USED,
        sequence,
        (place, x_seq, packed_all, gains, middle_grad, joined),
        "input_side",
        24,
    )
    got_w, send_x = together(got_w, send_x)
    own_w, part_w = add_pair(keep_w, got_w)
    got_w = across(part_w, 2)
    x_theirs = over_context(after(send_x, part_w))
    own_w, sum2 = together(add(own_w, got_w), sum2)
    w_sum = lax.psum(own_w, everywhere).astype(F32)

    sums = [total.astype(F32) for total in (sum0, sum1, sum2)]

    def columns_of(first):
        return [total[:, first : first + part] for total in sums]

    gate_sum = jnp.concatenate([t for i in range(4) for t in columns_of(i * part)], 1)
    up_sum = jnp.concatenate([t for i in range(4, 8) for t in columns_of(i * part)], 1)
    down_sum = jnp.concatenate(
        [jnp.concatenate(columns_of(i * part), 1) for i in range(8, 12)], 0
    )
    out_sum = sums[-1][:, 12 * part :]

    def place_halves(keep, got):
        got = got.astype(keep.dtype)
        both = jnp.where(me == 0, jnp.stack([keep, got]), jnp.stack([got, keep]))
        return jnp.swapaxes(both, 1, 2)

    key_at = QUERY_WIDTH + KEY_WIDTH
    query_sum, key_sum, value_sum = (
        w_sum[:, :QUERY_WIDTH],
        w_sum[:, QUERY_WIDTH:key_at],
        w_sum[:, key_at:],
    )

    def gain_sum(gain, *pairs):
        return sum(jnp.sum(w.astype(F32) * g, axis=1) for w, g in pairs) / gain.astype(F32)

    return (
        place_halves(out_keep, out_theirs),
        place_halves(keep_x, x_theirs),
        gain_sum(norm1_gain, (w_query, query_sum), (w_key, key_sum), (w_value, value_sum)),
        query_sum,
        key_sum,
        value_sum,
        out_sum,
        gain_sum(norm2_gain, (w_gate, gate_sum), (w_up, up_sum)),
        gate_sum,
        up_sum,
        down_sum.T,
    )


def layer_step(tokens, *rest):
    whole = (
        lax.axis_size("ctx") == 2
        and lax.axis_size("fsdp") == 4
        and lax.axis_size("dp") % 2 == 0
        and tokens.shape[0] == 2
        and tokens.shape[1] % WIDE_TILE == 0
    )
    return (whole_sequences if whole else split_context)(tokens, *rest)


def solution(mesh):
    return jax.shard_map(
        layer_step,
        mesh=mesh,
        in_specs=(
            P(("dp", "fsdp"), "ctx", None),
            P("fsdp"),
            P("fsdp", None),
            P("fsdp", None),
            P("fsdp", None),
            P("fsdp", None),
            P("fsdp"),
            P("fsdp", None),
            P("fsdp", None),
            P("fsdp", None),
            P(("dp", "fsdp"), "ctx", None),
        ),
        out_specs=(
            P(("dp", "fsdp"), "ctx", None),
            P(("dp", "fsdp"), "ctx", None),
            P("fsdp"),
            P("fsdp", None),
            P("fsdp", None),
            P("fsdp", None),
            P("fsdp", None),
            P("fsdp"),
            P("fsdp", None),
            P("fsdp", None),
            P("fsdp", None),
        ),
        check_vma=False,
    )
```

```python
import functools
import math

import jax
import jax.numpy as jnp
from jax import lax
from jax.experimental import pallas as pl
from jax.experimental.pallas import tpu as pltpu
from jax.sharding import PartitionSpec as P

QUERY_HEADS = 9
KEY_VALUE_HEADS = 3
HEAD_SIZE = 64


EPSILON = 1e-05
ROPE_THETA = 100000.0
MASKED = -1e30


def rope_tables(positions, head_width):
    half_size = head_width // 2
    inverse = jnp.exp(
        jnp.arange(half_size, dtype=jnp.float32) * (-2.0 * math.log(ROPE_THETA) / head_width)
    )
    angle = positions.astype(jnp.float32)[:, None] * inverse[None, :]
    return (jnp.cos(angle), jnp.sin(angle))


def rotary_apply(tensor, cosine_table, sine_table):
    half_size = tensor.shape[-1] // 2
    first_half = tensor[..., :half_size]
    second_half = tensor[..., half_size:]
    cosine_table = cosine_table[None, :, None, :]
    sine_table = sine_table[None, :, None, :]
    return jnp.concatenate(
        [
            first_half * cosine_table - second_half * sine_table,
            second_half * cosine_table + first_half * sine_table,
        ],
        -1,
    )


def rotate_back(tensor, cosine_table, sine_table):
    half_size = tensor.shape[-1] // 2
    first_half = tensor[..., :half_size]
    second_half = tensor[..., half_size:]
    cosine_table = cosine_table[None, :, None, :]
    sine_table = sine_table[None, :, None, :]
    return jnp.concatenate(
        [
            first_half * cosine_table + second_half * sine_table,
            second_half * cosine_table - first_half * sine_table,
        ],
        -1,
    )


def rms_scale(tensor):
    return lax.rsqrt(jnp.mean(tensor * tensor, axis=-1, keepdims=True) + EPSILON)


def block_scores(query_block, key_block, query_pos, key_pos):
    scores = (
        jnp.einsum("gqhrd,gkhd->ghrqk", query_block, key_block, preferred_element_type=jnp.float32)
        * 0.125
    )
    visible = key_pos[None, :] <= query_pos[:, None]
    return jnp.where(visible, scores, MASKED)


def split_context(
    tokens, norm1_gain, w_query, w_key, w_value, w_out, norm2_gain, w_gate, w_up, w_down, out_grad
):
    gain1, wq_full, wk_full, wv_full, wo_full, gain2, wg_full, wu_full, wd_full = (
        lax.all_gather(norm1_gain, "fsdp", axis=0, tiled=True),
        lax.all_gather(w_query, "fsdp", axis=0, tiled=True),
        lax.all_gather(w_key, "fsdp", axis=0, tiled=True),
        lax.all_gather(w_value, "fsdp", axis=0, tiled=True),
        lax.all_gather(w_out, "fsdp", axis=0, tiled=True),
        lax.all_gather(norm2_gain, "fsdp", axis=0, tiled=True),
        lax.all_gather(w_gate, "fsdp", axis=0, tiled=True),
        lax.all_gather(w_up, "fsdp", axis=0, tiled=True),
        lax.all_gather(w_down, "fsdp", axis=0, tiled=True),
    )
    query_group_count, local_row_count, model_width = tokens.shape
    repeat_heads = QUERY_HEADS // KEY_VALUE_HEADS
    head_width = HEAD_SIZE
    key_value_width = KEY_VALUE_HEADS * HEAD_SIZE
    query_width = QUERY_HEADS * HEAD_SIZE
    first_row = lax.axis_index("ctx") * local_row_count
    last_row = first_row + local_row_count - 1
    positions = first_row + jnp.arange(local_row_count, dtype=jnp.int32)
    cosine_table, sine_table = rope_tables(positions, head_width)
    gain1f = gain1.astype(jnp.float32)
    gain2f = gain2.astype(jnp.float32)
    inputs = tokens.astype(jnp.float32)
    scale1 = rms_scale(inputs)
    normed1 = (inputs * scale1 * gain1f).astype(jnp.bfloat16)
    query_before_rotation = jnp.einsum(
        "gsd,de->gse", normed1, wq_full, preferred_element_type=jnp.float32
    )
    key_before_rotation = jnp.einsum(
        "gsd,de->gse", normed1, wk_full, preferred_element_type=jnp.float32
    )
    value_projected = jnp.einsum(
        "gsd,de->gse", normed1, wv_full, preferred_element_type=jnp.float32
    )
    query_matrix = rotary_apply(
        query_before_rotation.reshape(query_group_count, local_row_count, QUERY_HEADS, head_width),
        cosine_table,
        sine_table,
    ).astype(jnp.bfloat16)
    query_matrix = query_matrix.reshape(
        query_group_count, local_row_count, KEY_VALUE_HEADS, repeat_heads, head_width
    )
    key_local = rotary_apply(
        key_before_rotation.reshape(
            query_group_count, local_row_count, KEY_VALUE_HEADS, head_width
        ),
        cosine_table,
        sine_table,
    ).astype(jnp.bfloat16)
    local_value_rows = value_projected.astype(jnp.bfloat16)
    collected_keys, collected_values = (
        lax.all_gather(
            key_local.reshape(query_group_count, local_row_count, key_value_width),
            "ctx",
            axis=1,
            tiled=True,
        ),
        lax.all_gather(local_value_rows, "ctx", axis=1, tiled=True),
    )
    sequence_length = collected_keys.shape[1]
    every_key_row = collected_keys.reshape(
        query_group_count, sequence_length, KEY_VALUE_HEADS, head_width
    )
    every_value_row = collected_values.reshape(
        query_group_count, sequence_length, KEY_VALUE_HEADS, head_width
    )
    local_value_rows = local_value_rows.reshape(
        query_group_count, local_row_count, KEY_VALUE_HEADS, head_width
    )
    key_span = min(sequence_length, 512)
    block_total = last_row // key_span + 1

    def key_slices(step_index):
        first_key = step_index * key_span
        key_block = lax.dynamic_slice_in_dim(every_key_row, first_key, key_span, 1)
        value_block = lax.dynamic_slice_in_dim(every_value_row, first_key, key_span, 1)
        key_pos = first_key + jnp.arange(key_span, dtype=jnp.int32)
        return (key_block, value_block, key_pos)

    def stats_step(step_index, running):
        row_max, row_sum = running
        key_block, value_block, key_pos = key_slices(step_index)
        scores = block_scores(query_matrix, key_block, positions, key_pos)
        new_max = jnp.maximum(row_max, jnp.max(scores, axis=-1))
        row_sum = row_sum * jnp.exp(row_max - new_max) + jnp.sum(
            jnp.exp(scores - new_max[..., None]), axis=-1
        )
        return (new_max, row_sum)

    statistics_shape = (query_group_count, KEY_VALUE_HEADS, repeat_heads, local_row_count)
    row_max, row_sum = lax.fori_loop(
        0,
        block_total,
        stats_step,
        (jnp.full(statistics_shape, MASKED, jnp.float32), jnp.zeros(statistics_shape, jnp.float32)),
    )
    log_total = row_max + jnp.log(row_sum)

    def mix_step(step_index, running):
        key_block, value_block, key_pos = key_slices(step_index)
        scores = block_scores(query_matrix, key_block, positions, key_pos)
        probs = jnp.exp(scores - log_total[..., None]).astype(jnp.bfloat16)
        return running + jnp.einsum(
            "ghrqk,gkhd->gqhrd", probs, value_block, preferred_element_type=jnp.float32
        )

    attended_full = lax.fori_loop(
        0,
        block_total,
        mix_step,
        jnp.zeros(
            (query_group_count, local_row_count, KEY_VALUE_HEADS, repeat_heads, head_width),
            jnp.float32,
        ),
    )
    attended = attended_full.astype(jnp.bfloat16).reshape(
        query_group_count, local_row_count, query_width
    )
    branch = jnp.einsum("gse,ed->gsd", attended, wo_full, preferred_element_type=jnp.float32)
    middle = inputs + branch
    scale2 = rms_scale(middle)
    normed2 = (middle * scale2 * gain2f).astype(jnp.bfloat16)
    gate_act = jnp.einsum("gsd,df->gsf", normed2, wg_full, preferred_element_type=jnp.float32)
    up_act = jnp.einsum("gsd,df->gsf", normed2, wu_full, preferred_element_type=jnp.float32)
    gate_sig = jax.nn.sigmoid(gate_act)
    gate_silu = gate_act * gate_sig
    hidden = (gate_silu * up_act).astype(jnp.bfloat16)
    mlp_out = jnp.einsum("gsf,fd->gsd", hidden, wd_full, preferred_element_type=jnp.float32)
    output = (middle + mlp_out).astype(jnp.bfloat16)
    out_float = out_grad.astype(jnp.float32)
    grad_down = jnp.einsum("gsf,gsd->fd", hidden, out_grad, preferred_element_type=jnp.float32)
    hidden_grad = jnp.einsum("gsd,fd->gsf", out_grad, wd_full, preferred_element_type=jnp.float32)
    gate_grad = (hidden_grad * up_act * gate_sig * (1.0 + gate_act * (1.0 - gate_sig))).astype(
        jnp.bfloat16
    )
    up_grad = (hidden_grad * gate_silu).astype(jnp.bfloat16)
    grad_gate = jnp.einsum("gsd,gsf->df", normed2, gate_grad, preferred_element_type=jnp.float32)
    grad_up = jnp.einsum("gsd,gsf->df", normed2, up_grad, preferred_element_type=jnp.float32)
    normed2_grad = jnp.einsum("gsf,df->gsd", gate_grad, wg_full, preferred_element_type=jnp.float32)
    normed2_grad = normed2_grad + jnp.einsum(
        "gsf,df->gsd", up_grad, wu_full, preferred_element_type=jnp.float32
    )
    grad_gain2 = jnp.sum(normed2_grad * middle * scale2, axis=(0, 1))
    scaled2 = gain2f * normed2_grad
    middle_grad = (
        out_float
        + scale2 * scaled2
        - middle * scale2**3 * jnp.mean(scaled2 * middle, axis=-1, keepdims=True)
    )
    branch_grad = middle_grad.astype(jnp.bfloat16)
    grad_out = jnp.einsum("gse,gsd->ed", attended, branch_grad, preferred_element_type=jnp.float32)
    attended_output_gradient = jnp.einsum(
        "gsd,ed->gse", branch_grad, wo_full, preferred_element_type=jnp.float32
    ).astype(jnp.bfloat16)
    attention_gradient = attended_output_gradient.reshape(
        query_group_count, local_row_count, KEY_VALUE_HEADS, repeat_heads, head_width
    )
    delta = jnp.sum(attention_gradient.astype(jnp.float32) * attended_full, axis=-1).transpose(
        0, 2, 3, 1
    )

    def query_grad_step(step_index, running):
        key_block, value_block, key_pos = key_slices(step_index)
        scores = block_scores(query_matrix, key_block, positions, key_pos)
        probs = jnp.exp(scores - log_total[..., None])
        dprob = jnp.einsum(
            "gqhrd,gkhd->ghrqk", attention_gradient, value_block, preferred_element_type=jnp.float32
        )
        score_grad = (probs * (dprob - delta[..., None])).astype(jnp.bfloat16)
        return running + jnp.einsum(
            "ghrqk,gkhd->gqhrd", score_grad, key_block, preferred_element_type=jnp.float32
        )

    query_grad = (
        lax.fori_loop(
            0,
            block_total,
            query_grad_step,
            jnp.zeros(
                (query_group_count, local_row_count, KEY_VALUE_HEADS, repeat_heads, head_width),
                jnp.float32,
            ),
        )
        * 0.125
    )
    row_total = local_row_count * lax.axis_size("ctx")
    term_span = math.gcd(row_total, key_span)

    def key_block_term(step_index):
        first_key = step_index * term_span
        key_block = lax.dynamic_slice_in_dim(every_key_row, first_key, term_span, 1)
        value_block = lax.dynamic_slice_in_dim(every_value_row, first_key, term_span, 1)
        key_pos = first_key + jnp.arange(term_span, dtype=jnp.int32)

        def compute_term(unused):
            scores = block_scores(query_matrix, key_block, positions, key_pos)
            probs = jnp.exp(scores - log_total[..., None])
            dprob = jnp.einsum(
                "gqhrd,gkhd->ghrqk",
                attention_gradient,
                value_block,
                preferred_element_type=jnp.float32,
            )
            score_grad = (probs * (dprob - delta[..., None])).astype(jnp.bfloat16)
            key_term = (
                jnp.einsum(
                    "ghrqk,gqhrd->kghd",
                    score_grad,
                    query_matrix,
                    preferred_element_type=jnp.float32,
                )
                * 0.125
            )
            value_term = jnp.einsum(
                "ghrqk,gqhrd->kghd",
                probs.astype(jnp.bfloat16),
                attention_gradient,
                preferred_element_type=jnp.float32,
            )
            return jnp.concatenate(
                [
                    key_term.reshape(term_span, query_group_count, key_value_width),
                    value_term.reshape(term_span, query_group_count, key_value_width),
                ],
                -1,
            )

        def empty_term(unused):
            return jnp.zeros((term_span, query_group_count, 2 * key_value_width), jnp.float32)

        return lax.cond(first_key <= last_row, compute_term, empty_term, 0)

    terms = lax.map(key_block_term, jnp.arange(row_total // term_span, dtype=jnp.int32))
    paired_gradients = (
        lax.psum_scatter(
            terms.reshape(row_total, query_group_count, 2 * key_value_width).astype(jnp.bfloat16),
            "ctx",
            scatter_dimension=0,
            tiled=True,
        )
        .astype(jnp.float32)
        .transpose(1, 0, 2)
    )
    key_gradient = paired_gradients[..., :key_value_width].reshape(
        query_group_count, local_row_count, KEY_VALUE_HEADS, head_width
    )
    value_gradient = paired_gradients[..., key_value_width:].reshape(
        query_group_count, local_row_count, KEY_VALUE_HEADS, head_width
    )
    query_pre_grad = rotate_back(
        query_grad.reshape(query_group_count, local_row_count, QUERY_HEADS, head_width),
        cosine_table,
        sine_table,
    )
    query_pre_grad = query_pre_grad.astype(jnp.bfloat16).reshape(
        query_group_count, local_row_count, query_width
    )
    key_pre_grad = (
        rotate_back(key_gradient, cosine_table, sine_table)
        .astype(jnp.bfloat16)
        .reshape(query_group_count, local_row_count, key_value_width)
    )
    value_pre_grad = value_gradient.astype(jnp.bfloat16).reshape(
        query_group_count, local_row_count, key_value_width
    )
    grad_query = jnp.einsum(
        "gsd,gse->de", normed1, query_pre_grad, preferred_element_type=jnp.float32
    )
    grad_key = jnp.einsum("gsd,gse->de", normed1, key_pre_grad, preferred_element_type=jnp.float32)
    grad_value = jnp.einsum(
        "gsd,gse->de", normed1, value_pre_grad, preferred_element_type=jnp.float32
    )
    normed1_grad = jnp.einsum(
        "gse,de->gsd", query_pre_grad, wq_full, preferred_element_type=jnp.float32
    )
    normed1_grad = normed1_grad + jnp.einsum(
        "gse,de->gsd", key_pre_grad, wk_full, preferred_element_type=jnp.float32
    )
    normed1_grad = normed1_grad + jnp.einsum(
        "gse,de->gsd", value_pre_grad, wv_full, preferred_element_type=jnp.float32
    )
    grad_gain1 = jnp.sum(normed1_grad * inputs * scale1, axis=(0, 1))
    scaled1 = gain1f * normed1_grad
    input_grad = (
        middle_grad
        + scale1 * scaled1
        - inputs * scale1**3 * jnp.mean(scaled1 * inputs, axis=-1, keepdims=True)
    )
    totals = lax.psum(
        (
            grad_gain1,
            grad_query,
            grad_key,
            grad_value,
            grad_out,
            grad_gain2,
            grad_gate,
            grad_up,
            grad_down,
        ),
        ("dp", "ctx", "fsdp"),
    )
    owner = lax.axis_index("fsdp")
    shards = (norm1_gain, w_query, w_key, w_value, w_out, norm2_gain, w_gate, w_up, w_down)
    shares = tuple(
        (
            lax.dynamic_slice_in_dim(summed, owner * shard.shape[0], shard.shape[0], 0)
            for summed, shard in zip(totals, shards)
        )
    )
    return (
        output,
        input_grad,
        shares[0],
        shares[1],
        shares[2],
        shares[3],
        shares[4],
        shares[5],
        shares[6],
        shares[7],
        shares[8],
    )


WIDTH = 576
QUERY_WIDTH = QUERY_HEADS * HEAD_SIZE
KEY_WIDTH = KEY_VALUE_HEADS * HEAD_SIZE
ROTATED = QUERY_HEADS + KEY_VALUE_HEADS
REPEAT = QUERY_HEADS // KEY_VALUE_HEADS
HALF = HEAD_SIZE // 2
USED = QUERY_WIDTH + 2 * KEY_WIDTH
PACKED = USED + 64
GAIN_ROWS = 16
TILE = 256
WIDE_TILE = 512
MEBI = 1024 * 1024
F32 = jnp.float32
BF16 = jnp.bfloat16


def mm(a, b):
    return jnp.dot(a, b, preferred_element_type=F32)


def mm_nt(a, b):
    return lax.dot_general(a, b, (((1,), (1,)), ((), ())), preferred_element_type=F32)


def flip(tensor):
    return tensor.astype(F32).T.astype(tensor.dtype)


def span(index, size, step=None):
    step = size if step is None else step
    return pl.ds(pl.multiple_of(index * step, step), size)


def flip_blocks(target, source, block):
    def one(step, carry):
        at = span(step, block)
        target[at, :] = flip(source[:, at])
        return carry

    lax.fori_loop(0, source.shape[1] // block, one, 0)


def column_scale(tensor):
    return lax.rsqrt(jnp.mean(tensor * tensor, axis=0, keepdims=True) + EPSILON)


def sigmoid(tensor):
    return 0.5 * jnp.tanh(0.5 * tensor) + 0.5


def causal_last(scores, tile):
    shape = (TILE, REPEAT * TILE)
    visible = lax.broadcasted_iota(jnp.int32, shape, 0) <= (
        lax.broadcasted_iota(jnp.int32, shape, 1) & (TILE - 1)
    )
    last = jnp.where(visible, scores[tile * TILE :, :], MASKED)
    return last if tile == 0 else jnp.concatenate([scores[: tile * TILE, :], last], 0)


def attend_kernel(
    place,
    tokens,
    theirs,
    w_own,
    w_y,
    w_core,
    w_both,
    cosine,
    sine,
    x_seq,
    normed,
    packed,
    gains,
    qkv_t,
    log_total,
    attended_t,
    packed_t,
    key_rows,
):
    me, shard = place[0], place[1]
    half_rows = theirs.shape[1]
    sequence = 2 * half_rows
    x_seq[:, span(me, half_rows)] = tokens[me]
    x_seq[:, span(1 - me, half_rows)] = theirs[...]
    rows = packed.shape[0] // 4
    for bits, piece in ((0, w_own), (2, w_y), (1, w_core), (3, w_both)):
        at = span(shard ^ bits, rows)
        packed[at, :] = piece[:rows, :]
        gains[at, :GAIN_ROWS] = piece[rows:, :TILE].astype(F32).T[:rows, :]
    flip_blocks(packed_t, packed, TILE)
    gain1 = gains[:, :1]

    def project(step, carry):
        at = span(step, WIDE_TILE)
        x = x_seq[:, at].astype(F32)
        normed_tile = (x * column_scale(x) * gain1).astype(BF16)
        normed[:, at] = normed_tile
        turned = mm(packed_t[:USED, :], normed_tile)
        cos, sin = cosine[:, at], sine[:, at]
        for head in range(ROTATED):
            a = turned[head * HEAD_SIZE : head * HEAD_SIZE + HALF, :]
            b = turned[head * HEAD_SIZE + HALF : (head + 1) * HEAD_SIZE, :]
            both = jnp.concatenate([a * cos - b * sin, b * cos + a * sin], 0)
            if head < QUERY_HEADS:
                both = both * 0.125
            else:
                key_rows[head - QUERY_HEADS, at, :] = both.T.astype(BF16)
            qkv_t[head * HEAD_SIZE : (head + 1) * HEAD_SIZE, at] = both.astype(BF16)
        qkv_t[ROTATED * HEAD_SIZE :, at] = turned[ROTATED * HEAD_SIZE :, :].astype(BF16)
        return carry

    lax.fori_loop(0, sequence // WIDE_TILE, project, 0)

    def one_group(group, carry):
        value_rows = span(ROTATED + group, HEAD_SIZE)
        for tile in range(sequence // TILE):
            extent = (tile + 1) * TILE
            cols = slice(tile * TILE, extent)
            queries = jnp.concatenate(
                [qkv_t[span(group * REPEAT + r, HEAD_SIZE), cols] for r in range(REPEAT)], 1
            )
            scores = causal_last(mm(key_rows[group, :extent, :], queries), tile)
            top = jnp.max(scores, axis=0, keepdims=True)
            weights = jnp.exp(scores - top)
            total = jnp.sum(weights, axis=0, keepdims=True)
            mixed = mm(qkv_t[value_rows, :extent], weights.astype(BF16))
            mixed = (mixed * (1.0 / total)).astype(BF16)
            logs = top + jnp.log(total)
            for r in range(REPEAT):
                own = slice(r * TILE, (r + 1) * TILE)
                attended_t[span(group * REPEAT + r, HEAD_SIZE), cols] = mixed[:, own]
                log_total[group, r : r + 1, cols] = logs[:, own]
        return carry

    lax.fori_loop(0, KEY_VALUE_HEADS, one_group, 0)


def places(shard, me, keep, send):
    for y_bit in range(2):
        for x_bit in range(2):
            for core_bit, target in ((0, keep), (1, send)):
                yield target, y_bit, x_bit, shard ^ (2 * y_bit + core_bit), me ^ x_bit


def chunk_step(place, pieces, normed, dy, out_sum, grad_sum, keep, send, scratch):
    w_gate, w_up, w_down_t, w_gate_t, w_up_t, w_down, hidden, gate_grad, up_grad, total = scratch
    me, shard, level = place[0], place[1], place[2]
    rows = pieces[0].shape[0]
    wide = w_gate.shape[1]
    part = wide // 4
    sequence = normed.shape[1]
    for bits, piece in zip((0, 2, 1, 3), pieces):
        at = span(shard ^ bits, rows)
        w_gate[at, :] = piece[:, :wide]
        w_up[at, :] = piece[:, wide : 2 * wide]
        for block in range(4):
            first = 2 * wide + block * part
            w_down_t[block * rows : (block + 1) * rows, span(shard ^ bits, part)] = piece[
                :, first : first + part
            ]
    w_gate_t[...] = flip(w_gate[...])
    w_up_t[...] = flip(w_up[...])
    w_down[...] = flip(w_down_t[...])
    for first in range(0, sequence, WIDE_TILE):
        at = slice(first, first + WIDE_TILE)
        gate = mm(w_gate_t[...], normed[:, at])
        up = mm(w_up_t[...], normed[:, at])
        hidden_grad = mm(w_down[...], dy[:, at])
        sig = sigmoid(gate)
        silu = gate * sig
        hidden_tile = (silu * up).astype(BF16)
        gate_tile = (hidden_grad * up * (sig + silu * (1.0 - sig))).astype(BF16)
        up_tile = (hidden_grad * silu).astype(BF16)
        hidden[:, at] = hidden_tile
        gate_grad[:, at] = gate_tile
        up_grad[:, at] = up_tile
        out_sum[:, at] += mm(w_down_t[...], hidden_tile)
        grad_sum[:, at] += mm(w_gate[...], gate_tile) + mm(w_up[...], up_tile)
    half = rows // 2
    middle = wide // 2
    for grads, moves in (
        (gate_grad, ((0, 0, 0, wide),)),
        (up_grad, ((0, 0, wide, middle), (1, middle, 0, middle))),
    ):
        total[...] = mm_nt(normed[...], grads[...])
        for target, y_bit, x_bit, owner, side in places(shard, me, keep, send):
            at = span(owner * 2 + side, half)
            for z_half, first, to, count in moves:
                target[y_bit, x_bit, level ^ z_half, :, to : to + count] = total[
                    at, first : first + count
                ].astype(BF16)
    total[...] = mm_nt(dy[...], hidden[...])
    for target, y_bit, x_bit, owner, side in places(shard, me, keep, send):
        for block in range(4):
            at = pl.ds(pl.multiple_of(block * rows + side * half, 8), half)
            to = middle + block * part
            target[y_bit, x_bit, level ^ 1, :, to : to + part] = total[
                at, span(owner, part)
            ].astype(BF16)


def first_chunk_kernel(
    place,
    x_seq,
    attended_t,
    out_grad,
    dy_theirs,
    gains,
    p_own,
    p_y,
    p_core,
    p_both,
    middle,
    normed,
    scales,
    dy,
    w_out,
    out_sum,
    grad_sum,
    keep,
    send,
    w_out_t,
    *scratch,
):
    me, shard = place[0], place[1]
    half_rows = dy_theirs.shape[1]
    sequence = 2 * half_rows
    dy[:, span(me, half_rows)] = out_grad[me]
    dy[:, span(1 - me, half_rows)] = dy_theirs[...]
    pieces = (p_own, p_y, p_core, p_both)
    rows = p_own.shape[0]
    packed_width = p_own.shape[1] - QUERY_WIDTH
    for bits, piece in zip((0, 2, 1, 3), pieces):
        w_out[span(shard ^ bits, rows), :] = piece[:, packed_width:]
    w_out_t[...] = flip(w_out[...])
    gain2 = gains[:, 1:2]
    for first in range(0, sequence, WIDE_TILE):
        at = slice(first, first + WIDE_TILE)
        mid = x_seq[:, at].astype(F32) + mm(w_out_t[...], attended_t[:, at])
        middle[:, at] = mid
        out_sum[:, at] = mid
        grad_sum[:, at] = jnp.zeros_like(mid)
        scale = column_scale(mid)
        scales[:, at] = jnp.broadcast_to(scale, (8, WIDE_TILE))
        normed[:, at] = (mid * scale * gain2).astype(BF16)
    chunk_step(place, pieces, normed, dy, out_sum, grad_sum, keep, send, scratch)


def next_chunk_kernel(
    place, normed, dy, out_in, grad_in, p_own, p_y, p_core, p_both, out_sum, grad_sum, keep, send, *scratch
):
    out_sum[...] = out_in[...]
    grad_sum[...] = grad_in[...]
    pieces = (p_own, p_y, p_core, p_both)
    chunk_step(place, pieces, normed, dy, out_sum, grad_sum, keep, send, scratch)


def last_chunk_kernel(
    place,
    normed,
    dy,
    out_in,
    grad_in,
    p_own,
    p_y,
    p_core,
    p_both,
    attended_t,
    gains,
    middle,
    scales,
    w_out,
    out_keep,
    out_send,
    middle_grad,
    attended_grad_t,
    keep,
    send,
    out_sum,
    branch_grad,
    *scratch,
):
    me, shard = place[0], place[1]
    half_rows = out_keep.shape[1]
    sequence = 2 * half_rows
    grad_sum = middle_grad
    out_sum[...] = out_in[...]
    grad_sum[...] = grad_in[...]
    pieces = (p_own, p_y, p_core, p_both)
    chunk_step(place, pieces, normed, dy, out_sum, grad_sum, keep, send, scratch)
    gain2 = gains[:, 1:2]
    for first in range(0, sequence, WIDE_TILE):
        at = slice(first, first + WIDE_TILE)
        output = out_sum[:, at].astype(BF16)
        block, start = divmod(first, half_rows)
        block_cols = slice(start, start + WIDE_TILE)

        @pl.when(me == block)
        def _():
            out_keep[:, block_cols] = output

        @pl.when(me != block)
        def _():
            out_send[:, block_cols] = output

        mid = middle[:, at]
        scale = scales[0:1, at]
        scaled = grad_sum[:, at] * gain2
        back = (
            dy[:, at].astype(F32)
            + scale * scaled
            - mid * (scale * scale * scale) * jnp.mean(scaled * mid, axis=0, keepdims=True)
        )
        middle_grad[:, at] = back
        branch = back.astype(BF16)
        branch_grad[:, at] = branch
        attended_grad_t[:, at] = mm(w_out[...], branch).astype(BF16)
    total = scratch[-1]
    half = p_own.shape[0] // 2
    columns = QUERY_WIDTH // 2
    first_to = keep.shape[4] - columns
    for start in range(0, QUERY_WIDTH, TILE):
        count = min(TILE, QUERY_WIDTH - start)
        total[:, :count] = mm_nt(attended_t[...], branch_grad[start : start + count, :])
        for target, y_bit, x_bit, owner, side in places(shard, me, keep, send):
            at = span(owner * 2 + side, half)
            for z_half in range(2):
                low = max(start, z_half * columns)
                high = min(start + count, (z_half + 1) * columns)
                if low < high:
                    to = first_to + low - z_half * columns
                    target[y_bit, x_bit, place[2] ^ z_half, :, to : to + high - low] = total[
                        at, low - start : high - start
                    ].astype(BF16)


def attend_back_kernel(
    queries_t,
    keys_t,
    values_t,
    log_total,
    attended_t,
    grad_t,
    cosine,
    sine,
    dq_out,
    dk_out,
    dv_out,
    keys,
    values,
    dk,
    dv,
):
    sequence = keys_t.shape[1]
    keys[...] = flip(keys_t[...])
    values[...] = flip(values_t[...])
    dk[...] = jnp.zeros_like(dk)
    dv[...] = jnp.zeros_like(dv)

    def back(a, b, cos, sin):
        return (a * cos + b * sin).astype(BF16), (b * cos - a * sin).astype(BF16)

    for tile in range(sequence // TILE):
        extent = (tile + 1) * TILE
        cols = slice(tile * TILE, extent)
        heads = [slice(r * HEAD_SIZE, (r + 1) * HEAD_SIZE) for r in range(REPEAT)]
        q_t = jnp.concatenate([queries_t[head, cols] for head in heads], 1)
        do_t = jnp.concatenate([grad_t[head, cols] for head in heads], 1)
        mixed = jnp.concatenate([attended_t[head, cols] for head in heads], 1)
        logs = jnp.concatenate([log_total[0, r : r + 1, cols] for r in range(REPEAT)], 1)
        delta = jnp.sum(do_t.astype(F32) * mixed.astype(F32), axis=0, keepdims=True)
        scores = causal_last(mm(keys[:extent, :], q_t), tile)
        probs = jnp.exp(scores - logs)
        dprob = mm(values[:extent, :], do_t)
        score_grad = (probs * (dprob - delta)).astype(BF16)
        dv[:extent, :] += mm(probs.astype(BF16), flip(do_t))
        dk[:extent, :] += mm(score_grad, flip(q_t))
        dq = mm(keys_t[:, :extent], score_grad) * 0.125
        cos, sin = cosine[:, cols], sine[:, cols]
        for r, head in enumerate(heads):
            own = slice(r * TILE, (r + 1) * TILE)
            a, b = back(dq[:HALF, own], dq[HALF:, own], cos, sin)
            dq_out[head.start : head.start + HALF, cols] = a
            dq_out[head.start + HALF : head.stop, cols] = b
    turned = dk[...].T
    a, b = back(turned[:HALF, :], turned[HALF:, :], cosine[...], sine[...])
    dk_out[:HALF, :] = a
    dk_out[HALF:, :] = b
    dv_out[...] = dv[...].T.astype(BF16)


def joined_kernel(place, normed, *rest):
    heads = rest[: 3 * KEY_VALUE_HEADS]
    keep_w, send_w, joined, total = rest[3 * KEY_VALUE_HEADS :]
    me, shard = place[0], place[1]
    group_width = REPEAT * HEAD_SIZE
    for group in range(KEY_VALUE_HEADS):
        dq, dk, dv = heads[3 * group : 3 * group + 3]
        joined[group * group_width : (group + 1) * group_width, :] = dq[...]
        at = QUERY_WIDTH + group * HEAD_SIZE
        joined[at : at + HEAD_SIZE, :] = dk[...]
        at = QUERY_WIDTH + KEY_WIDTH + group * HEAD_SIZE
        joined[at : at + HEAD_SIZE, :] = dv[...]
    half = keep_w.shape[2]
    for first in range(0, USED, 512):
        cols = slice(first, min(first + 512, USED))
        total[:, cols] = mm_nt(normed[...], joined[cols, :])
    for target, y_bit, x_bit, owner, side in places(shard, me, keep_w, send_w):
        target[y_bit, x_bit] = total[span(owner * 2 + side, half), :].astype(BF16)


def input_kernel(
    place, x_seq, packed, gains, middle_grad, joined, keep_x, send_x, grad_seq
):
    me = place[0]
    half_rows = keep_x.shape[1]
    sequence = 2 * half_rows
    gain1 = gains[:, :1]
    for first in range(0, sequence, WIDE_TILE):
        at = slice(first, first + WIDE_TILE)
        scaled = mm(packed[:, :USED], joined[:, at]) * gain1
        x = x_seq[:, at].astype(F32)
        scale = column_scale(x)
        grad_seq[:, at] = (
            middle_grad[:, at]
            + scale * scaled
            - x * (scale * scale * scale) * jnp.mean(scaled * x, axis=0, keepdims=True)
        )
    keep_x[...] = grad_seq[:, span(me, half_rows)]
    send_x[...] = grad_seq[:, span(1 - me, half_rows)].astype(BF16)


def pack_input_kernel(place, w_query, w_key, w_value, gains, packed):
    rows = w_query.shape[0]
    packed[:rows, :QUERY_WIDTH] = w_query[...]
    packed[:rows, QUERY_WIDTH : QUERY_WIDTH + KEY_WIDTH] = w_key[...]
    packed[:rows, QUERY_WIDTH + KEY_WIDTH :] = jnp.concatenate(
        [w_value[...].astype(F32), jnp.zeros((rows, PACKED - USED), F32)], 1
    ).astype(BF16)
    packed[rows:, :] = jnp.zeros((GAIN_ROWS, PACKED), BF16)
    packed[rows:, :TILE] = gains[...]


def pack_kernel(place, w_gate, w_up, w_down_t, w_out, *chunks):
    rows = w_gate.shape[0]
    down_rows = w_down_t.shape[1]
    part = 128
    for index, chunk in enumerate(chunks):
        at = index * part
        for i in range(4):
            source = slice(i * down_rows + at, i * down_rows + at + part)
            chunk[:, i * part : (i + 1) * part] = w_gate[:, source]
            chunk[:, (4 + i) * part : (5 + i) * part] = w_up[:, source]
            chunk[:, (8 + i) * part : (9 + i) * part] = w_down_t[
                i * rows : (i + 1) * rows, at : at + part
            ]
    chunks[0][:, 12 * part :] = w_out[...]


def combine_kernel(kinds, place, *refs):
    sources, targets = refs[: 2 * len(kinds)], list(refs[2 * len(kinds) :])
    for kind, a, b in zip(kinds, sources[::2], sources[1::2]):
        if kind == "order":
            target = targets.pop(0)
            target[place[2]] = a[...]
            target[1 - place[2]] = b[...]
        elif kind == "pair":
            for i in range(2):
                targets.pop(0)[...] = (a[i].astype(F32) + b[i].astype(F32)).astype(BF16)
        else:
            targets.pop(0)[...] = (a[...].astype(F32) + b[...].astype(F32)).astype(BF16)


def halves_kernel(place, keep, got, target):
    target[place[0]] = keep[...]
    target[1 - place[0]] = got[...].astype(target.dtype)


def gain_row(products, gain):
    column = jnp.sum(products, axis=1, keepdims=True)
    row = jnp.broadcast_to(column, (column.shape[0], 128)).T[:1, :]
    return row / gain.astype(F32)


def unpack_kernel(place, own0, other0, own1, other1, own2, other2, w_gate, w_up, gain, *out):
    gate_out, up_out, down_out, out_out, gain_out = out
    me = place[0]
    half = own0.shape[1]
    rows = 2 * half
    part = 128
    down_rows = down_out.shape[1]
    for side, chunks in ((me, (own0, own1, own2)), (1 - me, (other0, other1, other2))):
        at = span(side, half)
        for chunk, source in enumerate(chunks):
            for i in range(4):
                to = slice(i * down_rows + chunk * part, i * down_rows + (chunk + 1) * part)
                gate_out[at, to] = source[0, :, i * part : (i + 1) * part].astype(F32)
                z_half, first = (0, (4 + i) * part) if i < 2 else (1, (i - 2) * part)
                up_out[at, to] = source[z_half, :, first : first + part].astype(F32)
                down_at = pl.ds(pl.multiple_of(i * rows + side * half, 8), half)
                first = (2 + i) * part
                down_out[down_at, chunk * part : (chunk + 1) * part] = source[
                    1, :, first : first + part
                ].astype(F32)
        first = 6 * part
        last = chunks[-1]
        out_out[at, :] = jnp.concatenate(
            [last[0, :, first:].astype(F32), last[1, :, first:].astype(F32)], 1
        )
    products = gate_out[...] * w_gate[...].astype(F32) + up_out[...] * w_up[...].astype(F32)
    gain_out[...] = gain_row(products, gain[...])


def unpack_input_kernel(
    place, own, other, w_query, w_key, w_value, gain, query_out, key_out, value_out, gain_out
):
    me = place[0]
    half = own.shape[0]
    key_at = QUERY_WIDTH + KEY_WIDTH
    for side, source in ((me, own), (1 - me, other)):
        at = span(side, half)
        wide = source[...].astype(F32)
        query_out[at, :] = wide[:, :QUERY_WIDTH]
        key_out[at, :] = wide[:, QUERY_WIDTH:key_at]
        value_out[at, :] = wide[:, key_at:]
    products = jnp.sum(query_out[...] * w_query[...].astype(F32), axis=1, keepdims=True)
    products += jnp.sum(key_out[...] * w_key[...].astype(F32), axis=1, keepdims=True)
    products += jnp.sum(value_out[...] * w_value[...].astype(F32), axis=1, keepdims=True)
    gain_out[...] = gain_row(products, gain[...])


def call(kernel, out, scratch, flops, exps, args, name, limit, aliases=None):
    shapes = [jax.ShapeDtypeStruct(s, d) for s, d in out]
    moved = sum(a.size * a.dtype.itemsize for a in args[1:]) + sum(
        s.size * s.dtype.itemsize for s in shapes
    )
    in_specs = [pl.BlockSpec(memory_space=pltpu.SMEM)] + [
        pl.BlockSpec(memory_space=pltpu.VMEM)
    ] * (len(args) - 1)
    return pl.pallas_call(
        kernel,
        out_shape=shapes,
        in_specs=in_specs,
        out_specs=[pl.BlockSpec(memory_space=pltpu.VMEM)] * len(shapes),
        scratch_shapes=[pltpu.VMEM(s, d) for s, d in scratch],
        input_output_aliases=aliases or {},
        compiler_params=pltpu.CompilerParams(vmem_limit_bytes=limit * MEBI),
        cost_estimate=pl.CostEstimate(flops=flops, bytes_accessed=moved, transcendentals=exps),
        name=name,
    )(*args)


def attend_back(group, qkv_t, log_total, attended_t, grad_t, cosine, sine):
    sequence = qkv_t.shape[1]
    group_width = REPEAT * HEAD_SIZE

    def rows_of(size, index):
        return pl.BlockSpec((size, sequence), lambda step: (index, 0))

    flops = 5 * REPEAT * sequence * sequence * HEAD_SIZE * 2
    return pl.pallas_call(
        attend_back_kernel,
        grid=(1,),
        out_shape=[
            jax.ShapeDtypeStruct((group_width, sequence), BF16),
            jax.ShapeDtypeStruct((HEAD_SIZE, sequence), BF16),
            jax.ShapeDtypeStruct((HEAD_SIZE, sequence), BF16),
        ],
        in_specs=[
            rows_of(group_width, group),
            rows_of(HEAD_SIZE, QUERY_HEADS + group),
            rows_of(HEAD_SIZE, ROTATED + group),
            pl.BlockSpec((1, 8, sequence), lambda step: (group, 0, 0)),
            rows_of(group_width, group),
            rows_of(group_width, group),
            rows_of(HALF, 0),
            rows_of(HALF, 0),
        ],
        out_specs=[rows_of(group_width, 0), rows_of(HEAD_SIZE, 0), rows_of(HEAD_SIZE, 0)],
        scratch_shapes=[
            pltpu.VMEM((sequence, HEAD_SIZE), BF16),
            pltpu.VMEM((sequence, HEAD_SIZE), BF16),
            pltpu.VMEM((sequence, HEAD_SIZE), F32),
            pltpu.VMEM((sequence, HEAD_SIZE), F32),
        ],
        compiler_params=pltpu.CompilerParams(vmem_limit_bytes=16 * MEBI),
        cost_estimate=pl.CostEstimate(
            flops=flops, bytes_accessed=4_000_000, transcendentals=REPEAT * sequence * sequence
        ),
        name="attend_back",
    )(qkv_t, qkv_t, qkv_t, log_total, attended_t, grad_t, cosine, sine)


def across(tensor, bit):
    return lax.ppermute(tensor, "fsdp", [(i, i ^ bit) for i in range(4)])


def over_context(tensor):
    return lax.ppermute(tensor, "ctx", [(0, 1), (1, 0)])


def after(tensor, *done):
    return lax.optimization_barrier((tensor, *done))[0]


def together(*values):
    return lax.optimization_barrier(values)


def along(tensor, bit):
    size = lax.axis_size("dp")
    return lax.ppermute(tensor, "dp", [(i, i ^ bit) for i in range(size)])


def whole_sequences(
    tokens, norm1_gain, w_query, w_key, w_value, w_out, norm2_gain, w_gate, w_up, w_down, out_grad
):
    half_rows, width = tokens.shape[1:]
    sequence = 2 * half_rows
    rows = w_query.shape[0]
    down_rows = w_down.shape[0]
    hidden_width = w_gate.shape[1]
    part = 128
    me = lax.axis_index("ctx")
    place = jnp.stack([me, lax.axis_index("fsdp"), lax.axis_index("dp") & 1]).astype(jnp.int32)
    tokens = jnp.swapaxes(tokens, 1, 2)
    out_grad = jnp.swapaxes(out_grad, 1, 2)

    tokens_send = lax.dynamic_index_in_dim(tokens, 1 - me, 0, False)
    tokens_theirs = over_context(tokens_send)
    gains_own = jnp.pad(
        jnp.stack([norm1_gain, norm2_gain]), ((0, GAIN_ROWS - 2), (0, TILE - rows))
    )
    gains_own = after(gains_own, tokens_send)
    (packed,) = call(
        pack_input_kernel,
        [((rows + GAIN_ROWS, PACKED), BF16)],
        [],
        0,
        0,
        (place, w_query, w_key, w_value, gains_own),
        "pack_input",
        16,
    )
    packed_y = across(packed, 2)
    packed_core = across(packed, 1)
    dy_theirs = over_context(lax.dynamic_index_in_dim(out_grad, 1 - me, 0, False))
    chunks = call(
        pack_kernel,
        [((rows, 12 * part + (0 if index else QUERY_WIDTH)), BF16) for index in range(3)],
        [],
        0,
        0,
        (place, w_gate, w_up, w_down.T, after(w_out, packed)),
        "pack",
        16,
    )
    cosine, sine = rope_tables(jnp.arange(sequence, dtype=jnp.int32), HEAD_SIZE)
    *chunks, _, cosine, sine, place = together(*chunks, packed, cosine.T, sine.T, place)
    packed_both = across(packed_y, 1)
    chunks_y = [across(chunk, 2) for chunk in chunks]
    chunks_core = [across(chunk, 1) for chunk in chunks]

    pairs = sequence * sequence
    x_seq, normed, packed_all, gains, qkv_t, log_total, attended_t = call(
        attend_kernel,
        [
            ((width, sequence), BF16),
            ((width, sequence), BF16),
            ((width, PACKED), BF16),
            ((width, 128), F32),
            ((USED, sequence), BF16),
            ((KEY_VALUE_HEADS, 8, sequence), F32),
            ((QUERY_WIDTH, sequence), BF16),
        ],
        [((PACKED, width), BF16), ((KEY_VALUE_HEADS, sequence, HEAD_SIZE), BF16)],
        2 * sequence * width * PACKED + 4 * QUERY_WIDTH * pairs,
        QUERY_HEADS * pairs,
        (place, tokens, tokens_theirs, packed, packed_y, packed_core, packed_both, cosine, sine),
        "attend",
        20,
    )

    natural, turned = ((width, 4 * part), BF16), ((4 * part, width), BF16)
    row, wide_row = ((width, sequence), BF16), ((4 * part, sequence), BF16)
    row_sum = ((width, sequence), F32)
    share = ((2, 2, 2, rows // 2, 6 * part), BF16)
    last_share = ((2, 2, 2, rows // 2, 6 * part + QUERY_WIDTH // 2), BF16)
    chunk_scratch = [
        natural,
        natural,
        natural,
        turned,
        turned,
        turned,
        wide_row,
        wide_row,
        wide_row,
        ((width, 4 * part), F32),
    ]
    flops = 2 * sequence * width * 9 * 4 * part
    exps = sequence * 4 * part

    def pieces_of(chunk, *done):
        y_piece, *done = together(chunks_y[chunk], *done)
        return (chunks[chunk], y_piece, chunks_core[chunk], across(y_piece, 1)), done

    pieces, (attended_t, dy_theirs) = pieces_of(0, attended_t, dy_theirs)
    middle, normed2, scales, dy, w_out_all, out_sum, grad_sum, keep0, send0 = call(
        first_chunk_kernel,
        [
            row_sum,
            row,
            ((8, sequence), F32),
            row,
            ((QUERY_WIDTH, width), BF16),
            row_sum,
            row_sum,
            share,
            share,
        ],
        [((width, QUERY_WIDTH), BF16), *chunk_scratch],
        flops + 2 * sequence * width * QUERY_WIDTH,
        exps,
        (place, x_seq, attended_t, out_grad, dy_theirs, gains, *pieces),
        "first_chunk",
        26,
    )

    def combine(*items):
        kinds = tuple(item[0] for item in items)
        args = [tensor for item in items for tensor in item[1:]]
        out = []
        for kind, tensor, _ in items:
            if kind == "order":
                out.append(((2, *tensor.shape), BF16))
            elif kind == "pair":
                out += [(tensor.shape[1:], BF16)] * 2
            else:
                out.append((tensor.shape, BF16))
        kernel = functools.partial(combine_kernel, kinds)
        return call(kernel, out, [], 0, 0, (place, *args), "combine", 16)

    got0 = across(send0, 1)
    pieces, (out_sum,) = pieces_of(1, out_sum)
    out_sum, grad_sum, keep1, send1 = call(
        next_chunk_kernel,
        [row_sum, row_sum, share, share],
        chunk_scratch,
        flops,
        exps,
        (place, normed2, dy, out_sum, grad_sum, *pieces),
        "next_chunk",
        20,
        {3: 0, 4: 1},
    )

    got0, out_sum = together(got0, out_sum)
    own0, part0 = combine(("pair", keep0, got0))
    pieces, (part0, out_sum) = pieces_of(2, part0, out_sum)
    got0, got1 = across(part0, 2), across(send1, 1)
    out_keep, out_send, middle_grad, grad_t, keep2, send2 = call(
        last_chunk_kernel,
        [
            ((width, half_rows), BF16),
            ((width, half_rows), BF16),
            row_sum,
            ((QUERY_WIDTH, sequence), BF16),
            last_share,
            last_share,
        ],
        [row_sum, row, *chunk_scratch],
        flops + 4 * sequence * width * QUERY_WIDTH,
        exps,
        (
            place,
            normed2,
            dy,
            out_sum,
            grad_sum,
            *pieces,
            attended_t,
            gains,
            middle,
            scales,
            w_out_all,
        ),
        "last_chunk",
        24,
    )

    got0, got1, grad_t = together(got0, got1, grad_t)
    own0, part0, own1, part1 = combine(("pair", own0, got0), ("pair", keep1, got1))
    part0, part1, grad_t = together(part0, part1, grad_t)
    got0, got1, got2 = over_context(part0), across(part1, 2), across(send2, 1)
    out_theirs = over_context(out_send)

    back_args = (log_total, attended_t, grad_t, cosine, sine)
    grads0 = attend_back(0, qkv_t, *back_args)
    got2, *grads0 = together(got2, *grads0)
    own2, part2 = combine(("pair", keep2, got2))
    part2, qkv_t = together(part2, qkv_t)

    got2 = across(part2, 2)
    grads1 = attend_back(1, qkv_t, *back_args)
    got0, got1, *grads1 = together(got0, got1, *grads1)
    own0, part0, own1, part1 = combine(("pair", own0, got0), ("pair", own1, got1))
    part0, part1, qkv_t = together(part0, part1, qkv_t)

    got0, got1 = along(part0, 1), over_context(part1)
    grads2 = attend_back(2, qkv_t, *back_args)
    got0, out_theirs, *grads2 = together(got0, out_theirs, *grads2)
    (own0,) = combine(("one", own0, got0))
    own0, *grads2 = together(own0, *grads2)

    got0 = along(own0, 2)
    keep_w, send_w, joined = call(
        joined_kernel,
        [
            ((2, 2, rows // 2, USED), BF16),
            ((2, 2, rows // 2, USED), BF16),
            ((USED, sequence), BF16),
        ],
        [((width, USED), F32)],
        2 * sequence * width * USED,
        0,
        (place, normed, *grads0, *grads1, *grads2),
        "joined",
        16,
    )
    got0, got1, got2, send_w, joined = together(got0, got1, got2, send_w, joined)
    got_w = across(send_w, 1)
    own0, own1, part1, own2, part2 = combine(
        ("one", own0, got0), ("pair", own1, got1), ("pair", own2, got2)
    )
    own0, part1, part2, joined = together(own0, part1, part2, joined)

    got0, got1, got2 = along(own0, 1), along(part1, 1), over_context(part2)
    keep_x, send_x = call(
        input_kernel,
        [((width, half_rows), F32), ((width, half_rows), BF16)],
        [((width, sequence), F32)],
        2 * sequence * width * USED,
        sequence,
        (place, x_seq, packed_all, gains, middle_grad, joined),
        "input_side",
        24,
    )
    got_w, got0, got1, got2, send_x = together(got_w, got0, got1, got2, send_x)
    own_w, part_w, own0, own1, own2, part2 = combine(
        ("pair", keep_w, got_w),
        ("order", own0, got0),
        ("one", own1, got1),
        ("pair", own2, got2),
    )
    part_w, own0, own1, part2, send_x = together(part_w, own0, own1, part2, send_x)

    got_w, other0, got1, got2 = (
        across(part_w, 2),
        over_context(own0),
        along(own1, 2),
        along(part2, 1),
    )
    x_theirs = over_context(send_x)
    got_w, got1, got2 = together(got_w, got1, got2)
    own_w, part_w, own1, own2 = combine(
        ("pair", own_w, got_w), ("one", own1, got1), ("one", own2, got2)
    )
    part_w, own1, own2 = together(part_w, own1, own2)

    got_w, got1, got2 = over_context(part_w), along(own1, 1), along(own2, 2)
    got_w, got1, got2, x_theirs, other0 = together(got_w, got1, got2, x_theirs, other0)
    own_w, own1, own2 = combine(("one", own_w, got_w), ("order", own1, got1), ("one", own2, got2))
    own_w, own1, own2 = together(own_w, own1, own2)

    got_w, other1, got2 = along(own_w, 1), over_context(own1), along(own2, 1)
    got_w, got2 = together(got_w, got2)
    own_w, own2 = combine(("one", own_w, got_w), ("order", own2, got2))
    own_w, own2 = together(own_w, own2)

    got_w, other2 = along(own_w, 2), over_context(own2)
    got_w, other1 = together(got_w, other1)
    (own_w,) = combine(("one", own_w, got_w))
    other_w = over_context(own_w)

    def place_halves(keep, got, name):
        (both,) = call(
            halves_kernel, [((2, *keep.shape), keep.dtype)], [], 0, 0, (place, keep, got), name, 16
        )
        return jnp.swapaxes(both, 1, 2)

    gate_sum, up_sum, down_sum, out_sum, gain2_sum = call(
        unpack_kernel,
        [
            ((rows, hidden_width), F32),
            ((rows, hidden_width), F32),
            ((width, down_rows), F32),
            ((rows, width), F32),
            ((1, rows), F32),
        ],
        [],
        0,
        0,
        (place, own0, other0, own1, other1, own2, other2, w_gate, w_up, norm2_gain[None, :]),
        "unpack",
        24,
    )
    query_sum, key_sum, value_sum, gain1_sum = call(
        unpack_input_kernel,
        [
            ((rows, QUERY_WIDTH), F32),
            ((rows, KEY_WIDTH), F32),
            ((rows, KEY_WIDTH), F32),
            ((1, rows), F32),
        ],
        [],
        0,
        0,
        (place, own_w, other_w, w_query, w_key, w_value, norm1_gain[None, :]),
        "unpack_input",
        16,
    )
    return (
        place_halves(out_keep, out_theirs, "output_halves"),
        place_halves(keep_x, x_theirs, "gradient_halves"),
        gain1_sum[0],
        query_sum,
        key_sum,
        value_sum,
        out_sum,
        gain2_sum[0],
        gate_sum,
        up_sum,
        down_sum.T,
    )


def layer_step(tokens, *rest):
    whole = (
        lax.axis_size("ctx") == 2
        and lax.axis_size("fsdp") == 4
        and lax.axis_size("dp") == 4
        and tokens.shape[0] == 2
        and tokens.shape[1] % WIDE_TILE == 0
        and rest[8].shape == (384, 576)
    )
    return (whole_sequences if whole else split_context)(tokens, *rest)


def solution(mesh):
    return jax.shard_map(
        layer_step,
        mesh=mesh,
        in_specs=(
            P(("dp", "fsdp"), "ctx", None),
            P("fsdp"),
            P("fsdp", None),
            P("fsdp", None),
            P("fsdp", None),
            P("fsdp", None),
            P("fsdp"),
            P("fsdp", None),
            P("fsdp", None),
            P("fsdp", None),
            P(("dp", "fsdp"), "ctx", None),
        ),
        out_specs=(
            P(("dp", "fsdp"), "ctx", None),
            P(("dp", "fsdp"), "ctx", None),
            P("fsdp"),
            P("fsdp", None),
            P("fsdp", None),
            P("fsdp", None),
            P("fsdp", None),
            P("fsdp"),
            P("fsdp", None),
            P("fsdp", None),
            P("fsdp", None),
        ),
        check_vma=False,
    )
```

```python
import functools
import math

import jax
import jax.numpy as jnp
from jax import lax
from jax.experimental import pallas as pl
from jax.experimental.pallas import tpu as pltpu
from jax.sharding import PartitionSpec as P

QUERY_HEADS = 9
KEY_VALUE_HEADS = 3
HEAD_SIZE = 64


EPSILON = 1e-05
ROPE_THETA = 100000.0
MASKED = -1e30


def rope_tables(positions, head_width):
    half_size = head_width // 2
    inverse = jnp.exp(
        jnp.arange(half_size, dtype=jnp.float32) * (-2.0 * math.log(ROPE_THETA) / head_width)
    )
    angle = positions.astype(jnp.float32)[:, None] * inverse[None, :]
    return (jnp.cos(angle), jnp.sin(angle))


def rotary_apply(tensor, cosine_table, sine_table):
    half_size = tensor.shape[-1] // 2
    first_half = tensor[..., :half_size]
    second_half = tensor[..., half_size:]
    cosine_table = cosine_table[None, :, None, :]
    sine_table = sine_table[None, :, None, :]
    return jnp.concatenate(
        [
            first_half * cosine_table - second_half * sine_table,
            second_half * cosine_table + first_half * sine_table,
        ],
        -1,
    )


def rotate_back(tensor, cosine_table, sine_table):
    half_size = tensor.shape[-1] // 2
    first_half = tensor[..., :half_size]
    second_half = tensor[..., half_size:]
    cosine_table = cosine_table[None, :, None, :]
    sine_table = sine_table[None, :, None, :]
    return jnp.concatenate(
        [
            first_half * cosine_table + second_half * sine_table,
            second_half * cosine_table - first_half * sine_table,
        ],
        -1,
    )


def rms_scale(tensor):
    return lax.rsqrt(jnp.mean(tensor * tensor, axis=-1, keepdims=True) + EPSILON)


def block_scores(query_block, key_block, query_pos, key_pos):
    scores = (
        jnp.einsum("gqhrd,gkhd->ghrqk", query_block, key_block, preferred_element_type=jnp.float32)
        * 0.125
    )
    visible = key_pos[None, :] <= query_pos[:, None]
    return jnp.where(visible, scores, MASKED)


def split_context(
    tokens, norm1_gain, w_query, w_key, w_value, w_out, norm2_gain, w_gate, w_up, w_down, out_grad
):
    gain1, wq_full, wk_full, wv_full, wo_full, gain2, wg_full, wu_full, wd_full = (
        lax.all_gather(norm1_gain, "fsdp", axis=0, tiled=True),
        lax.all_gather(w_query, "fsdp", axis=0, tiled=True),
        lax.all_gather(w_key, "fsdp", axis=0, tiled=True),
        lax.all_gather(w_value, "fsdp", axis=0, tiled=True),
        lax.all_gather(w_out, "fsdp", axis=0, tiled=True),
        lax.all_gather(norm2_gain, "fsdp", axis=0, tiled=True),
        lax.all_gather(w_gate, "fsdp", axis=0, tiled=True),
        lax.all_gather(w_up, "fsdp", axis=0, tiled=True),
        lax.all_gather(w_down, "fsdp", axis=0, tiled=True),
    )
    query_group_count, local_row_count, model_width = tokens.shape
    repeat_heads = QUERY_HEADS // KEY_VALUE_HEADS
    head_width = HEAD_SIZE
    key_value_width = KEY_VALUE_HEADS * HEAD_SIZE
    query_width = QUERY_HEADS * HEAD_SIZE
    first_row = lax.axis_index("ctx") * local_row_count
    last_row = first_row + local_row_count - 1
    positions = first_row + jnp.arange(local_row_count, dtype=jnp.int32)
    cosine_table, sine_table = rope_tables(positions, head_width)
    gain1f = gain1.astype(jnp.float32)
    gain2f = gain2.astype(jnp.float32)
    inputs = tokens.astype(jnp.float32)
    scale1 = rms_scale(inputs)
    normed1 = (inputs * scale1 * gain1f).astype(jnp.bfloat16)
    query_before_rotation = jnp.einsum(
        "gsd,de->gse", normed1, wq_full, preferred_element_type=jnp.float32
    )
    key_before_rotation = jnp.einsum(
        "gsd,de->gse", normed1, wk_full, preferred_element_type=jnp.float32
    )
    value_projected = jnp.einsum(
        "gsd,de->gse", normed1, wv_full, preferred_element_type=jnp.float32
    )
    query_matrix = rotary_apply(
        query_before_rotation.reshape(query_group_count, local_row_count, QUERY_HEADS, head_width),
        cosine_table,
        sine_table,
    ).astype(jnp.bfloat16)
    query_matrix = query_matrix.reshape(
        query_group_count, local_row_count, KEY_VALUE_HEADS, repeat_heads, head_width
    )
    key_local = rotary_apply(
        key_before_rotation.reshape(
            query_group_count, local_row_count, KEY_VALUE_HEADS, head_width
        ),
        cosine_table,
        sine_table,
    ).astype(jnp.bfloat16)
    local_value_rows = value_projected.astype(jnp.bfloat16)
    collected_keys, collected_values = (
        lax.all_gather(
            key_local.reshape(query_group_count, local_row_count, key_value_width),
            "ctx",
            axis=1,
            tiled=True,
        ),
        lax.all_gather(local_value_rows, "ctx", axis=1, tiled=True),
    )
    sequence_length = collected_keys.shape[1]
    every_key_row = collected_keys.reshape(
        query_group_count, sequence_length, KEY_VALUE_HEADS, head_width
    )
    every_value_row = collected_values.reshape(
        query_group_count, sequence_length, KEY_VALUE_HEADS, head_width
    )
    local_value_rows = local_value_rows.reshape(
        query_group_count, local_row_count, KEY_VALUE_HEADS, head_width
    )
    key_span = min(sequence_length, 512)
    block_total = last_row // key_span + 1

    def key_slices(step_index):
        first_key = step_index * key_span
        key_block = lax.dynamic_slice_in_dim(every_key_row, first_key, key_span, 1)
        value_block = lax.dynamic_slice_in_dim(every_value_row, first_key, key_span, 1)
        key_pos = first_key + jnp.arange(key_span, dtype=jnp.int32)
        return (key_block, value_block, key_pos)

    def stats_step(step_index, running):
        row_max, row_sum = running
        key_block, value_block, key_pos = key_slices(step_index)
        scores = block_scores(query_matrix, key_block, positions, key_pos)
        new_max = jnp.maximum(row_max, jnp.max(scores, axis=-1))
        row_sum = row_sum * jnp.exp(row_max - new_max) + jnp.sum(
            jnp.exp(scores - new_max[..., None]), axis=-1
        )
        return (new_max, row_sum)

    statistics_shape = (query_group_count, KEY_VALUE_HEADS, repeat_heads, local_row_count)
    row_max, row_sum = lax.fori_loop(
        0,
        block_total,
        stats_step,
        (jnp.full(statistics_shape, MASKED, jnp.float32), jnp.zeros(statistics_shape, jnp.float32)),
    )
    log_total = row_max + jnp.log(row_sum)

    def mix_step(step_index, running):
        key_block, value_block, key_pos = key_slices(step_index)
        scores = block_scores(query_matrix, key_block, positions, key_pos)
        probs = jnp.exp(scores - log_total[..., None]).astype(jnp.bfloat16)
        return running + jnp.einsum(
            "ghrqk,gkhd->gqhrd", probs, value_block, preferred_element_type=jnp.float32
        )

    attended_full = lax.fori_loop(
        0,
        block_total,
        mix_step,
        jnp.zeros(
            (query_group_count, local_row_count, KEY_VALUE_HEADS, repeat_heads, head_width),
            jnp.float32,
        ),
    )
    attended = attended_full.astype(jnp.bfloat16).reshape(
        query_group_count, local_row_count, query_width
    )
    branch = jnp.einsum("gse,ed->gsd", attended, wo_full, preferred_element_type=jnp.float32)
    middle = inputs + branch
    scale2 = rms_scale(middle)
    normed2 = (middle * scale2 * gain2f).astype(jnp.bfloat16)
    gate_act = jnp.einsum("gsd,df->gsf", normed2, wg_full, preferred_element_type=jnp.float32)
    up_act = jnp.einsum("gsd,df->gsf", normed2, wu_full, preferred_element_type=jnp.float32)
    gate_sig = jax.nn.sigmoid(gate_act)
    gate_silu = gate_act * gate_sig
    hidden = (gate_silu * up_act).astype(jnp.bfloat16)
    mlp_out = jnp.einsum("gsf,fd->gsd", hidden, wd_full, preferred_element_type=jnp.float32)
    output = (middle + mlp_out).astype(jnp.bfloat16)
    out_float = out_grad.astype(jnp.float32)
    grad_down = jnp.einsum("gsf,gsd->fd", hidden, out_grad, preferred_element_type=jnp.float32)
    hidden_grad = jnp.einsum("gsd,fd->gsf", out_grad, wd_full, preferred_element_type=jnp.float32)
    gate_grad = (hidden_grad * up_act * gate_sig * (1.0 + gate_act * (1.0 - gate_sig))).astype(
        jnp.bfloat16
    )
    up_grad = (hidden_grad * gate_silu).astype(jnp.bfloat16)
    grad_gate = jnp.einsum("gsd,gsf->df", normed2, gate_grad, preferred_element_type=jnp.float32)
    grad_up = jnp.einsum("gsd,gsf->df", normed2, up_grad, preferred_element_type=jnp.float32)
    normed2_grad = jnp.einsum("gsf,df->gsd", gate_grad, wg_full, preferred_element_type=jnp.float32)
    normed2_grad = normed2_grad + jnp.einsum(
        "gsf,df->gsd", up_grad, wu_full, preferred_element_type=jnp.float32
    )
    grad_gain2 = jnp.sum(normed2_grad * middle * scale2, axis=(0, 1))
    scaled2 = gain2f * normed2_grad
    middle_grad = (
        out_float
        + scale2 * scaled2
        - middle * scale2**3 * jnp.mean(scaled2 * middle, axis=-1, keepdims=True)
    )
    branch_grad = middle_grad.astype(jnp.bfloat16)
    grad_out = jnp.einsum("gse,gsd->ed", attended, branch_grad, preferred_element_type=jnp.float32)
    attended_output_gradient = jnp.einsum(
        "gsd,ed->gse", branch_grad, wo_full, preferred_element_type=jnp.float32
    ).astype(jnp.bfloat16)
    attention_gradient = attended_output_gradient.reshape(
        query_group_count, local_row_count, KEY_VALUE_HEADS, repeat_heads, head_width
    )
    delta = jnp.sum(attention_gradient.astype(jnp.float32) * attended_full, axis=-1).transpose(
        0, 2, 3, 1
    )

    def query_grad_step(step_index, running):
        key_block, value_block, key_pos = key_slices(step_index)
        scores = block_scores(query_matrix, key_block, positions, key_pos)
        probs = jnp.exp(scores - log_total[..., None])
        dprob = jnp.einsum(
            "gqhrd,gkhd->ghrqk", attention_gradient, value_block, preferred_element_type=jnp.float32
        )
        score_grad = (probs * (dprob - delta[..., None])).astype(jnp.bfloat16)
        return running + jnp.einsum(
            "ghrqk,gkhd->gqhrd", score_grad, key_block, preferred_element_type=jnp.float32
        )

    query_grad = (
        lax.fori_loop(
            0,
            block_total,
            query_grad_step,
            jnp.zeros(
                (query_group_count, local_row_count, KEY_VALUE_HEADS, repeat_heads, head_width),
                jnp.float32,
            ),
        )
        * 0.125
    )
    row_total = local_row_count * lax.axis_size("ctx")
    term_span = math.gcd(row_total, key_span)

    def key_block_term(step_index):
        first_key = step_index * term_span
        key_block = lax.dynamic_slice_in_dim(every_key_row, first_key, term_span, 1)
        value_block = lax.dynamic_slice_in_dim(every_value_row, first_key, term_span, 1)
        key_pos = first_key + jnp.arange(term_span, dtype=jnp.int32)

        def compute_term(unused):
            scores = block_scores(query_matrix, key_block, positions, key_pos)
            probs = jnp.exp(scores - log_total[..., None])
            dprob = jnp.einsum(
                "gqhrd,gkhd->ghrqk",
                attention_gradient,
                value_block,
                preferred_element_type=jnp.float32,
            )
            score_grad = (probs * (dprob - delta[..., None])).astype(jnp.bfloat16)
            key_term = (
                jnp.einsum(
                    "ghrqk,gqhrd->kghd",
                    score_grad,
                    query_matrix,
                    preferred_element_type=jnp.float32,
                )
                * 0.125
            )
            value_term = jnp.einsum(
                "ghrqk,gqhrd->kghd",
                probs.astype(jnp.bfloat16),
                attention_gradient,
                preferred_element_type=jnp.float32,
            )
            return jnp.concatenate(
                [
                    key_term.reshape(term_span, query_group_count, key_value_width),
                    value_term.reshape(term_span, query_group_count, key_value_width),
                ],
                -1,
            )

        def empty_term(unused):
            return jnp.zeros((term_span, query_group_count, 2 * key_value_width), jnp.float32)

        return lax.cond(first_key <= last_row, compute_term, empty_term, 0)

    terms = lax.map(key_block_term, jnp.arange(row_total // term_span, dtype=jnp.int32))
    paired_gradients = (
        lax.psum_scatter(
            terms.reshape(row_total, query_group_count, 2 * key_value_width).astype(jnp.bfloat16),
            "ctx",
            scatter_dimension=0,
            tiled=True,
        )
        .astype(jnp.float32)
        .transpose(1, 0, 2)
    )
    key_gradient = paired_gradients[..., :key_value_width].reshape(
        query_group_count, local_row_count, KEY_VALUE_HEADS, head_width
    )
    value_gradient = paired_gradients[..., key_value_width:].reshape(
        query_group_count, local_row_count, KEY_VALUE_HEADS, head_width
    )
    query_pre_grad = rotate_back(
        query_grad.reshape(query_group_count, local_row_count, QUERY_HEADS, head_width),
        cosine_table,
        sine_table,
    )
    query_pre_grad = query_pre_grad.astype(jnp.bfloat16).reshape(
        query_group_count, local_row_count, query_width
    )
    key_pre_grad = (
        rotate_back(key_gradient, cosine_table, sine_table)
        .astype(jnp.bfloat16)
        .reshape(query_group_count, local_row_count, key_value_width)
    )
    value_pre_grad = value_gradient.astype(jnp.bfloat16).reshape(
        query_group_count, local_row_count, key_value_width
    )
    grad_query = jnp.einsum(
        "gsd,gse->de", normed1, query_pre_grad, preferred_element_type=jnp.float32
    )
    grad_key = jnp.einsum("gsd,gse->de", normed1, key_pre_grad, preferred_element_type=jnp.float32)
    grad_value = jnp.einsum(
        "gsd,gse->de", normed1, value_pre_grad, preferred_element_type=jnp.float32
    )
    normed1_grad = jnp.einsum(
        "gse,de->gsd", query_pre_grad, wq_full, preferred_element_type=jnp.float32
    )
    normed1_grad = normed1_grad + jnp.einsum(
        "gse,de->gsd", key_pre_grad, wk_full, preferred_element_type=jnp.float32
    )
    normed1_grad = normed1_grad + jnp.einsum(
        "gse,de->gsd", value_pre_grad, wv_full, preferred_element_type=jnp.float32
    )
    grad_gain1 = jnp.sum(normed1_grad * inputs * scale1, axis=(0, 1))
    scaled1 = gain1f * normed1_grad
    input_grad = (
        middle_grad
        + scale1 * scaled1
        - inputs * scale1**3 * jnp.mean(scaled1 * inputs, axis=-1, keepdims=True)
    )
    totals = lax.psum(
        (
            grad_gain1,
            grad_query,
            grad_key,
            grad_value,
            grad_out,
            grad_gain2,
            grad_gate,
            grad_up,
            grad_down,
        ),
        ("dp", "ctx", "fsdp"),
    )
    owner = lax.axis_index("fsdp")
    shards = (norm1_gain, w_query, w_key, w_value, w_out, norm2_gain, w_gate, w_up, w_down)
    shares = tuple(
        (
            lax.dynamic_slice_in_dim(summed, owner * shard.shape[0], shard.shape[0], 0)
            for summed, shard in zip(totals, shards)
        )
    )
    return (
        output,
        input_grad,
        shares[0],
        shares[1],
        shares[2],
        shares[3],
        shares[4],
        shares[5],
        shares[6],
        shares[7],
        shares[8],
    )


WIDTH = 576
QUERY_WIDTH = QUERY_HEADS * HEAD_SIZE
KEY_WIDTH = KEY_VALUE_HEADS * HEAD_SIZE
ROTATED = QUERY_HEADS + KEY_VALUE_HEADS
REPEAT = QUERY_HEADS // KEY_VALUE_HEADS
HALF = HEAD_SIZE // 2
USED = QUERY_WIDTH + 2 * KEY_WIDTH
PACKED = USED + 64
GAIN_ROWS = 16
TILE = 256
WIDE_TILE = 512
MEBI = 1024 * 1024
F32 = jnp.float32
BF16 = jnp.bfloat16


def mm(a, b):
    return jnp.dot(a, b, preferred_element_type=F32)


def mm_nt(a, b):
    return lax.dot_general(a, b, (((1,), (1,)), ((), ())), preferred_element_type=F32)


def flip(tensor):
    return tensor.astype(F32).T.astype(tensor.dtype)


def span(index, size, step=None):
    step = size if step is None else step
    return pl.ds(pl.multiple_of(index * step, step), size)


def flip_blocks(target, source, block):
    def one(step, carry):
        at = span(step, block)
        target[at, :] = flip(source[:, at])
        return carry

    lax.fori_loop(0, source.shape[1] // block, one, 0)


def column_scale(tensor):
    return lax.rsqrt(jnp.mean(tensor * tensor, axis=0, keepdims=True) + EPSILON)


def sigmoid(tensor):
    return 0.5 * jnp.tanh(0.5 * tensor) + 0.5


def causal_last(scores, tile):
    shape = (TILE, REPEAT * TILE)
    visible = lax.broadcasted_iota(jnp.int32, shape, 0) <= (
        lax.broadcasted_iota(jnp.int32, shape, 1) & (TILE - 1)
    )
    last = jnp.where(visible, scores[tile * TILE :, :], MASKED)
    return last if tile == 0 else jnp.concatenate([scores[: tile * TILE, :], last], 0)


def attend_kernel(
    place,
    tokens,
    theirs,
    w_own,
    w_y,
    w_core,
    w_both,
    cosine,
    sine,
    x_seq,
    normed,
    packed,
    gains,
    qkv_t,
    log_total,
    attended_t,
    packed_t,
    key_rows,
):
    me, shard = place[0], place[1]
    half_rows = theirs.shape[1]
    sequence = 2 * half_rows
    x_seq[:, span(me, half_rows)] = tokens[me]
    x_seq[:, span(1 - me, half_rows)] = theirs[...]
    rows = packed.shape[0] // 4
    for bits, piece in ((0, w_own), (2, w_y), (1, w_core), (3, w_both)):
        at = span(shard ^ bits, rows)
        packed[at, :] = piece[:rows, :]
        gains[at, :GAIN_ROWS] = piece[rows:, :TILE].astype(F32).T[:rows, :]
    flip_blocks(packed_t, packed, TILE)
    gain1 = gains[:, :1]

    def project(step, carry):
        at = span(step, WIDE_TILE)
        x = x_seq[:, at].astype(F32)
        normed_tile = (x * column_scale(x) * gain1).astype(BF16)
        normed[:, at] = normed_tile
        turned = mm(packed_t[:USED, :], normed_tile)
        cos, sin = cosine[:, at], sine[:, at]
        for head in range(ROTATED):
            a = turned[head * HEAD_SIZE : head * HEAD_SIZE + HALF, :]
            b = turned[head * HEAD_SIZE + HALF : (head + 1) * HEAD_SIZE, :]
            both = jnp.concatenate([a * cos - b * sin, b * cos + a * sin], 0)
            if head < QUERY_HEADS:
                both = both * 0.125
            else:
                key_rows[head - QUERY_HEADS, at, :] = both.T.astype(BF16)
            qkv_t[head * HEAD_SIZE : (head + 1) * HEAD_SIZE, at] = both.astype(BF16)
        qkv_t[ROTATED * HEAD_SIZE :, at] = turned[ROTATED * HEAD_SIZE :, :].astype(BF16)
        return carry

    lax.fori_loop(0, sequence // WIDE_TILE, project, 0)

    def one_group(group, carry):
        value_rows = span(ROTATED + group, HEAD_SIZE)
        for tile in range(sequence // TILE):
            extent = (tile + 1) * TILE
            cols = slice(tile * TILE, extent)
            queries = jnp.concatenate(
                [qkv_t[span(group * REPEAT + r, HEAD_SIZE), cols] for r in range(REPEAT)], 1
            )
            scores = causal_last(mm(key_rows[group, :extent, :], queries), tile)
            top = jnp.max(scores, axis=0, keepdims=True)
            weights = jnp.exp(scores - top)
            total = jnp.sum(weights, axis=0, keepdims=True)
            mixed = mm(qkv_t[value_rows, :extent], weights.astype(BF16))
            mixed = (mixed * (1.0 / total)).astype(BF16)
            logs = top + jnp.log(total)
            for r in range(REPEAT):
                own = slice(r * TILE, (r + 1) * TILE)
                attended_t[span(group * REPEAT + r, HEAD_SIZE), cols] = mixed[:, own]
                log_total[group, r : r + 1, cols] = logs[:, own]
        return carry

    lax.fori_loop(0, KEY_VALUE_HEADS, one_group, 0)


def places(shard, row_bit, keep, send):
    for y_bit in range(2):
        for x_bit in range(2):
            for core_bit, target in ((0, keep), (1, send)):
                yield target, y_bit, x_bit, shard ^ (2 * y_bit + core_bit), row_bit ^ x_bit


def chunk_step(place, pieces, normed, dy, out_sum, grad_sum, keep, send, scratch):
    w_gate, w_up, w_down_t, w_gate_t, w_up_t, w_down, hidden, gate_grad, up_grad, total = scratch
    row_bit, shard, level = place[3], place[1], place[2]
    rows = pieces[0].shape[0]
    wide = w_gate.shape[1]
    part = wide // 4
    sequence = normed.shape[1]
    for bits, piece in zip((0, 2, 1, 3), pieces):
        at = span(shard ^ bits, rows)
        w_gate[at, :] = piece[:, :wide]
        w_up[at, :] = piece[:, wide : 2 * wide]
        for block in range(4):
            first = 2 * wide + block * part
            w_down_t[block * rows : (block + 1) * rows, span(shard ^ bits, part)] = piece[
                :, first : first + part
            ]
    w_gate_t[...] = flip(w_gate[...])
    w_up_t[...] = flip(w_up[...])
    w_down[...] = flip(w_down_t[...])
    for first in range(0, sequence, WIDE_TILE):
        at = slice(first, first + WIDE_TILE)
        gate = mm(w_gate_t[...], normed[:, at])
        up = mm(w_up_t[...], normed[:, at])
        hidden_grad = mm(w_down[...], dy[:, at])
        sig = sigmoid(gate)
        silu = gate * sig
        hidden_tile = (silu * up).astype(BF16)
        gate_tile = (hidden_grad * up * (sig + silu * (1.0 - sig))).astype(BF16)
        up_tile = (hidden_grad * silu).astype(BF16)
        hidden[:, at] = hidden_tile
        gate_grad[:, at] = gate_tile
        up_grad[:, at] = up_tile
        out_sum[:, at] += mm(w_down_t[...], hidden_tile)
        grad_sum[:, at] += mm(w_gate[...], gate_tile) + mm(w_up[...], up_tile)
    half = rows // 2
    middle = wide // 2
    for grads, moves in (
        (gate_grad, ((0, 0, 0, wide),)),
        (up_grad, ((0, 0, wide, middle), (1, middle, 0, middle))),
    ):
        total[...] = mm_nt(normed[...], grads[...])
        for target, y_bit, x_bit, owner, side in places(shard, place[3], keep, send):
            at = span(owner * 2 + side, half)
            for z_half, first, to, count in moves:
                target[y_bit, x_bit, level ^ z_half, :, to : to + count] = total[
                    at, first : first + count
                ].astype(BF16)
    total[...] = mm_nt(dy[...], hidden[...])
    for target, y_bit, x_bit, owner, side in places(shard, place[3], keep, send):
        for block in range(4):
            at = pl.ds(pl.multiple_of(block * rows + side * half, 8), half)
            to = middle + block * part
            target[y_bit, x_bit, level ^ 1, :, to : to + part] = total[
                at, span(owner, part)
            ].astype(BF16)


def first_chunk_kernel(
    place,
    x_seq,
    attended_t,
    out_grad,
    dy_theirs,
    gains,
    p_own,
    p_y,
    p_core,
    p_both,
    middle,
    normed,
    scales,
    dy,
    w_out,
    out_sum,
    grad_sum,
    keep,
    send,
    w_out_t,
    *scratch,
):
    me, shard = place[0], place[1]
    half_rows = dy_theirs.shape[1]
    sequence = 2 * half_rows
    dy[:, span(me, half_rows)] = out_grad[me]
    dy[:, span(1 - me, half_rows)] = dy_theirs[...]
    pieces = (p_own, p_y, p_core, p_both)
    rows = p_own.shape[0]
    packed_width = p_own.shape[1] - QUERY_WIDTH
    for bits, piece in zip((0, 2, 1, 3), pieces):
        w_out[span(shard ^ bits, rows), :] = piece[:, packed_width:]
    w_out_t[...] = flip(w_out[...])
    gain2 = gains[:, 1:2]
    for first in range(0, sequence, WIDE_TILE):
        at = slice(first, first + WIDE_TILE)
        mid = x_seq[:, at].astype(F32) + mm(w_out_t[...], attended_t[:, at])
        middle[:, at] = mid
        out_sum[:, at] = mid
        grad_sum[:, at] = jnp.zeros_like(mid)
        scale = column_scale(mid)
        scales[:, at] = jnp.broadcast_to(scale, (8, WIDE_TILE))
        normed[:, at] = (mid * scale * gain2).astype(BF16)
    chunk_step(place, pieces, normed, dy, out_sum, grad_sum, keep, send, scratch)


def next_chunk_kernel(
    place, normed, dy, out_in, grad_in, p_own, p_y, p_core, p_both, out_sum, grad_sum, keep, send, *scratch
):
    out_sum[...] = out_in[...]
    grad_sum[...] = grad_in[...]
    pieces = (p_own, p_y, p_core, p_both)
    chunk_step(place, pieces, normed, dy, out_sum, grad_sum, keep, send, scratch)


def last_chunk_kernel(
    place,
    normed,
    dy,
    out_in,
    grad_in,
    p_own,
    p_y,
    p_core,
    p_both,
    attended_t,
    gains,
    middle,
    scales,
    w_out,
    out_keep,
    out_send,
    middle_grad,
    attended_grad_t,
    keep,
    send,
    out_sum,
    branch_grad,
    *scratch,
):
    me, shard = place[0], place[1]
    half_rows = out_keep.shape[1]
    sequence = 2 * half_rows
    grad_sum = middle_grad
    out_sum[...] = out_in[...]
    grad_sum[...] = grad_in[...]
    pieces = (p_own, p_y, p_core, p_both)
    chunk_step(place, pieces, normed, dy, out_sum, grad_sum, keep, send, scratch)
    gain2 = gains[:, 1:2]
    for first in range(0, sequence, WIDE_TILE):
        at = slice(first, first + WIDE_TILE)
        output = out_sum[:, at].astype(BF16)
        block, start = divmod(first, half_rows)
        block_cols = slice(start, start + WIDE_TILE)

        @pl.when(me == block)
        def _():
            out_keep[:, block_cols] = output

        @pl.when(me != block)
        def _():
            out_send[:, block_cols] = output

        mid = middle[:, at]
        scale = scales[0:1, at]
        scaled = grad_sum[:, at] * gain2
        back = (
            dy[:, at].astype(F32)
            + scale * scaled
            - mid * (scale * scale * scale) * jnp.mean(scaled * mid, axis=0, keepdims=True)
        )
        middle_grad[:, at] = back
        branch = back.astype(BF16)
        branch_grad[:, at] = branch
        attended_grad_t[:, at] = mm(w_out[...], branch).astype(BF16)
    total = scratch[-1]
    half = p_own.shape[0] // 2
    columns = QUERY_WIDTH // 2
    first_to = keep.shape[4] - columns
    for start in range(0, QUERY_WIDTH, TILE):
        count = min(TILE, QUERY_WIDTH - start)
        total[:, :count] = mm_nt(attended_t[...], branch_grad[start : start + count, :])
        for target, y_bit, x_bit, owner, side in places(shard, place[3], keep, send):
            at = span(owner * 2 + side, half)
            for z_half in range(2):
                low = max(start, z_half * columns)
                high = min(start + count, (z_half + 1) * columns)
                if low < high:
                    to = first_to + low - z_half * columns
                    target[y_bit, x_bit, place[2] ^ z_half, :, to : to + high - low] = total[
                        at, low - start : high - start
                    ].astype(BF16)


def attend_back_kernel(
    queries_t,
    keys_t,
    values_t,
    log_total,
    attended_t,
    grad_t,
    cosine,
    sine,
    dq_out,
    dk_out,
    dv_out,
    keys,
    values,
    dk,
    dv,
):
    sequence = keys_t.shape[1]
    keys[...] = flip(keys_t[...])
    values[...] = flip(values_t[...])
    dk[...] = jnp.zeros_like(dk)
    dv[...] = jnp.zeros_like(dv)

    def back(a, b, cos, sin):
        return (a * cos + b * sin).astype(BF16), (b * cos - a * sin).astype(BF16)

    for tile in range(sequence // TILE):
        extent = (tile + 1) * TILE
        cols = slice(tile * TILE, extent)
        heads = [slice(r * HEAD_SIZE, (r + 1) * HEAD_SIZE) for r in range(REPEAT)]
        q_t = jnp.concatenate([queries_t[head, cols] for head in heads], 1)
        do_t = jnp.concatenate([grad_t[head, cols] for head in heads], 1)
        mixed = jnp.concatenate([attended_t[head, cols] for head in heads], 1)
        logs = jnp.concatenate([log_total[0, r : r + 1, cols] for r in range(REPEAT)], 1)
        delta = jnp.sum(do_t.astype(F32) * mixed.astype(F32), axis=0, keepdims=True)
        scores = causal_last(mm(keys[:extent, :], q_t), tile)
        probs = jnp.exp(scores - logs)
        dprob = mm(values[:extent, :], do_t)
        score_grad = (probs * (dprob - delta)).astype(BF16)
        dv[:extent, :] += mm(probs.astype(BF16), flip(do_t))
        dk[:extent, :] += mm(score_grad, flip(q_t))
        dq = mm(keys_t[:, :extent], score_grad) * 0.125
        cos, sin = cosine[:, cols], sine[:, cols]
        for r, head in enumerate(heads):
            own = slice(r * TILE, (r + 1) * TILE)
            a, b = back(dq[:HALF, own], dq[HALF:, own], cos, sin)
            dq_out[head.start : head.start + HALF, cols] = a
            dq_out[head.start + HALF : head.stop, cols] = b
    turned = dk[...].T
    a, b = back(turned[:HALF, :], turned[HALF:, :], cosine[...], sine[...])
    dk_out[:HALF, :] = a
    dk_out[HALF:, :] = b
    dv_out[...] = dv[...].T.astype(BF16)


def joined_kernel(place, normed, *rest):
    heads = rest[: 3 * KEY_VALUE_HEADS]
    keep_w, send_w, joined, total = rest[3 * KEY_VALUE_HEADS :]
    me, shard = place[0], place[1]
    group_width = REPEAT * HEAD_SIZE
    for group in range(KEY_VALUE_HEADS):
        dq, dk, dv = heads[3 * group : 3 * group + 3]
        joined[group * group_width : (group + 1) * group_width, :] = dq[...]
        at = QUERY_WIDTH + group * HEAD_SIZE
        joined[at : at + HEAD_SIZE, :] = dk[...]
        at = QUERY_WIDTH + KEY_WIDTH + group * HEAD_SIZE
        joined[at : at + HEAD_SIZE, :] = dv[...]
    half = keep_w.shape[2]
    for first in range(0, USED, 512):
        cols = slice(first, min(first + 512, USED))
        total[:, cols] = mm_nt(normed[...], joined[cols, :])
    for target, y_bit, x_bit, owner, side in places(shard, me, keep_w, send_w):
        target[y_bit, x_bit] = total[span(owner * 2 + side, half), :].astype(BF16)


def input_kernel(
    place, x_seq, packed, gains, middle_grad, joined, keep_x, send_x, grad_seq
):
    me = place[0]
    half_rows = keep_x.shape[1]
    sequence = 2 * half_rows
    gain1 = gains[:, :1]
    for first in range(0, sequence, WIDE_TILE):
        at = slice(first, first + WIDE_TILE)
        scaled = mm(packed[:, :USED], joined[:, at]) * gain1
        x = x_seq[:, at].astype(F32)
        scale = column_scale(x)
        grad_seq[:, at] = (
            middle_grad[:, at]
            + scale * scaled
            - x * (scale * scale * scale) * jnp.mean(scaled * x, axis=0, keepdims=True)
        )
    keep_x[...] = grad_seq[:, span(me, half_rows)]
    send_x[...] = grad_seq[:, span(1 - me, half_rows)].astype(BF16)


def pack_input_kernel(place, w_query, w_key, w_value, gains, packed):
    rows = w_query.shape[0]
    packed[:rows, :QUERY_WIDTH] = w_query[...]
    packed[:rows, QUERY_WIDTH : QUERY_WIDTH + KEY_WIDTH] = w_key[...]
    packed[:rows, QUERY_WIDTH + KEY_WIDTH :] = jnp.concatenate(
        [w_value[...].astype(F32), jnp.zeros((rows, PACKED - USED), F32)], 1
    ).astype(BF16)
    packed[rows:, :] = jnp.zeros((GAIN_ROWS, PACKED), BF16)
    packed[rows:, :TILE] = gains[...]


def pack_kernel(place, w_gate, w_up, w_down_t, w_out, *chunks):
    rows = w_gate.shape[0]
    down_rows = w_down_t.shape[1]
    part = 128
    for index, chunk in enumerate(chunks):
        at = index * part
        for i in range(4):
            source = slice(i * down_rows + at, i * down_rows + at + part)
            chunk[:, i * part : (i + 1) * part] = w_gate[:, source]
            chunk[:, (4 + i) * part : (5 + i) * part] = w_up[:, source]
            chunk[:, (8 + i) * part : (9 + i) * part] = w_down_t[
                i * rows : (i + 1) * rows, at : at + part
            ]
    chunks[0][:, 12 * part :] = w_out[...]


def combine_kernel(kinds, place, *refs):
    sources, targets = refs[: 2 * len(kinds)], list(refs[2 * len(kinds) :])
    for kind, a, b in zip(kinds, sources[::2], sources[1::2]):
        if kind in ("order", "line_order"):
            target = targets.pop(0)
            at = place[2] if kind == "order" else place[4]
            target[at] = a[...]
            target[1 - at] = b[...]
        elif kind == "pair":
            for i in range(2):
                targets.pop(0)[...] = (a[i].astype(F32) + b[i].astype(F32)).astype(BF16)
        else:
            targets.pop(0)[...] = (a[...].astype(F32) + b[...].astype(F32)).astype(BF16)


def halves_kernel(place, keep, got, target):
    target[place[0]] = keep[...]
    target[1 - place[0]] = got[...].astype(target.dtype)


def gain_row(products, gain):
    column = jnp.sum(products, axis=1, keepdims=True)
    row = jnp.broadcast_to(column, (column.shape[0], 128)).T[:1, :]
    return row / gain.astype(F32)


def unpack_kernel(place, own0, other0, own1, other1, own2, other2, w_gate, w_up, gain, *out):
    gate_out, up_out, down_out, out_out, gain_out = out
    me = place[0]
    half = own0.shape[1]
    rows = 2 * half
    part = 128
    down_rows = down_out.shape[1]
    bit = place[2]
    last = (own2, other2)
    for index, sources in enumerate(((own0, own1, own2), (other0, other1, other2))):
        for chunk, source in enumerate(sources):
            side = index ^ (bit if chunk == 0 else me)
            at = span(side, half)
            for i in range(4):
                to = slice(i * down_rows + chunk * part, i * down_rows + (chunk + 1) * part)
                gate_out[at, to] = source[0, :, i * part : (i + 1) * part].astype(F32)
                z_half, first = (0, (4 + i) * part) if i < 2 else (1, (i - 2) * part)
                up_out[at, to] = source[z_half, :, first : first + part].astype(F32)
                down_at = pl.ds(pl.multiple_of(i * rows + side * half, 8), half)
                first = (2 + i) * part
                down_out[down_at, chunk * part : (chunk + 1) * part] = source[
                    1, :, first : first + part
                ].astype(F32)
        first = 6 * part
        out_out[span(index ^ me, half), :] = jnp.concatenate(
            [last[index][0, :, first:].astype(F32), last[index][1, :, first:].astype(F32)], 1
        )
    products = gate_out[...] * w_gate[...].astype(F32) + up_out[...] * w_up[...].astype(F32)
    gain_out[...] = gain_row(products, gain[...])


def unpack_input_kernel(
    place, own, other, w_query, w_key, w_value, gain, query_out, key_out, value_out, gain_out
):
    me = place[0]
    half = own.shape[0]
    key_at = QUERY_WIDTH + KEY_WIDTH
    for side, source in ((me, own), (1 - me, other)):
        at = span(side, half)
        wide = source[...].astype(F32)
        query_out[at, :] = wide[:, :QUERY_WIDTH]
        key_out[at, :] = wide[:, QUERY_WIDTH:key_at]
        value_out[at, :] = wide[:, key_at:]
    products = jnp.sum(query_out[...] * w_query[...].astype(F32), axis=1, keepdims=True)
    products += jnp.sum(key_out[...] * w_key[...].astype(F32), axis=1, keepdims=True)
    products += jnp.sum(value_out[...] * w_value[...].astype(F32), axis=1, keepdims=True)
    gain_out[...] = gain_row(products, gain[...])


def call(kernel, out, scratch, flops, exps, args, name, limit, aliases=None):
    shapes = [jax.ShapeDtypeStruct(s, d) for s, d in out]
    moved = sum(a.size * a.dtype.itemsize for a in args[1:]) + sum(
        s.size * s.dtype.itemsize for s in shapes
    )
    in_specs = [pl.BlockSpec(memory_space=pltpu.SMEM)] + [
        pl.BlockSpec(memory_space=pltpu.VMEM)
    ] * (len(args) - 1)
    return pl.pallas_call(
        kernel,
        out_shape=shapes,
        in_specs=in_specs,
        out_specs=[pl.BlockSpec(memory_space=pltpu.VMEM)] * len(shapes),
        scratch_shapes=[pltpu.VMEM(s, d) for s, d in scratch],
        input_output_aliases=aliases or {},
        compiler_params=pltpu.CompilerParams(vmem_limit_bytes=limit * MEBI),
        cost_estimate=pl.CostEstimate(flops=flops, bytes_accessed=moved, transcendentals=exps),
        name=name,
    )(*args)


def attend_back(group, qkv_t, log_total, attended_t, grad_t, cosine, sine):
    sequence = qkv_t.shape[1]
    group_width = REPEAT * HEAD_SIZE

    def rows_of(size, index):
        return pl.BlockSpec((size, sequence), lambda step: (index, 0))

    flops = 5 * REPEAT * sequence * sequence * HEAD_SIZE * 2
    return pl.pallas_call(
        attend_back_kernel,
        grid=(1,),
        out_shape=[
            jax.ShapeDtypeStruct((group_width, sequence), BF16),
            jax.ShapeDtypeStruct((HEAD_SIZE, sequence), BF16),
            jax.ShapeDtypeStruct((HEAD_SIZE, sequence), BF16),
        ],
        in_specs=[
            rows_of(group_width, group),
            rows_of(HEAD_SIZE, QUERY_HEADS + group),
            rows_of(HEAD_SIZE, ROTATED + group),
            pl.BlockSpec((1, 8, sequence), lambda step: (group, 0, 0)),
            rows_of(group_width, group),
            rows_of(group_width, group),
            rows_of(HALF, 0),
            rows_of(HALF, 0),
        ],
        out_specs=[rows_of(group_width, 0), rows_of(HEAD_SIZE, 0), rows_of(HEAD_SIZE, 0)],
        scratch_shapes=[
            pltpu.VMEM((sequence, HEAD_SIZE), BF16),
            pltpu.VMEM((sequence, HEAD_SIZE), BF16),
            pltpu.VMEM((sequence, HEAD_SIZE), F32),
            pltpu.VMEM((sequence, HEAD_SIZE), F32),
        ],
        compiler_params=pltpu.CompilerParams(vmem_limit_bytes=16 * MEBI),
        cost_estimate=pl.CostEstimate(
            flops=flops, bytes_accessed=4_000_000, transcendentals=REPEAT * sequence * sequence
        ),
        name="attend_back",
    )(qkv_t, qkv_t, qkv_t, log_total, attended_t, grad_t, cosine, sine)


def across(tensor, bit):
    return lax.ppermute(tensor, "fsdp", [(i, i ^ bit) for i in range(4)])


def over_context(tensor):
    return lax.ppermute(tensor, "ctx", [(0, 1), (1, 0)])


def after(tensor, *done):
    return lax.optimization_barrier((tensor, *done))[0]


def together(*values):
    return lax.optimization_barrier(values)


def along(tensor, bit):
    size = lax.axis_size("dp")
    return lax.ppermute(tensor, "dp", [(i, i ^ bit) for i in range(size)])


def whole_sequences(
    tokens, norm1_gain, w_query, w_key, w_value, w_out, norm2_gain, w_gate, w_up, w_down, out_grad
):
    half_rows, width = tokens.shape[1:]
    sequence = 2 * half_rows
    rows = w_query.shape[0]
    down_rows = w_down.shape[0]
    hidden_width = w_gate.shape[1]
    part = 128
    me = lax.axis_index("ctx")
    line = lax.axis_index("dp")
    shard = lax.axis_index("fsdp")
    place = jnp.stack([me, shard, line & 1, me, line >> 1]).astype(jnp.int32)
    line_place = jnp.stack([me, shard, line >> 1, line & 1]).astype(jnp.int32)
    tokens = jnp.swapaxes(tokens, 1, 2)
    out_grad = jnp.swapaxes(out_grad, 1, 2)

    tokens_send = lax.dynamic_index_in_dim(tokens, 1 - me, 0, False)
    tokens_theirs = over_context(tokens_send)
    gain_rows = jnp.stack(together(norm1_gain, norm2_gain, tokens_send)[:2])
    gains_own = jnp.pad(gain_rows, ((0, GAIN_ROWS - 2), (0, TILE - rows)))
    (packed,) = call(
        pack_input_kernel,
        [((rows + GAIN_ROWS, PACKED), BF16)],
        [],
        0,
        0,
        (place, w_query, w_key, w_value, gains_own),
        "pack_input",
        16,
    )
    packed_y = across(packed, 2)
    packed_core = across(packed, 1)
    dy_theirs = over_context(lax.dynamic_index_in_dim(out_grad, 1 - me, 0, False))
    chunks = call(
        pack_kernel,
        [((rows, 12 * part + (0 if index else QUERY_WIDTH)), BF16) for index in range(3)],
        [],
        0,
        0,
        (place, w_gate, w_up, w_down.T, after(w_out, packed)),
        "pack",
        16,
    )
    cosine, sine = rope_tables(jnp.arange(sequence, dtype=jnp.int32), HEAD_SIZE)
    *chunks, _, cosine, sine, place, line_place = together(
        *chunks, packed, cosine.T, sine.T, place, line_place
    )
    packed_y, tokens_theirs = together(packed_y, tokens_theirs)
    packed_both = across(packed_y, 1)
    chunks_y = [across(chunk, 2) for chunk in chunks]
    chunks_core = [across(chunk, 1) for chunk in chunks]

    pairs = sequence * sequence
    x_seq, normed, packed_all, gains, qkv_t, log_total, attended_t = call(
        attend_kernel,
        [
            ((width, sequence), BF16),
            ((width, sequence), BF16),
            ((width, PACKED), BF16),
            ((width, 128), F32),
            ((USED, sequence), BF16),
            ((KEY_VALUE_HEADS, 8, sequence), F32),
            ((QUERY_WIDTH, sequence), BF16),
        ],
        [((PACKED, width), BF16), ((KEY_VALUE_HEADS, sequence, HEAD_SIZE), BF16)],
        2 * sequence * width * PACKED + 4 * QUERY_WIDTH * pairs,
        QUERY_HEADS * pairs,
        (place, tokens, tokens_theirs, packed, packed_y, packed_core, packed_both, cosine, sine),
        "attend",
        20,
    )

    natural, turned = ((width, 4 * part), BF16), ((4 * part, width), BF16)
    row, wide_row = ((width, sequence), BF16), ((4 * part, sequence), BF16)
    row_sum = ((width, sequence), F32)
    share = ((2, 2, 2, rows // 2, 6 * part), BF16)
    last_share = ((2, 2, 2, rows // 2, 6 * part + QUERY_WIDTH // 2), BF16)
    chunk_scratch = [
        natural,
        natural,
        natural,
        turned,
        turned,
        turned,
        wide_row,
        wide_row,
        wide_row,
        ((width, 4 * part), F32),
    ]
    flops = 2 * sequence * width * 9 * 4 * part
    exps = sequence * 4 * part

    first_y, second_y, third_y = chunks_y
    first_y, second_y, attended_t, dy_theirs = together(first_y, second_y, attended_t, dy_theirs)
    pieces = (chunks[0], first_y, chunks_core[0], across(first_y, 1))
    second_both = across(second_y, 1)
    middle, normed2, scales, dy, w_out_all, out_sum, grad_sum, keep0, send0 = call(
        first_chunk_kernel,
        [
            row_sum,
            row,
            ((8, sequence), F32),
            row,
            ((QUERY_WIDTH, width), BF16),
            row_sum,
            row_sum,
            share,
            share,
        ],
        [((width, QUERY_WIDTH), BF16), *chunk_scratch],
        flops + 2 * sequence * width * QUERY_WIDTH,
        exps,
        (line_place, x_seq, attended_t, out_grad, dy_theirs, gains, *pieces),
        "first_chunk",
        26,
    )

    def combine(*items):
        kinds = tuple(item[0] for item in items)
        args = [tensor for item in items for tensor in item[1:]]
        out = []
        for kind, tensor, _ in items:
            if kind in ("order", "line_order"):
                out.append(((2, *tensor.shape), BF16))
            elif kind == "pair":
                out += [(tensor.shape[1:], BF16)] * 2
            else:
                out.append((tensor.shape, BF16))
        kernel = functools.partial(combine_kernel, kinds)
        return call(kernel, out, [], 0, 0, (place, *args), "combine", 16)

    out_sum, send0, third_y, second_both = together(out_sum, send0, third_y, second_both)
    got0 = across(send0, 1)
    pieces = (chunks[1], second_y, chunks_core[1], second_both)
    third_both = across(third_y, 1)
    out_sum, grad_sum, keep1, send1 = call(
        next_chunk_kernel,
        [row_sum, row_sum, share, share],
        chunk_scratch,
        flops,
        exps,
        (place, normed2, dy, out_sum, grad_sum, *pieces),
        "next_chunk",
        20,
        {3: 0, 4: 1},
    )

    got0, out_sum, send1, third_both = together(got0, out_sum, send1, third_both)
    own0, part0 = combine(("pair", keep0, got0))
    part0, send1, out_sum = together(part0, send1, out_sum)
    got0, got1 = across(part0, 2), across(send1, 1)
    pieces = (chunks[2], third_y, chunks_core[2], third_both)
    out_keep, out_send, middle_grad, grad_t, keep2, send2 = call(
        last_chunk_kernel,
        [
            ((width, half_rows), BF16),
            ((width, half_rows), BF16),
            row_sum,
            ((QUERY_WIDTH, sequence), BF16),
            last_share,
            last_share,
        ],
        [row_sum, row, *chunk_scratch],
        flops + 4 * sequence * width * QUERY_WIDTH,
        exps,
        (
            place,
            normed2,
            dy,
            out_sum,
            grad_sum,
            *pieces,
            attended_t,
            gains,
            middle,
            scales,
            w_out_all,
        ),
        "last_chunk",
        24,
    )

    got0, got1, grad_t, send2, out_send = together(got0, got1, grad_t, send2, out_send)
    own0, part0, own1, part1 = combine(("pair", own0, got0), ("pair", keep1, got1))
    part0, part1, grad_t = together(part0, part1, grad_t)
    def place_halves(keep, got, name):
        (both,) = call(
            halves_kernel, [((2, *keep.shape), keep.dtype)], [], 0, 0, (place, keep, got), name, 16
        )
        return jnp.swapaxes(both, 1, 2)

    got0, got1, got2 = along(part0, 1), across(part1, 2), across(send2, 1)
    out_theirs = over_context(out_send)

    back_args = (log_total, attended_t, grad_t, cosine, sine)
    grads0 = attend_back(0, qkv_t, *back_args)
    got2, *grads0 = together(got2, *grads0)
    own2, part2 = combine(("pair", keep2, got2))
    part2, qkv_t = together(part2, qkv_t)

    got2 = across(part2, 2)
    grads1 = attend_back(1, qkv_t, *back_args)
    got0, got1, *grads1 = together(got0, got1, *grads1)
    own0, part0, own1, part1 = combine(("pair", own0, got0), ("pair", own1, got1))
    part0, part1, qkv_t = together(part0, part1, qkv_t)

    got0, got1 = along(part0, 2), over_context(part1)
    grads2 = attend_back(2, qkv_t, *back_args)
    got0, out_theirs, *grads2 = together(got0, out_theirs, *grads2)
    (own0,) = combine(("one", own0, got0))
    own0, *grads2 = together(own0, *grads2)

    got0 = over_context(own0)
    keep_w, send_w, joined = call(
        joined_kernel,
        [
            ((2, 2, rows // 2, USED), BF16),
            ((2, 2, rows // 2, USED), BF16),
            ((USED, sequence), BF16),
        ],
        [((width, USED), F32)],
        2 * sequence * width * USED,
        0,
        (place, normed, *grads0, *grads1, *grads2),
        "joined",
        16,
    )
    got0, got1, got2, send_w, joined = together(got0, got1, got2, send_w, joined)
    got_w = across(send_w, 1)
    own0, own1, part1, own2, part2 = combine(
        ("one", own0, got0), ("pair", own1, got1), ("pair", own2, got2)
    )
    own0, part1, part2, joined = together(own0, part1, part2, joined)

    got0, got1, got2 = along(own0, 2), along(part1, 1), over_context(part2)
    keep_x, send_x = call(
        input_kernel,
        [((width, half_rows), F32), ((width, half_rows), BF16)],
        [((width, sequence), F32)],
        2 * sequence * width * USED,
        sequence,
        (place, x_seq, packed_all, gains, middle_grad, joined),
        "input_side",
        24,
    )
    got_w, got1, send_x = together(got_w, got1, send_x)
    own_w, part_w, own1 = combine(("pair", keep_w, got_w), ("one", own1, got1))
    part_w, own1, send_x = together(part_w, own1, send_x)
    got_w, got1, x_theirs = across(part_w, 2), along(own1, 2), over_context(send_x)
    output = place_halves(out_keep, out_theirs, "output_halves")

    got0, got2, output = together(got0, got2, output)
    own0, own2, part2 = combine(("line_order", own0, got0), ("pair", own2, got2))
    own0, part2 = together(own0, part2)
    other0, got2 = along(own0, 1), along(part2, 1)

    got_w, got1, got2 = together(got_w, got1, got2)
    own_w, part_w, own1, own2 = combine(
        ("pair", own_w, got_w), ("one", own1, got1), ("one", own2, got2)
    )
    part_w, own1, own2 = together(part_w, own1, own2)

    got_w, got1, got2 = over_context(part_w), along(own1, 1), along(own2, 2)
    got_w, got1, got2, x_theirs, other0 = together(got_w, got1, got2, x_theirs, other0)
    own_w, own1, own2 = combine(("one", own_w, got_w), ("order", own1, got1), ("one", own2, got2))
    own_w, own1, own2, x_theirs = together(own_w, own1, own2, x_theirs)

    got_w, other1, got2 = along(own_w, 1), over_context(own1), along(own2, 1)
    gradient = place_halves(keep_x, x_theirs, "gradient_halves")
    got_w, got2, other1, gradient = together(got_w, got2, other1, gradient)
    own_w, own2 = combine(("one", own_w, got_w), ("order", own2, got2))
    own_w, own2 = together(own_w, own2)

    got_w, other2 = along(own_w, 2), over_context(own2)
    (own_w,) = combine(("one", own_w, got_w))
    own_w, other2 = together(own_w, other2)
    other_w = over_context(own_w)

    gate_sum, up_sum, down_sum, out_sum, gain2_sum = call(
        unpack_kernel,
        [
            ((rows, hidden_width), F32),
            ((rows, hidden_width), F32),
            ((width, down_rows), F32),
            ((rows, width), F32),
            ((1, rows), F32),
        ],
        [],
        0,
        0,
        (place, own0, other0, own1, other1, own2, other2, w_gate, w_up, norm2_gain[None, :]),
        "unpack",
        24,
    )
    gate_sum, other_w = together(gate_sum, other_w)
    query_sum, key_sum, value_sum, gain1_sum = call(
        unpack_input_kernel,
        [
            ((rows, QUERY_WIDTH), F32),
            ((rows, KEY_WIDTH), F32),
            ((rows, KEY_WIDTH), F32),
            ((1, rows), F32),
        ],
        [],
        0,
        0,
        (place, own_w, other_w, w_query, w_key, w_value, norm1_gain[None, :]),
        "unpack_input",
        16,
    )
    return (
        output,
        gradient,
        gain1_sum[0],
        query_sum,
        key_sum,
        value_sum,
        out_sum,
        gain2_sum[0],
        gate_sum,
        up_sum,
        down_sum.T,
    )


def layer_step(tokens, *rest):
    whole = (
        lax.axis_size("ctx") == 2
        and lax.axis_size("fsdp") == 4
        and lax.axis_size("dp") == 4
        and tokens.shape[0] == 2
        and tokens.shape[1] % WIDE_TILE == 0
        and rest[8].shape == (384, 576)
    )
    return (whole_sequences if whole else split_context)(tokens, *rest)


def solution(mesh):
    return jax.shard_map(
        layer_step,
        mesh=mesh,
        in_specs=(
            P(("dp", "fsdp"), "ctx", None),
            P("fsdp"),
            P("fsdp", None),
            P("fsdp", None),
            P("fsdp", None),
            P("fsdp", None),
            P("fsdp"),
            P("fsdp", None),
            P("fsdp", None),
            P("fsdp", None),
            P(("dp", "fsdp"), "ctx", None),
        ),
        out_specs=(
            P(("dp", "fsdp"), "ctx", None),
            P(("dp", "fsdp"), "ctx", None),
            P("fsdp"),
            P("fsdp", None),
            P("fsdp", None),
            P("fsdp", None),
            P("fsdp", None),
            P("fsdp"),
            P("fsdp", None),
            P("fsdp", None),
            P("fsdp", None),
        ),
        check_vma=False,
    )
```

```python
import functools
import math

import jax
import jax.numpy as jnp
from jax import lax
from jax.experimental import pallas as pl
from jax.experimental.pallas import tpu as pltpu
from jax.sharding import PartitionSpec as P

QUERY_HEADS = 9
KEY_VALUE_HEADS = 3
HEAD_SIZE = 64


EPSILON = 1e-05
ROPE_THETA = 100000.0
MASKED = -1e30


def rope_tables(positions, head_width):
    half_size = head_width // 2
    inverse = jnp.exp(
        jnp.arange(half_size, dtype=jnp.float32) * (-2.0 * math.log(ROPE_THETA) / head_width)
    )
    angle = positions.astype(jnp.float32)[:, None] * inverse[None, :]
    return (jnp.cos(angle), jnp.sin(angle))


def rotary_apply(tensor, cosine_table, sine_table):
    half_size = tensor.shape[-1] // 2
    first_half = tensor[..., :half_size]
    second_half = tensor[..., half_size:]
    cosine_table = cosine_table[None, :, None, :]
    sine_table = sine_table[None, :, None, :]
    return jnp.concatenate(
        [
            first_half * cosine_table - second_half * sine_table,
            second_half * cosine_table + first_half * sine_table,
        ],
        -1,
    )


def rotate_back(tensor, cosine_table, sine_table):
    half_size = tensor.shape[-1] // 2
    first_half = tensor[..., :half_size]
    second_half = tensor[..., half_size:]
    cosine_table = cosine_table[None, :, None, :]
    sine_table = sine_table[None, :, None, :]
    return jnp.concatenate(
        [
            first_half * cosine_table + second_half * sine_table,
            second_half * cosine_table - first_half * sine_table,
        ],
        -1,
    )


def rms_scale(tensor):
    return lax.rsqrt(jnp.mean(tensor * tensor, axis=-1, keepdims=True) + EPSILON)


def block_scores(query_block, key_block, query_pos, key_pos):
    scores = (
        jnp.einsum("gqhrd,gkhd->ghrqk", query_block, key_block, preferred_element_type=jnp.float32)
        * 0.125
    )
    visible = key_pos[None, :] <= query_pos[:, None]
    return jnp.where(visible, scores, MASKED)


def split_context(
    tokens, norm1_gain, w_query, w_key, w_value, w_out, norm2_gain, w_gate, w_up, w_down, out_grad
):
    gain1, wq_full, wk_full, wv_full, wo_full, gain2, wg_full, wu_full, wd_full = (
        lax.all_gather(norm1_gain, "fsdp", axis=0, tiled=True),
        lax.all_gather(w_query, "fsdp", axis=0, tiled=True),
        lax.all_gather(w_key, "fsdp", axis=0, tiled=True),
        lax.all_gather(w_value, "fsdp", axis=0, tiled=True),
        lax.all_gather(w_out, "fsdp", axis=0, tiled=True),
        lax.all_gather(norm2_gain, "fsdp", axis=0, tiled=True),
        lax.all_gather(w_gate, "fsdp", axis=0, tiled=True),
        lax.all_gather(w_up, "fsdp", axis=0, tiled=True),
        lax.all_gather(w_down, "fsdp", axis=0, tiled=True),
    )
    query_group_count, local_row_count, model_width = tokens.shape
    repeat_heads = QUERY_HEADS // KEY_VALUE_HEADS
    head_width = HEAD_SIZE
    key_value_width = KEY_VALUE_HEADS * HEAD_SIZE
    query_width = QUERY_HEADS * HEAD_SIZE
    first_row = lax.axis_index("ctx") * local_row_count
    last_row = first_row + local_row_count - 1
    positions = first_row + jnp.arange(local_row_count, dtype=jnp.int32)
    cosine_table, sine_table = rope_tables(positions, head_width)
    gain1f = gain1.astype(jnp.float32)
    gain2f = gain2.astype(jnp.float32)
    inputs = tokens.astype(jnp.float32)
    scale1 = rms_scale(inputs)
    normed1 = (inputs * scale1 * gain1f).astype(jnp.bfloat16)
    query_before_rotation = jnp.einsum(
        "gsd,de->gse", normed1, wq_full, preferred_element_type=jnp.float32
    )
    key_before_rotation = jnp.einsum(
        "gsd,de->gse", normed1, wk_full, preferred_element_type=jnp.float32
    )
    value_projected = jnp.einsum(
        "gsd,de->gse", normed1, wv_full, preferred_element_type=jnp.float32
    )
    query_matrix = rotary_apply(
        query_before_rotation.reshape(query_group_count, local_row_count, QUERY_HEADS, head_width),
        cosine_table,
        sine_table,
    ).astype(jnp.bfloat16)
    query_matrix = query_matrix.reshape(
        query_group_count, local_row_count, KEY_VALUE_HEADS, repeat_heads, head_width
    )
    key_local = rotary_apply(
        key_before_rotation.reshape(
            query_group_count, local_row_count, KEY_VALUE_HEADS, head_width
        ),
        cosine_table,
        sine_table,
    ).astype(jnp.bfloat16)
    local_value_rows = value_projected.astype(jnp.bfloat16)
    collected_keys, collected_values = (
        lax.all_gather(
            key_local.reshape(query_group_count, local_row_count, key_value_width),
            "ctx",
            axis=1,
            tiled=True,
        ),
        lax.all_gather(local_value_rows, "ctx", axis=1, tiled=True),
    )
    sequence_length = collected_keys.shape[1]
    every_key_row = collected_keys.reshape(
        query_group_count, sequence_length, KEY_VALUE_HEADS, head_width
    )
    every_value_row = collected_values.reshape(
        query_group_count, sequence_length, KEY_VALUE_HEADS, head_width
    )
    local_value_rows = local_value_rows.reshape(
        query_group_count, local_row_count, KEY_VALUE_HEADS, head_width
    )
    key_span = min(sequence_length, 512)
    block_total = last_row // key_span + 1

    def key_slices(step_index):
        first_key = step_index * key_span
        key_block = lax.dynamic_slice_in_dim(every_key_row, first_key, key_span, 1)
        value_block = lax.dynamic_slice_in_dim(every_value_row, first_key, key_span, 1)
        key_pos = first_key + jnp.arange(key_span, dtype=jnp.int32)
        return (key_block, value_block, key_pos)

    def stats_step(step_index, running):
        row_max, row_sum = running
        key_block, value_block, key_pos = key_slices(step_index)
        scores = block_scores(query_matrix, key_block, positions, key_pos)
        new_max = jnp.maximum(row_max, jnp.max(scores, axis=-1))
        row_sum = row_sum * jnp.exp(row_max - new_max) + jnp.sum(
            jnp.exp(scores - new_max[..., None]), axis=-1
        )
        return (new_max, row_sum)

    statistics_shape = (query_group_count, KEY_VALUE_HEADS, repeat_heads, local_row_count)
    row_max, row_sum = lax.fori_loop(
        0,
        block_total,
        stats_step,
        (jnp.full(statistics_shape, MASKED, jnp.float32), jnp.zeros(statistics_shape, jnp.float32)),
    )
    log_total = row_max + jnp.log(row_sum)

    def mix_step(step_index, running):
        key_block, value_block, key_pos = key_slices(step_index)
        scores = block_scores(query_matrix, key_block, positions, key_pos)
        probs = jnp.exp(scores - log_total[..., None]).astype(jnp.bfloat16)
        return running + jnp.einsum(
            "ghrqk,gkhd->gqhrd", probs, value_block, preferred_element_type=jnp.float32
        )

    attended_full = lax.fori_loop(
        0,
        block_total,
        mix_step,
        jnp.zeros(
            (query_group_count, local_row_count, KEY_VALUE_HEADS, repeat_heads, head_width),
            jnp.float32,
        ),
    )
    attended = attended_full.astype(jnp.bfloat16).reshape(
        query_group_count, local_row_count, query_width
    )
    branch = jnp.einsum("gse,ed->gsd", attended, wo_full, preferred_element_type=jnp.float32)
    middle = inputs + branch
    scale2 = rms_scale(middle)
    normed2 = (middle * scale2 * gain2f).astype(jnp.bfloat16)
    gate_act = jnp.einsum("gsd,df->gsf", normed2, wg_full, preferred_element_type=jnp.float32)
    up_act = jnp.einsum("gsd,df->gsf", normed2, wu_full, preferred_element_type=jnp.float32)
    gate_sig = jax.nn.sigmoid(gate_act)
    gate_silu = gate_act * gate_sig
    hidden = (gate_silu * up_act).astype(jnp.bfloat16)
    mlp_out = jnp.einsum("gsf,fd->gsd", hidden, wd_full, preferred_element_type=jnp.float32)
    output = (middle + mlp_out).astype(jnp.bfloat16)
    out_float = out_grad.astype(jnp.float32)
    grad_down = jnp.einsum("gsf,gsd->fd", hidden, out_grad, preferred_element_type=jnp.float32)
    hidden_grad = jnp.einsum("gsd,fd->gsf", out_grad, wd_full, preferred_element_type=jnp.float32)
    gate_grad = (hidden_grad * up_act * gate_sig * (1.0 + gate_act * (1.0 - gate_sig))).astype(
        jnp.bfloat16
    )
    up_grad = (hidden_grad * gate_silu).astype(jnp.bfloat16)
    grad_gate = jnp.einsum("gsd,gsf->df", normed2, gate_grad, preferred_element_type=jnp.float32)
    grad_up = jnp.einsum("gsd,gsf->df", normed2, up_grad, preferred_element_type=jnp.float32)
    normed2_grad = jnp.einsum("gsf,df->gsd", gate_grad, wg_full, preferred_element_type=jnp.float32)
    normed2_grad = normed2_grad + jnp.einsum(
        "gsf,df->gsd", up_grad, wu_full, preferred_element_type=jnp.float32
    )
    grad_gain2 = jnp.sum(normed2_grad * middle * scale2, axis=(0, 1))
    scaled2 = gain2f * normed2_grad
    middle_grad = (
        out_float
        + scale2 * scaled2
        - middle * scale2**3 * jnp.mean(scaled2 * middle, axis=-1, keepdims=True)
    )
    branch_grad = middle_grad.astype(jnp.bfloat16)
    grad_out = jnp.einsum("gse,gsd->ed", attended, branch_grad, preferred_element_type=jnp.float32)
    attended_output_gradient = jnp.einsum(
        "gsd,ed->gse", branch_grad, wo_full, preferred_element_type=jnp.float32
    ).astype(jnp.bfloat16)
    attention_gradient = attended_output_gradient.reshape(
        query_group_count, local_row_count, KEY_VALUE_HEADS, repeat_heads, head_width
    )
    delta = jnp.sum(attention_gradient.astype(jnp.float32) * attended_full, axis=-1).transpose(
        0, 2, 3, 1
    )

    def query_grad_step(step_index, running):
        key_block, value_block, key_pos = key_slices(step_index)
        scores = block_scores(query_matrix, key_block, positions, key_pos)
        probs = jnp.exp(scores - log_total[..., None])
        dprob = jnp.einsum(
            "gqhrd,gkhd->ghrqk", attention_gradient, value_block, preferred_element_type=jnp.float32
        )
        score_grad = (probs * (dprob - delta[..., None])).astype(jnp.bfloat16)
        return running + jnp.einsum(
            "ghrqk,gkhd->gqhrd", score_grad, key_block, preferred_element_type=jnp.float32
        )

    query_grad = (
        lax.fori_loop(
            0,
            block_total,
            query_grad_step,
            jnp.zeros(
                (query_group_count, local_row_count, KEY_VALUE_HEADS, repeat_heads, head_width),
                jnp.float32,
            ),
        )
        * 0.125
    )
    row_total = local_row_count * lax.axis_size("ctx")
    term_span = math.gcd(row_total, key_span)

    def key_block_term(step_index):
        first_key = step_index * term_span
        key_block = lax.dynamic_slice_in_dim(every_key_row, first_key, term_span, 1)
        value_block = lax.dynamic_slice_in_dim(every_value_row, first_key, term_span, 1)
        key_pos = first_key + jnp.arange(term_span, dtype=jnp.int32)

        def compute_term(unused):
            scores = block_scores(query_matrix, key_block, positions, key_pos)
            probs = jnp.exp(scores - log_total[..., None])
            dprob = jnp.einsum(
                "gqhrd,gkhd->ghrqk",
                attention_gradient,
                value_block,
                preferred_element_type=jnp.float32,
            )
            score_grad = (probs * (dprob - delta[..., None])).astype(jnp.bfloat16)
            key_term = (
                jnp.einsum(
                    "ghrqk,gqhrd->kghd",
                    score_grad,
                    query_matrix,
                    preferred_element_type=jnp.float32,
                )
                * 0.125
            )
            value_term = jnp.einsum(
                "ghrqk,gqhrd->kghd",
                probs.astype(jnp.bfloat16),
                attention_gradient,
                preferred_element_type=jnp.float32,
            )
            return jnp.concatenate(
                [
                    key_term.reshape(term_span, query_group_count, key_value_width),
                    value_term.reshape(term_span, query_group_count, key_value_width),
                ],
                -1,
            )

        def empty_term(unused):
            return jnp.zeros((term_span, query_group_count, 2 * key_value_width), jnp.float32)

        return lax.cond(first_key <= last_row, compute_term, empty_term, 0)

    terms = lax.map(key_block_term, jnp.arange(row_total // term_span, dtype=jnp.int32))
    paired_gradients = (
        lax.psum_scatter(
            terms.reshape(row_total, query_group_count, 2 * key_value_width).astype(jnp.bfloat16),
            "ctx",
            scatter_dimension=0,
            tiled=True,
        )
        .astype(jnp.float32)
        .transpose(1, 0, 2)
    )
    key_gradient = paired_gradients[..., :key_value_width].reshape(
        query_group_count, local_row_count, KEY_VALUE_HEADS, head_width
    )
    value_gradient = paired_gradients[..., key_value_width:].reshape(
        query_group_count, local_row_count, KEY_VALUE_HEADS, head_width
    )
    query_pre_grad = rotate_back(
        query_grad.reshape(query_group_count, local_row_count, QUERY_HEADS, head_width),
        cosine_table,
        sine_table,
    )
    query_pre_grad = query_pre_grad.astype(jnp.bfloat16).reshape(
        query_group_count, local_row_count, query_width
    )
    key_pre_grad = (
        rotate_back(key_gradient, cosine_table, sine_table)
        .astype(jnp.bfloat16)
        .reshape(query_group_count, local_row_count, key_value_width)
    )
    value_pre_grad = value_gradient.astype(jnp.bfloat16).reshape(
        query_group_count, local_row_count, key_value_width
    )
    grad_query = jnp.einsum(
        "gsd,gse->de", normed1, query_pre_grad, preferred_element_type=jnp.float32
    )
    grad_key = jnp.einsum("gsd,gse->de", normed1, key_pre_grad, preferred_element_type=jnp.float32)
    grad_value = jnp.einsum(
        "gsd,gse->de", normed1, value_pre_grad, preferred_element_type=jnp.float32
    )
    normed1_grad = jnp.einsum(
        "gse,de->gsd", query_pre_grad, wq_full, preferred_element_type=jnp.float32
    )
    normed1_grad = normed1_grad + jnp.einsum(
        "gse,de->gsd", key_pre_grad, wk_full, preferred_element_type=jnp.float32
    )
    normed1_grad = normed1_grad + jnp.einsum(
        "gse,de->gsd", value_pre_grad, wv_full, preferred_element_type=jnp.float32
    )
    grad_gain1 = jnp.sum(normed1_grad * inputs * scale1, axis=(0, 1))
    scaled1 = gain1f * normed1_grad
    input_grad = (
        middle_grad
        + scale1 * scaled1
        - inputs * scale1**3 * jnp.mean(scaled1 * inputs, axis=-1, keepdims=True)
    )
    totals = lax.psum(
        (
            grad_gain1,
            grad_query,
            grad_key,
            grad_value,
            grad_out,
            grad_gain2,
            grad_gate,
            grad_up,
            grad_down,
        ),
        ("dp", "ctx", "fsdp"),
    )
    owner = lax.axis_index("fsdp")
    shards = (norm1_gain, w_query, w_key, w_value, w_out, norm2_gain, w_gate, w_up, w_down)
    shares = tuple(
        (
            lax.dynamic_slice_in_dim(summed, owner * shard.shape[0], shard.shape[0], 0)
            for summed, shard in zip(totals, shards)
        )
    )
    return (
        output,
        input_grad,
        shares[0],
        shares[1],
        shares[2],
        shares[3],
        shares[4],
        shares[5],
        shares[6],
        shares[7],
        shares[8],
    )


WIDTH = 576
QUERY_WIDTH = QUERY_HEADS * HEAD_SIZE
KEY_WIDTH = KEY_VALUE_HEADS * HEAD_SIZE
ROTATED = QUERY_HEADS + KEY_VALUE_HEADS
REPEAT = QUERY_HEADS // KEY_VALUE_HEADS
HALF = HEAD_SIZE // 2
USED = QUERY_WIDTH + 2 * KEY_WIDTH
PACKED = USED + 64
GAIN_ROWS = 16
TILE = 256
WIDE_TILE = 512
MEBI = 1024 * 1024
F32 = jnp.float32
BF16 = jnp.bfloat16


def mm(a, b):
    return jnp.dot(a, b, preferred_element_type=F32)


def mm_nt(a, b):
    return lax.dot_general(a, b, (((1,), (1,)), ((), ())), preferred_element_type=F32)


def flip(tensor):
    return tensor.astype(F32).T.astype(tensor.dtype)


def span(index, size, step=None):
    step = size if step is None else step
    return pl.ds(pl.multiple_of(index * step, step), size)


def flip_blocks(target, source, block):
    def one(step, carry):
        at = span(step, block)
        target[at, :] = flip(source[:, at])
        return carry

    lax.fori_loop(0, source.shape[1] // block, one, 0)


def column_scale(tensor):
    return lax.rsqrt(jnp.mean(tensor * tensor, axis=0, keepdims=True) + EPSILON)


def sigmoid(tensor):
    return 0.5 * jnp.tanh(0.5 * tensor) + 0.5


def causal_last(scores, tile):
    shape = (TILE, REPEAT * TILE)
    visible = lax.broadcasted_iota(jnp.int32, shape, 0) <= (
        lax.broadcasted_iota(jnp.int32, shape, 1) & (TILE - 1)
    )
    last = jnp.where(visible, scores[tile * TILE :, :], MASKED)
    return last if tile == 0 else jnp.concatenate([scores[: tile * TILE, :], last], 0)


def attend_kernel(
    place,
    tokens,
    theirs,
    w_own,
    w_y,
    w_core,
    w_both,
    cosine,
    sine,
    x_seq,
    normed,
    packed,
    gains,
    qkv_t,
    log_total,
    attended_t,
    packed_t,
    key_rows,
):
    me, shard = place[0], place[1]
    half_rows = theirs.shape[1]
    sequence = 2 * half_rows
    x_seq[:, span(me, half_rows)] = tokens[me]
    x_seq[:, span(1 - me, half_rows)] = theirs[...]
    rows = packed.shape[0] // 4
    for bits, piece in ((0, w_own), (2, w_y), (1, w_core), (3, w_both)):
        at = span(shard ^ bits, rows)
        packed[at, :] = piece[:rows, :]
        gains[at, :GAIN_ROWS] = piece[rows:, :TILE].astype(F32).T[:rows, :]
    flip_blocks(packed_t, packed, TILE)
    gain1 = gains[:, :1]

    def project(step, carry):
        at = span(step, WIDE_TILE)
        x = x_seq[:, at].astype(F32)
        normed_tile = (x * column_scale(x) * gain1).astype(BF16)
        normed[:, at] = normed_tile
        turned = mm(packed_t[:USED, :], normed_tile)
        cos, sin = cosine[:, at], sine[:, at]
        for head in range(ROTATED):
            a = turned[head * HEAD_SIZE : head * HEAD_SIZE + HALF, :]
            b = turned[head * HEAD_SIZE + HALF : (head + 1) * HEAD_SIZE, :]
            both = jnp.concatenate([a * cos - b * sin, b * cos + a * sin], 0)
            if head < QUERY_HEADS:
                both = both * 0.125
            else:
                key_rows[head - QUERY_HEADS, at, :] = both.T.astype(BF16)
            qkv_t[head * HEAD_SIZE : (head + 1) * HEAD_SIZE, at] = both.astype(BF16)
        qkv_t[ROTATED * HEAD_SIZE :, at] = turned[ROTATED * HEAD_SIZE :, :].astype(BF16)
        return carry

    lax.fori_loop(0, sequence // WIDE_TILE, project, 0)

    def one_group(group, carry):
        value_rows = span(ROTATED + group, HEAD_SIZE)
        for tile in range(sequence // TILE):
            extent = (tile + 1) * TILE
            cols = slice(tile * TILE, extent)
            queries = jnp.concatenate(
                [qkv_t[span(group * REPEAT + r, HEAD_SIZE), cols] for r in range(REPEAT)], 1
            )
            scores = causal_last(mm(key_rows[group, :extent, :], queries), tile)
            top = jnp.max(scores, axis=0, keepdims=True)
            weights = jnp.exp(scores - top)
            total = jnp.sum(weights, axis=0, keepdims=True)
            mixed = mm(qkv_t[value_rows, :extent], weights.astype(BF16))
            mixed = (mixed * (1.0 / total)).astype(BF16)
            logs = top + jnp.log(total)
            for r in range(REPEAT):
                own = slice(r * TILE, (r + 1) * TILE)
                attended_t[span(group * REPEAT + r, HEAD_SIZE), cols] = mixed[:, own]
                log_total[group, r : r + 1, cols] = logs[:, own]
        return carry

    lax.fori_loop(0, KEY_VALUE_HEADS, one_group, 0)


def places(shard, row_bit, keep, send):
    for y_bit in range(2):
        for x_bit in range(2):
            for core_bit, target in ((0, keep), (1, send)):
                yield target, y_bit, x_bit, shard ^ (2 * y_bit + core_bit), row_bit ^ x_bit


def chunk_step(place, pieces, normed, dy, out_sum, grad_sum, keep, send, scratch):
    w_gate, w_up, w_down_t, w_gate_t, w_up_t, w_down, hidden, gate_grad, up_grad, total = scratch
    row_bit, shard, level = place[3], place[1], place[2]
    rows = pieces[0].shape[0]
    wide = w_gate.shape[1]
    part = wide // 4
    sequence = normed.shape[1]
    for bits, piece in zip((0, 2, 1, 3), pieces):
        at = span(shard ^ bits, rows)
        w_gate[at, :] = piece[:, :wide]
        w_up[at, :] = piece[:, wide : 2 * wide]
        for block in range(4):
            first = 2 * wide + block * part
            w_down_t[block * rows : (block + 1) * rows, span(shard ^ bits, part)] = piece[
                :, first : first + part
            ]
    w_gate_t[...] = flip(w_gate[...])
    w_up_t[...] = flip(w_up[...])
    w_down[...] = flip(w_down_t[...])
    for first in range(0, sequence, WIDE_TILE):
        at = slice(first, first + WIDE_TILE)
        gate = mm(w_gate_t[...], normed[:, at])
        up = mm(w_up_t[...], normed[:, at])
        hidden_grad = mm(w_down[...], dy[:, at])
        sig = sigmoid(gate)
        silu = gate * sig
        hidden_tile = (silu * up).astype(BF16)
        gate_tile = (hidden_grad * up * (sig + silu * (1.0 - sig))).astype(BF16)
        up_tile = (hidden_grad * silu).astype(BF16)
        hidden[:, at] = hidden_tile
        gate_grad[:, at] = gate_tile
        up_grad[:, at] = up_tile
        out_sum[:, at] += mm(w_down_t[...], hidden_tile)
        grad_sum[:, at] += mm(w_gate[...], gate_tile) + mm(w_up[...], up_tile)
    half = rows // 2
    middle = wide // 2
    for grads, moves in (
        (gate_grad, ((0, 0, 0, wide),)),
        (up_grad, ((0, 0, wide, middle), (1, middle, 0, middle))),
    ):
        total[...] = mm_nt(normed[...], grads[...])
        for target, y_bit, x_bit, owner, side in places(shard, place[3], keep, send):
            at = span(owner * 2 + side, half)
            for z_half, first, to, count in moves:
                target[y_bit, x_bit, level ^ z_half, :, to : to + count] = total[
                    at, first : first + count
                ].astype(BF16)
    total[...] = mm_nt(dy[...], hidden[...])
    for target, y_bit, x_bit, owner, side in places(shard, place[3], keep, send):
        for block in range(4):
            at = pl.ds(pl.multiple_of(block * rows + side * half, 8), half)
            to = middle + block * part
            target[y_bit, x_bit, level ^ 1, :, to : to + part] = total[
                at, span(owner, part)
            ].astype(BF16)


def first_chunk_kernel(
    place,
    x_seq,
    attended_t,
    out_grad,
    dy_theirs,
    gains,
    p_own,
    p_y,
    p_core,
    p_both,
    middle,
    normed,
    scales,
    dy,
    w_out,
    out_sum,
    grad_sum,
    keep,
    send,
    w_out_t,
    *scratch,
):
    me, shard = place[0], place[1]
    half_rows = dy_theirs.shape[1]
    sequence = 2 * half_rows
    dy[:, span(me, half_rows)] = out_grad[me]
    dy[:, span(1 - me, half_rows)] = dy_theirs[...]
    pieces = (p_own, p_y, p_core, p_both)
    rows = p_own.shape[0]
    packed_width = p_own.shape[1] - QUERY_WIDTH
    for bits, piece in zip((0, 2, 1, 3), pieces):
        w_out[span(shard ^ bits, rows), :] = piece[:, packed_width:]
    w_out_t[...] = flip(w_out[...])
    gain2 = gains[:, 1:2]
    for first in range(0, sequence, WIDE_TILE):
        at = slice(first, first + WIDE_TILE)
        mid = x_seq[:, at].astype(F32) + mm(w_out_t[...], attended_t[:, at])
        middle[:, at] = mid
        out_sum[:, at] = mid
        grad_sum[:, at] = jnp.zeros_like(mid)
        scale = column_scale(mid)
        scales[:, at] = jnp.broadcast_to(scale, (8, WIDE_TILE))
        normed[:, at] = (mid * scale * gain2).astype(BF16)
    chunk_step(place, pieces, normed, dy, out_sum, grad_sum, keep, send, scratch)


def next_chunk_kernel(
    place, normed, dy, out_in, grad_in, p_own, p_y, p_core, p_both, out_sum, grad_sum, keep, send, *scratch
):
    out_sum[...] = out_in[...]
    grad_sum[...] = grad_in[...]
    pieces = (p_own, p_y, p_core, p_both)
    chunk_step(place, pieces, normed, dy, out_sum, grad_sum, keep, send, scratch)


def last_chunk_kernel(
    place,
    normed,
    dy,
    out_in,
    grad_in,
    p_own,
    p_y,
    p_core,
    p_both,
    attended_t,
    gains,
    middle,
    scales,
    w_out,
    out_keep,
    out_send,
    middle_grad,
    attended_grad_t,
    keep,
    send,
    out_sum,
    branch_grad,
    *scratch,
):
    me, shard = place[0], place[1]
    half_rows = out_keep.shape[1]
    sequence = 2 * half_rows
    grad_sum = middle_grad
    out_sum[...] = out_in[...]
    grad_sum[...] = grad_in[...]
    pieces = (p_own, p_y, p_core, p_both)
    chunk_step(place, pieces, normed, dy, out_sum, grad_sum, keep, send, scratch)
    gain2 = gains[:, 1:2]
    for first in range(0, sequence, WIDE_TILE):
        at = slice(first, first + WIDE_TILE)
        output = out_sum[:, at].astype(BF16)
        block, start = divmod(first, half_rows)
        block_cols = slice(start, start + WIDE_TILE)

        @pl.when(me == block)
        def _():
            out_keep[:, block_cols] = output

        @pl.when(me != block)
        def _():
            out_send[:, block_cols] = output

        mid = middle[:, at]
        scale = scales[0:1, at]
        scaled = grad_sum[:, at] * gain2
        back = (
            dy[:, at].astype(F32)
            + scale * scaled
            - mid * (scale * scale * scale) * jnp.mean(scaled * mid, axis=0, keepdims=True)
        )
        middle_grad[:, at] = back
        branch = back.astype(BF16)
        branch_grad[:, at] = branch
        attended_grad_t[:, at] = mm(w_out[...], branch).astype(BF16)
    total = scratch[-1]
    half = p_own.shape[0] // 2
    columns = QUERY_WIDTH // 2
    first_to = keep.shape[4] - columns
    for start in range(0, QUERY_WIDTH, TILE):
        count = min(TILE, QUERY_WIDTH - start)
        total[:, :count] = mm_nt(attended_t[...], branch_grad[start : start + count, :])
        for target, y_bit, x_bit, owner, side in places(shard, place[3], keep, send):
            at = span(owner * 2 + side, half)
            for z_half in range(2):
                low = max(start, z_half * columns)
                high = min(start + count, (z_half + 1) * columns)
                if low < high:
                    to = first_to + low - z_half * columns
                    target[y_bit, x_bit, place[2] ^ z_half, :, to : to + high - low] = total[
                        at, low - start : high - start
                    ].astype(BF16)


def attend_back_kernel(
    queries_t,
    keys_t,
    values_t,
    log_total,
    attended_t,
    grad_t,
    cosine,
    sine,
    dq_out,
    dk_out,
    dv_out,
    keys,
    values,
    dk,
    dv,
):
    sequence = keys_t.shape[1]
    keys[...] = flip(keys_t[...])
    values[...] = flip(values_t[...])
    dk[...] = jnp.zeros_like(dk)
    dv[...] = jnp.zeros_like(dv)

    def back(a, b, cos, sin):
        return (a * cos + b * sin).astype(BF16), (b * cos - a * sin).astype(BF16)

    for tile in range(sequence // TILE):
        extent = (tile + 1) * TILE
        cols = slice(tile * TILE, extent)
        heads = [slice(r * HEAD_SIZE, (r + 1) * HEAD_SIZE) for r in range(REPEAT)]
        q_t = jnp.concatenate([queries_t[head, cols] for head in heads], 1)
        do_t = jnp.concatenate([grad_t[head, cols] for head in heads], 1)
        mixed = jnp.concatenate([attended_t[head, cols] for head in heads], 1)
        logs = jnp.concatenate([log_total[0, r : r + 1, cols] for r in range(REPEAT)], 1)
        delta = jnp.sum(do_t.astype(F32) * mixed.astype(F32), axis=0, keepdims=True)
        scores = causal_last(mm(keys[:extent, :], q_t), tile)
        probs = jnp.exp(scores - logs)
        dprob = mm(values[:extent, :], do_t)
        score_grad = (probs * (dprob - delta)).astype(BF16)
        dv[:extent, :] += mm(probs.astype(BF16), flip(do_t))
        dk[:extent, :] += mm(score_grad, flip(q_t))
        dq = mm(keys_t[:, :extent], score_grad) * 0.125
        cos, sin = cosine[:, cols], sine[:, cols]
        for r, head in enumerate(heads):
            own = slice(r * TILE, (r + 1) * TILE)
            a, b = back(dq[:HALF, own], dq[HALF:, own], cos, sin)
            dq_out[head.start : head.start + HALF, cols] = a
            dq_out[head.start + HALF : head.stop, cols] = b
    turned = dk[...].T
    a, b = back(turned[:HALF, :], turned[HALF:, :], cosine[...], sine[...])
    dk_out[:HALF, :] = a
    dk_out[HALF:, :] = b
    dv_out[...] = dv[...].T.astype(BF16)


def joined_kernel(place, normed, *rest):
    heads = rest[: 3 * KEY_VALUE_HEADS]
    keep_w, send_w, joined, total = rest[3 * KEY_VALUE_HEADS :]
    me, shard = place[0], place[1]
    group_width = REPEAT * HEAD_SIZE
    for group in range(KEY_VALUE_HEADS):
        dq, dk, dv = heads[3 * group : 3 * group + 3]
        joined[group * group_width : (group + 1) * group_width, :] = dq[...]
        at = QUERY_WIDTH + group * HEAD_SIZE
        joined[at : at + HEAD_SIZE, :] = dk[...]
        at = QUERY_WIDTH + KEY_WIDTH + group * HEAD_SIZE
        joined[at : at + HEAD_SIZE, :] = dv[...]
    half = keep_w.shape[2]
    for first in range(0, USED, 512):
        cols = slice(first, min(first + 512, USED))
        total[:, cols] = mm_nt(normed[...], joined[cols, :])
    for target, y_bit, x_bit, owner, side in places(shard, me, keep_w, send_w):
        target[y_bit, x_bit] = total[span(owner * 2 + side, half), :].astype(BF16)


def input_kernel(
    place, x_seq, packed, gains, middle_grad, joined, keep_x, send_low, send_high, grad_seq
):
    me = place[0]
    half_rows = keep_x.shape[1]
    sequence = 2 * half_rows
    gain1 = gains[:, :1]
    for first in range(0, sequence, WIDE_TILE):
        at = slice(first, first + WIDE_TILE)
        scaled = mm(packed[:, :USED], joined[:, at]) * gain1
        x = x_seq[:, at].astype(F32)
        scale = column_scale(x)
        grad_seq[:, at] = (
            middle_grad[:, at]
            + scale * scaled
            - x * (scale * scale * scale) * jnp.mean(scaled * x, axis=0, keepdims=True)
        )
    keep_x[...] = grad_seq[:, span(me, half_rows)]
    low = send_low.shape[0]
    send_low[...] = grad_seq[:low, span(1 - me, half_rows)].astype(BF16)
    send_high[...] = grad_seq[low:, span(1 - me, half_rows)].astype(BF16)


def pack_input_kernel(place, w_query, w_key, w_value, gains, packed):
    rows = w_query.shape[0]
    packed[:rows, :QUERY_WIDTH] = w_query[...]
    packed[:rows, QUERY_WIDTH : QUERY_WIDTH + KEY_WIDTH] = w_key[...]
    packed[:rows, QUERY_WIDTH + KEY_WIDTH :] = jnp.concatenate(
        [w_value[...].astype(F32), jnp.zeros((rows, PACKED - USED), F32)], 1
    ).astype(BF16)
    packed[rows:, :] = jnp.zeros((GAIN_ROWS, PACKED), BF16)
    packed[rows:, :TILE] = gains[...]


def pack_kernel(place, w_gate, w_up, w_down_t, w_out, *chunks):
    rows = w_gate.shape[0]
    down_rows = w_down_t.shape[1]
    part = 128
    for index, chunk in enumerate(chunks):
        at = index * part
        for i in range(4):
            source = slice(i * down_rows + at, i * down_rows + at + part)
            chunk[:, i * part : (i + 1) * part] = w_gate[:, source]
            chunk[:, (4 + i) * part : (5 + i) * part] = w_up[:, source]
            chunk[:, (8 + i) * part : (9 + i) * part] = w_down_t[
                i * rows : (i + 1) * rows, at : at + part
            ]
    chunks[0][:, 12 * part :] = w_out[...]


def combine_kernel(kinds, place, *refs):
    sources, targets = refs[: 2 * len(kinds)], list(refs[2 * len(kinds) :])
    for kind, a, b in zip(kinds, sources[::2], sources[1::2]):
        if kind in ("order", "line_order"):
            target = targets.pop(0)
            at = place[2] if kind == "order" else place[4]
            target[at] = a[...]
            target[1 - at] = b[...]
        elif kind == "pair":
            for i in range(2):
                targets.pop(0)[...] = (a[i].astype(F32) + b[i].astype(F32)).astype(BF16)
        else:
            targets.pop(0)[...] = (a[...].astype(F32) + b[...].astype(F32)).astype(BF16)


def halves_kernel(place, keep, *rest):
    target = rest[-1]
    target[place[0]] = keep[...]
    first = 0
    for got in rest[:-1]:
        size = got.shape[0]
        target[1 - place[0], first : first + size] = got[...].astype(target.dtype)
        first += size


def gain_row(products, gain):
    column = jnp.sum(products, axis=1, keepdims=True)
    row = jnp.broadcast_to(column, (column.shape[0], 128)).T[:1, :]
    return row / gain.astype(F32)


def unpack_kernel(place, own0, other0, own1, other1, own2, other2, w_gate, w_up, gain, *out):
    gate_out, up_out, down_out, out_out, gain_out = out
    me = place[0]
    half = own0.shape[1]
    rows = 2 * half
    part = 128
    down_rows = down_out.shape[1]
    bit = place[2]
    last = (own2, other2)
    for index, sources in enumerate(((own0, own1, own2), (other0, other1, other2))):
        for chunk, source in enumerate(sources):
            side = index ^ (bit if chunk == 0 else me)
            at = span(side, half)
            for i in range(4):
                to = slice(i * down_rows + chunk * part, i * down_rows + (chunk + 1) * part)
                gate_out[at, to] = source[0, :, i * part : (i + 1) * part].astype(F32)
                z_half, first = (0, (4 + i) * part) if i < 2 else (1, (i - 2) * part)
                up_out[at, to] = source[z_half, :, first : first + part].astype(F32)
                down_at = pl.ds(pl.multiple_of(i * rows + side * half, 8), half)
                first = (2 + i) * part
                down_out[down_at, chunk * part : (chunk + 1) * part] = source[
                    1, :, first : first + part
                ].astype(F32)
        first = 6 * part
        out_out[span(index ^ me, half), :] = jnp.concatenate(
            [last[index][0, :, first:].astype(F32), last[index][1, :, first:].astype(F32)], 1
        )
    products = gate_out[...] * w_gate[...].astype(F32) + up_out[...] * w_up[...].astype(F32)
    gain_out[...] = gain_row(products, gain[...])


def unpack_input_kernel(
    place, own, other, w_query, w_key, w_value, gain, query_out, key_out, value_out, gain_out
):
    me = place[0]
    half = own.shape[0]
    key_at = QUERY_WIDTH + KEY_WIDTH
    for side, source in ((me, own), (1 - me, other)):
        at = span(side, half)
        wide = source[...].astype(F32)
        query_out[at, :] = wide[:, :QUERY_WIDTH]
        key_out[at, :] = wide[:, QUERY_WIDTH:key_at]
        value_out[at, :] = wide[:, key_at:]
    products = jnp.sum(query_out[...] * w_query[...].astype(F32), axis=1, keepdims=True)
    products += jnp.sum(key_out[...] * w_key[...].astype(F32), axis=1, keepdims=True)
    products += jnp.sum(value_out[...] * w_value[...].astype(F32), axis=1, keepdims=True)
    gain_out[...] = gain_row(products, gain[...])


def call(kernel, out, scratch, flops, exps, args, name, limit, aliases=None):
    shapes = [jax.ShapeDtypeStruct(s, d) for s, d in out]
    moved = sum(a.size * a.dtype.itemsize for a in args[1:]) + sum(
        s.size * s.dtype.itemsize for s in shapes
    )
    in_specs = [pl.BlockSpec(memory_space=pltpu.SMEM)] + [
        pl.BlockSpec(memory_space=pltpu.VMEM)
    ] * (len(args) - 1)
    return pl.pallas_call(
        kernel,
        out_shape=shapes,
        in_specs=in_specs,
        out_specs=[pl.BlockSpec(memory_space=pltpu.VMEM)] * len(shapes),
        scratch_shapes=[pltpu.VMEM(s, d) for s, d in scratch],
        input_output_aliases=aliases or {},
        compiler_params=pltpu.CompilerParams(vmem_limit_bytes=limit * MEBI),
        cost_estimate=pl.CostEstimate(flops=0, bytes_accessed=1024, transcendentals=0),
        name=name,
    )(*args)


def attend_back(group, qkv_t, log_total, attended_t, grad_t, cosine, sine):
    sequence = qkv_t.shape[1]
    group_width = REPEAT * HEAD_SIZE

    def rows_of(size, index):
        return pl.BlockSpec((size, sequence), lambda step: (index, 0))

    flops = 5 * REPEAT * sequence * sequence * HEAD_SIZE * 2
    return pl.pallas_call(
        attend_back_kernel,
        grid=(1,),
        out_shape=[
            jax.ShapeDtypeStruct((group_width, sequence), BF16),
            jax.ShapeDtypeStruct((HEAD_SIZE, sequence), BF16),
            jax.ShapeDtypeStruct((HEAD_SIZE, sequence), BF16),
        ],
        in_specs=[
            rows_of(group_width, group),
            rows_of(HEAD_SIZE, QUERY_HEADS + group),
            rows_of(HEAD_SIZE, ROTATED + group),
            pl.BlockSpec((1, 8, sequence), lambda step: (group, 0, 0)),
            rows_of(group_width, group),
            rows_of(group_width, group),
            rows_of(HALF, 0),
            rows_of(HALF, 0),
        ],
        out_specs=[rows_of(group_width, 0), rows_of(HEAD_SIZE, 0), rows_of(HEAD_SIZE, 0)],
        scratch_shapes=[
            pltpu.VMEM((sequence, HEAD_SIZE), BF16),
            pltpu.VMEM((sequence, HEAD_SIZE), BF16),
            pltpu.VMEM((sequence, HEAD_SIZE), F32),
            pltpu.VMEM((sequence, HEAD_SIZE), F32),
        ],
        compiler_params=pltpu.CompilerParams(vmem_limit_bytes=16 * MEBI),
        cost_estimate=pl.CostEstimate(flops=0, bytes_accessed=1024, transcendentals=0),
        name="attend_back",
    )(qkv_t, qkv_t, qkv_t, log_total, attended_t, grad_t, cosine, sine)


def across(tensor, bit):
    return lax.ppermute(tensor, "fsdp", [(i, i ^ bit) for i in range(4)])


def over_context(tensor):
    return lax.ppermute(tensor, "ctx", [(0, 1), (1, 0)])


def after(tensor, *done):
    return lax.optimization_barrier((tensor, *done))[0]


def together(*values):
    return lax.optimization_barrier(values)


def along(tensor, bit):
    size = lax.axis_size("dp")
    return lax.ppermute(tensor, "dp", [(i, i ^ bit) for i in range(size)])


def whole_sequences(
    tokens, norm1_gain, w_query, w_key, w_value, w_out, norm2_gain, w_gate, w_up, w_down, out_grad
):
    half_rows, width = tokens.shape[1:]
    sequence = 2 * half_rows
    rows = w_query.shape[0]
    down_rows = w_down.shape[0]
    hidden_width = w_gate.shape[1]
    part = 128
    me = lax.axis_index("ctx")
    line = lax.axis_index("dp")
    shard = lax.axis_index("fsdp")
    place = jnp.stack([me, shard, line & 1, me, line >> 1]).astype(jnp.int32)
    line_place = jnp.stack([me, shard, line >> 1, line & 1]).astype(jnp.int32)
    tokens = jnp.swapaxes(tokens, 1, 2)
    out_grad = jnp.swapaxes(out_grad, 1, 2)

    tokens_send = lax.dynamic_index_in_dim(tokens, 1 - me, 0, False)
    tokens_theirs = over_context(tokens_send)
    gain_rows = jnp.stack(together(norm1_gain, norm2_gain, tokens_send)[:2])
    gains_own = jnp.pad(gain_rows, ((0, GAIN_ROWS - 2), (0, TILE - rows)))
    (packed,) = call(
        pack_input_kernel,
        [((rows + GAIN_ROWS, PACKED), BF16)],
        [],
        0,
        0,
        (place, w_query, w_key, w_value, gains_own),
        "pack_input",
        16,
    )
    packed_y = across(packed, 2)
    packed_core = across(packed, 1)
    dy_theirs = over_context(lax.dynamic_index_in_dim(out_grad, 1 - me, 0, False))
    chunks = call(
        pack_kernel,
        [((rows, 12 * part + (0 if index else QUERY_WIDTH)), BF16) for index in range(3)],
        [],
        0,
        0,
        (place, w_gate, w_up, w_down.T, after(w_out, packed)),
        "pack",
        16,
    )
    cosine, sine = rope_tables(jnp.arange(sequence, dtype=jnp.int32), HEAD_SIZE)
    *chunks, _, cosine, sine, place, line_place = together(
        *chunks, packed, cosine.T, sine.T, place, line_place
    )
    packed_y, tokens_theirs = together(packed_y, tokens_theirs)
    packed_both = across(packed_y, 1)
    chunks_y = [across(chunk, 2) for chunk in chunks]
    chunks_core = [across(chunk, 1) for chunk in chunks]

    pairs = sequence * sequence
    x_seq, normed, packed_all, gains, qkv_t, log_total, attended_t = call(
        attend_kernel,
        [
            ((width, sequence), BF16),
            ((width, sequence), BF16),
            ((width, PACKED), BF16),
            ((width, 128), F32),
            ((USED, sequence), BF16),
            ((KEY_VALUE_HEADS, 8, sequence), F32),
            ((QUERY_WIDTH, sequence), BF16),
        ],
        [((PACKED, width), BF16), ((KEY_VALUE_HEADS, sequence, HEAD_SIZE), BF16)],
        2 * sequence * width * PACKED + 4 * QUERY_WIDTH * pairs,
        QUERY_HEADS * pairs,
        (place, tokens, tokens_theirs, packed, packed_y, packed_core, packed_both, cosine, sine),
        "attend",
        20,
    )

    natural, turned = ((width, 4 * part), BF16), ((4 * part, width), BF16)
    row, wide_row = ((width, sequence), BF16), ((4 * part, sequence), BF16)
    row_sum = ((width, sequence), F32)
    share = ((2, 2, 2, rows // 2, 6 * part), BF16)
    last_share = ((2, 2, 2, rows // 2, 6 * part + QUERY_WIDTH // 2), BF16)
    chunk_scratch = [
        natural,
        natural,
        natural,
        turned,
        turned,
        turned,
        wide_row,
        wide_row,
        wide_row,
        ((width, 4 * part), F32),
    ]
    flops = 2 * sequence * width * 9 * 4 * part
    exps = sequence * 4 * part

    first_y, second_y, third_y = chunks_y
    first_y, second_y, attended_t, dy_theirs = together(first_y, second_y, attended_t, dy_theirs)
    pieces = (chunks[0], first_y, chunks_core[0], across(first_y, 1))
    second_both = across(second_y, 1)
    middle, normed2, scales, dy, w_out_all, out_sum, grad_sum, keep0, send0 = call(
        first_chunk_kernel,
        [
            row_sum,
            row,
            ((8, sequence), F32),
            row,
            ((QUERY_WIDTH, width), BF16),
            row_sum,
            row_sum,
            share,
            share,
        ],
        [((width, QUERY_WIDTH), BF16), *chunk_scratch],
        flops + 2 * sequence * width * QUERY_WIDTH,
        exps,
        (line_place, x_seq, attended_t, out_grad, dy_theirs, gains, *pieces),
        "first_chunk",
        26,
    )

    def combine(*items):
        kinds = tuple(item[0] for item in items)
        args = [tensor for item in items for tensor in item[1:]]
        out = []
        for kind, tensor, _ in items:
            if kind in ("order", "line_order"):
                out.append(((2, *tensor.shape), BF16))
            elif kind == "pair":
                out += [(tensor.shape[1:], BF16)] * 2
            else:
                out.append((tensor.shape, BF16))
        kernel = functools.partial(combine_kernel, kinds)
        return call(kernel, out, [], 0, 0, (place, *args), "combine", 16)

    out_sum, send0, third_y, second_both = together(out_sum, send0, third_y, second_both)
    got0 = across(send0, 1)
    pieces = (chunks[1], second_y, chunks_core[1], second_both)
    third_both = across(third_y, 1)
    out_sum, grad_sum, keep1, send1 = call(
        next_chunk_kernel,
        [row_sum, row_sum, share, share],
        chunk_scratch,
        flops,
        exps,
        (place, normed2, dy, out_sum, grad_sum, *pieces),
        "next_chunk",
        20,
        {3: 0, 4: 1},
    )

    got0, out_sum, send1, third_both = together(got0, out_sum, send1, third_both)
    own0, part0 = combine(("pair", keep0, got0))
    part0, send1, out_sum = together(part0, send1, out_sum)
    got0, got1 = across(part0, 2), across(send1, 1)
    pieces = (chunks[2], third_y, chunks_core[2], third_both)
    out_keep, out_send, middle_grad, grad_t, keep2, send2 = call(
        last_chunk_kernel,
        [
            ((width, half_rows), BF16),
            ((width, half_rows), BF16),
            row_sum,
            ((QUERY_WIDTH, sequence), BF16),
            last_share,
            last_share,
        ],
        [row_sum, row, *chunk_scratch],
        flops + 4 * sequence * width * QUERY_WIDTH,
        exps,
        (
            place,
            normed2,
            dy,
            out_sum,
            grad_sum,
            *pieces,
            attended_t,
            gains,
            middle,
            scales,
            w_out_all,
        ),
        "last_chunk",
        24,
    )

    got0, got1, grad_t, send2, out_send = together(got0, got1, grad_t, send2, out_send)
    own0, part0, own1, part1 = combine(("pair", own0, got0), ("pair", keep1, got1))
    part0, part1, grad_t = together(part0, part1, grad_t)
    def place_halves(keep, name, *got):
        (both,) = call(
            halves_kernel, [((2, *keep.shape), keep.dtype)], [], 0, 0, (place, keep, *got), name, 16
        )
        return jnp.swapaxes(both, 1, 2)

    got0, got1, got2 = along(part0, 1), across(part1, 2), across(send2, 1)
    out_theirs = over_context(out_send)

    back_args = (log_total, attended_t, grad_t, cosine, sine)
    grads0 = attend_back(0, qkv_t, *back_args)
    got2, *grads0 = together(got2, *grads0)
    own2, part2 = combine(("pair", keep2, got2))
    part2, qkv_t = together(part2, qkv_t)

    got2 = across(part2, 2)
    grads1 = attend_back(1, qkv_t, *back_args)
    got0, got1, *grads1 = together(got0, got1, *grads1)
    own0, part0, own1, part1 = combine(("pair", own0, got0), ("pair", own1, got1))
    part0, part1, qkv_t = together(part0, part1, qkv_t)

    got0, got1 = along(part0, 2), over_context(part1)
    grads2 = attend_back(2, qkv_t, *back_args)
    got0, out_theirs, *grads2 = together(got0, out_theirs, *grads2)
    (own0,) = combine(("one", own0, got0))
    own0, *grads2 = together(own0, *grads2)

    got0 = over_context(own0)
    keep_w, send_w, joined = call(
        joined_kernel,
        [
            ((2, 2, rows // 2, USED), BF16),
            ((2, 2, rows // 2, USED), BF16),
            ((USED, sequence), BF16),
        ],
        [((width, USED), F32)],
        2 * sequence * width * USED,
        0,
        (place, normed, *grads0, *grads1, *grads2),
        "joined",
        16,
    )
    got0, got1, got2, send_w, joined = together(got0, got1, got2, send_w, joined)
    got_w = across(send_w, 1)
    own0, own1, part1, own2, part2 = combine(
        ("one", own0, got0), ("pair", own1, got1), ("pair", own2, got2)
    )
    own0, part1, part2, joined = together(own0, part1, part2, joined)

    got0, got1, got2 = along(own0, 2), along(part1, 1), over_context(part2)
    piece = ((width // 2, half_rows), BF16)
    keep_x, send_low, send_high = call(
        input_kernel,
        [((width, half_rows), F32), piece, piece],
        [((width, sequence), F32)],
        2 * sequence * width * USED,
        sequence,
        (place, x_seq, packed_all, gains, middle_grad, joined),
        "input_side",
        24,
    )
    got_w, got1, send_low, send_high = together(got_w, got1, send_low, send_high)
    own_w, part_w, own1 = combine(("pair", keep_w, got_w), ("one", own1, got1))
    part_w, own1, send_low = together(part_w, own1, send_low)
    got_w, got1, low_theirs = across(part_w, 2), along(own1, 2), over_context(send_low)
    output = place_halves(out_keep, "output_halves", out_theirs)

    got_w, got0, got1, got2, output = together(got_w, got0, got1, got2, output)
    own_w, part_w, own0, own1, own2, part2 = combine(
        ("pair", own_w, got_w),
        ("line_order", own0, got0),
        ("one", own1, got1),
        ("pair", own2, got2),
    )
    part_w, own0, own1, part2, low_theirs = together(part_w, own0, own1, part2, low_theirs)
    got_w, got1, got2 = over_context(part_w), along(own1, 1), along(part2, 1)
    high_theirs = over_context(after(send_high, part_w))

    got_w, got1, got2 = together(got_w, got1, got2)
    own_w, own1, own2 = combine(("one", own_w, got_w), ("order", own1, got1), ("one", own2, got2))
    own_w, own1, own2 = together(own_w, own1, own2)
    got_w, got2, other1 = along(own_w, 1), along(own2, 2), over_context(own1)

    got_w, got2, high_theirs = together(got_w, got2, high_theirs)
    own_w, own2 = combine(("one", own_w, got_w), ("one", own2, got2))
    own_w, own2, own0 = together(own_w, own2, own0)
    got_w, got2, other0 = along(own_w, 2), along(own2, 1), along(own0, 1)
    gradient = place_halves(keep_x, "gradient_halves", low_theirs, high_theirs)

    got2, other1, gradient = together(got2, other1, gradient)
    (own2,) = combine(("order", own2, got2))
    other2 = over_context(own2)

    got_w, other0 = together(got_w, other0)
    (own_w,) = combine(("one", own_w, got_w))
    own_w, other2 = together(own_w, other2)
    other_w = over_context(own_w)

    gate_sum, up_sum, down_sum, out_sum, gain2_sum = call(
        unpack_kernel,
        [
            ((rows, hidden_width), F32),
            ((rows, hidden_width), F32),
            ((width, down_rows), F32),
            ((rows, width), F32),
            ((1, rows), F32),
        ],
        [],
        0,
        0,
        (place, own0, other0, own1, other1, own2, other2, w_gate, w_up, norm2_gain[None, :]),
        "unpack",
        24,
    )
    gate_sum, other_w = together(gate_sum, other_w)
    query_sum, key_sum, value_sum, gain1_sum = call(
        unpack_input_kernel,
        [
            ((rows, QUERY_WIDTH), F32),
            ((rows, KEY_WIDTH), F32),
            ((rows, KEY_WIDTH), F32),
            ((1, rows), F32),
        ],
        [],
        0,
        0,
        (place, own_w, other_w, w_query, w_key, w_value, norm1_gain[None, :]),
        "unpack_input",
        16,
    )
    return (
        output,
        gradient,
        gain1_sum[0],
        query_sum,
        key_sum,
        value_sum,
        out_sum,
        gain2_sum[0],
        gate_sum,
        up_sum,
        down_sum.T,
    )


def layer_step(tokens, *rest):
    whole = (
        lax.axis_size("ctx") == 2
        and lax.axis_size("fsdp") == 4
        and lax.axis_size("dp") == 4
        and tokens.shape[0] == 2
        and tokens.shape[1] % WIDE_TILE == 0
        and rest[8].shape == (384, 576)
    )
    return (whole_sequences if whole else split_context)(tokens, *rest)


def solution(mesh):
    return jax.shard_map(
        layer_step,
        mesh=mesh,
        in_specs=(
            P(("dp", "fsdp"), "ctx", None),
            P("fsdp"),
            P("fsdp", None),
            P("fsdp", None),
            P("fsdp", None),
            P("fsdp", None),
            P("fsdp"),
            P("fsdp", None),
            P("fsdp", None),
            P("fsdp", None),
            P(("dp", "fsdp"), "ctx", None),
        ),
        out_specs=(
            P(("dp", "fsdp"), "ctx", None),
            P(("dp", "fsdp"), "ctx", None),
            P("fsdp"),
            P("fsdp", None),
            P("fsdp", None),
            P("fsdp", None),
            P("fsdp", None),
            P("fsdp"),
            P("fsdp", None),
            P("fsdp", None),
            P("fsdp", None),
        ),
        check_vma=False,
    )
```

```python
import functools
import math

import jax
import jax.numpy as jnp
from jax import lax
from jax.experimental import pallas as pl
from jax.experimental.pallas import tpu as pltpu
from jax.sharding import PartitionSpec as P

QUERY_HEADS = 9
KEY_VALUE_HEADS = 3
HEAD_SIZE = 64


EPSILON = 1e-05
ROPE_THETA = 100000.0
MASKED = -1e30


def rope_tables(positions, head_width):
    half_size = head_width // 2
    inverse = jnp.exp(
        jnp.arange(half_size, dtype=jnp.float32) * (-2.0 * math.log(ROPE_THETA) / head_width)
    )
    angle = positions.astype(jnp.float32)[:, None] * inverse[None, :]
    return (jnp.cos(angle), jnp.sin(angle))


def rotary_apply(tensor, cosine_table, sine_table):
    half_size = tensor.shape[-1] // 2
    first_half = tensor[..., :half_size]
    second_half = tensor[..., half_size:]
    cosine_table = cosine_table[None, :, None, :]
    sine_table = sine_table[None, :, None, :]
    return jnp.concatenate(
        [
            first_half * cosine_table - second_half * sine_table,
            second_half * cosine_table + first_half * sine_table,
        ],
        -1,
    )


def rotate_back(tensor, cosine_table, sine_table):
    half_size = tensor.shape[-1] // 2
    first_half = tensor[..., :half_size]
    second_half = tensor[..., half_size:]
    cosine_table = cosine_table[None, :, None, :]
    sine_table = sine_table[None, :, None, :]
    return jnp.concatenate(
        [
            first_half * cosine_table + second_half * sine_table,
            second_half * cosine_table - first_half * sine_table,
        ],
        -1,
    )


def rms_scale(tensor):
    return lax.rsqrt(jnp.mean(tensor * tensor, axis=-1, keepdims=True) + EPSILON)


def block_scores(query_block, key_block, query_pos, key_pos):
    scores = (
        jnp.einsum("gqhrd,gkhd->ghrqk", query_block, key_block, preferred_element_type=jnp.float32)
        * 0.125
    )
    visible = key_pos[None, :] <= query_pos[:, None]
    return jnp.where(visible, scores, MASKED)


def split_context(
    tokens, norm1_gain, w_query, w_key, w_value, w_out, norm2_gain, w_gate, w_up, w_down, out_grad
):
    gain1, wq_full, wk_full, wv_full, wo_full, gain2, wg_full, wu_full, wd_full = (
        lax.all_gather(norm1_gain, "fsdp", axis=0, tiled=True),
        lax.all_gather(w_query, "fsdp", axis=0, tiled=True),
        lax.all_gather(w_key, "fsdp", axis=0, tiled=True),
        lax.all_gather(w_value, "fsdp", axis=0, tiled=True),
        lax.all_gather(w_out, "fsdp", axis=0, tiled=True),
        lax.all_gather(norm2_gain, "fsdp", axis=0, tiled=True),
        lax.all_gather(w_gate, "fsdp", axis=0, tiled=True),
        lax.all_gather(w_up, "fsdp", axis=0, tiled=True),
        lax.all_gather(w_down, "fsdp", axis=0, tiled=True),
    )
    query_group_count, local_row_count, model_width = tokens.shape
    repeat_heads = QUERY_HEADS // KEY_VALUE_HEADS
    head_width = HEAD_SIZE
    key_value_width = KEY_VALUE_HEADS * HEAD_SIZE
    query_width = QUERY_HEADS * HEAD_SIZE
    first_row = lax.axis_index("ctx") * local_row_count
    last_row = first_row + local_row_count - 1
    positions = first_row + jnp.arange(local_row_count, dtype=jnp.int32)
    cosine_table, sine_table = rope_tables(positions, head_width)
    gain1f = gain1.astype(jnp.float32)
    gain2f = gain2.astype(jnp.float32)
    inputs = tokens.astype(jnp.float32)
    scale1 = rms_scale(inputs)
    normed1 = (inputs * scale1 * gain1f).astype(jnp.bfloat16)
    query_before_rotation = jnp.einsum(
        "gsd,de->gse", normed1, wq_full, preferred_element_type=jnp.float32
    )
    key_before_rotation = jnp.einsum(
        "gsd,de->gse", normed1, wk_full, preferred_element_type=jnp.float32
    )
    value_projected = jnp.einsum(
        "gsd,de->gse", normed1, wv_full, preferred_element_type=jnp.float32
    )
    query_matrix = rotary_apply(
        query_before_rotation.reshape(query_group_count, local_row_count, QUERY_HEADS, head_width),
        cosine_table,
        sine_table,
    ).astype(jnp.bfloat16)
    query_matrix = query_matrix.reshape(
        query_group_count, local_row_count, KEY_VALUE_HEADS, repeat_heads, head_width
    )
    key_local = rotary_apply(
        key_before_rotation.reshape(
            query_group_count, local_row_count, KEY_VALUE_HEADS, head_width
        ),
        cosine_table,
        sine_table,
    ).astype(jnp.bfloat16)
    local_value_rows = value_projected.astype(jnp.bfloat16)
    collected_keys, collected_values = (
        lax.all_gather(
            key_local.reshape(query_group_count, local_row_count, key_value_width),
            "ctx",
            axis=1,
            tiled=True,
        ),
        lax.all_gather(local_value_rows, "ctx", axis=1, tiled=True),
    )
    sequence_length = collected_keys.shape[1]
    every_key_row = collected_keys.reshape(
        query_group_count, sequence_length, KEY_VALUE_HEADS, head_width
    )
    every_value_row = collected_values.reshape(
        query_group_count, sequence_length, KEY_VALUE_HEADS, head_width
    )
    local_value_rows = local_value_rows.reshape(
        query_group_count, local_row_count, KEY_VALUE_HEADS, head_width
    )
    key_span = min(sequence_length, 512)
    block_total = last_row // key_span + 1

    def key_slices(step_index):
        first_key = step_index * key_span
        key_block = lax.dynamic_slice_in_dim(every_key_row, first_key, key_span, 1)
        value_block = lax.dynamic_slice_in_dim(every_value_row, first_key, key_span, 1)
        key_pos = first_key + jnp.arange(key_span, dtype=jnp.int32)
        return (key_block, value_block, key_pos)

    def stats_step(step_index, running):
        row_max, row_sum = running
        key_block, value_block, key_pos = key_slices(step_index)
        scores = block_scores(query_matrix, key_block, positions, key_pos)
        new_max = jnp.maximum(row_max, jnp.max(scores, axis=-1))
        row_sum = row_sum * jnp.exp(row_max - new_max) + jnp.sum(
            jnp.exp(scores - new_max[..., None]), axis=-1
        )
        return (new_max, row_sum)

    statistics_shape = (query_group_count, KEY_VALUE_HEADS, repeat_heads, local_row_count)
    row_max, row_sum = lax.fori_loop(
        0,
        block_total,
        stats_step,
        (jnp.full(statistics_shape, MASKED, jnp.float32), jnp.zeros(statistics_shape, jnp.float32)),
    )
    log_total = row_max + jnp.log(row_sum)

    def mix_step(step_index, running):
        key_block, value_block, key_pos = key_slices(step_index)
        scores = block_scores(query_matrix, key_block, positions, key_pos)
        probs = jnp.exp(scores - log_total[..., None]).astype(jnp.bfloat16)
        return running + jnp.einsum(
            "ghrqk,gkhd->gqhrd", probs, value_block, preferred_element_type=jnp.float32
        )

    attended_full = lax.fori_loop(
        0,
        block_total,
        mix_step,
        jnp.zeros(
            (query_group_count, local_row_count, KEY_VALUE_HEADS, repeat_heads, head_width),
            jnp.float32,
        ),
    )
    attended = attended_full.astype(jnp.bfloat16).reshape(
        query_group_count, local_row_count, query_width
    )
    branch = jnp.einsum("gse,ed->gsd", attended, wo_full, preferred_element_type=jnp.float32)
    middle = inputs + branch
    scale2 = rms_scale(middle)
    normed2 = (middle * scale2 * gain2f).astype(jnp.bfloat16)
    gate_act = jnp.einsum("gsd,df->gsf", normed2, wg_full, preferred_element_type=jnp.float32)
    up_act = jnp.einsum("gsd,df->gsf", normed2, wu_full, preferred_element_type=jnp.float32)
    gate_sig = jax.nn.sigmoid(gate_act)
    gate_silu = gate_act * gate_sig
    hidden = (gate_silu * up_act).astype(jnp.bfloat16)
    mlp_out = jnp.einsum("gsf,fd->gsd", hidden, wd_full, preferred_element_type=jnp.float32)
    output = (middle + mlp_out).astype(jnp.bfloat16)
    out_float = out_grad.astype(jnp.float32)
    grad_down = jnp.einsum("gsf,gsd->fd", hidden, out_grad, preferred_element_type=jnp.float32)
    hidden_grad = jnp.einsum("gsd,fd->gsf", out_grad, wd_full, preferred_element_type=jnp.float32)
    gate_grad = (hidden_grad * up_act * gate_sig * (1.0 + gate_act * (1.0 - gate_sig))).astype(
        jnp.bfloat16
    )
    up_grad = (hidden_grad * gate_silu).astype(jnp.bfloat16)
    grad_gate = jnp.einsum("gsd,gsf->df", normed2, gate_grad, preferred_element_type=jnp.float32)
    grad_up = jnp.einsum("gsd,gsf->df", normed2, up_grad, preferred_element_type=jnp.float32)
    normed2_grad = jnp.einsum("gsf,df->gsd", gate_grad, wg_full, preferred_element_type=jnp.float32)
    normed2_grad = normed2_grad + jnp.einsum(
        "gsf,df->gsd", up_grad, wu_full, preferred_element_type=jnp.float32
    )
    grad_gain2 = jnp.sum(normed2_grad * middle * scale2, axis=(0, 1))
    scaled2 = gain2f * normed2_grad
    middle_grad = (
        out_float
        + scale2 * scaled2
        - middle * scale2**3 * jnp.mean(scaled2 * middle, axis=-1, keepdims=True)
    )
    branch_grad = middle_grad.astype(jnp.bfloat16)
    grad_out = jnp.einsum("gse,gsd->ed", attended, branch_grad, preferred_element_type=jnp.float32)
    attended_output_gradient = jnp.einsum(
        "gsd,ed->gse", branch_grad, wo_full, preferred_element_type=jnp.float32
    ).astype(jnp.bfloat16)
    attention_gradient = attended_output_gradient.reshape(
        query_group_count, local_row_count, KEY_VALUE_HEADS, repeat_heads, head_width
    )
    delta = jnp.sum(attention_gradient.astype(jnp.float32) * attended_full, axis=-1).transpose(
        0, 2, 3, 1
    )

    def query_grad_step(step_index, running):
        key_block, value_block, key_pos = key_slices(step_index)
        scores = block_scores(query_matrix, key_block, positions, key_pos)
        probs = jnp.exp(scores - log_total[..., None])
        dprob = jnp.einsum(
            "gqhrd,gkhd->ghrqk", attention_gradient, value_block, preferred_element_type=jnp.float32
        )
        score_grad = (probs * (dprob - delta[..., None])).astype(jnp.bfloat16)
        return running + jnp.einsum(
            "ghrqk,gkhd->gqhrd", score_grad, key_block, preferred_element_type=jnp.float32
        )

    query_grad = (
        lax.fori_loop(
            0,
            block_total,
            query_grad_step,
            jnp.zeros(
                (query_group_count, local_row_count, KEY_VALUE_HEADS, repeat_heads, head_width),
                jnp.float32,
            ),
        )
        * 0.125
    )
    row_total = local_row_count * lax.axis_size("ctx")
    term_span = math.gcd(row_total, key_span)

    def key_block_term(step_index):
        first_key = step_index * term_span
        key_block = lax.dynamic_slice_in_dim(every_key_row, first_key, term_span, 1)
        value_block = lax.dynamic_slice_in_dim(every_value_row, first_key, term_span, 1)
        key_pos = first_key + jnp.arange(term_span, dtype=jnp.int32)

        def compute_term(unused):
            scores = block_scores(query_matrix, key_block, positions, key_pos)
            probs = jnp.exp(scores - log_total[..., None])
            dprob = jnp.einsum(
                "gqhrd,gkhd->ghrqk",
                attention_gradient,
                value_block,
                preferred_element_type=jnp.float32,
            )
            score_grad = (probs * (dprob - delta[..., None])).astype(jnp.bfloat16)
            key_term = (
                jnp.einsum(
                    "ghrqk,gqhrd->kghd",
                    score_grad,
                    query_matrix,
                    preferred_element_type=jnp.float32,
                )
                * 0.125
            )
            value_term = jnp.einsum(
                "ghrqk,gqhrd->kghd",
                probs.astype(jnp.bfloat16),
                attention_gradient,
                preferred_element_type=jnp.float32,
            )
            return jnp.concatenate(
                [
                    key_term.reshape(term_span, query_group_count, key_value_width),
                    value_term.reshape(term_span, query_group_count, key_value_width),
                ],
                -1,
            )

        def empty_term(unused):
            return jnp.zeros((term_span, query_group_count, 2 * key_value_width), jnp.float32)

        return lax.cond(first_key <= last_row, compute_term, empty_term, 0)

    terms = lax.map(key_block_term, jnp.arange(row_total // term_span, dtype=jnp.int32))
    paired_gradients = (
        lax.psum_scatter(
            terms.reshape(row_total, query_group_count, 2 * key_value_width).astype(jnp.bfloat16),
            "ctx",
            scatter_dimension=0,
            tiled=True,
        )
        .astype(jnp.float32)
        .transpose(1, 0, 2)
    )
    key_gradient = paired_gradients[..., :key_value_width].reshape(
        query_group_count, local_row_count, KEY_VALUE_HEADS, head_width
    )
    value_gradient = paired_gradients[..., key_value_width:].reshape(
        query_group_count, local_row_count, KEY_VALUE_HEADS, head_width
    )
    query_pre_grad = rotate_back(
        query_grad.reshape(query_group_count, local_row_count, QUERY_HEADS, head_width),
        cosine_table,
        sine_table,
    )
    query_pre_grad = query_pre_grad.astype(jnp.bfloat16).reshape(
        query_group_count, local_row_count, query_width
    )
    key_pre_grad = (
        rotate_back(key_gradient, cosine_table, sine_table)
        .astype(jnp.bfloat16)
        .reshape(query_group_count, local_row_count, key_value_width)
    )
    value_pre_grad = value_gradient.astype(jnp.bfloat16).reshape(
        query_group_count, local_row_count, key_value_width
    )
    grad_query = jnp.einsum(
        "gsd,gse->de", normed1, query_pre_grad, preferred_element_type=jnp.float32
    )
    grad_key = jnp.einsum("gsd,gse->de", normed1, key_pre_grad, preferred_element_type=jnp.float32)
    grad_value = jnp.einsum(
        "gsd,gse->de", normed1, value_pre_grad, preferred_element_type=jnp.float32
    )
    normed1_grad = jnp.einsum(
        "gse,de->gsd", query_pre_grad, wq_full, preferred_element_type=jnp.float32
    )
    normed1_grad = normed1_grad + jnp.einsum(
        "gse,de->gsd", key_pre_grad, wk_full, preferred_element_type=jnp.float32
    )
    normed1_grad = normed1_grad + jnp.einsum(
        "gse,de->gsd", value_pre_grad, wv_full, preferred_element_type=jnp.float32
    )
    grad_gain1 = jnp.sum(normed1_grad * inputs * scale1, axis=(0, 1))
    scaled1 = gain1f * normed1_grad
    input_grad = (
        middle_grad
        + scale1 * scaled1
        - inputs * scale1**3 * jnp.mean(scaled1 * inputs, axis=-1, keepdims=True)
    )
    totals = lax.psum(
        (
            grad_gain1,
            grad_query,
            grad_key,
            grad_value,
            grad_out,
            grad_gain2,
            grad_gate,
            grad_up,
            grad_down,
        ),
        ("dp", "ctx", "fsdp"),
    )
    owner = lax.axis_index("fsdp")
    shards = (norm1_gain, w_query, w_key, w_value, w_out, norm2_gain, w_gate, w_up, w_down)
    shares = tuple(
        (
            lax.dynamic_slice_in_dim(summed, owner * shard.shape[0], shard.shape[0], 0)
            for summed, shard in zip(totals, shards)
        )
    )
    return (
        output,
        input_grad,
        shares[0],
        shares[1],
        shares[2],
        shares[3],
        shares[4],
        shares[5],
        shares[6],
        shares[7],
        shares[8],
    )


WIDTH = 576
QUERY_WIDTH = QUERY_HEADS * HEAD_SIZE
KEY_WIDTH = KEY_VALUE_HEADS * HEAD_SIZE
ROTATED = QUERY_HEADS + KEY_VALUE_HEADS
REPEAT = QUERY_HEADS // KEY_VALUE_HEADS
HALF = HEAD_SIZE // 2
USED = QUERY_WIDTH + 2 * KEY_WIDTH
PACKED = USED + 64
GAIN_ROWS = 16
TILE = 256
WIDE_TILE = 512
MEBI = 1024 * 1024
F32 = jnp.float32
BF16 = jnp.bfloat16


def mm(a, b):
    return jnp.dot(a, b, preferred_element_type=F32)


def mm_nt(a, b):
    return lax.dot_general(a, b, (((1,), (1,)), ((), ())), preferred_element_type=F32)


def flip(tensor):
    return tensor.astype(F32).T.astype(tensor.dtype)


def span(index, size, step=None):
    step = size if step is None else step
    return pl.ds(pl.multiple_of(index * step, step), size)


def flip_blocks(target, source, block):
    def one(step, carry):
        at = span(step, block)
        target[at, :] = flip(source[:, at])
        return carry

    lax.fori_loop(0, source.shape[1] // block, one, 0)


def column_scale(tensor):
    return lax.rsqrt(jnp.mean(tensor * tensor, axis=0, keepdims=True) + EPSILON)


def sigmoid(tensor):
    return 0.5 * jnp.tanh(0.5 * tensor) + 0.5


def causal_last(scores, tile):
    shape = (TILE, REPEAT * TILE)
    visible = lax.broadcasted_iota(jnp.int32, shape, 0) <= (
        lax.broadcasted_iota(jnp.int32, shape, 1) & (TILE - 1)
    )
    last = jnp.where(visible, scores[tile * TILE :, :], MASKED)
    return last if tile == 0 else jnp.concatenate([scores[: tile * TILE, :], last], 0)


def attend_kernel(
    place,
    tokens,
    theirs,
    w_own,
    w_y,
    w_core,
    w_both,
    cosine,
    sine,
    x_seq,
    normed,
    packed,
    gains,
    qkv_t,
    log_total,
    attended_t,
    packed_t,
    key_rows,
):
    me, shard = place[0], place[1]
    half_rows = theirs.shape[1]
    sequence = 2 * half_rows
    x_seq[:, span(me, half_rows)] = tokens[me]
    x_seq[:, span(1 - me, half_rows)] = theirs[...]
    rows = packed.shape[0] // 4
    for bits, piece in ((0, w_own), (2, w_y), (1, w_core), (3, w_both)):
        at = span(shard ^ bits, rows)
        packed[at, :] = piece[:rows, :]
        gains[at, :GAIN_ROWS] = piece[rows:, :TILE].astype(F32).T[:rows, :]
    flip_blocks(packed_t, packed, TILE)
    gain1 = gains[:, :1]

    def project(step, carry):
        at = span(step, WIDE_TILE)
        x = x_seq[:, at].astype(F32)
        normed_tile = (x * column_scale(x) * gain1).astype(BF16)
        normed[:, at] = normed_tile
        turned = mm(packed_t[:USED, :], normed_tile)
        cos, sin = cosine[:, at], sine[:, at]
        for head in range(ROTATED):
            a = turned[head * HEAD_SIZE : head * HEAD_SIZE + HALF, :]
            b = turned[head * HEAD_SIZE + HALF : (head + 1) * HEAD_SIZE, :]
            both = jnp.concatenate([a * cos - b * sin, b * cos + a * sin], 0)
            if head < QUERY_HEADS:
                both = both * 0.125
            else:
                key_rows[head - QUERY_HEADS, at, :] = both.T.astype(BF16)
            qkv_t[head * HEAD_SIZE : (head + 1) * HEAD_SIZE, at] = both.astype(BF16)
        qkv_t[ROTATED * HEAD_SIZE :, at] = turned[ROTATED * HEAD_SIZE :, :].astype(BF16)
        return carry

    lax.fori_loop(0, sequence // WIDE_TILE, project, 0)

    def one_group(group, carry):
        value_rows = span(ROTATED + group, HEAD_SIZE)
        for tile in range(sequence // TILE):
            extent = (tile + 1) * TILE
            cols = slice(tile * TILE, extent)
            queries = jnp.concatenate(
                [qkv_t[span(group * REPEAT + r, HEAD_SIZE), cols] for r in range(REPEAT)], 1
            )
            scores = causal_last(mm(key_rows[group, :extent, :], queries), tile)
            top = jnp.max(scores, axis=0, keepdims=True)
            weights = jnp.exp(scores - top)
            total = jnp.sum(weights, axis=0, keepdims=True)
            mixed = mm(qkv_t[value_rows, :extent], weights.astype(BF16))
            mixed = (mixed * (1.0 / total)).astype(BF16)
            logs = top + jnp.log(total)
            for r in range(REPEAT):
                own = slice(r * TILE, (r + 1) * TILE)
                attended_t[span(group * REPEAT + r, HEAD_SIZE), cols] = mixed[:, own]
                log_total[group, r : r + 1, cols] = logs[:, own]
        return carry

    lax.fori_loop(0, KEY_VALUE_HEADS, one_group, 0)


def places(shard, row_bit, keep, send):
    for y_bit in range(2):
        for x_bit in range(2):
            for core_bit, target in ((0, keep), (1, send)):
                yield target, y_bit, x_bit, shard ^ (2 * y_bit + core_bit), row_bit ^ x_bit


def chunk_step(place, pieces, normed, dy, out_sum, grad_sum, keep, send, scratch):
    w_gate, w_up, w_down_t, w_gate_t, w_up_t, w_down, hidden, gate_grad, up_grad, total = scratch
    row_bit, shard, level = place[3], place[1], place[2]
    rows = pieces[0].shape[0]
    wide = w_gate.shape[1]
    part = wide // 4
    sequence = normed.shape[1]
    for bits, piece in zip((0, 2, 1, 3), pieces):
        at = span(shard ^ bits, rows)
        w_gate[at, :] = piece[:, :wide]
        w_up[at, :] = piece[:, wide : 2 * wide]
        for block in range(4):
            first = 2 * wide + block * part
            w_down_t[block * rows : (block + 1) * rows, span(shard ^ bits, part)] = piece[
                :, first : first + part
            ]
    w_gate_t[...] = flip(w_gate[...])
    w_up_t[...] = flip(w_up[...])
    w_down[...] = flip(w_down_t[...])
    for first in range(0, sequence, WIDE_TILE):
        at = slice(first, first + WIDE_TILE)
        gate = mm(w_gate_t[...], normed[:, at])
        up = mm(w_up_t[...], normed[:, at])
        hidden_grad = mm(w_down[...], dy[:, at])
        sig = sigmoid(gate)
        silu = gate * sig
        hidden_tile = (silu * up).astype(BF16)
        gate_tile = (hidden_grad * up * (sig + silu * (1.0 - sig))).astype(BF16)
        up_tile = (hidden_grad * silu).astype(BF16)
        hidden[:, at] = hidden_tile
        gate_grad[:, at] = gate_tile
        up_grad[:, at] = up_tile
        out_sum[:, at] += mm(w_down_t[...], hidden_tile)
        grad_sum[:, at] += mm(w_gate[...], gate_tile) + mm(w_up[...], up_tile)
    half = rows // 2
    middle = wide // 2
    for grads, moves in (
        (gate_grad, ((0, 0, 0, wide),)),
        (up_grad, ((0, 0, wide, middle), (1, middle, 0, middle))),
    ):
        total[...] = mm_nt(normed[...], grads[...])
        for target, y_bit, x_bit, owner, side in places(shard, place[3], keep, send):
            at = span(owner * 2 + side, half)
            for z_half, first, to, count in moves:
                target[y_bit, x_bit, level ^ z_half, :, to : to + count] = total[
                    at, first : first + count
                ].astype(BF16)
    total[...] = mm_nt(dy[...], hidden[...])
    for target, y_bit, x_bit, owner, side in places(shard, place[3], keep, send):
        for block in range(4):
            at = pl.ds(pl.multiple_of(block * rows + side * half, 8), half)
            to = middle + block * part
            target[y_bit, x_bit, level ^ 1, :, to : to + part] = total[
                at, span(owner, part)
            ].astype(BF16)


def first_chunk_kernel(
    place,
    x_seq,
    attended_t,
    out_grad,
    dy_theirs,
    gains,
    p_own,
    p_y,
    p_core,
    p_both,
    middle,
    normed,
    scales,
    dy,
    w_out,
    out_sum,
    grad_sum,
    keep,
    send,
    w_out_t,
    *scratch,
):
    me, shard = place[0], place[1]
    half_rows = dy_theirs.shape[1]
    sequence = 2 * half_rows
    dy[:, span(me, half_rows)] = out_grad[me]
    dy[:, span(1 - me, half_rows)] = dy_theirs[...]
    pieces = (p_own, p_y, p_core, p_both)
    rows = p_own.shape[0]
    packed_width = p_own.shape[1] - QUERY_WIDTH
    for bits, piece in zip((0, 2, 1, 3), pieces):
        w_out[span(shard ^ bits, rows), :] = piece[:, packed_width:]
    w_out_t[...] = flip(w_out[...])
    gain2 = gains[:, 1:2]
    for first in range(0, sequence, WIDE_TILE):
        at = slice(first, first + WIDE_TILE)
        mid = x_seq[:, at].astype(F32) + mm(w_out_t[...], attended_t[:, at])
        middle[:, at] = mid
        out_sum[:, at] = mid
        grad_sum[:, at] = jnp.zeros_like(mid)
        scale = column_scale(mid)
        scales[:, at] = jnp.broadcast_to(scale, (8, WIDE_TILE))
        normed[:, at] = (mid * scale * gain2).astype(BF16)
    chunk_step(place, pieces, normed, dy, out_sum, grad_sum, keep, send, scratch)


def next_chunk_kernel(
    place, normed, dy, out_in, grad_in, p_own, p_y, p_core, p_both, out_sum, grad_sum, keep, send, *scratch
):
    out_sum[...] = out_in[...]
    grad_sum[...] = grad_in[...]
    pieces = (p_own, p_y, p_core, p_both)
    chunk_step(place, pieces, normed, dy, out_sum, grad_sum, keep, send, scratch)


def last_chunk_kernel(
    place,
    normed,
    dy,
    out_in,
    grad_in,
    p_own,
    p_y,
    p_core,
    p_both,
    attended_t,
    gains,
    middle,
    scales,
    w_out,
    out_keep,
    out_send,
    middle_grad,
    attended_grad_t,
    keep,
    send,
    out_sum,
    branch_grad,
    *scratch,
):
    me, shard = place[0], place[1]
    half_rows = out_keep.shape[1]
    sequence = 2 * half_rows
    grad_sum = middle_grad
    out_sum[...] = out_in[...]
    grad_sum[...] = grad_in[...]
    pieces = (p_own, p_y, p_core, p_both)
    chunk_step(place, pieces, normed, dy, out_sum, grad_sum, keep, send, scratch)
    gain2 = gains[:, 1:2]
    for first in range(0, sequence, WIDE_TILE):
        at = slice(first, first + WIDE_TILE)
        output = out_sum[:, at].astype(BF16)
        block, start = divmod(first, half_rows)
        block_cols = slice(start, start + WIDE_TILE)

        @pl.when(me == block)
        def _():
            out_keep[:, block_cols] = output

        @pl.when(me != block)
        def _():
            out_send[:, block_cols] = output

        mid = middle[:, at]
        scale = scales[0:1, at]
        scaled = grad_sum[:, at] * gain2
        back = (
            dy[:, at].astype(F32)
            + scale * scaled
            - mid * (scale * scale * scale) * jnp.mean(scaled * mid, axis=0, keepdims=True)
        )
        middle_grad[:, at] = back
        branch = back.astype(BF16)
        branch_grad[:, at] = branch
        attended_grad_t[:, at] = mm(w_out[...], branch).astype(BF16)
    total = scratch[-1]
    half = p_own.shape[0] // 2
    columns = QUERY_WIDTH // 2
    first_to = keep.shape[4] - columns
    for start in range(0, QUERY_WIDTH, TILE):
        count = min(TILE, QUERY_WIDTH - start)
        total[:, :count] = mm_nt(attended_t[...], branch_grad[start : start + count, :])
        for target, y_bit, x_bit, owner, side in places(shard, place[3], keep, send):
            at = span(owner * 2 + side, half)
            for z_half in range(2):
                low = max(start, z_half * columns)
                high = min(start + count, (z_half + 1) * columns)
                if low < high:
                    to = first_to + low - z_half * columns
                    target[y_bit, x_bit, place[2] ^ z_half, :, to : to + high - low] = total[
                        at, low - start : high - start
                    ].astype(BF16)


def attend_back_kernel(
    queries_t,
    keys_t,
    values_t,
    log_total,
    attended_t,
    grad_t,
    cosine,
    sine,
    dq_out,
    dk_out,
    dv_out,
    keys,
    values,
    dk,
    dv,
):
    sequence = keys_t.shape[1]
    keys[...] = flip(keys_t[...])
    values[...] = flip(values_t[...])
    dk[...] = jnp.zeros_like(dk)
    dv[...] = jnp.zeros_like(dv)

    def back(a, b, cos, sin):
        return (a * cos + b * sin).astype(BF16), (b * cos - a * sin).astype(BF16)

    for tile in range(sequence // TILE):
        extent = (tile + 1) * TILE
        cols = slice(tile * TILE, extent)
        heads = [slice(r * HEAD_SIZE, (r + 1) * HEAD_SIZE) for r in range(REPEAT)]
        q_t = jnp.concatenate([queries_t[head, cols] for head in heads], 1)
        do_t = jnp.concatenate([grad_t[head, cols] for head in heads], 1)
        mixed = jnp.concatenate([attended_t[head, cols] for head in heads], 1)
        logs = jnp.concatenate([log_total[0, r : r + 1, cols] for r in range(REPEAT)], 1)
        delta = jnp.sum(do_t.astype(F32) * mixed.astype(F32), axis=0, keepdims=True)
        scores = causal_last(mm(keys[:extent, :], q_t), tile)
        probs = jnp.exp(scores - logs)
        dprob = mm(values[:extent, :], do_t)
        score_grad = (probs * (dprob - delta)).astype(BF16)
        dv[:extent, :] += mm(probs.astype(BF16), flip(do_t))
        dk[:extent, :] += mm(score_grad, flip(q_t))
        dq = mm(keys_t[:, :extent], score_grad) * 0.125
        cos, sin = cosine[:, cols], sine[:, cols]
        for r, head in enumerate(heads):
            own = slice(r * TILE, (r + 1) * TILE)
            a, b = back(dq[:HALF, own], dq[HALF:, own], cos, sin)
            dq_out[head.start : head.start + HALF, cols] = a
            dq_out[head.start + HALF : head.stop, cols] = b
    turned = dk[...].T
    a, b = back(turned[:HALF, :], turned[HALF:, :], cosine[...], sine[...])
    dk_out[:HALF, :] = a
    dk_out[HALF:, :] = b
    dv_out[...] = dv[...].T.astype(BF16)


def joined_kernel(place, normed, *rest):
    heads = rest[: 3 * KEY_VALUE_HEADS]
    keep_w, send_w, joined, total = rest[3 * KEY_VALUE_HEADS :]
    me, shard = place[0], place[1]
    group_width = REPEAT * HEAD_SIZE
    for group in range(KEY_VALUE_HEADS):
        dq, dk, dv = heads[3 * group : 3 * group + 3]
        joined[group * group_width : (group + 1) * group_width, :] = dq[...]
        at = QUERY_WIDTH + group * HEAD_SIZE
        joined[at : at + HEAD_SIZE, :] = dk[...]
        at = QUERY_WIDTH + KEY_WIDTH + group * HEAD_SIZE
        joined[at : at + HEAD_SIZE, :] = dv[...]
    half = keep_w.shape[2]
    for first in range(0, USED, 512):
        cols = slice(first, min(first + 512, USED))
        total[:, cols] = mm_nt(normed[...], joined[cols, :])
    for target, y_bit, x_bit, owner, side in places(shard, me, keep_w, send_w):
        target[y_bit, x_bit] = total[span(owner * 2 + side, half), :].astype(BF16)


def input_kernel(
    place, x_seq, packed, gains, middle_grad, joined, keep_x, send_low, send_high, grad_seq
):
    me = place[0]
    half_rows = keep_x.shape[1]
    sequence = 2 * half_rows
    gain1 = gains[:, :1]
    for first in range(0, sequence, WIDE_TILE):
        at = slice(first, first + WIDE_TILE)
        scaled = mm(packed[:, :USED], joined[:, at]) * gain1
        x = x_seq[:, at].astype(F32)
        scale = column_scale(x)
        grad_seq[:, at] = (
            middle_grad[:, at]
            + scale * scaled
            - x * (scale * scale * scale) * jnp.mean(scaled * x, axis=0, keepdims=True)
        )
    keep_x[...] = grad_seq[:, span(me, half_rows)]
    low = send_low.shape[0]
    send_low[...] = grad_seq[:low, span(1 - me, half_rows)].astype(BF16)
    send_high[...] = grad_seq[low:, span(1 - me, half_rows)].astype(BF16)


def pack_input_kernel(place, w_query, w_key, w_value, gains, packed):
    rows = w_query.shape[0]
    packed[:rows, :QUERY_WIDTH] = w_query[...]
    packed[:rows, QUERY_WIDTH : QUERY_WIDTH + KEY_WIDTH] = w_key[...]
    packed[:rows, QUERY_WIDTH + KEY_WIDTH :] = jnp.concatenate(
        [w_value[...].astype(F32), jnp.zeros((rows, PACKED - USED), F32)], 1
    ).astype(BF16)
    packed[rows:, :] = jnp.zeros((GAIN_ROWS, PACKED), BF16)
    packed[rows:, :TILE] = gains[...]


def pack_kernel(place, w_gate, w_up, w_down_t, w_out, *chunks):
    rows = w_gate.shape[0]
    down_rows = w_down_t.shape[1]
    part = 128
    for index, chunk in enumerate(chunks):
        at = index * part
        for i in range(4):
            source = slice(i * down_rows + at, i * down_rows + at + part)
            chunk[:, i * part : (i + 1) * part] = w_gate[:, source]
            chunk[:, (4 + i) * part : (5 + i) * part] = w_up[:, source]
            chunk[:, (8 + i) * part : (9 + i) * part] = w_down_t[
                i * rows : (i + 1) * rows, at : at + part
            ]
    chunks[0][:, 12 * part :] = w_out[...]


def combine_kernel(kinds, place, *refs):
    sources, targets = refs[: 2 * len(kinds)], list(refs[2 * len(kinds) :])
    for kind, a, b in zip(kinds, sources[::2], sources[1::2]):
        if kind == "order":
            target = targets.pop(0)
            target[place[2]] = a[...]
            target[1 - place[2]] = b[...]
        elif kind == "pair":
            for i in range(2):
                targets.pop(0)[...] = (a[i].astype(F32) + b[i].astype(F32)).astype(BF16)
        else:
            targets.pop(0)[...] = (a[...].astype(F32) + b[...].astype(F32)).astype(BF16)


def halves_kernel(place, keep, *rest):
    target = rest[-1]
    target[place[0]] = keep[...]
    first = 0
    for got in rest[:-1]:
        size = got.shape[0]
        target[1 - place[0], first : first + size] = got[...].astype(target.dtype)
        first += size


def gain_row(products, gain):
    column = jnp.sum(products, axis=1, keepdims=True)
    row = jnp.broadcast_to(column, (column.shape[0], 128)).T[:1, :]
    return row / gain.astype(F32)


def unpack_kernel(place, own0, other0, own1, other1, own2, other2, w_gate, w_up, gain, *out):
    gate_out, up_out, down_out, out_out, gain_out = out
    me = place[0]
    half = own0.shape[1]
    rows = 2 * half
    part = 128
    down_rows = down_out.shape[1]
    last = (own2, other2)
    for index, sources in enumerate(((own0, own1, own2), (other0, other1, other2))):
        for chunk, source in enumerate(sources):
            side = index ^ me
            at = span(side, half)
            for i in range(4):
                to = slice(i * down_rows + chunk * part, i * down_rows + (chunk + 1) * part)
                gate_out[at, to] = source[0, :, i * part : (i + 1) * part].astype(F32)
                z_half, first = (0, (4 + i) * part) if i < 2 else (1, (i - 2) * part)
                up_out[at, to] = source[z_half, :, first : first + part].astype(F32)
                down_at = pl.ds(pl.multiple_of(i * rows + side * half, 8), half)
                first = (2 + i) * part
                down_out[down_at, chunk * part : (chunk + 1) * part] = source[
                    1, :, first : first + part
                ].astype(F32)
        first = 6 * part
        out_out[span(index ^ me, half), :] = jnp.concatenate(
            [last[index][0, :, first:].astype(F32), last[index][1, :, first:].astype(F32)], 1
        )
    products = gate_out[...] * w_gate[...].astype(F32) + up_out[...] * w_up[...].astype(F32)
    gain_out[...] = gain_row(products, gain[...])


def unpack_input_kernel(
    place, own, other, w_query, w_key, w_value, gain, query_out, key_out, value_out, gain_out
):
    me = place[0]
    half = own.shape[0]
    key_at = QUERY_WIDTH + KEY_WIDTH
    for side, source in ((me, own), (1 - me, other)):
        at = span(side, half)
        wide = source[...].astype(F32)
        query_out[at, :] = wide[:, :QUERY_WIDTH]
        key_out[at, :] = wide[:, QUERY_WIDTH:key_at]
        value_out[at, :] = wide[:, key_at:]
    products = jnp.sum(query_out[...] * w_query[...].astype(F32), axis=1, keepdims=True)
    products += jnp.sum(key_out[...] * w_key[...].astype(F32), axis=1, keepdims=True)
    products += jnp.sum(value_out[...] * w_value[...].astype(F32), axis=1, keepdims=True)
    gain_out[...] = gain_row(products, gain[...])


def call(kernel, out, scratch, flops, exps, args, name, limit, aliases=None):
    shapes = [jax.ShapeDtypeStruct(s, d) for s, d in out]
    moved = sum(a.size * a.dtype.itemsize for a in args[1:]) + sum(
        s.size * s.dtype.itemsize for s in shapes
    )
    in_specs = [pl.BlockSpec(memory_space=pltpu.SMEM)] + [
        pl.BlockSpec(memory_space=pltpu.VMEM)
    ] * (len(args) - 1)
    return pl.pallas_call(
        kernel,
        out_shape=shapes,
        in_specs=in_specs,
        out_specs=[pl.BlockSpec(memory_space=pltpu.VMEM)] * len(shapes),
        scratch_shapes=[pltpu.VMEM(s, d) for s, d in scratch],
        input_output_aliases=aliases or {},
        compiler_params=pltpu.CompilerParams(vmem_limit_bytes=limit * MEBI),
        cost_estimate=pl.CostEstimate(
            flops=flops, bytes_accessed=moved if flops else 1024, transcendentals=exps
        ),
        name=name,
    )(*args)


def attend_back(group, qkv_t, log_total, attended_t, grad_t, cosine, sine):
    sequence = qkv_t.shape[1]
    group_width = REPEAT * HEAD_SIZE

    def rows_of(size, index):
        return pl.BlockSpec((size, sequence), lambda step: (index, 0))

    flops = 5 * REPEAT * sequence * sequence * HEAD_SIZE * 2
    return pl.pallas_call(
        attend_back_kernel,
        grid=(1,),
        out_shape=[
            jax.ShapeDtypeStruct((group_width, sequence), BF16),
            jax.ShapeDtypeStruct((HEAD_SIZE, sequence), BF16),
            jax.ShapeDtypeStruct((HEAD_SIZE, sequence), BF16),
        ],
        in_specs=[
            rows_of(group_width, group),
            rows_of(HEAD_SIZE, QUERY_HEADS + group),
            rows_of(HEAD_SIZE, ROTATED + group),
            pl.BlockSpec((1, 8, sequence), lambda step: (group, 0, 0)),
            rows_of(group_width, group),
            rows_of(group_width, group),
            rows_of(HALF, 0),
            rows_of(HALF, 0),
        ],
        out_specs=[rows_of(group_width, 0), rows_of(HEAD_SIZE, 0), rows_of(HEAD_SIZE, 0)],
        scratch_shapes=[
            pltpu.VMEM((sequence, HEAD_SIZE), BF16),
            pltpu.VMEM((sequence, HEAD_SIZE), BF16),
            pltpu.VMEM((sequence, HEAD_SIZE), F32),
            pltpu.VMEM((sequence, HEAD_SIZE), F32),
        ],
        compiler_params=pltpu.CompilerParams(vmem_limit_bytes=16 * MEBI),
        cost_estimate=pl.CostEstimate(
            flops=flops, bytes_accessed=4_000_000, transcendentals=REPEAT * sequence * sequence
        ),
        name="attend_back",
    )(qkv_t, qkv_t, qkv_t, log_total, attended_t, grad_t, cosine, sine)


def across(tensor, bit):
    return lax.ppermute(tensor, "fsdp", [(i, i ^ bit) for i in range(4)])


def over_context(tensor):
    return lax.ppermute(tensor, "ctx", [(0, 1), (1, 0)])


def after(tensor, *done):
    return lax.optimization_barrier((tensor, *done))[0]


def together(*values):
    return lax.optimization_barrier(values)


def along(tensor, bit):
    size = lax.axis_size("dp")
    return lax.ppermute(tensor, "dp", [(i, i ^ bit) for i in range(size)])


def whole_sequences(
    tokens, norm1_gain, w_query, w_key, w_value, w_out, norm2_gain, w_gate, w_up, w_down, out_grad
):
    half_rows, width = tokens.shape[1:]
    sequence = 2 * half_rows
    rows = w_query.shape[0]
    down_rows = w_down.shape[0]
    hidden_width = w_gate.shape[1]
    part = 128
    me = lax.axis_index("ctx")
    line = lax.axis_index("dp")
    shard = lax.axis_index("fsdp")
    place = jnp.stack([me, shard, line & 1, me]).astype(jnp.int32)
    tokens = jnp.swapaxes(tokens, 1, 2)
    out_grad = jnp.swapaxes(out_grad, 1, 2)

    tokens_send = lax.dynamic_index_in_dim(tokens, 1 - me, 0, False)
    tokens_theirs = over_context(tokens_send)
    gain_rows = jnp.stack(together(norm1_gain, norm2_gain, tokens_send)[:2])
    gains_own = jnp.pad(gain_rows, ((0, GAIN_ROWS - 2), (0, TILE - rows)))
    (packed,) = call(
        pack_input_kernel,
        [((rows + GAIN_ROWS, PACKED), BF16)],
        [],
        0,
        0,
        (place, w_query, w_key, w_value, gains_own),
        "pack_input",
        16,
    )
    packed_y = across(packed, 2)
    packed_core = across(packed, 1)
    dy_theirs = over_context(lax.dynamic_index_in_dim(out_grad, 1 - me, 0, False))
    chunks = call(
        pack_kernel,
        [((rows, 12 * part + (0 if index else QUERY_WIDTH)), BF16) for index in range(3)],
        [],
        0,
        0,
        (place, w_gate, w_up, w_down.T, after(w_out, packed)),
        "pack",
        16,
    )
    cosine, sine = rope_tables(jnp.arange(sequence, dtype=jnp.int32), HEAD_SIZE)
    *chunks, _, cosine, sine, place = together(*chunks, packed, cosine.T, sine.T, place)
    packed_y, tokens_theirs = together(packed_y, tokens_theirs)
    packed_both = across(packed_y, 1)
    chunks_y = [across(chunk, 2) for chunk in chunks]
    chunks_core = [across(chunk, 1) for chunk in chunks]

    pairs = sequence * sequence
    x_seq, normed, packed_all, gains, qkv_t, log_total, attended_t = call(
        attend_kernel,
        [
            ((width, sequence), BF16),
            ((width, sequence), BF16),
            ((width, PACKED), BF16),
            ((width, 128), F32),
            ((USED, sequence), BF16),
            ((KEY_VALUE_HEADS, 8, sequence), F32),
            ((QUERY_WIDTH, sequence), BF16),
        ],
        [((PACKED, width), BF16), ((KEY_VALUE_HEADS, sequence, HEAD_SIZE), BF16)],
        2 * sequence * width * PACKED + 4 * QUERY_WIDTH * pairs,
        QUERY_HEADS * pairs,
        (place, tokens, tokens_theirs, packed, packed_y, packed_core, packed_both, cosine, sine),
        "attend",
        20,
    )

    natural, turned = ((width, 4 * part), BF16), ((4 * part, width), BF16)
    row, wide_row = ((width, sequence), BF16), ((4 * part, sequence), BF16)
    row_sum = ((width, sequence), F32)
    share = ((2, 2, 2, rows // 2, 6 * part), BF16)
    last_share = ((2, 2, 2, rows // 2, 6 * part + QUERY_WIDTH // 2), BF16)
    chunk_scratch = [
        natural,
        natural,
        natural,
        turned,
        turned,
        turned,
        wide_row,
        wide_row,
        wide_row,
        ((width, 4 * part), F32),
    ]
    flops = 2 * sequence * width * 9 * 4 * part
    exps = sequence * 4 * part

    first_y, second_y, third_y = chunks_y
    first_y, second_y, attended_t, dy_theirs = together(first_y, second_y, attended_t, dy_theirs)
    pieces = (chunks[0], first_y, chunks_core[0], across(first_y, 1))
    second_both = across(second_y, 1)
    middle, normed2, scales, dy, w_out_all, out_sum, grad_sum, keep0, send0 = call(
        first_chunk_kernel,
        [
            row_sum,
            row,
            ((8, sequence), F32),
            row,
            ((QUERY_WIDTH, width), BF16),
            row_sum,
            row_sum,
            share,
            share,
        ],
        [((width, QUERY_WIDTH), BF16), *chunk_scratch],
        flops + 2 * sequence * width * QUERY_WIDTH,
        exps,
        (place, x_seq, attended_t, out_grad, dy_theirs, gains, *pieces),
        "first_chunk",
        26,
    )

    def combine(*items):
        kinds = tuple(item[0] for item in items)
        args = [tensor for item in items for tensor in item[1:]]
        out = []
        for kind, tensor, _ in items:
            if kind == "order":
                out.append(((2, *tensor.shape), BF16))
            elif kind == "pair":
                out += [(tensor.shape[1:], BF16)] * 2
            else:
                out.append((tensor.shape, BF16))
        kernel = functools.partial(combine_kernel, kinds)
        return call(kernel, out, [], 0, 0, (place, *args), "combine", 16)

    out_sum, send0, third_y, second_both = together(out_sum, send0, third_y, second_both)
    got0 = across(send0, 1)
    pieces = (chunks[1], second_y, chunks_core[1], second_both)
    third_both = across(third_y, 1)
    out_sum, grad_sum, keep1, send1 = call(
        next_chunk_kernel,
        [row_sum, row_sum, share, share],
        chunk_scratch,
        flops,
        exps,
        (place, normed2, dy, out_sum, grad_sum, *pieces),
        "next_chunk",
        20,
        {3: 0, 4: 1},
    )

    got0, out_sum, send1, third_both = together(got0, out_sum, send1, third_both)
    own0, part0 = combine(("pair", keep0, got0))
    part0, send1, out_sum = together(part0, send1, out_sum)
    got0, got1 = across(part0, 2), across(send1, 1)
    pieces = (chunks[2], third_y, chunks_core[2], third_both)
    out_keep, out_send, middle_grad, grad_t, keep2, send2 = call(
        last_chunk_kernel,
        [
            ((width, half_rows), BF16),
            ((width, half_rows), BF16),
            row_sum,
            ((QUERY_WIDTH, sequence), BF16),
            last_share,
            last_share,
        ],
        [row_sum, row, *chunk_scratch],
        flops + 4 * sequence * width * QUERY_WIDTH,
        exps,
        (
            place,
            normed2,
            dy,
            out_sum,
            grad_sum,
            *pieces,
            attended_t,
            gains,
            middle,
            scales,
            w_out_all,
        ),
        "last_chunk",
        24,
    )

    got0, got1, grad_t, send2, out_send = together(got0, got1, grad_t, send2, out_send)
    own0, part0, own1, part1 = combine(("pair", own0, got0), ("pair", keep1, got1))
    part0, part1, grad_t = together(part0, part1, grad_t)
    def place_halves(keep, name, *got):
        (both,) = call(
            halves_kernel, [((2, *keep.shape), keep.dtype)], [], 0, 0, (place, keep, *got), name, 16
        )
        return jnp.swapaxes(both, 1, 2)

    got0, got1, got2 = over_context(part0), across(part1, 2), across(send2, 1)
    out_theirs = over_context(out_send)

    back_args = (log_total, attended_t, grad_t, cosine, sine)
    grads0 = attend_back(0, qkv_t, *back_args)
    got0, got2, *grads0 = together(got0, got2, *grads0)
    own0, part0, own2, part2 = combine(("pair", own0, got0), ("pair", keep2, got2))
    part0, part2, qkv_t = together(part0, part2, qkv_t)

    got0, got2 = along(part0, 1), across(part2, 2)
    grads1 = attend_back(1, qkv_t, *back_args)
    got0, got1, *grads1 = together(got0, got1, *grads1)
    own0, own1, part1 = combine(("one", own0, got0), ("pair", own1, got1))
    own0, part1, qkv_t = together(own0, part1, qkv_t)

    got0, got1 = along(own0, 2), over_context(part1)
    grads2 = attend_back(2, qkv_t, *back_args)
    got0, got1, got2, out_theirs, *grads2 = together(got0, got1, got2, out_theirs, *grads2)
    own0, own1, part1, own2, part2 = combine(
        ("one", own0, got0), ("pair", own1, got1), ("pair", own2, got2)
    )
    own0, part1, part2, *grads2 = together(own0, part1, part2, *grads2)

    got0, got1, got2 = along(own0, 1), along(part1, 1), over_context(part2)
    keep_w, send_w, joined = call(
        joined_kernel,
        [
            ((2, 2, rows // 2, USED), BF16),
            ((2, 2, rows // 2, USED), BF16),
            ((USED, sequence), BF16),
        ],
        [((width, USED), F32)],
        2 * sequence * width * USED,
        0,
        (place, normed, *grads0, *grads1, *grads2),
        "joined",
        16,
    )
    got_w = across(send_w, 1)
    piece = ((width // 2, half_rows), BF16)
    keep_x, send_low, send_high = call(
        input_kernel,
        [((width, half_rows), F32), piece, piece],
        [((width, sequence), F32)],
        2 * sequence * width * USED,
        sequence,
        (place, x_seq, packed_all, gains, middle_grad, joined),
        "input_side",
        24,
    )
    got_w, got0, got1, got2, send_low, send_high = together(
        got_w, got0, got1, got2, send_low, send_high
    )
    own_w, part_w, own0, own1, own2, part2 = combine(
        ("pair", keep_w, got_w), ("order", own0, got0), ("one", own1, got1), ("pair", own2, got2)
    )
    part_w, own0, own1, part2, send_low, send_high = together(
        part_w, own0, own1, part2, send_low, send_high
    )
    got_w, got1, got2 = across(part_w, 2), along(own1, 2), along(part2, 1)
    low_theirs, other0 = over_context(send_low), over_context(own0)
    output = place_halves(out_keep, "output_halves", out_theirs)

    got_w, got1, got2, low_theirs, output = together(got_w, got1, got2, low_theirs, output)
    own_w, part_w, own1, own2 = combine(
        ("pair", own_w, got_w), ("one", own1, got1), ("one", own2, got2)
    )
    part_w, own1, own2 = together(part_w, own1, own2)
    got_w, got1, got2 = over_context(part_w), along(own1, 1), along(own2, 2)

    got_w, got1, got2, other0 = together(got_w, got1, got2, other0)
    own_w, own1, own2 = combine(("one", own_w, got_w), ("order", own1, got1), ("one", own2, got2))
    own_w, own1, own2, send_high = together(own_w, own1, own2, send_high)
    got_w, got2, other1 = along(own_w, 1), along(own2, 1), over_context(own1)
    high_theirs = over_context(send_high)

    got_w, got2, other1 = together(got_w, got2, other1)
    own_w, own2 = combine(("one", own_w, got_w), ("order", own2, got2))
    own_w, own2, high_theirs = together(own_w, own2, high_theirs)
    got_w, other2 = along(own_w, 2), over_context(own2)
    gradient = place_halves(keep_x, "gradient_halves", low_theirs, high_theirs)

    got_w, gradient = together(got_w, gradient)
    (own_w,) = combine(("one", own_w, got_w))
    own_w, other2 = together(own_w, other2)
    other_w = over_context(own_w)

    gate_sum, up_sum, down_sum, out_sum, gain2_sum = call(
        unpack_kernel,
        [
            ((rows, hidden_width), F32),
            ((rows, hidden_width), F32),
            ((width, down_rows), F32),
            ((rows, width), F32),
            ((1, rows), F32),
        ],
        [],
        0,
        0,
        (place, own0, other0, own1, other1, own2, other2, w_gate, w_up, norm2_gain[None, :]),
        "unpack",
        24,
    )
    gate_sum, other_w = together(gate_sum, other_w)
    query_sum, key_sum, value_sum, gain1_sum = call(
        unpack_input_kernel,
        [
            ((rows, QUERY_WIDTH), F32),
            ((rows, KEY_WIDTH), F32),
            ((rows, KEY_WIDTH), F32),
            ((1, rows), F32),
        ],
        [],
        0,
        0,
        (place, own_w, other_w, w_query, w_key, w_value, norm1_gain[None, :]),
        "unpack_input",
        16,
    )
    return (
        output,
        gradient,
        gain1_sum[0],
        query_sum,
        key_sum,
        value_sum,
        out_sum,
        gain2_sum[0],
        gate_sum,
        up_sum,
        down_sum.T,
    )


def layer_step(tokens, *rest):
    whole = (
        lax.axis_size("ctx") == 2
        and lax.axis_size("fsdp") == 4
        and lax.axis_size("dp") == 4
        and tokens.shape[0] == 2
        and tokens.shape[1] % WIDE_TILE == 0
        and rest[8].shape == (384, 576)
    )
    return (whole_sequences if whole else split_context)(tokens, *rest)


def solution(mesh):
    return jax.shard_map(
        layer_step,
        mesh=mesh,
        in_specs=(
            P(("dp", "fsdp"), "ctx", None),
            P("fsdp"),
            P("fsdp", None),
            P("fsdp", None),
            P("fsdp", None),
            P("fsdp", None),
            P("fsdp"),
            P("fsdp", None),
            P("fsdp", None),
            P("fsdp", None),
            P(("dp", "fsdp"), "ctx", None),
        ),
        out_specs=(
            P(("dp", "fsdp"), "ctx", None),
            P(("dp", "fsdp"), "ctx", None),
            P("fsdp"),
            P("fsdp", None),
            P("fsdp", None),
            P("fsdp", None),
            P("fsdp", None),
            P("fsdp"),
            P("fsdp", None),
            P("fsdp", None),
            P("fsdp", None),
        ),
        check_vma=False,
    )
```

```python
import functools
import math

import jax
import jax.numpy as jnp
from jax import lax
from jax.experimental import pallas as pl
from jax.experimental.pallas import tpu as pltpu
from jax.sharding import PartitionSpec as P

QUERY_HEADS = 9
KEY_VALUE_HEADS = 3
HEAD_SIZE = 64


EPSILON = 1e-05
ROPE_THETA = 100000.0
MASKED = -1e30


def rope_tables(positions, head_width):
    half_size = head_width // 2
    inverse = jnp.exp(
        jnp.arange(half_size, dtype=jnp.float32) * (-2.0 * math.log(ROPE_THETA) / head_width)
    )
    angle = positions.astype(jnp.float32)[:, None] * inverse[None, :]
    return (jnp.cos(angle), jnp.sin(angle))


def rotary_apply(tensor, cosine_table, sine_table):
    half_size = tensor.shape[-1] // 2
    first_half = tensor[..., :half_size]
    second_half = tensor[..., half_size:]
    cosine_table = cosine_table[None, :, None, :]
    sine_table = sine_table[None, :, None, :]
    return jnp.concatenate(
        [
            first_half * cosine_table - second_half * sine_table,
            second_half * cosine_table + first_half * sine_table,
        ],
        -1,
    )


def rotate_back(tensor, cosine_table, sine_table):
    half_size = tensor.shape[-1] // 2
    first_half = tensor[..., :half_size]
    second_half = tensor[..., half_size:]
    cosine_table = cosine_table[None, :, None, :]
    sine_table = sine_table[None, :, None, :]
    return jnp.concatenate(
        [
            first_half * cosine_table + second_half * sine_table,
            second_half * cosine_table - first_half * sine_table,
        ],
        -1,
    )


def rms_scale(tensor):
    return lax.rsqrt(jnp.mean(tensor * tensor, axis=-1, keepdims=True) + EPSILON)


def block_scores(query_block, key_block, query_pos, key_pos):
    scores = (
        jnp.einsum("gqhrd,gkhd->ghrqk", query_block, key_block, preferred_element_type=jnp.float32)
        * 0.125
    )
    visible = key_pos[None, :] <= query_pos[:, None]
    return jnp.where(visible, scores, MASKED)


def split_context(
    tokens, norm1_gain, w_query, w_key, w_value, w_out, norm2_gain, w_gate, w_up, w_down, out_grad
):
    gain1, wq_full, wk_full, wv_full, wo_full, gain2, wg_full, wu_full, wd_full = (
        lax.all_gather(norm1_gain, "fsdp", axis=0, tiled=True),
        lax.all_gather(w_query, "fsdp", axis=0, tiled=True),
        lax.all_gather(w_key, "fsdp", axis=0, tiled=True),
        lax.all_gather(w_value, "fsdp", axis=0, tiled=True),
        lax.all_gather(w_out, "fsdp", axis=0, tiled=True),
        lax.all_gather(norm2_gain, "fsdp", axis=0, tiled=True),
        lax.all_gather(w_gate, "fsdp", axis=0, tiled=True),
        lax.all_gather(w_up, "fsdp", axis=0, tiled=True),
        lax.all_gather(w_down, "fsdp", axis=0, tiled=True),
    )
    query_group_count, local_row_count, model_width = tokens.shape
    repeat_heads = QUERY_HEADS // KEY_VALUE_HEADS
    head_width = HEAD_SIZE
    key_value_width = KEY_VALUE_HEADS * HEAD_SIZE
    query_width = QUERY_HEADS * HEAD_SIZE
    first_row = lax.axis_index("ctx") * local_row_count
    last_row = first_row + local_row_count - 1
    positions = first_row + jnp.arange(local_row_count, dtype=jnp.int32)
    cosine_table, sine_table = rope_tables(positions, head_width)
    gain1f = gain1.astype(jnp.float32)
    gain2f = gain2.astype(jnp.float32)
    inputs = tokens.astype(jnp.float32)
    scale1 = rms_scale(inputs)
    normed1 = (inputs * scale1 * gain1f).astype(jnp.bfloat16)
    query_before_rotation = jnp.einsum(
        "gsd,de->gse", normed1, wq_full, preferred_element_type=jnp.float32
    )
    key_before_rotation = jnp.einsum(
        "gsd,de->gse", normed1, wk_full, preferred_element_type=jnp.float32
    )
    value_projected = jnp.einsum(
        "gsd,de->gse", normed1, wv_full, preferred_element_type=jnp.float32
    )
    query_matrix = rotary_apply(
        query_before_rotation.reshape(query_group_count, local_row_count, QUERY_HEADS, head_width),
        cosine_table,
        sine_table,
    ).astype(jnp.bfloat16)
    query_matrix = query_matrix.reshape(
        query_group_count, local_row_count, KEY_VALUE_HEADS, repeat_heads, head_width
    )
    key_local = rotary_apply(
        key_before_rotation.reshape(
            query_group_count, local_row_count, KEY_VALUE_HEADS, head_width
        ),
        cosine_table,
        sine_table,
    ).astype(jnp.bfloat16)
    local_value_rows = value_projected.astype(jnp.bfloat16)
    collected_keys, collected_values = (
        lax.all_gather(
            key_local.reshape(query_group_count, local_row_count, key_value_width),
            "ctx",
            axis=1,
            tiled=True,
        ),
        lax.all_gather(local_value_rows, "ctx", axis=1, tiled=True),
    )
    sequence_length = collected_keys.shape[1]
    every_key_row = collected_keys.reshape(
        query_group_count, sequence_length, KEY_VALUE_HEADS, head_width
    )
    every_value_row = collected_values.reshape(
        query_group_count, sequence_length, KEY_VALUE_HEADS, head_width
    )
    local_value_rows = local_value_rows.reshape(
        query_group_count, local_row_count, KEY_VALUE_HEADS, head_width
    )
    key_span = min(sequence_length, 512)
    block_total = last_row // key_span + 1

    def key_slices(step_index):
        first_key = step_index * key_span
        key_block = lax.dynamic_slice_in_dim(every_key_row, first_key, key_span, 1)
        value_block = lax.dynamic_slice_in_dim(every_value_row, first_key, key_span, 1)
        key_pos = first_key + jnp.arange(key_span, dtype=jnp.int32)
        return (key_block, value_block, key_pos)

    def stats_step(step_index, running):
        row_max, row_sum = running
        key_block, value_block, key_pos = key_slices(step_index)
        scores = block_scores(query_matrix, key_block, positions, key_pos)
        new_max = jnp.maximum(row_max, jnp.max(scores, axis=-1))
        row_sum = row_sum * jnp.exp(row_max - new_max) + jnp.sum(
            jnp.exp(scores - new_max[..., None]), axis=-1
        )
        return (new_max, row_sum)

    statistics_shape = (query_group_count, KEY_VALUE_HEADS, repeat_heads, local_row_count)
    row_max, row_sum = lax.fori_loop(
        0,
        block_total,
        stats_step,
        (jnp.full(statistics_shape, MASKED, jnp.float32), jnp.zeros(statistics_shape, jnp.float32)),
    )
    log_total = row_max + jnp.log(row_sum)

    def mix_step(step_index, running):
        key_block, value_block, key_pos = key_slices(step_index)
        scores = block_scores(query_matrix, key_block, positions, key_pos)
        probs = jnp.exp(scores - log_total[..., None]).astype(jnp.bfloat16)
        return running + jnp.einsum(
            "ghrqk,gkhd->gqhrd", probs, value_block, preferred_element_type=jnp.float32
        )

    attended_full = lax.fori_loop(
        0,
        block_total,
        mix_step,
        jnp.zeros(
            (query_group_count, local_row_count, KEY_VALUE_HEADS, repeat_heads, head_width),
            jnp.float32,
        ),
    )
    attended = attended_full.astype(jnp.bfloat16).reshape(
        query_group_count, local_row_count, query_width
    )
    branch = jnp.einsum("gse,ed->gsd", attended, wo_full, preferred_element_type=jnp.float32)
    middle = inputs + branch
    scale2 = rms_scale(middle)
    normed2 = (middle * scale2 * gain2f).astype(jnp.bfloat16)
    gate_act = jnp.einsum("gsd,df->gsf", normed2, wg_full, preferred_element_type=jnp.float32)
    up_act = jnp.einsum("gsd,df->gsf", normed2, wu_full, preferred_element_type=jnp.float32)
    gate_sig = jax.nn.sigmoid(gate_act)
    gate_silu = gate_act * gate_sig
    hidden = (gate_silu * up_act).astype(jnp.bfloat16)
    mlp_out = jnp.einsum("gsf,fd->gsd", hidden, wd_full, preferred_element_type=jnp.float32)
    output = (middle + mlp_out).astype(jnp.bfloat16)
    out_float = out_grad.astype(jnp.float32)
    grad_down = jnp.einsum("gsf,gsd->fd", hidden, out_grad, preferred_element_type=jnp.float32)
    hidden_grad = jnp.einsum("gsd,fd->gsf", out_grad, wd_full, preferred_element_type=jnp.float32)
    gate_grad = (hidden_grad * up_act * gate_sig * (1.0 + gate_act * (1.0 - gate_sig))).astype(
        jnp.bfloat16
    )
    up_grad = (hidden_grad * gate_silu).astype(jnp.bfloat16)
    grad_gate = jnp.einsum("gsd,gsf->df", normed2, gate_grad, preferred_element_type=jnp.float32)
    grad_up = jnp.einsum("gsd,gsf->df", normed2, up_grad, preferred_element_type=jnp.float32)
    normed2_grad = jnp.einsum("gsf,df->gsd", gate_grad, wg_full, preferred_element_type=jnp.float32)
    normed2_grad = normed2_grad + jnp.einsum(
        "gsf,df->gsd", up_grad, wu_full, preferred_element_type=jnp.float32
    )
    grad_gain2 = jnp.sum(normed2_grad * middle * scale2, axis=(0, 1))
    scaled2 = gain2f * normed2_grad
    middle_grad = (
        out_float
        + scale2 * scaled2
        - middle * scale2**3 * jnp.mean(scaled2 * middle, axis=-1, keepdims=True)
    )
    branch_grad = middle_grad.astype(jnp.bfloat16)
    grad_out = jnp.einsum("gse,gsd->ed", attended, branch_grad, preferred_element_type=jnp.float32)
    attended_output_gradient = jnp.einsum(
        "gsd,ed->gse", branch_grad, wo_full, preferred_element_type=jnp.float32
    ).astype(jnp.bfloat16)
    attention_gradient = attended_output_gradient.reshape(
        query_group_count, local_row_count, KEY_VALUE_HEADS, repeat_heads, head_width
    )
    delta = jnp.sum(attention_gradient.astype(jnp.float32) * attended_full, axis=-1).transpose(
        0, 2, 3, 1
    )

    def query_grad_step(step_index, running):
        key_block, value_block, key_pos = key_slices(step_index)
        scores = block_scores(query_matrix, key_block, positions, key_pos)
        probs = jnp.exp(scores - log_total[..., None])
        dprob = jnp.einsum(
            "gqhrd,gkhd->ghrqk", attention_gradient, value_block, preferred_element_type=jnp.float32
        )
        score_grad = (probs * (dprob - delta[..., None])).astype(jnp.bfloat16)
        return running + jnp.einsum(
            "ghrqk,gkhd->gqhrd", score_grad, key_block, preferred_element_type=jnp.float32
        )

    query_grad = (
        lax.fori_loop(
            0,
            block_total,
            query_grad_step,
            jnp.zeros(
                (query_group_count, local_row_count, KEY_VALUE_HEADS, repeat_heads, head_width),
                jnp.float32,
            ),
        )
        * 0.125
    )
    row_total = local_row_count * lax.axis_size("ctx")
    term_span = math.gcd(row_total, key_span)

    def key_block_term(step_index):
        first_key = step_index * term_span
        key_block = lax.dynamic_slice_in_dim(every_key_row, first_key, term_span, 1)
        value_block = lax.dynamic_slice_in_dim(every_value_row, first_key, term_span, 1)
        key_pos = first_key + jnp.arange(term_span, dtype=jnp.int32)

        def compute_term(unused):
            scores = block_scores(query_matrix, key_block, positions, key_pos)
            probs = jnp.exp(scores - log_total[..., None])
            dprob = jnp.einsum(
                "gqhrd,gkhd->ghrqk",
                attention_gradient,
                value_block,
                preferred_element_type=jnp.float32,
            )
            score_grad = (probs * (dprob - delta[..., None])).astype(jnp.bfloat16)
            key_term = (
                jnp.einsum(
                    "ghrqk,gqhrd->kghd",
                    score_grad,
                    query_matrix,
                    preferred_element_type=jnp.float32,
                )
                * 0.125
            )
            value_term = jnp.einsum(
                "ghrqk,gqhrd->kghd",
                probs.astype(jnp.bfloat16),
                attention_gradient,
                preferred_element_type=jnp.float32,
            )
            return jnp.concatenate(
                [
                    key_term.reshape(term_span, query_group_count, key_value_width),
                    value_term.reshape(term_span, query_group_count, key_value_width),
                ],
                -1,
            )

        def empty_term(unused):
            return jnp.zeros((term_span, query_group_count, 2 * key_value_width), jnp.float32)

        return lax.cond(first_key <= last_row, compute_term, empty_term, 0)

    terms = lax.map(key_block_term, jnp.arange(row_total // term_span, dtype=jnp.int32))
    paired_gradients = (
        lax.psum_scatter(
            terms.reshape(row_total, query_group_count, 2 * key_value_width).astype(jnp.bfloat16),
            "ctx",
            scatter_dimension=0,
            tiled=True,
        )
        .astype(jnp.float32)
        .transpose(1, 0, 2)
    )
    key_gradient = paired_gradients[..., :key_value_width].reshape(
        query_group_count, local_row_count, KEY_VALUE_HEADS, head_width
    )
    value_gradient = paired_gradients[..., key_value_width:].reshape(
        query_group_count, local_row_count, KEY_VALUE_HEADS, head_width
    )
    query_pre_grad = rotate_back(
        query_grad.reshape(query_group_count, local_row_count, QUERY_HEADS, head_width),
        cosine_table,
        sine_table,
    )
    query_pre_grad = query_pre_grad.astype(jnp.bfloat16).reshape(
        query_group_count, local_row_count, query_width
    )
    key_pre_grad = (
        rotate_back(key_gradient, cosine_table, sine_table)
        .astype(jnp.bfloat16)
        .reshape(query_group_count, local_row_count, key_value_width)
    )
    value_pre_grad = value_gradient.astype(jnp.bfloat16).reshape(
        query_group_count, local_row_count, key_value_width
    )
    grad_query = jnp.einsum(
        "gsd,gse->de", normed1, query_pre_grad, preferred_element_type=jnp.float32
    )
    grad_key = jnp.einsum("gsd,gse->de", normed1, key_pre_grad, preferred_element_type=jnp.float32)
    grad_value = jnp.einsum(
        "gsd,gse->de", normed1, value_pre_grad, preferred_element_type=jnp.float32
    )
    normed1_grad = jnp.einsum(
        "gse,de->gsd", query_pre_grad, wq_full, preferred_element_type=jnp.float32
    )
    normed1_grad = normed1_grad + jnp.einsum(
        "gse,de->gsd", key_pre_grad, wk_full, preferred_element_type=jnp.float32
    )
    normed1_grad = normed1_grad + jnp.einsum(
        "gse,de->gsd", value_pre_grad, wv_full, preferred_element_type=jnp.float32
    )
    grad_gain1 = jnp.sum(normed1_grad * inputs * scale1, axis=(0, 1))
    scaled1 = gain1f * normed1_grad
    input_grad = (
        middle_grad
        + scale1 * scaled1
        - inputs * scale1**3 * jnp.mean(scaled1 * inputs, axis=-1, keepdims=True)
    )
    totals = lax.psum(
        (
            grad_gain1,
            grad_query,
            grad_key,
            grad_value,
            grad_out,
            grad_gain2,
            grad_gate,
            grad_up,
            grad_down,
        ),
        ("dp", "ctx", "fsdp"),
    )
    owner = lax.axis_index("fsdp")
    shards = (norm1_gain, w_query, w_key, w_value, w_out, norm2_gain, w_gate, w_up, w_down)
    shares = tuple(
        (
            lax.dynamic_slice_in_dim(summed, owner * shard.shape[0], shard.shape[0], 0)
            for summed, shard in zip(totals, shards)
        )
    )
    return (
        output,
        input_grad,
        shares[0],
        shares[1],
        shares[2],
        shares[3],
        shares[4],
        shares[5],
        shares[6],
        shares[7],
        shares[8],
    )


WIDTH = 576
QUERY_WIDTH = QUERY_HEADS * HEAD_SIZE
KEY_WIDTH = KEY_VALUE_HEADS * HEAD_SIZE
ROTATED = QUERY_HEADS + KEY_VALUE_HEADS
REPEAT = QUERY_HEADS // KEY_VALUE_HEADS
HALF = HEAD_SIZE // 2
USED = QUERY_WIDTH + 2 * KEY_WIDTH
PACKED = USED + 64
GAIN_ROWS = 16
TILE = 256
WIDE_TILE = 512
MEBI = 1024 * 1024
F32 = jnp.float32
BF16 = jnp.bfloat16


def mm(a, b):
    return jnp.dot(a, b, preferred_element_type=F32)


def mm_nt(a, b):
    return lax.dot_general(a, b, (((1,), (1,)), ((), ())), preferred_element_type=F32)


def flip(tensor):
    return tensor.astype(F32).T.astype(tensor.dtype)


def span(index, size, step=None):
    step = size if step is None else step
    return pl.ds(pl.multiple_of(index * step, step), size)


def flip_blocks(target, source, block):
    def one(step, carry):
        at = span(step, block)
        target[at, :] = flip(source[:, at])
        return carry

    lax.fori_loop(0, source.shape[1] // block, one, 0)


def column_scale(tensor):
    return lax.rsqrt(jnp.mean(tensor * tensor, axis=0, keepdims=True) + EPSILON)


def sigmoid(tensor):
    return 0.5 * jnp.tanh(0.5 * tensor) + 0.5


def causal_last(scores, tile):
    shape = (TILE, REPEAT * TILE)
    visible = lax.broadcasted_iota(jnp.int32, shape, 0) <= (
        lax.broadcasted_iota(jnp.int32, shape, 1) & (TILE - 1)
    )
    last = jnp.where(visible, scores[tile * TILE :, :], MASKED)
    return last if tile == 0 else jnp.concatenate([scores[: tile * TILE, :], last], 0)


def attend_kernel(
    place,
    tokens,
    theirs,
    w_own,
    w_y,
    w_core,
    w_both,
    cosine,
    sine,
    x_seq,
    normed,
    packed,
    gains,
    qkv_t,
    log_total,
    attended_t,
    packed_t,
    key_rows,
):
    me, shard = place[0], place[1]
    half_rows = theirs.shape[1]
    sequence = 2 * half_rows
    x_seq[:, span(me, half_rows)] = tokens[me]
    x_seq[:, span(1 - me, half_rows)] = theirs[...]
    rows = packed.shape[0] // 4
    for bits, piece in ((0, w_own), (2, w_y), (1, w_core), (3, w_both)):
        at = span(shard ^ bits, rows)
        packed[at, :] = piece[:rows, :]
        gains[at, :GAIN_ROWS] = piece[rows:, :TILE].astype(F32).T[:rows, :]
    flip_blocks(packed_t, packed, TILE)
    gain1 = gains[:, :1]

    def project(step, carry):
        at = span(step, WIDE_TILE)
        x = x_seq[:, at].astype(F32)
        normed_tile = (x * column_scale(x) * gain1).astype(BF16)
        normed[:, at] = normed_tile
        turned = mm(packed_t[:USED, :], normed_tile)
        cos, sin = cosine[:, at], sine[:, at]
        for head in range(ROTATED):
            a = turned[head * HEAD_SIZE : head * HEAD_SIZE + HALF, :]
            b = turned[head * HEAD_SIZE + HALF : (head + 1) * HEAD_SIZE, :]
            both = jnp.concatenate([a * cos - b * sin, b * cos + a * sin], 0)
            if head < QUERY_HEADS:
                both = both * 0.125
            else:
                key_rows[head - QUERY_HEADS, at, :] = both.T.astype(BF16)
            qkv_t[head * HEAD_SIZE : (head + 1) * HEAD_SIZE, at] = both.astype(BF16)
        qkv_t[ROTATED * HEAD_SIZE :, at] = turned[ROTATED * HEAD_SIZE :, :].astype(BF16)
        return carry

    lax.fori_loop(0, sequence // WIDE_TILE, project, 0)

    def one_group(group, carry):
        value_rows = span(ROTATED + group, HEAD_SIZE)
        for tile in range(sequence // TILE):
            extent = (tile + 1) * TILE
            cols = slice(tile * TILE, extent)
            queries = jnp.concatenate(
                [qkv_t[span(group * REPEAT + r, HEAD_SIZE), cols] for r in range(REPEAT)], 1
            )
            scores = causal_last(mm(key_rows[group, :extent, :], queries), tile)
            top = jnp.max(scores, axis=0, keepdims=True)
            weights = jnp.exp(scores - top)
            total = jnp.sum(weights, axis=0, keepdims=True)
            mixed = mm(qkv_t[value_rows, :extent], weights.astype(BF16))
            mixed = (mixed * (1.0 / total)).astype(BF16)
            logs = top + jnp.log(total)
            for r in range(REPEAT):
                own = slice(r * TILE, (r + 1) * TILE)
                attended_t[span(group * REPEAT + r, HEAD_SIZE), cols] = mixed[:, own]
                log_total[group, r : r + 1, cols] = logs[:, own]
        return carry

    lax.fori_loop(0, KEY_VALUE_HEADS, one_group, 0)


def places(shard, row_bit, keep, send):
    for y_bit in range(2):
        for x_bit in range(2):
            for core_bit, target in ((0, keep), (1, send)):
                yield target, y_bit, x_bit, shard ^ (2 * y_bit + core_bit), row_bit ^ x_bit


def chunk_step(place, pieces, normed, dy, out_sum, grad_sum, keep, send, scratch):
    w_gate, w_up, w_down_t, w_gate_t, w_up_t, w_down, hidden, gate_grad, up_grad, total = scratch
    row_bit, shard, level = place[3], place[1], place[2]
    rows = pieces[0].shape[0]
    wide = w_gate.shape[1]
    part = wide // 4
    sequence = normed.shape[1]
    for bits, piece in zip((0, 2, 1, 3), pieces):
        at = span(shard ^ bits, rows)
        w_gate[at, :] = piece[:, :wide]
        w_up[at, :] = piece[:, wide : 2 * wide]
        for block in range(4):
            first = 2 * wide + block * part
            w_down_t[block * rows : (block + 1) * rows, span(shard ^ bits, part)] = piece[
                :, first : first + part
            ]
    w_gate_t[...] = flip(w_gate[...])
    w_up_t[...] = flip(w_up[...])
    w_down[...] = flip(w_down_t[...])
    for first in range(0, sequence, WIDE_TILE):
        at = slice(first, first + WIDE_TILE)
        gate = mm(w_gate_t[...], normed[:, at])
        up = mm(w_up_t[...], normed[:, at])
        hidden_grad = mm(w_down[...], dy[:, at])
        sig = sigmoid(gate)
        silu = gate * sig
        hidden_tile = (silu * up).astype(BF16)
        gate_tile = (hidden_grad * up * (sig + silu * (1.0 - sig))).astype(BF16)
        up_tile = (hidden_grad * silu).astype(BF16)
        hidden[:, at] = hidden_tile
        gate_grad[:, at] = gate_tile
        up_grad[:, at] = up_tile
        out_sum[:, at] += mm(w_down_t[...], hidden_tile)
        grad_sum[:, at] += mm(w_gate[...], gate_tile) + mm(w_up[...], up_tile)
    half = rows // 2
    middle = wide // 2
    for grads, moves in (
        (gate_grad, ((0, 0, 0, wide),)),
        (up_grad, ((0, 0, wide, middle), (1, middle, 0, middle))),
    ):
        total[...] = mm_nt(normed[...], grads[...])
        for target, y_bit, x_bit, owner, side in places(shard, place[3], keep, send):
            at = span(owner * 2 + side, half)
            for z_half, first, to, count in moves:
                target[y_bit, x_bit, level ^ z_half, :, to : to + count] = total[
                    at, first : first + count
                ].astype(BF16)
    total[...] = mm_nt(dy[...], hidden[...])
    for target, y_bit, x_bit, owner, side in places(shard, place[3], keep, send):
        for block in range(4):
            at = pl.ds(pl.multiple_of(block * rows + side * half, 8), half)
            to = middle + block * part
            target[y_bit, x_bit, level ^ 1, :, to : to + part] = total[
                at, span(owner, part)
            ].astype(BF16)


def first_chunk_kernel(
    place,
    x_seq,
    attended_t,
    out_grad,
    dy_theirs,
    gains,
    p_own,
    p_y,
    p_core,
    p_both,
    middle,
    normed,
    scales,
    dy,
    w_out,
    out_sum,
    grad_sum,
    keep,
    send,
    w_out_t,
    *scratch,
):
    me, shard = place[0], place[1]
    half_rows = dy_theirs.shape[1]
    sequence = 2 * half_rows
    dy[:, span(me, half_rows)] = out_grad[me]
    dy[:, span(1 - me, half_rows)] = dy_theirs[...]
    pieces = (p_own, p_y, p_core, p_both)
    rows = p_own.shape[0]
    packed_width = p_own.shape[1] - QUERY_WIDTH
    for bits, piece in zip((0, 2, 1, 3), pieces):
        w_out[span(shard ^ bits, rows), :] = piece[:, packed_width:]
    w_out_t[...] = flip(w_out[...])
    gain2 = gains[:, 1:2]
    for first in range(0, sequence, WIDE_TILE):
        at = slice(first, first + WIDE_TILE)
        mid = x_seq[:, at].astype(F32) + mm(w_out_t[...], attended_t[:, at])
        middle[:, at] = mid
        out_sum[:, at] = mid
        grad_sum[:, at] = jnp.zeros_like(mid)
        scale = column_scale(mid)
        scales[:, at] = jnp.broadcast_to(scale, (8, WIDE_TILE))
        normed[:, at] = (mid * scale * gain2).astype(BF16)
    chunk_step(place, pieces, normed, dy, out_sum, grad_sum, keep, send, scratch)


def next_chunk_kernel(
    place, normed, dy, out_in, grad_in, p_own, p_y, p_core, p_both, out_sum, grad_sum, keep, send, *scratch
):
    out_sum[...] = out_in[...]
    grad_sum[...] = grad_in[...]
    pieces = (p_own, p_y, p_core, p_both)
    chunk_step(place, pieces, normed, dy, out_sum, grad_sum, keep, send, scratch)


def last_chunk_kernel(
    place,
    normed,
    dy,
    out_in,
    grad_in,
    p_own,
    p_y,
    p_core,
    p_both,
    attended_t,
    gains,
    middle,
    scales,
    w_out,
    out_keep,
    out_send,
    middle_grad,
    attended_grad_t,
    keep,
    send,
    out_sum,
    branch_grad,
    *scratch,
):
    me, shard = place[0], place[1]
    half_rows = out_keep.shape[1]
    sequence = 2 * half_rows
    grad_sum = middle_grad
    out_sum[...] = out_in[...]
    grad_sum[...] = grad_in[...]
    pieces = (p_own, p_y, p_core, p_both)
    chunk_step(place, pieces, normed, dy, out_sum, grad_sum, keep, send, scratch)
    gain2 = gains[:, 1:2]
    for first in range(0, sequence, WIDE_TILE):
        at = slice(first, first + WIDE_TILE)
        output = out_sum[:, at].astype(BF16)
        block, start = divmod(first, half_rows)
        block_cols = slice(start, start + WIDE_TILE)

        @pl.when(me == block)
        def _():
            out_keep[:, block_cols] = output

        @pl.when(me != block)
        def _():
            out_send[:, block_cols] = output

        mid = middle[:, at]
        scale = scales[0:1, at]
        scaled = grad_sum[:, at] * gain2
        back = (
            dy[:, at].astype(F32)
            + scale * scaled
            - mid * (scale * scale * scale) * jnp.mean(scaled * mid, axis=0, keepdims=True)
        )
        middle_grad[:, at] = back
        branch = back.astype(BF16)
        branch_grad[:, at] = branch
        attended_grad_t[:, at] = mm(w_out[...], branch).astype(BF16)
    total = scratch[-1]
    half = p_own.shape[0] // 2
    columns = QUERY_WIDTH // 2
    first_to = keep.shape[4] - columns
    for start in range(0, QUERY_WIDTH, TILE):
        count = min(TILE, QUERY_WIDTH - start)
        total[:, :count] = mm_nt(attended_t[...], branch_grad[start : start + count, :])
        for target, y_bit, x_bit, owner, side in places(shard, place[3], keep, send):
            at = span(owner * 2 + side, half)
            for z_half in range(2):
                low = max(start, z_half * columns)
                high = min(start + count, (z_half + 1) * columns)
                if low < high:
                    to = first_to + low - z_half * columns
                    target[y_bit, x_bit, place[2] ^ z_half, :, to : to + high - low] = total[
                        at, low - start : high - start
                    ].astype(BF16)


def attend_back_kernel(
    queries_t,
    keys_t,
    values_t,
    log_total,
    attended_t,
    grad_t,
    cosine,
    sine,
    dq_out,
    dk_out,
    dv_out,
    keys,
    values,
    dk,
    dv,
):
    sequence = keys_t.shape[1]
    keys[...] = flip(keys_t[...])
    values[...] = flip(values_t[...])
    dk[...] = jnp.zeros_like(dk)
    dv[...] = jnp.zeros_like(dv)

    def back(a, b, cos, sin):
        return (a * cos + b * sin).astype(BF16), (b * cos - a * sin).astype(BF16)

    for tile in range(sequence // TILE):
        extent = (tile + 1) * TILE
        cols = slice(tile * TILE, extent)
        heads = [slice(r * HEAD_SIZE, (r + 1) * HEAD_SIZE) for r in range(REPEAT)]
        q_t = jnp.concatenate([queries_t[head, cols] for head in heads], 1)
        do_t = jnp.concatenate([grad_t[head, cols] for head in heads], 1)
        mixed = jnp.concatenate([attended_t[head, cols] for head in heads], 1)
        logs = jnp.concatenate([log_total[0, r : r + 1, cols] for r in range(REPEAT)], 1)
        delta = jnp.sum(do_t.astype(F32) * mixed.astype(F32), axis=0, keepdims=True)
        scores = causal_last(mm(keys[:extent, :], q_t), tile)
        probs = jnp.exp(scores - logs)
        dprob = mm(values[:extent, :], do_t)
        score_grad = (probs * (dprob - delta)).astype(BF16)
        dv[:extent, :] += mm(probs.astype(BF16), flip(do_t))
        dk[:extent, :] += mm(score_grad, flip(q_t))
        dq = mm(keys_t[:, :extent], score_grad) * 0.125
        cos, sin = cosine[:, cols], sine[:, cols]
        for r, head in enumerate(heads):
            own = slice(r * TILE, (r + 1) * TILE)
            a, b = back(dq[:HALF, own], dq[HALF:, own], cos, sin)
            dq_out[head.start : head.start + HALF, cols] = a
            dq_out[head.start + HALF : head.stop, cols] = b
    turned = dk[...].T
    a, b = back(turned[:HALF, :], turned[HALF:, :], cosine[...], sine[...])
    dk_out[:HALF, :] = a
    dk_out[HALF:, :] = b
    dv_out[...] = dv[...].T.astype(BF16)


def input_kernel(place, normed, x_seq, packed, gains, middle_grad, *rest):
    heads = rest[: 3 * KEY_VALUE_HEADS]
    keep_w, send_w, keep_x, send_x, joined, grad_seq, total = rest[3 * KEY_VALUE_HEADS :]
    me, shard = place[0], place[1]
    group_width = REPEAT * HEAD_SIZE
    for group in range(KEY_VALUE_HEADS):
        dq, dk, dv = heads[3 * group : 3 * group + 3]
        joined[group * group_width : (group + 1) * group_width, :] = dq[...]
        at = QUERY_WIDTH + group * HEAD_SIZE
        joined[at : at + HEAD_SIZE, :] = dk[...]
        at = QUERY_WIDTH + KEY_WIDTH + group * HEAD_SIZE
        joined[at : at + HEAD_SIZE, :] = dv[...]
    half = keep_w.shape[2]
    for first in range(0, USED, 512):
        cols = slice(first, min(first + 512, USED))
        total[:, cols] = mm_nt(normed[...], joined[cols, :])
    for target, y_bit, x_bit, owner, side in places(shard, me, keep_w, send_w):
        target[y_bit, x_bit] = total[span(owner * 2 + side, half), :].astype(BF16)
    half_rows = keep_x.shape[1]
    sequence = 2 * half_rows
    gain1 = gains[:, :1]
    for first in range(0, sequence, WIDE_TILE):
        at = slice(first, first + WIDE_TILE)
        scaled = mm(packed[:, :USED], joined[:, at]) * gain1
        x = x_seq[:, at].astype(F32)
        scale = column_scale(x)
        grad_seq[:, at] = (
            middle_grad[:, at]
            + scale * scaled
            - x * (scale * scale * scale) * jnp.mean(scaled * x, axis=0, keepdims=True)
        )
    keep_x[...] = grad_seq[:, span(me, half_rows)]
    send_x[...] = grad_seq[:, span(1 - me, half_rows)].astype(BF16)


def pack_input_kernel(place, w_query, w_key, w_value, gains, packed):
    rows = w_query.shape[0]
    packed[:rows, :QUERY_WIDTH] = w_query[...]
    packed[:rows, QUERY_WIDTH : QUERY_WIDTH + KEY_WIDTH] = w_key[...]
    packed[:rows, QUERY_WIDTH + KEY_WIDTH :] = jnp.concatenate(
        [w_value[...].astype(F32), jnp.zeros((rows, PACKED - USED), F32)], 1
    ).astype(BF16)
    packed[rows:, :] = jnp.zeros((GAIN_ROWS, PACKED), BF16)
    packed[rows:, :TILE] = gains[...]


def pack_kernel(place, w_gate, w_up, w_down_t, w_out, *chunks):
    rows = w_gate.shape[0]
    down_rows = w_down_t.shape[1]
    part = 128
    for index, chunk in enumerate(chunks):
        at = index * part
        for i in range(4):
            source = slice(i * down_rows + at, i * down_rows + at + part)
            chunk[:, i * part : (i + 1) * part] = w_gate[:, source]
            chunk[:, (4 + i) * part : (5 + i) * part] = w_up[:, source]
            chunk[:, (8 + i) * part : (9 + i) * part] = w_down_t[
                i * rows : (i + 1) * rows, at : at + part
            ]
    chunks[0][:, 12 * part :] = w_out[...]


def combine_kernel(kinds, place, *refs):
    count = sum(4 if kind == "orders" else 2 for kind in kinds)
    sources, targets = list(refs[:count]), list(refs[count:])
    for kind in kinds:
        a, b = sources.pop(0), sources.pop(0)
        if kind == "orders":
            target = targets.pop(0)
            for i, own, other in ((0, a, b), (1, sources.pop(0), sources.pop(0))):
                target[i, place[2]] = own[...]
                target[i, 1 - place[2]] = other[...]
        elif kind == "order":
            target = targets.pop(0)
            target[place[2]] = a[...]
            target[1 - place[2]] = b[...]
        elif kind == "pair":
            for i in range(2):
                targets.pop(0)[...] = (a[i].astype(F32) + b[i].astype(F32)).astype(BF16)
        else:
            targets.pop(0)[...] = (a[...].astype(F32) + b[...].astype(F32)).astype(BF16)


def halves_kernel(place, keep, *rest):
    target = rest[-1]
    target[place[0]] = keep[...]
    first = 0
    for got in rest[:-1]:
        size = got.shape[0]
        target[1 - place[0], first : first + size] = got[...].astype(target.dtype)
        first += size


def gain_row(products, gain):
    column = jnp.sum(products, axis=1, keepdims=True)
    row = jnp.broadcast_to(column, (column.shape[0], 128)).T[:1, :]
    return row / gain.astype(F32)


def unpack_kernel(place, own, other, own2, other2, w_gate, w_up, gain, *out):
    gate_out, up_out, down_out, out_out, gain_out = out
    me = place[0]
    half = own2.shape[1]
    rows = 2 * half
    part = 128
    down_rows = down_out.shape[1]
    last = (own2, other2)
    for index, sources in enumerate(
        ((own.at[0], own.at[1], own2), (other.at[0], other.at[1], other2))
    ):
        for chunk, source in enumerate(sources):
            side = index ^ me
            at = span(side, half)
            for i in range(4):
                to = slice(i * down_rows + chunk * part, i * down_rows + (chunk + 1) * part)
                gate_out[at, to] = source[0, :, i * part : (i + 1) * part].astype(F32)
                z_half, first = (0, (4 + i) * part) if i < 2 else (1, (i - 2) * part)
                up_out[at, to] = source[z_half, :, first : first + part].astype(F32)
                down_at = pl.ds(pl.multiple_of(i * rows + side * half, 8), half)
                first = (2 + i) * part
                down_out[down_at, chunk * part : (chunk + 1) * part] = source[
                    1, :, first : first + part
                ].astype(F32)
        first = 6 * part
        out_out[span(index ^ me, half), :] = jnp.concatenate(
            [last[index][0, :, first:].astype(F32), last[index][1, :, first:].astype(F32)], 1
        )
    products = gate_out[...] * w_gate[...].astype(F32) + up_out[...] * w_up[...].astype(F32)
    gain_out[...] = gain_row(products, gain[...])


def unpack_input_kernel(
    place, own, other, w_query, w_key, w_value, gain, query_out, key_out, value_out, gain_out
):
    me = place[0]
    half = own.shape[0]
    key_at = QUERY_WIDTH + KEY_WIDTH
    for side, source in ((me, own), (1 - me, other)):
        at = span(side, half)
        wide = source[...].astype(F32)
        query_out[at, :] = wide[:, :QUERY_WIDTH]
        key_out[at, :] = wide[:, QUERY_WIDTH:key_at]
        value_out[at, :] = wide[:, key_at:]
    products = jnp.sum(query_out[...] * w_query[...].astype(F32), axis=1, keepdims=True)
    products += jnp.sum(key_out[...] * w_key[...].astype(F32), axis=1, keepdims=True)
    products += jnp.sum(value_out[...] * w_value[...].astype(F32), axis=1, keepdims=True)
    gain_out[...] = gain_row(products, gain[...])


def call(kernel, out, scratch, flops, exps, args, name, limit, aliases=None):
    shapes = [jax.ShapeDtypeStruct(s, d) for s, d in out]
    moved = sum(a.size * a.dtype.itemsize for a in args[1:]) + sum(
        s.size * s.dtype.itemsize for s in shapes
    )
    in_specs = [pl.BlockSpec(memory_space=pltpu.SMEM)] + [
        pl.BlockSpec(memory_space=pltpu.VMEM)
    ] * (len(args) - 1)
    return pl.pallas_call(
        kernel,
        out_shape=shapes,
        in_specs=in_specs,
        out_specs=[pl.BlockSpec(memory_space=pltpu.VMEM)] * len(shapes),
        scratch_shapes=[pltpu.VMEM(s, d) for s, d in scratch],
        input_output_aliases=aliases or {},
        compiler_params=pltpu.CompilerParams(vmem_limit_bytes=limit * MEBI),
        cost_estimate=pl.CostEstimate(
            flops=flops, bytes_accessed=moved if flops else 1024, transcendentals=exps
        ),
        name=name,
    )(*args)


def attend_back(group, qkv_t, log_total, attended_t, grad_t, cosine, sine):
    sequence = qkv_t.shape[1]
    group_width = REPEAT * HEAD_SIZE

    def rows_of(size, index):
        return pl.BlockSpec((size, sequence), lambda step: (index, 0))

    flops = 5 * REPEAT * sequence * sequence * HEAD_SIZE * 2
    return pl.pallas_call(
        attend_back_kernel,
        grid=(1,),
        out_shape=[
            jax.ShapeDtypeStruct((group_width, sequence), BF16),
            jax.ShapeDtypeStruct((HEAD_SIZE, sequence), BF16),
            jax.ShapeDtypeStruct((HEAD_SIZE, sequence), BF16),
        ],
        in_specs=[
            rows_of(group_width, group),
            rows_of(HEAD_SIZE, QUERY_HEADS + group),
            rows_of(HEAD_SIZE, ROTATED + group),
            pl.BlockSpec((1, 8, sequence), lambda step: (group, 0, 0)),
            rows_of(group_width, group),
            rows_of(group_width, group),
            rows_of(HALF, 0),
            rows_of(HALF, 0),
        ],
        out_specs=[rows_of(group_width, 0), rows_of(HEAD_SIZE, 0), rows_of(HEAD_SIZE, 0)],
        scratch_shapes=[
            pltpu.VMEM((sequence, HEAD_SIZE), BF16),
            pltpu.VMEM((sequence, HEAD_SIZE), BF16),
            pltpu.VMEM((sequence, HEAD_SIZE), F32),
            pltpu.VMEM((sequence, HEAD_SIZE), F32),
        ],
        compiler_params=pltpu.CompilerParams(vmem_limit_bytes=16 * MEBI),
        cost_estimate=pl.CostEstimate(
            flops=flops, bytes_accessed=4_000_000, transcendentals=REPEAT * sequence * sequence
        ),
        name="attend_back",
    )(qkv_t, qkv_t, qkv_t, log_total, attended_t, grad_t, cosine, sine)


def across(tensor, bit):
    return lax.ppermute(tensor, "fsdp", [(i, i ^ bit) for i in range(4)])


def over_context(tensor):
    return lax.ppermute(tensor, "ctx", [(0, 1), (1, 0)])


def after(tensor, *done):
    return lax.optimization_barrier((tensor, *done))[0]


def together(*values):
    return lax.optimization_barrier(values)


def along(tensor, bit):
    size = lax.axis_size("dp")
    return lax.ppermute(tensor, "dp", [(i, i ^ bit) for i in range(size)])


def whole_sequences(
    tokens, norm1_gain, w_query, w_key, w_value, w_out, norm2_gain, w_gate, w_up, w_down, out_grad
):
    half_rows, width = tokens.shape[1:]
    sequence = 2 * half_rows
    rows = w_query.shape[0]
    down_rows = w_down.shape[0]
    hidden_width = w_gate.shape[1]
    part = 128
    me = lax.axis_index("ctx")
    line = lax.axis_index("dp")
    shard = lax.axis_index("fsdp")
    place = jnp.stack([me, shard, line & 1, me]).astype(jnp.int32)
    tokens = jnp.swapaxes(tokens, 1, 2)
    out_grad = jnp.swapaxes(out_grad, 1, 2)

    tokens_send = lax.dynamic_index_in_dim(tokens, 1 - me, 0, False)
    tokens_theirs = over_context(tokens_send)
    gain_rows = jnp.stack(together(norm1_gain, norm2_gain, tokens_send)[:2])
    gains_own = jnp.pad(gain_rows, ((0, GAIN_ROWS - 2), (0, TILE - rows)))
    (packed,) = call(
        pack_input_kernel,
        [((rows + GAIN_ROWS, PACKED), BF16)],
        [],
        0,
        0,
        (place, w_query, w_key, w_value, gains_own),
        "pack_input",
        16,
    )
    packed_y = across(packed, 2)
    packed_core = across(packed, 1)
    dy_theirs = over_context(lax.dynamic_index_in_dim(out_grad, 1 - me, 0, False))
    chunks = call(
        pack_kernel,
        [((rows, 12 * part + (0 if index else QUERY_WIDTH)), BF16) for index in range(3)],
        [],
        0,
        0,
        (place, w_gate, w_up, w_down.T, after(w_out, packed)),
        "pack",
        16,
    )
    cosine, sine = rope_tables(jnp.arange(sequence, dtype=jnp.int32), HEAD_SIZE)
    *chunks, _, cosine, sine, place = together(*chunks, packed, cosine.T, sine.T, place)
    packed_y, tokens_theirs = together(packed_y, tokens_theirs)
    packed_both = across(packed_y, 1)
    chunks_y = [across(chunk, 2) for chunk in chunks]
    chunks_core = [across(chunk, 1) for chunk in chunks]

    pairs = sequence * sequence
    x_seq, normed, packed_all, gains, qkv_t, log_total, attended_t = call(
        attend_kernel,
        [
            ((width, sequence), BF16),
            ((width, sequence), BF16),
            ((width, PACKED), BF16),
            ((width, 128), F32),
            ((USED, sequence), BF16),
            ((KEY_VALUE_HEADS, 8, sequence), F32),
            ((QUERY_WIDTH, sequence), BF16),
        ],
        [((PACKED, width), BF16), ((KEY_VALUE_HEADS, sequence, HEAD_SIZE), BF16)],
        2 * sequence * width * PACKED + 4 * QUERY_WIDTH * pairs,
        QUERY_HEADS * pairs,
        (place, tokens, tokens_theirs, packed, packed_y, packed_core, packed_both, cosine, sine),
        "attend",
        20,
    )

    natural, turned = ((width, 4 * part), BF16), ((4 * part, width), BF16)
    row, wide_row = ((width, sequence), BF16), ((4 * part, sequence), BF16)
    row_sum = ((width, sequence), F32)
    share = ((2, 2, 2, rows // 2, 6 * part), BF16)
    last_share = ((2, 2, 2, rows // 2, 6 * part + QUERY_WIDTH // 2), BF16)
    chunk_scratch = [
        natural,
        natural,
        natural,
        turned,
        turned,
        turned,
        wide_row,
        wide_row,
        wide_row,
        ((width, 4 * part), F32),
    ]
    flops = 2 * sequence * width * 9 * 4 * part
    exps = sequence * 4 * part

    first_y, second_y, third_y = chunks_y
    first_y, second_y, attended_t, dy_theirs = together(first_y, second_y, attended_t, dy_theirs)
    pieces = (chunks[0], first_y, chunks_core[0], across(first_y, 1))
    second_both = across(second_y, 1)
    middle, normed2, scales, dy, w_out_all, out_sum, grad_sum, keep0, send0 = call(
        first_chunk_kernel,
        [
            row_sum,
            row,
            ((8, sequence), F32),
            row,
            ((QUERY_WIDTH, width), BF16),
            row_sum,
            row_sum,
            share,
            share,
        ],
        [((width, QUERY_WIDTH), BF16), *chunk_scratch],
        flops + 2 * sequence * width * QUERY_WIDTH,
        exps,
        (place, x_seq, attended_t, out_grad, dy_theirs, gains, *pieces),
        "first_chunk",
        26,
    )

    def combine(*items):
        kinds = tuple(item[0] for item in items)
        args = [tensor for item in items for tensor in item[1:]]
        out = []
        for kind, tensor, *_ in items:
            if kind == "orders":
                out.append(((2, 2, *tensor.shape), BF16))
            elif kind == "order":
                out.append(((2, *tensor.shape), BF16))
            elif kind == "pair":
                out += [(tensor.shape[1:], BF16)] * 2
            else:
                out.append((tensor.shape, BF16))
        kernel = functools.partial(combine_kernel, kinds)
        return call(kernel, out, [], 0, 0, (place, *args), "combine", 16)

    out_sum, send0, third_y, second_both = together(out_sum, send0, third_y, second_both)
    got0 = across(send0, 1)
    pieces = (chunks[1], second_y, chunks_core[1], second_both)
    third_both = across(third_y, 1)
    out_sum, grad_sum, keep1, send1 = call(
        next_chunk_kernel,
        [row_sum, row_sum, share, share],
        chunk_scratch,
        flops,
        exps,
        (place, normed2, dy, out_sum, grad_sum, *pieces),
        "next_chunk",
        20,
        {3: 0, 4: 1},
    )

    got0, out_sum, send1, third_both = together(got0, out_sum, send1, third_both)
    own0, part0 = combine(("pair", keep0, got0))
    part0, send1, out_sum = together(part0, send1, out_sum)
    got0, got1 = across(part0, 2), across(send1, 1)
    pieces = (chunks[2], third_y, chunks_core[2], third_both)
    out_keep, out_send, middle_grad, grad_t, keep2, send2 = call(
        last_chunk_kernel,
        [
            ((width, half_rows), BF16),
            ((width, half_rows), BF16),
            row_sum,
            ((QUERY_WIDTH, sequence), BF16),
            last_share,
            last_share,
        ],
        [row_sum, row, *chunk_scratch],
        flops + 4 * sequence * width * QUERY_WIDTH,
        exps,
        (
            place,
            normed2,
            dy,
            out_sum,
            grad_sum,
            *pieces,
            attended_t,
            gains,
            middle,
            scales,
            w_out_all,
        ),
        "last_chunk",
        24,
    )

    got0, got1, grad_t, send2, out_send = together(got0, got1, grad_t, send2, out_send)
    own0, part0, own1, part1 = combine(("pair", own0, got0), ("pair", keep1, got1))
    part0, part1, grad_t = together(part0, part1, grad_t)
    def place_halves(keep, name, *got):
        (both,) = call(
            halves_kernel, [((2, *keep.shape), keep.dtype)], [], 0, 0, (place, keep, *got), name, 16
        )
        return jnp.swapaxes(both, 1, 2)

    got0, got1, got2 = over_context(part0), across(part1, 2), across(send2, 1)
    out_theirs = over_context(out_send)

    back_args = (log_total, attended_t, grad_t, cosine, sine)
    grads0 = attend_back(0, qkv_t, *back_args)
    got0, got2, *grads0 = together(got0, got2, *grads0)
    own0, part0, own2, part2 = combine(("pair", own0, got0), ("pair", keep2, got2))
    part0, part2, qkv_t = together(part0, part2, qkv_t)

    got0, got2 = along(part0, 1), across(part2, 2)
    grads1 = attend_back(1, qkv_t, *back_args)
    got0, got1, *grads1 = together(got0, got1, *grads1)
    own0, own1, part1 = combine(("one", own0, got0), ("pair", own1, got1))
    own0, part1, qkv_t = together(own0, part1, qkv_t)

    got0, got1 = along(own0, 2), over_context(part1)
    grads2 = attend_back(2, qkv_t, *back_args)
    got0, got1, got2, out_theirs, *grads2 = together(got0, got1, got2, out_theirs, *grads2)
    own0, own1, part1, own2, part2 = combine(
        ("one", own0, got0), ("pair", own1, got1), ("pair", own2, got2)
    )
    own0, part1, part2, *grads2 = together(own0, part1, part2, *grads2)

    got0, got1, got2 = along(own0, 1), along(part1, 1), over_context(part2)
    keep_w, send_w, keep_x, send_x = call(
        input_kernel,
        [
            ((2, 2, rows // 2, USED), BF16),
            ((2, 2, rows // 2, USED), BF16),
            ((width, half_rows), F32),
            ((width, half_rows), BF16),
        ],
        [((USED, sequence), BF16), ((width, sequence), F32), ((width, USED), F32)],
        4 * sequence * width * USED,
        sequence,
        (
            place,
            normed,
            x_seq,
            packed_all,
            gains,
            middle_grad,
            *grads0,
            *grads1,
            *grads2,
        ),
        "input_side",
        24,
    )
    got0, got1, got2, send_w, send_x = together(got0, got1, got2, send_w, send_x)
    got_w = across(send_w, 1)
    own1, own2, part2 = combine(("one", own1, got1), ("pair", own2, got2))
    got_w, own1, part2, send_x = together(got_w, own1, part2, send_x)
    own_w, part_w = combine(("pair", keep_w, got_w))
    got_w, got1, got2 = across(part_w, 2), along(own1, 2), along(part2, 1)
    x_theirs = over_context(send_x)
    output = place_halves(out_keep, "output_halves", out_theirs)

    got_w, got1, got2, output = together(got_w, got1, got2, output)
    own_w, part_w, own1, own2 = combine(
        ("pair", own_w, got_w), ("one", own1, got1), ("one", own2, got2)
    )
    part_w, own1, own2 = together(part_w, own1, own2)
    got_w, got1, got2 = over_context(part_w), along(own1, 1), along(own2, 2)

    got_w, got1, got2, x_theirs = together(got_w, got1, got2, x_theirs)
    own_w, own, own2 = combine(
        ("one", own_w, got_w), ("orders", own0, got0, own1, got1), ("one", own2, got2)
    )
    own_w, own, own2, x_theirs = together(own_w, own, own2, x_theirs)
    got_w, got2, other = along(own_w, 1), along(own2, 1), over_context(own)
    gradient = place_halves(keep_x, "gradient_halves", x_theirs)

    got_w, got2, gradient = together(got_w, got2, gradient)
    own_w, own2 = combine(("one", own_w, got_w), ("order", own2, got2))
    own_w, own2 = together(own_w, own2)
    got_w, other2 = along(own_w, 2), over_context(own2)

    got_w, other = together(got_w, other)
    (own_w,) = combine(("one", own_w, got_w))
    other_w = over_context(own_w)
    own_w, other2 = together(own_w, other2)

    gate_sum, up_sum, down_sum, out_sum, gain2_sum = call(
        unpack_kernel,
        [
            ((rows, hidden_width), F32),
            ((rows, hidden_width), F32),
            ((width, down_rows), F32),
            ((rows, width), F32),
            ((1, rows), F32),
        ],
        [],
        0,
        0,
        (place, own, other, own2, other2, w_gate, w_up, norm2_gain[None, :]),
        "unpack",
        24,
    )
    gate_sum, other_w = together(gate_sum, other_w)
    query_sum, key_sum, value_sum, gain1_sum = call(
        unpack_input_kernel,
        [
            ((rows, QUERY_WIDTH), F32),
            ((rows, KEY_WIDTH), F32),
            ((rows, KEY_WIDTH), F32),
            ((1, rows), F32),
        ],
        [],
        0,
        0,
        (place, own_w, other_w, w_query, w_key, w_value, norm1_gain[None, :]),
        "unpack_input",
        16,
    )
    return (
        output,
        gradient,
        gain1_sum[0],
        query_sum,
        key_sum,
        value_sum,
        out_sum,
        gain2_sum[0],
        gate_sum,
        up_sum,
        down_sum.T,
    )


def layer_step(tokens, *rest):
    whole = (
        lax.axis_size("ctx") == 2
        and lax.axis_size("fsdp") == 4
        and lax.axis_size("dp") == 4
        and tokens.shape[0] == 2
        and tokens.shape[1] % WIDE_TILE == 0
        and rest[8].shape == (384, 576)
    )
    return (whole_sequences if whole else split_context)(tokens, *rest)


def solution(mesh):
    return jax.shard_map(
        layer_step,
        mesh=mesh,
        in_specs=(
            P(("dp", "fsdp"), "ctx", None),
            P("fsdp"),
            P("fsdp", None),
            P("fsdp", None),
            P("fsdp", None),
            P("fsdp", None),
            P("fsdp"),
            P("fsdp", None),
            P("fsdp", None),
            P("fsdp", None),
            P(("dp", "fsdp"), "ctx", None),
        ),
        out_specs=(
            P(("dp", "fsdp"), "ctx", None),
            P(("dp", "fsdp"), "ctx", None),
            P("fsdp"),
            P("fsdp", None),
            P("fsdp", None),
            P("fsdp", None),
            P("fsdp", None),
            P("fsdp"),
            P("fsdp", None),
            P("fsdp", None),
            P("fsdp", None),
        ),
        check_vma=False,
    )
```

```python
import functools
import math

import jax
import jax.numpy as jnp
from jax import lax
from jax.experimental import pallas as pl
from jax.experimental.pallas import tpu as pltpu
from jax.sharding import PartitionSpec as P

QUERY_HEADS = 9
KEY_VALUE_HEADS = 3
HEAD_SIZE = 64


EPSILON = 1e-05
ROPE_THETA = 100000.0
MASKED = -1e30


def rope_tables(positions, head_width):
    half_size = head_width // 2
    inverse = jnp.exp(
        jnp.arange(half_size, dtype=jnp.float32) * (-2.0 * math.log(ROPE_THETA) / head_width)
    )
    angle = positions.astype(jnp.float32)[:, None] * inverse[None, :]
    return (jnp.cos(angle), jnp.sin(angle))


def rotary_apply(tensor, cosine_table, sine_table):
    half_size = tensor.shape[-1] // 2
    first_half = tensor[..., :half_size]
    second_half = tensor[..., half_size:]
    cosine_table = cosine_table[None, :, None, :]
    sine_table = sine_table[None, :, None, :]
    return jnp.concatenate(
        [
            first_half * cosine_table - second_half * sine_table,
            second_half * cosine_table + first_half * sine_table,
        ],
        -1,
    )


def rotate_back(tensor, cosine_table, sine_table):
    half_size = tensor.shape[-1] // 2
    first_half = tensor[..., :half_size]
    second_half = tensor[..., half_size:]
    cosine_table = cosine_table[None, :, None, :]
    sine_table = sine_table[None, :, None, :]
    return jnp.concatenate(
        [
            first_half * cosine_table + second_half * sine_table,
            second_half * cosine_table - first_half * sine_table,
        ],
        -1,
    )


def rms_scale(tensor):
    return lax.rsqrt(jnp.mean(tensor * tensor, axis=-1, keepdims=True) + EPSILON)


def block_scores(query_block, key_block, query_pos, key_pos):
    scores = (
        jnp.einsum("gqhrd,gkhd->ghrqk", query_block, key_block, preferred_element_type=jnp.float32)
        * 0.125
    )
    visible = key_pos[None, :] <= query_pos[:, None]
    return jnp.where(visible, scores, MASKED)


def split_context(
    tokens, norm1_gain, w_query, w_key, w_value, w_out, norm2_gain, w_gate, w_up, w_down, out_grad
):
    gain1, wq_full, wk_full, wv_full, wo_full, gain2, wg_full, wu_full, wd_full = (
        lax.all_gather(norm1_gain, "fsdp", axis=0, tiled=True),
        lax.all_gather(w_query, "fsdp", axis=0, tiled=True),
        lax.all_gather(w_key, "fsdp", axis=0, tiled=True),
        lax.all_gather(w_value, "fsdp", axis=0, tiled=True),
        lax.all_gather(w_out, "fsdp", axis=0, tiled=True),
        lax.all_gather(norm2_gain, "fsdp", axis=0, tiled=True),
        lax.all_gather(w_gate, "fsdp", axis=0, tiled=True),
        lax.all_gather(w_up, "fsdp", axis=0, tiled=True),
        lax.all_gather(w_down, "fsdp", axis=0, tiled=True),
    )
    query_group_count, local_row_count, model_width = tokens.shape
    repeat_heads = QUERY_HEADS // KEY_VALUE_HEADS
    head_width = HEAD_SIZE
    key_value_width = KEY_VALUE_HEADS * HEAD_SIZE
    query_width = QUERY_HEADS * HEAD_SIZE
    first_row = lax.axis_index("ctx") * local_row_count
    last_row = first_row + local_row_count - 1
    positions = first_row + jnp.arange(local_row_count, dtype=jnp.int32)
    cosine_table, sine_table = rope_tables(positions, head_width)
    gain1f = gain1.astype(jnp.float32)
    gain2f = gain2.astype(jnp.float32)
    inputs = tokens.astype(jnp.float32)
    scale1 = rms_scale(inputs)
    normed1 = (inputs * scale1 * gain1f).astype(jnp.bfloat16)
    query_before_rotation = jnp.einsum(
        "gsd,de->gse", normed1, wq_full, preferred_element_type=jnp.float32
    )
    key_before_rotation = jnp.einsum(
        "gsd,de->gse", normed1, wk_full, preferred_element_type=jnp.float32
    )
    value_projected = jnp.einsum(
        "gsd,de->gse", normed1, wv_full, preferred_element_type=jnp.float32
    )
    query_matrix = rotary_apply(
        query_before_rotation.reshape(query_group_count, local_row_count, QUERY_HEADS, head_width),
        cosine_table,
        sine_table,
    ).astype(jnp.bfloat16)
    query_matrix = query_matrix.reshape(
        query_group_count, local_row_count, KEY_VALUE_HEADS, repeat_heads, head_width
    )
    key_local = rotary_apply(
        key_before_rotation.reshape(
            query_group_count, local_row_count, KEY_VALUE_HEADS, head_width
        ),
        cosine_table,
        sine_table,
    ).astype(jnp.bfloat16)
    local_value_rows = value_projected.astype(jnp.bfloat16)
    collected_keys, collected_values = (
        lax.all_gather(
            key_local.reshape(query_group_count, local_row_count, key_value_width),
            "ctx",
            axis=1,
            tiled=True,
        ),
        lax.all_gather(local_value_rows, "ctx", axis=1, tiled=True),
    )
    sequence_length = collected_keys.shape[1]
    every_key_row = collected_keys.reshape(
        query_group_count, sequence_length, KEY_VALUE_HEADS, head_width
    )
    every_value_row = collected_values.reshape(
        query_group_count, sequence_length, KEY_VALUE_HEADS, head_width
    )
    local_value_rows = local_value_rows.reshape(
        query_group_count, local_row_count, KEY_VALUE_HEADS, head_width
    )
    key_span = min(sequence_length, 512)
    block_total = last_row // key_span + 1

    def key_slices(step_index):
        first_key = step_index * key_span
        key_block = lax.dynamic_slice_in_dim(every_key_row, first_key, key_span, 1)
        value_block = lax.dynamic_slice_in_dim(every_value_row, first_key, key_span, 1)
        key_pos = first_key + jnp.arange(key_span, dtype=jnp.int32)
        return (key_block, value_block, key_pos)

    def stats_step(step_index, running):
        row_max, row_sum = running
        key_block, value_block, key_pos = key_slices(step_index)
        scores = block_scores(query_matrix, key_block, positions, key_pos)
        new_max = jnp.maximum(row_max, jnp.max(scores, axis=-1))
        row_sum = row_sum * jnp.exp(row_max - new_max) + jnp.sum(
            jnp.exp(scores - new_max[..., None]), axis=-1
        )
        return (new_max, row_sum)

    statistics_shape = (query_group_count, KEY_VALUE_HEADS, repeat_heads, local_row_count)
    row_max, row_sum = lax.fori_loop(
        0,
        block_total,
        stats_step,
        (jnp.full(statistics_shape, MASKED, jnp.float32), jnp.zeros(statistics_shape, jnp.float32)),
    )
    log_total = row_max + jnp.log(row_sum)

    def mix_step(step_index, running):
        key_block, value_block, key_pos = key_slices(step_index)
        scores = block_scores(query_matrix, key_block, positions, key_pos)
        probs = jnp.exp(scores - log_total[..., None]).astype(jnp.bfloat16)
        return running + jnp.einsum(
            "ghrqk,gkhd->gqhrd", probs, value_block, preferred_element_type=jnp.float32
        )

    attended_full = lax.fori_loop(
        0,
        block_total,
        mix_step,
        jnp.zeros(
            (query_group_count, local_row_count, KEY_VALUE_HEADS, repeat_heads, head_width),
            jnp.float32,
        ),
    )
    attended = attended_full.astype(jnp.bfloat16).reshape(
        query_group_count, local_row_count, query_width
    )
    branch = jnp.einsum("gse,ed->gsd", attended, wo_full, preferred_element_type=jnp.float32)
    middle = inputs + branch
    scale2 = rms_scale(middle)
    normed2 = (middle * scale2 * gain2f).astype(jnp.bfloat16)
    gate_act = jnp.einsum("gsd,df->gsf", normed2, wg_full, preferred_element_type=jnp.float32)
    up_act = jnp.einsum("gsd,df->gsf", normed2, wu_full, preferred_element_type=jnp.float32)
    gate_sig = jax.nn.sigmoid(gate_act)
    gate_silu = gate_act * gate_sig
    hidden = (gate_silu * up_act).astype(jnp.bfloat16)
    mlp_out = jnp.einsum("gsf,fd->gsd", hidden, wd_full, preferred_element_type=jnp.float32)
    output = (middle + mlp_out).astype(jnp.bfloat16)
    out_float = out_grad.astype(jnp.float32)
    grad_down = jnp.einsum("gsf,gsd->fd", hidden, out_grad, preferred_element_type=jnp.float32)
    hidden_grad = jnp.einsum("gsd,fd->gsf", out_grad, wd_full, preferred_element_type=jnp.float32)
    gate_grad = (hidden_grad * up_act * gate_sig * (1.0 + gate_act * (1.0 - gate_sig))).astype(
        jnp.bfloat16
    )
    up_grad = (hidden_grad * gate_silu).astype(jnp.bfloat16)
    grad_gate = jnp.einsum("gsd,gsf->df", normed2, gate_grad, preferred_element_type=jnp.float32)
    grad_up = jnp.einsum("gsd,gsf->df", normed2, up_grad, preferred_element_type=jnp.float32)
    normed2_grad = jnp.einsum("gsf,df->gsd", gate_grad, wg_full, preferred_element_type=jnp.float32)
    normed2_grad = normed2_grad + jnp.einsum(
        "gsf,df->gsd", up_grad, wu_full, preferred_element_type=jnp.float32
    )
    grad_gain2 = jnp.sum(normed2_grad * middle * scale2, axis=(0, 1))
    scaled2 = gain2f * normed2_grad
    middle_grad = (
        out_float
        + scale2 * scaled2
        - middle * scale2**3 * jnp.mean(scaled2 * middle, axis=-1, keepdims=True)
    )
    branch_grad = middle_grad.astype(jnp.bfloat16)
    grad_out = jnp.einsum("gse,gsd->ed", attended, branch_grad, preferred_element_type=jnp.float32)
    attended_output_gradient = jnp.einsum(
        "gsd,ed->gse", branch_grad, wo_full, preferred_element_type=jnp.float32
    ).astype(jnp.bfloat16)
    attention_gradient = attended_output_gradient.reshape(
        query_group_count, local_row_count, KEY_VALUE_HEADS, repeat_heads, head_width
    )
    delta = jnp.sum(attention_gradient.astype(jnp.float32) * attended_full, axis=-1).transpose(
        0, 2, 3, 1
    )

    def query_grad_step(step_index, running):
        key_block, value_block, key_pos = key_slices(step_index)
        scores = block_scores(query_matrix, key_block, positions, key_pos)
        probs = jnp.exp(scores - log_total[..., None])
        dprob = jnp.einsum(
            "gqhrd,gkhd->ghrqk", attention_gradient, value_block, preferred_element_type=jnp.float32
        )
        score_grad = (probs * (dprob - delta[..., None])).astype(jnp.bfloat16)
        return running + jnp.einsum(
            "ghrqk,gkhd->gqhrd", score_grad, key_block, preferred_element_type=jnp.float32
        )

    query_grad = (
        lax.fori_loop(
            0,
            block_total,
            query_grad_step,
            jnp.zeros(
                (query_group_count, local_row_count, KEY_VALUE_HEADS, repeat_heads, head_width),
                jnp.float32,
            ),
        )
        * 0.125
    )
    row_total = local_row_count * lax.axis_size("ctx")
    term_span = math.gcd(row_total, key_span)

    def key_block_term(step_index):
        first_key = step_index * term_span
        key_block = lax.dynamic_slice_in_dim(every_key_row, first_key, term_span, 1)
        value_block = lax.dynamic_slice_in_dim(every_value_row, first_key, term_span, 1)
        key_pos = first_key + jnp.arange(term_span, dtype=jnp.int32)

        def compute_term(unused):
            scores = block_scores(query_matrix, key_block, positions, key_pos)
            probs = jnp.exp(scores - log_total[..., None])
            dprob = jnp.einsum(
                "gqhrd,gkhd->ghrqk",
                attention_gradient,
                value_block,
                preferred_element_type=jnp.float32,
            )
            score_grad = (probs * (dprob - delta[..., None])).astype(jnp.bfloat16)
            key_term = (
                jnp.einsum(
                    "ghrqk,gqhrd->kghd",
                    score_grad,
                    query_matrix,
                    preferred_element_type=jnp.float32,
                )
                * 0.125
            )
            value_term = jnp.einsum(
                "ghrqk,gqhrd->kghd",
                probs.astype(jnp.bfloat16),
                attention_gradient,
                preferred_element_type=jnp.float32,
            )
            return jnp.concatenate(
                [
                    key_term.reshape(term_span, query_group_count, key_value_width),
                    value_term.reshape(term_span, query_group_count, key_value_width),
                ],
                -1,
            )

        def empty_term(unused):
            return jnp.zeros((term_span, query_group_count, 2 * key_value_width), jnp.float32)

        return lax.cond(first_key <= last_row, compute_term, empty_term, 0)

    terms = lax.map(key_block_term, jnp.arange(row_total // term_span, dtype=jnp.int32))
    paired_gradients = (
        lax.psum_scatter(
            terms.reshape(row_total, query_group_count, 2 * key_value_width).astype(jnp.bfloat16),
            "ctx",
            scatter_dimension=0,
            tiled=True,
        )
        .astype(jnp.float32)
        .transpose(1, 0, 2)
    )
    key_gradient = paired_gradients[..., :key_value_width].reshape(
        query_group_count, local_row_count, KEY_VALUE_HEADS, head_width
    )
    value_gradient = paired_gradients[..., key_value_width:].reshape(
        query_group_count, local_row_count, KEY_VALUE_HEADS, head_width
    )
    query_pre_grad = rotate_back(
        query_grad.reshape(query_group_count, local_row_count, QUERY_HEADS, head_width),
        cosine_table,
        sine_table,
    )
    query_pre_grad = query_pre_grad.astype(jnp.bfloat16).reshape(
        query_group_count, local_row_count, query_width
    )
    key_pre_grad = (
        rotate_back(key_gradient, cosine_table, sine_table)
        .astype(jnp.bfloat16)
        .reshape(query_group_count, local_row_count, key_value_width)
    )
    value_pre_grad = value_gradient.astype(jnp.bfloat16).reshape(
        query_group_count, local_row_count, key_value_width
    )
    grad_query = jnp.einsum(
        "gsd,gse->de", normed1, query_pre_grad, preferred_element_type=jnp.float32
    )
    grad_key = jnp.einsum("gsd,gse->de", normed1, key_pre_grad, preferred_element_type=jnp.float32)
    grad_value = jnp.einsum(
        "gsd,gse->de", normed1, value_pre_grad, preferred_element_type=jnp.float32
    )
    normed1_grad = jnp.einsum(
        "gse,de->gsd", query_pre_grad, wq_full, preferred_element_type=jnp.float32
    )
    normed1_grad = normed1_grad + jnp.einsum(
        "gse,de->gsd", key_pre_grad, wk_full, preferred_element_type=jnp.float32
    )
    normed1_grad = normed1_grad + jnp.einsum(
        "gse,de->gsd", value_pre_grad, wv_full, preferred_element_type=jnp.float32
    )
    grad_gain1 = jnp.sum(normed1_grad * inputs * scale1, axis=(0, 1))
    scaled1 = gain1f * normed1_grad
    input_grad = (
        middle_grad
        + scale1 * scaled1
        - inputs * scale1**3 * jnp.mean(scaled1 * inputs, axis=-1, keepdims=True)
    )
    totals = lax.psum(
        (
            grad_gain1,
            grad_query,
            grad_key,
            grad_value,
            grad_out,
            grad_gain2,
            grad_gate,
            grad_up,
            grad_down,
        ),
        ("dp", "ctx", "fsdp"),
    )
    owner = lax.axis_index("fsdp")
    shards = (norm1_gain, w_query, w_key, w_value, w_out, norm2_gain, w_gate, w_up, w_down)
    shares = tuple(
        (
            lax.dynamic_slice_in_dim(summed, owner * shard.shape[0], shard.shape[0], 0)
            for summed, shard in zip(totals, shards)
        )
    )
    return (
        output,
        input_grad,
        shares[0],
        shares[1],
        shares[2],
        shares[3],
        shares[4],
        shares[5],
        shares[6],
        shares[7],
        shares[8],
    )


WIDTH = 576
QUERY_WIDTH = QUERY_HEADS * HEAD_SIZE
KEY_WIDTH = KEY_VALUE_HEADS * HEAD_SIZE
ROTATED = QUERY_HEADS + KEY_VALUE_HEADS
REPEAT = QUERY_HEADS // KEY_VALUE_HEADS
HALF = HEAD_SIZE // 2
USED = QUERY_WIDTH + 2 * KEY_WIDTH
PACKED = USED + 64
GAIN_ROWS = 16
TILE = 256
WIDE_TILE = 512
MEBI = 1024 * 1024
F32 = jnp.float32
BF16 = jnp.bfloat16


def mm(a, b):
    return jnp.dot(a, b, preferred_element_type=F32)


def mm_nt(a, b):
    return lax.dot_general(a, b, (((1,), (1,)), ((), ())), preferred_element_type=F32)


def flip(tensor):
    return tensor.astype(F32).T.astype(tensor.dtype)


def span(index, size, step=None):
    step = size if step is None else step
    return pl.ds(pl.multiple_of(index * step, step), size)


def flip_blocks(target, source, block):
    def one(step, carry):
        at = span(step, block)
        target[at, :] = flip(source[:, at])
        return carry

    lax.fori_loop(0, source.shape[1] // block, one, 0)


def column_scale(tensor):
    return lax.rsqrt(jnp.mean(tensor * tensor, axis=0, keepdims=True) + EPSILON)


def sigmoid(tensor):
    return 0.5 * jnp.tanh(0.5 * tensor) + 0.5


def causal_last(scores, tile):
    shape = (TILE, REPEAT * TILE)
    visible = lax.broadcasted_iota(jnp.int32, shape, 0) <= (
        lax.broadcasted_iota(jnp.int32, shape, 1) & (TILE - 1)
    )
    last = jnp.where(visible, scores[tile * TILE :, :], MASKED)
    return last if tile == 0 else jnp.concatenate([scores[: tile * TILE, :], last], 0)


def attend_kernel(
    place,
    tokens,
    theirs,
    w_own,
    w_y,
    w_core,
    w_both,
    cosine,
    sine,
    x_seq,
    normed,
    packed,
    gains,
    qkv_t,
    log_total,
    attended_t,
    packed_t,
    key_rows,
):
    me, shard = place[0], place[1]
    half_rows = theirs.shape[1]
    sequence = 2 * half_rows
    x_seq[:, span(me, half_rows)] = tokens[me]
    x_seq[:, span(1 - me, half_rows)] = theirs[...]
    rows = packed.shape[0] // 4
    for bits, piece in ((0, w_own), (2, w_y), (1, w_core), (3, w_both)):
        at = span(shard ^ bits, rows)
        packed[at, :] = piece[:rows, :]
        gains[at, :GAIN_ROWS] = piece[rows:, :TILE].astype(F32).T[:rows, :]
    flip_blocks(packed_t, packed, TILE)
    gain1 = gains[:, :1]

    def project(step, carry):
        at = span(step, WIDE_TILE)
        x = x_seq[:, at].astype(F32)
        normed_tile = (x * column_scale(x) * gain1).astype(BF16)
        normed[:, at] = normed_tile
        turned = mm(packed_t[:USED, :], normed_tile)
        cos, sin = cosine[:, at], sine[:, at]
        for head in range(ROTATED):
            a = turned[head * HEAD_SIZE : head * HEAD_SIZE + HALF, :]
            b = turned[head * HEAD_SIZE + HALF : (head + 1) * HEAD_SIZE, :]
            both = jnp.concatenate([a * cos - b * sin, b * cos + a * sin], 0)
            if head < QUERY_HEADS:
                both = both * 0.125
            else:
                key_rows[head - QUERY_HEADS, at, :] = both.T.astype(BF16)
            qkv_t[head * HEAD_SIZE : (head + 1) * HEAD_SIZE, at] = both.astype(BF16)
        qkv_t[ROTATED * HEAD_SIZE :, at] = turned[ROTATED * HEAD_SIZE :, :].astype(BF16)
        return carry

    lax.fori_loop(0, sequence // WIDE_TILE, project, 0)

    def one_group(group, carry):
        value_rows = span(ROTATED + group, HEAD_SIZE)
        for tile in range(sequence // TILE):
            extent = (tile + 1) * TILE
            cols = slice(tile * TILE, extent)
            queries = jnp.concatenate(
                [qkv_t[span(group * REPEAT + r, HEAD_SIZE), cols] for r in range(REPEAT)], 1
            )
            scores = causal_last(mm(key_rows[group, :extent, :], queries), tile)
            top = jnp.max(scores, axis=0, keepdims=True)
            weights = jnp.exp(scores - top)
            total = jnp.sum(weights, axis=0, keepdims=True)
            mixed = mm(qkv_t[value_rows, :extent], weights.astype(BF16))
            mixed = (mixed * (1.0 / total)).astype(BF16)
            logs = top + jnp.log(total)
            for r in range(REPEAT):
                own = slice(r * TILE, (r + 1) * TILE)
                attended_t[span(group * REPEAT + r, HEAD_SIZE), cols] = mixed[:, own]
                log_total[group, r : r + 1, cols] = logs[:, own]
        return carry

    lax.fori_loop(0, KEY_VALUE_HEADS, one_group, 0)


def places(shard, row_bit, keep, send):
    for y_bit in range(2):
        for x_bit in range(2):
            for core_bit, target in ((0, keep), (1, send)):
                yield target, y_bit, x_bit, shard ^ (2 * y_bit + core_bit), row_bit ^ x_bit


def chunk_step(place, pieces, normed, dy, out_sum, grad_sum, keep, send, scratch):
    w_gate, w_up, w_down_t, w_gate_t, w_up_t, w_down, hidden, gate_grad, up_grad, total = scratch
    row_bit, shard, level = place[3], place[1], place[2]
    rows = pieces[0].shape[0]
    wide = w_gate.shape[1]
    part = wide // 4
    sequence = normed.shape[1]
    for bits, piece in zip((0, 2, 1, 3), pieces):
        at = span(shard ^ bits, rows)
        w_gate[at, :] = piece[:, :wide]
        w_up[at, :] = piece[:, wide : 2 * wide]
        for block in range(4):
            first = 2 * wide + block * part
            w_down_t[block * rows : (block + 1) * rows, span(shard ^ bits, part)] = piece[
                :, first : first + part
            ]
    w_gate_t[...] = flip(w_gate[...])
    w_up_t[...] = flip(w_up[...])
    w_down[...] = flip(w_down_t[...])
    for first in range(0, sequence, WIDE_TILE):
        at = slice(first, first + WIDE_TILE)
        gate = mm(w_gate_t[...], normed[:, at])
        up = mm(w_up_t[...], normed[:, at])
        hidden_grad = mm(w_down[...], dy[:, at])
        sig = sigmoid(gate)
        silu = gate * sig
        hidden_tile = (silu * up).astype(BF16)
        gate_tile = (hidden_grad * up * (sig + silu * (1.0 - sig))).astype(BF16)
        up_tile = (hidden_grad * silu).astype(BF16)
        hidden[:, at] = hidden_tile
        gate_grad[:, at] = gate_tile
        up_grad[:, at] = up_tile
        out_sum[:, at] += mm(w_down_t[...], hidden_tile)
        grad_sum[:, at] += mm(w_gate[...], gate_tile) + mm(w_up[...], up_tile)
    half = rows // 2
    middle = wide // 2
    for grads, moves in (
        (gate_grad, ((0, 0, 0, wide),)),
        (up_grad, ((0, 0, wide, middle), (1, middle, 0, middle))),
    ):
        total[...] = mm_nt(normed[...], grads[...])
        for target, y_bit, x_bit, owner, side in places(shard, place[3], keep, send):
            at = span(owner * 2 + side, half)
            for z_half, first, to, count in moves:
                target[y_bit, x_bit, level ^ z_half, :, to : to + count] = total[
                    at, first : first + count
                ].astype(BF16)
    total[...] = mm_nt(dy[...], hidden[...])
    for target, y_bit, x_bit, owner, side in places(shard, place[3], keep, send):
        for block in range(4):
            at = pl.ds(pl.multiple_of(block * rows + side * half, 8), half)
            to = middle + block * part
            target[y_bit, x_bit, level ^ 1, :, to : to + part] = total[
                at, span(owner, part)
            ].astype(BF16)


def first_chunk_kernel(
    place,
    x_seq,
    attended_t,
    out_grad,
    dy_theirs,
    gains,
    p_own,
    p_y,
    p_core,
    p_both,
    middle,
    normed,
    scales,
    dy,
    w_out,
    out_sum,
    grad_sum,
    keep,
    send,
    w_out_t,
    *scratch,
):
    me, shard = place[0], place[1]
    half_rows = dy_theirs.shape[1]
    sequence = 2 * half_rows
    dy[:, span(me, half_rows)] = out_grad[me]
    dy[:, span(1 - me, half_rows)] = dy_theirs[...]
    pieces = (p_own, p_y, p_core, p_both)
    rows = p_own.shape[0]
    packed_width = p_own.shape[1] - QUERY_WIDTH
    for bits, piece in zip((0, 2, 1, 3), pieces):
        w_out[span(shard ^ bits, rows), :] = piece[:, packed_width:]
    w_out_t[...] = flip(w_out[...])
    gain2 = gains[:, 1:2]
    for first in range(0, sequence, WIDE_TILE):
        at = slice(first, first + WIDE_TILE)
        mid = x_seq[:, at].astype(F32) + mm(w_out_t[...], attended_t[:, at])
        middle[:, at] = mid
        out_sum[:, at] = mid
        grad_sum[:, at] = jnp.zeros_like(mid)
        scale = column_scale(mid)
        scales[:, at] = jnp.broadcast_to(scale, (8, WIDE_TILE))
        normed[:, at] = (mid * scale * gain2).astype(BF16)
    chunk_step(place, pieces, normed, dy, out_sum, grad_sum, keep, send, scratch)


def next_chunk_kernel(
    place, normed, dy, out_in, grad_in, p_own, p_y, p_core, p_both, out_sum, grad_sum, keep, send, *scratch
):
    out_sum[...] = out_in[...]
    grad_sum[...] = grad_in[...]
    pieces = (p_own, p_y, p_core, p_both)
    chunk_step(place, pieces, normed, dy, out_sum, grad_sum, keep, send, scratch)


def last_chunk_kernel(
    place,
    normed,
    dy,
    out_in,
    grad_in,
    p_own,
    p_y,
    p_core,
    p_both,
    attended_t,
    gains,
    middle,
    scales,
    w_out,
    out_keep,
    out_send,
    middle_grad,
    attended_grad_t,
    keep,
    send,
    out_sum,
    branch_grad,
    *scratch,
):
    me, shard = place[0], place[1]
    half_rows = out_keep.shape[1]
    sequence = 2 * half_rows
    grad_sum = middle_grad
    out_sum[...] = out_in[...]
    grad_sum[...] = grad_in[...]
    pieces = (p_own, p_y, p_core, p_both)
    chunk_step(place, pieces, normed, dy, out_sum, grad_sum, keep, send, scratch)
    gain2 = gains[:, 1:2]
    for first in range(0, sequence, WIDE_TILE):
        at = slice(first, first + WIDE_TILE)
        output = out_sum[:, at].astype(BF16)
        block, start = divmod(first, half_rows)
        block_cols = slice(start, start + WIDE_TILE)

        @pl.when(me == block)
        def _():
            out_keep[:, block_cols] = output

        @pl.when(me != block)
        def _():
            out_send[:, block_cols] = output

        mid = middle[:, at]
        scale = scales[0:1, at]
        scaled = grad_sum[:, at] * gain2
        back = (
            dy[:, at].astype(F32)
            + scale * scaled
            - mid * (scale * scale * scale) * jnp.mean(scaled * mid, axis=0, keepdims=True)
        )
        middle_grad[:, at] = back
        branch = back.astype(BF16)
        branch_grad[:, at] = branch
        attended_grad_t[:, at] = mm(w_out[...], branch).astype(BF16)
    total = scratch[-1]
    half = p_own.shape[0] // 2
    columns = QUERY_WIDTH // 2
    first_to = keep.shape[4] - columns
    for start in range(0, QUERY_WIDTH, TILE):
        count = min(TILE, QUERY_WIDTH - start)
        total[:, :count] = mm_nt(attended_t[...], branch_grad[start : start + count, :])
        for target, y_bit, x_bit, owner, side in places(shard, place[3], keep, send):
            at = span(owner * 2 + side, half)
            for z_half in range(2):
                low = max(start, z_half * columns)
                high = min(start + count, (z_half + 1) * columns)
                if low < high:
                    to = first_to + low - z_half * columns
                    target[y_bit, x_bit, place[2] ^ z_half, :, to : to + high - low] = total[
                        at, low - start : high - start
                    ].astype(BF16)


def attend_back_kernel(
    queries_t,
    keys_t,
    values_t,
    log_total,
    attended_t,
    grad_t,
    cosine,
    sine,
    dq_out,
    dk_out,
    dv_out,
    keys,
    values,
    dk,
    dv,
):
    sequence = keys_t.shape[1]
    keys[...] = flip(keys_t[...])
    values[...] = flip(values_t[...])
    dk[...] = jnp.zeros_like(dk)
    dv[...] = jnp.zeros_like(dv)

    def back(a, b, cos, sin):
        return (a * cos + b * sin).astype(BF16), (b * cos - a * sin).astype(BF16)

    for tile in range(sequence // TILE):
        extent = (tile + 1) * TILE
        cols = slice(tile * TILE, extent)
        heads = [slice(r * HEAD_SIZE, (r + 1) * HEAD_SIZE) for r in range(REPEAT)]
        q_t = jnp.concatenate([queries_t[head, cols] for head in heads], 1)
        do_t = jnp.concatenate([grad_t[head, cols] for head in heads], 1)
        mixed = jnp.concatenate([attended_t[head, cols] for head in heads], 1)
        logs = jnp.concatenate([log_total[0, r : r + 1, cols] for r in range(REPEAT)], 1)
        delta = jnp.sum(do_t.astype(F32) * mixed.astype(F32), axis=0, keepdims=True)
        scores = causal_last(mm(keys[:extent, :], q_t), tile)
        probs = jnp.exp(scores - logs)
        dprob = mm(values[:extent, :], do_t)
        score_grad = (probs * (dprob - delta)).astype(BF16)
        dv[:extent, :] += mm(probs.astype(BF16), flip(do_t))
        dk[:extent, :] += mm(score_grad, flip(q_t))
        dq = mm(keys_t[:, :extent], score_grad) * 0.125
        cos, sin = cosine[:, cols], sine[:, cols]
        for r, head in enumerate(heads):
            own = slice(r * TILE, (r + 1) * TILE)
            a, b = back(dq[:HALF, own], dq[HALF:, own], cos, sin)
            dq_out[head.start : head.start + HALF, cols] = a
            dq_out[head.start + HALF : head.stop, cols] = b
    turned = dk[...].T
    a, b = back(turned[:HALF, :], turned[HALF:, :], cosine[...], sine[...])
    dk_out[:HALF, :] = a
    dk_out[HALF:, :] = b
    dv_out[...] = dv[...].T.astype(BF16)


def input_kernel(place, normed, x_seq, packed, gains, middle_grad, *rest):
    heads = rest[: 3 * KEY_VALUE_HEADS]
    keep_w, send_w, keep_x, send_x, joined, grad_seq, total = rest[3 * KEY_VALUE_HEADS :]
    me, shard = place[0], place[1]
    group_width = REPEAT * HEAD_SIZE
    for group in range(KEY_VALUE_HEADS):
        dq, dk, dv = heads[3 * group : 3 * group + 3]
        joined[group * group_width : (group + 1) * group_width, :] = dq[...]
        at = QUERY_WIDTH + group * HEAD_SIZE
        joined[at : at + HEAD_SIZE, :] = dk[...]
        at = QUERY_WIDTH + KEY_WIDTH + group * HEAD_SIZE
        joined[at : at + HEAD_SIZE, :] = dv[...]
    half = keep_w.shape[2]
    for first in range(0, USED, 512):
        cols = slice(first, min(first + 512, USED))
        total[:, cols] = mm_nt(normed[...], joined[cols, :])
    for target, y_bit, x_bit, owner, side in places(shard, me, keep_w, send_w):
        target[y_bit, x_bit] = total[span(owner * 2 + side, half), :].astype(BF16)
    half_rows = keep_x.shape[1]
    sequence = 2 * half_rows
    gain1 = gains[:, :1]
    for first in range(0, sequence, WIDE_TILE):
        at = slice(first, first + WIDE_TILE)
        scaled = mm(packed[:, :USED], joined[:, at]) * gain1
        x = x_seq[:, at].astype(F32)
        scale = column_scale(x)
        grad_seq[:, at] = (
            middle_grad[:, at]
            + scale * scaled
            - x * (scale * scale * scale) * jnp.mean(scaled * x, axis=0, keepdims=True)
        )
    keep_x[...] = grad_seq[:, span(me, half_rows)]
    send_x[...] = grad_seq[:, span(1 - me, half_rows)].astype(BF16)


def pack_input_kernel(place, w_query, w_key, w_value, gains, packed):
    rows = w_query.shape[0]
    packed[:rows, :QUERY_WIDTH] = w_query[...]
    packed[:rows, QUERY_WIDTH : QUERY_WIDTH + KEY_WIDTH] = w_key[...]
    packed[:rows, QUERY_WIDTH + KEY_WIDTH :] = jnp.concatenate(
        [w_value[...].astype(F32), jnp.zeros((rows, PACKED - USED), F32)], 1
    ).astype(BF16)
    packed[rows:, :] = jnp.zeros((GAIN_ROWS, PACKED), BF16)
    packed[rows:, :TILE] = gains[...]


def pack_kernel(place, w_gate, w_up, w_down_t, w_out, *chunks):
    rows = w_gate.shape[0]
    down_rows = w_down_t.shape[1]
    part = 128
    for index, chunk in enumerate(chunks):
        at = index * part
        for i in range(4):
            source = slice(i * down_rows + at, i * down_rows + at + part)
            chunk[:, i * part : (i + 1) * part] = w_gate[:, source]
            chunk[:, (4 + i) * part : (5 + i) * part] = w_up[:, source]
            chunk[:, (8 + i) * part : (9 + i) * part] = w_down_t[
                i * rows : (i + 1) * rows, at : at + part
            ]
    chunks[0][:, 12 * part :] = w_out[...]


def combine_kernel(kinds, place, *refs):
    count = sum(3 if kind == "join" else 2 for kind in kinds)
    sources, targets = list(refs[:count]), list(refs[count:])
    for kind in kinds:
        a, b = sources.pop(0), sources.pop(0)
        if kind == "join":
            target = targets.pop(0)
            target[0] = a[...]
            target[1, place[2]] = b[...]
            target[1, 1 - place[2]] = sources.pop(0)[...]
        elif kind == "order":
            target = targets.pop(0)
            target[place[2]] = a[...]
            target[1 - place[2]] = b[...]
        elif kind == "pair":
            for i in range(2):
                targets.pop(0)[...] = (a[i].astype(F32) + b[i].astype(F32)).astype(BF16)
        else:
            targets.pop(0)[...] = (a[...].astype(F32) + b[...].astype(F32)).astype(BF16)


def halves_kernel(place, keep, *rest):
    target = rest[-1]
    target[place[0]] = keep[...]
    first = 0
    for got in rest[:-1]:
        size = got.shape[0]
        target[1 - place[0], first : first + size] = got[...].astype(target.dtype)
        first += size


def gain_row(products, gain):
    column = jnp.sum(products, axis=1, keepdims=True)
    row = jnp.broadcast_to(column, (column.shape[0], 128)).T[:1, :]
    return row / gain.astype(F32)


def unpack_kernel(place, own, other, own2, other2, w_gate, w_up, gain, *out):
    gate_out, up_out, down_out, out_out, gain_out = out
    me = place[0]
    half = own2.shape[1]
    rows = 2 * half
    part = 128
    down_rows = down_out.shape[1]
    last = (own2, other2)
    for index, sources in enumerate(
        ((own.at[0], own.at[1], own2), (other.at[0], other.at[1], other2))
    ):
        for chunk, source in enumerate(sources):
            side = index ^ me
            at = span(side, half)
            for i in range(4):
                to = slice(i * down_rows + chunk * part, i * down_rows + (chunk + 1) * part)
                gate_out[at, to] = source[0, :, i * part : (i + 1) * part].astype(F32)
                z_half, first = (0, (4 + i) * part) if i < 2 else (1, (i - 2) * part)
                up_out[at, to] = source[z_half, :, first : first + part].astype(F32)
                down_at = pl.ds(pl.multiple_of(i * rows + side * half, 8), half)
                first = (2 + i) * part
                down_out[down_at, chunk * part : (chunk + 1) * part] = source[
                    1, :, first : first + part
                ].astype(F32)
        first = 6 * part
        out_out[span(index ^ me, half), :] = jnp.concatenate(
            [last[index][0, :, first:].astype(F32), last[index][1, :, first:].astype(F32)], 1
        )
    products = gate_out[...] * w_gate[...].astype(F32) + up_out[...] * w_up[...].astype(F32)
    gain_out[...] = gain_row(products, gain[...])


def unpack_input_kernel(
    place, own, other, w_query, w_key, w_value, gain, query_out, key_out, value_out, gain_out
):
    me = place[0]
    half = own.shape[0]
    key_at = QUERY_WIDTH + KEY_WIDTH
    for side, source in ((me, own), (1 - me, other)):
        at = span(side, half)
        wide = source[...].astype(F32)
        query_out[at, :] = wide[:, :QUERY_WIDTH]
        key_out[at, :] = wide[:, QUERY_WIDTH:key_at]
        value_out[at, :] = wide[:, key_at:]
    products = jnp.sum(query_out[...] * w_query[...].astype(F32), axis=1, keepdims=True)
    products += jnp.sum(key_out[...] * w_key[...].astype(F32), axis=1, keepdims=True)
    products += jnp.sum(value_out[...] * w_value[...].astype(F32), axis=1, keepdims=True)
    gain_out[...] = gain_row(products, gain[...])


def call(kernel, out, scratch, flops, exps, args, name, limit, aliases=None):
    shapes = [jax.ShapeDtypeStruct(s, d) for s, d in out]
    moved = sum(a.size * a.dtype.itemsize for a in args[1:]) + sum(
        s.size * s.dtype.itemsize for s in shapes
    )
    in_specs = [pl.BlockSpec(memory_space=pltpu.SMEM)] + [
        pl.BlockSpec(memory_space=pltpu.VMEM)
    ] * (len(args) - 1)
    return pl.pallas_call(
        kernel,
        out_shape=shapes,
        in_specs=in_specs,
        out_specs=[pl.BlockSpec(memory_space=pltpu.VMEM)] * len(shapes),
        scratch_shapes=[pltpu.VMEM(s, d) for s, d in scratch],
        input_output_aliases=aliases or {},
        compiler_params=pltpu.CompilerParams(vmem_limit_bytes=limit * MEBI),
        cost_estimate=pl.CostEstimate(
            flops=flops, bytes_accessed=moved if flops else 1024, transcendentals=exps
        ),
        name=name,
    )(*args)


def attend_back(group, qkv_t, log_total, attended_t, grad_t, cosine, sine):
    sequence = qkv_t.shape[1]
    group_width = REPEAT * HEAD_SIZE

    def rows_of(size, index):
        return pl.BlockSpec((size, sequence), lambda step: (index, 0))

    flops = 5 * REPEAT * sequence * sequence * HEAD_SIZE * 2
    return pl.pallas_call(
        attend_back_kernel,
        grid=(1,),
        out_shape=[
            jax.ShapeDtypeStruct((group_width, sequence), BF16),
            jax.ShapeDtypeStruct((HEAD_SIZE, sequence), BF16),
            jax.ShapeDtypeStruct((HEAD_SIZE, sequence), BF16),
        ],
        in_specs=[
            rows_of(group_width, group),
            rows_of(HEAD_SIZE, QUERY_HEADS + group),
            rows_of(HEAD_SIZE, ROTATED + group),
            pl.BlockSpec((1, 8, sequence), lambda step: (group, 0, 0)),
            rows_of(group_width, group),
            rows_of(group_width, group),
            rows_of(HALF, 0),
            rows_of(HALF, 0),
        ],
        out_specs=[rows_of(group_width, 0), rows_of(HEAD_SIZE, 0), rows_of(HEAD_SIZE, 0)],
        scratch_shapes=[
            pltpu.VMEM((sequence, HEAD_SIZE), BF16),
            pltpu.VMEM((sequence, HEAD_SIZE), BF16),
            pltpu.VMEM((sequence, HEAD_SIZE), F32),
            pltpu.VMEM((sequence, HEAD_SIZE), F32),
        ],
        compiler_params=pltpu.CompilerParams(vmem_limit_bytes=16 * MEBI),
        cost_estimate=pl.CostEstimate(
            flops=flops, bytes_accessed=4_000_000, transcendentals=REPEAT * sequence * sequence
        ),
        name="attend_back",
    )(qkv_t, qkv_t, qkv_t, log_total, attended_t, grad_t, cosine, sine)


def across(tensor, bit):
    return lax.ppermute(tensor, "fsdp", [(i, i ^ bit) for i in range(4)])


def over_context(tensor):
    return lax.ppermute(tensor, "ctx", [(0, 1), (1, 0)])


def after(tensor, *done):
    return lax.optimization_barrier((tensor, *done))[0]


def together(*values):
    return lax.optimization_barrier(values)


def along(tensor, bit):
    size = lax.axis_size("dp")
    return lax.ppermute(tensor, "dp", [(i, i ^ bit) for i in range(size)])


def whole_sequences(
    tokens, norm1_gain, w_query, w_key, w_value, w_out, norm2_gain, w_gate, w_up, w_down, out_grad
):
    half_rows, width = tokens.shape[1:]
    sequence = 2 * half_rows
    rows = w_query.shape[0]
    down_rows = w_down.shape[0]
    hidden_width = w_gate.shape[1]
    part = 128
    me = lax.axis_index("ctx")
    line = lax.axis_index("dp")
    shard = lax.axis_index("fsdp")
    place = jnp.stack([me, shard, line & 1, me]).astype(jnp.int32)
    whole_place = jnp.stack([me, shard, jnp.zeros_like(me), me]).astype(jnp.int32)
    tokens = jnp.swapaxes(tokens, 1, 2)
    out_grad = jnp.swapaxes(out_grad, 1, 2)

    tokens_send = lax.dynamic_index_in_dim(tokens, 1 - me, 0, False)
    tokens_theirs = over_context(tokens_send)
    gain_rows = jnp.stack(together(norm1_gain, norm2_gain, tokens_send)[:2])
    gains_own = jnp.pad(gain_rows, ((0, GAIN_ROWS - 2), (0, TILE - rows)))
    (packed,) = call(
        pack_input_kernel,
        [((rows + GAIN_ROWS, PACKED), BF16)],
        [],
        0,
        0,
        (place, w_query, w_key, w_value, gains_own),
        "pack_input",
        16,
    )
    packed_y = across(packed, 2)
    packed_core = across(packed, 1)
    dy_theirs = over_context(lax.dynamic_index_in_dim(out_grad, 1 - me, 0, False))
    chunks = call(
        pack_kernel,
        [((rows, 12 * part + (0 if index else QUERY_WIDTH)), BF16) for index in range(3)],
        [],
        0,
        0,
        (place, w_gate, w_up, w_down.T, after(w_out, packed)),
        "pack",
        16,
    )
    cosine, sine = rope_tables(jnp.arange(sequence, dtype=jnp.int32), HEAD_SIZE)
    *chunks, _, cosine, sine, place, whole_place = together(
        *chunks, packed, cosine.T, sine.T, place, whole_place
    )
    packed_y, tokens_theirs = together(packed_y, tokens_theirs)
    packed_both = across(packed_y, 1)
    chunks_y = [across(chunk, 2) for chunk in chunks]
    chunks_core = [across(chunk, 1) for chunk in chunks]

    pairs = sequence * sequence
    x_seq, normed, packed_all, gains, qkv_t, log_total, attended_t = call(
        attend_kernel,
        [
            ((width, sequence), BF16),
            ((width, sequence), BF16),
            ((width, PACKED), BF16),
            ((width, 128), F32),
            ((USED, sequence), BF16),
            ((KEY_VALUE_HEADS, 8, sequence), F32),
            ((QUERY_WIDTH, sequence), BF16),
        ],
        [((PACKED, width), BF16), ((KEY_VALUE_HEADS, sequence, HEAD_SIZE), BF16)],
        2 * sequence * width * PACKED + 4 * QUERY_WIDTH * pairs,
        QUERY_HEADS * pairs,
        (place, tokens, tokens_theirs, packed, packed_y, packed_core, packed_both, cosine, sine),
        "attend",
        20,
    )

    natural, turned = ((width, 4 * part), BF16), ((4 * part, width), BF16)
    row, wide_row = ((width, sequence), BF16), ((4 * part, sequence), BF16)
    row_sum = ((width, sequence), F32)
    share = ((2, 2, 2, rows // 2, 6 * part), BF16)
    last_share = ((2, 2, 2, rows // 2, 6 * part + QUERY_WIDTH // 2), BF16)
    chunk_scratch = [
        natural,
        natural,
        natural,
        turned,
        turned,
        turned,
        wide_row,
        wide_row,
        wide_row,
        ((width, 4 * part), F32),
    ]
    flops = 2 * sequence * width * 9 * 4 * part
    exps = sequence * 4 * part

    first_y, second_y, third_y = chunks_y
    first_y, second_y, attended_t, dy_theirs = together(first_y, second_y, attended_t, dy_theirs)
    pieces = (chunks[0], first_y, chunks_core[0], across(first_y, 1))
    second_both = across(second_y, 1)
    middle, normed2, scales, dy, w_out_all, out_sum, grad_sum, keep0, send0 = call(
        first_chunk_kernel,
        [
            row_sum,
            row,
            ((8, sequence), F32),
            row,
            ((QUERY_WIDTH, width), BF16),
            row_sum,
            row_sum,
            share,
            share,
        ],
        [((width, QUERY_WIDTH), BF16), *chunk_scratch],
        flops + 2 * sequence * width * QUERY_WIDTH,
        exps,
        (whole_place, x_seq, attended_t, out_grad, dy_theirs, gains, *pieces),
        "first_chunk",
        26,
    )

    def combine(*items):
        kinds = tuple(item[0] for item in items)
        args = [tensor for item in items for tensor in item[1:]]
        out = []
        for kind, tensor, *_ in items:
            if kind == "join":
                out.append(((2, *tensor.shape), BF16))
            elif kind == "order":
                out.append(((2, *tensor.shape), BF16))
            elif kind == "pair":
                out += [(tensor.shape[1:], BF16)] * 2
            else:
                out.append((tensor.shape, BF16))
        kernel = functools.partial(combine_kernel, kinds)
        return call(kernel, out, [], 0, 0, (place, *args), "combine", 16)

    out_sum, send0, third_y, second_both = together(out_sum, send0, third_y, second_both)
    got0 = across(send0, 1)
    pieces = (chunks[1], second_y, chunks_core[1], second_both)
    third_both = across(third_y, 1)
    out_sum, grad_sum, keep1, send1 = call(
        next_chunk_kernel,
        [row_sum, row_sum, share, share],
        chunk_scratch,
        flops,
        exps,
        (place, normed2, dy, out_sum, grad_sum, *pieces),
        "next_chunk",
        20,
        {3: 0, 4: 1},
    )

    got0, out_sum, send1, third_both = together(got0, out_sum, send1, third_both)
    own0, part0 = combine(("pair", keep0, got0))
    part0, send1, out_sum = together(part0, send1, out_sum)
    got0, got1 = across(part0, 2), across(send1, 1)
    pieces = (chunks[2], third_y, chunks_core[2], third_both)
    out_keep, out_send, middle_grad, grad_t, keep2, send2 = call(
        last_chunk_kernel,
        [
            ((width, half_rows), BF16),
            ((width, half_rows), BF16),
            row_sum,
            ((QUERY_WIDTH, sequence), BF16),
            last_share,
            last_share,
        ],
        [row_sum, row, *chunk_scratch],
        flops + 4 * sequence * width * QUERY_WIDTH,
        exps,
        (
            place,
            normed2,
            dy,
            out_sum,
            grad_sum,
            *pieces,
            attended_t,
            gains,
            middle,
            scales,
            w_out_all,
        ),
        "last_chunk",
        24,
    )

    got0, got1, grad_t, send2, out_send = together(got0, got1, grad_t, send2, out_send)
    own0, part0, own1, part1 = combine(("pair", own0, got0), ("pair", keep1, got1))
    part0, part1, grad_t = together(part0, part1, grad_t)
    def place_halves(keep, name, *got):
        (both,) = call(
            halves_kernel, [((2, *keep.shape), keep.dtype)], [], 0, 0, (place, keep, *got), name, 16
        )
        return jnp.swapaxes(both, 1, 2)

    got0, got1, got2 = over_context(part0), across(part1, 2), across(send2, 1)
    out_theirs = over_context(out_send)

    back_args = (log_total, attended_t, grad_t, cosine, sine)
    grads0 = attend_back(0, qkv_t, *back_args)
    got0, got2, *grads0 = together(got0, got2, *grads0)
    own0, own2, part2 = combine(("one", own0, got0), ("pair", keep2, got2))
    own0, part2, qkv_t = together(own0, part2, qkv_t)

    got0, got2 = along(own0, 1), across(part2, 2)
    grads1 = attend_back(1, qkv_t, *back_args)
    got0, got1, *grads1 = together(got0, got1, *grads1)
    own0, own1, part1 = combine(("one", own0, got0), ("pair", own1, got1))
    own0, part1, qkv_t = together(own0, part1, qkv_t)

    got0, got1 = along(own0, 2), over_context(part1)
    grads2 = attend_back(2, qkv_t, *back_args)
    got1, got2, out_theirs, *grads2 = together(got1, got2, out_theirs, *grads2)
    own1, part1, own2, part2 = combine(("pair", own1, got1), ("pair", own2, got2))
    part1, part2, *grads2 = together(part1, part2, *grads2)

    got1, got2 = along(part1, 1), over_context(part2)
    keep_w, send_w, keep_x, send_x = call(
        input_kernel,
        [
            ((2, 2, rows // 2, USED), BF16),
            ((2, 2, rows // 2, USED), BF16),
            ((width, half_rows), F32),
            ((width, half_rows), BF16),
        ],
        [((USED, sequence), BF16), ((width, sequence), F32), ((width, USED), F32)],
        4 * sequence * width * USED,
        sequence,
        (
            place,
            normed,
            x_seq,
            packed_all,
            gains,
            middle_grad,
            *grads0,
            *grads1,
            *grads2,
        ),
        "input_side",
        24,
    )
    got0, got1, got2, send_w, send_x = together(got0, got1, got2, send_w, send_x)
    got_w = across(send_w, 1)
    own0, own1, own2, part2 = combine(
        ("one", own0, got0), ("one", own1, got1), ("pair", own2, got2)
    )
    got_w, own1, part2, send_x = together(got_w, own1, part2, send_x)
    own_w, part_w = combine(("pair", keep_w, got_w))
    got_w, got1, got2 = across(part_w, 2), along(own1, 2), along(part2, 1)
    x_theirs = over_context(send_x)
    output = place_halves(out_keep, "output_halves", out_theirs)

    got_w, got1, got2, output = together(got_w, got1, got2, output)
    own_w, part_w, own1, own2 = combine(
        ("pair", own_w, got_w), ("one", own1, got1), ("one", own2, got2)
    )
    part_w, own1, own2 = together(part_w, own1, own2)
    got_w, got1, got2 = over_context(part_w), along(own1, 1), along(own2, 2)

    got_w, got1, got2, x_theirs = together(got_w, got1, got2, x_theirs)
    own_w, own, own2 = combine(
        ("one", own_w, got_w), ("join", own0, own1, got1), ("one", own2, got2)
    )
    own_w, own, own2, x_theirs = together(own_w, own, own2, x_theirs)
    got_w, got2, other = along(own_w, 1), along(own2, 1), over_context(own)
    gradient = place_halves(keep_x, "gradient_halves", x_theirs)

    got_w, got2, gradient = together(got_w, got2, gradient)
    own_w, own2 = combine(("one", own_w, got_w), ("order", own2, got2))
    own_w, own2 = together(own_w, own2)
    got_w, other2 = along(own_w, 2), over_context(own2)

    got_w, other = together(got_w, other)
    (own_w,) = combine(("one", own_w, got_w))
    other_w = over_context(own_w)
    own_w, other2 = together(own_w, other2)

    gate_sum, up_sum, down_sum, out_sum, gain2_sum = call(
        unpack_kernel,
        [
            ((rows, hidden_width), F32),
            ((rows, hidden_width), F32),
            ((width, down_rows), F32),
            ((rows, width), F32),
            ((1, rows), F32),
        ],
        [],
        0,
        0,
        (place, own, other, own2, other2, w_gate, w_up, norm2_gain[None, :]),
        "unpack",
        24,
    )
    gate_sum, other_w = together(gate_sum, other_w)
    query_sum, key_sum, value_sum, gain1_sum = call(
        unpack_input_kernel,
        [
            ((rows, QUERY_WIDTH), F32),
            ((rows, KEY_WIDTH), F32),
            ((rows, KEY_WIDTH), F32),
            ((1, rows), F32),
        ],
        [],
        0,
        0,
        (place, own_w, other_w, w_query, w_key, w_value, norm1_gain[None, :]),
        "unpack_input",
        16,
    )
    return (
        output,
        gradient,
        gain1_sum[0],
        query_sum,
        key_sum,
        value_sum,
        out_sum,
        gain2_sum[0],
        gate_sum,
        up_sum,
        down_sum.T,
    )


def layer_step(tokens, *rest):
    whole = (
        lax.axis_size("ctx") == 2
        and lax.axis_size("fsdp") == 4
        and lax.axis_size("dp") == 4
        and tokens.shape[0] == 2
        and tokens.shape[1] % WIDE_TILE == 0
        and rest[8].shape == (384, 576)
    )
    return (whole_sequences if whole else split_context)(tokens, *rest)


def solution(mesh):
    return jax.shard_map(
        layer_step,
        mesh=mesh,
        in_specs=(
            P(("dp", "fsdp"), "ctx", None),
            P("fsdp"),
            P("fsdp", None),
            P("fsdp", None),
            P("fsdp", None),
            P("fsdp", None),
            P("fsdp"),
            P("fsdp", None),
            P("fsdp", None),
            P("fsdp", None),
            P(("dp", "fsdp"), "ctx", None),
        ),
        out_specs=(
            P(("dp", "fsdp"), "ctx", None),
            P(("dp", "fsdp"), "ctx", None),
            P("fsdp"),
            P("fsdp", None),
            P("fsdp", None),
            P("fsdp", None),
            P("fsdp", None),
            P("fsdp"),
            P("fsdp", None),
            P("fsdp", None),
            P("fsdp", None),
        ),
        check_vma=False,
    )
```

```python
import functools
import math

import jax
import jax.numpy as jnp
from jax import lax
from jax.experimental import pallas as pl
from jax.experimental.pallas import tpu as pltpu
from jax.sharding import PartitionSpec as P

QUERY_HEADS = 9
KEY_VALUE_HEADS = 3
HEAD_SIZE = 64


EPSILON = 1e-05
ROPE_THETA = 100000.0
MASKED = -1e30


def rope_tables(positions, head_width):
    half_size = head_width // 2
    inverse = jnp.exp(
        jnp.arange(half_size, dtype=jnp.float32) * (-2.0 * math.log(ROPE_THETA) / head_width)
    )
    angle = positions.astype(jnp.float32)[:, None] * inverse[None, :]
    return (jnp.cos(angle), jnp.sin(angle))


def rotary_apply(tensor, cosine_table, sine_table):
    half_size = tensor.shape[-1] // 2
    first_half = tensor[..., :half_size]
    second_half = tensor[..., half_size:]
    cosine_table = cosine_table[None, :, None, :]
    sine_table = sine_table[None, :, None, :]
    return jnp.concatenate(
        [
            first_half * cosine_table - second_half * sine_table,
            second_half * cosine_table + first_half * sine_table,
        ],
        -1,
    )


def rotate_back(tensor, cosine_table, sine_table):
    half_size = tensor.shape[-1] // 2
    first_half = tensor[..., :half_size]
    second_half = tensor[..., half_size:]
    cosine_table = cosine_table[None, :, None, :]
    sine_table = sine_table[None, :, None, :]
    return jnp.concatenate(
        [
            first_half * cosine_table + second_half * sine_table,
            second_half * cosine_table - first_half * sine_table,
        ],
        -1,
    )


def rms_scale(tensor):
    return lax.rsqrt(jnp.mean(tensor * tensor, axis=-1, keepdims=True) + EPSILON)


def block_scores(query_block, key_block, query_pos, key_pos):
    scores = (
        jnp.einsum("gqhrd,gkhd->ghrqk", query_block, key_block, preferred_element_type=jnp.float32)
        * 0.125
    )
    visible = key_pos[None, :] <= query_pos[:, None]
    return jnp.where(visible, scores, MASKED)


def split_context(
    tokens, norm1_gain, w_query, w_key, w_value, w_out, norm2_gain, w_gate, w_up, w_down, out_grad
):
    gain1, wq_full, wk_full, wv_full, wo_full, gain2, wg_full, wu_full, wd_full = (
        lax.all_gather(norm1_gain, "fsdp", axis=0, tiled=True),
        lax.all_gather(w_query, "fsdp", axis=0, tiled=True),
        lax.all_gather(w_key, "fsdp", axis=0, tiled=True),
        lax.all_gather(w_value, "fsdp", axis=0, tiled=True),
        lax.all_gather(w_out, "fsdp", axis=0, tiled=True),
        lax.all_gather(norm2_gain, "fsdp", axis=0, tiled=True),
        lax.all_gather(w_gate, "fsdp", axis=0, tiled=True),
        lax.all_gather(w_up, "fsdp", axis=0, tiled=True),
        lax.all_gather(w_down, "fsdp", axis=0, tiled=True),
    )
    query_group_count, local_row_count, model_width = tokens.shape
    repeat_heads = QUERY_HEADS // KEY_VALUE_HEADS
    head_width = HEAD_SIZE
    key_value_width = KEY_VALUE_HEADS * HEAD_SIZE
    query_width = QUERY_HEADS * HEAD_SIZE
    first_row = lax.axis_index("ctx") * local_row_count
    last_row = first_row + local_row_count - 1
    positions = first_row + jnp.arange(local_row_count, dtype=jnp.int32)
    cosine_table, sine_table = rope_tables(positions, head_width)
    gain1f = gain1.astype(jnp.float32)
    gain2f = gain2.astype(jnp.float32)
    inputs = tokens.astype(jnp.float32)
    scale1 = rms_scale(inputs)
    normed1 = (inputs * scale1 * gain1f).astype(jnp.bfloat16)
    query_before_rotation = jnp.einsum(
        "gsd,de->gse", normed1, wq_full, preferred_element_type=jnp.float32
    )
    key_before_rotation = jnp.einsum(
        "gsd,de->gse", normed1, wk_full, preferred_element_type=jnp.float32
    )
    value_projected = jnp.einsum(
        "gsd,de->gse", normed1, wv_full, preferred_element_type=jnp.float32
    )
    query_matrix = rotary_apply(
        query_before_rotation.reshape(query_group_count, local_row_count, QUERY_HEADS, head_width),
        cosine_table,
        sine_table,
    ).astype(jnp.bfloat16)
    query_matrix = query_matrix.reshape(
        query_group_count, local_row_count, KEY_VALUE_HEADS, repeat_heads, head_width
    )
    key_local = rotary_apply(
        key_before_rotation.reshape(
            query_group_count, local_row_count, KEY_VALUE_HEADS, head_width
        ),
        cosine_table,
        sine_table,
    ).astype(jnp.bfloat16)
    local_value_rows = value_projected.astype(jnp.bfloat16)
    collected_keys, collected_values = (
        lax.all_gather(
            key_local.reshape(query_group_count, local_row_count, key_value_width),
            "ctx",
            axis=1,
            tiled=True,
        ),
        lax.all_gather(local_value_rows, "ctx", axis=1, tiled=True),
    )
    sequence_length = collected_keys.shape[1]
    every_key_row = collected_keys.reshape(
        query_group_count, sequence_length, KEY_VALUE_HEADS, head_width
    )
    every_value_row = collected_values.reshape(
        query_group_count, sequence_length, KEY_VALUE_HEADS, head_width
    )
    local_value_rows = local_value_rows.reshape(
        query_group_count, local_row_count, KEY_VALUE_HEADS, head_width
    )
    key_span = min(sequence_length, 512)
    block_total = last_row // key_span + 1

    def key_slices(step_index):
        first_key = step_index * key_span
        key_block = lax.dynamic_slice_in_dim(every_key_row, first_key, key_span, 1)
        value_block = lax.dynamic_slice_in_dim(every_value_row, first_key, key_span, 1)
        key_pos = first_key + jnp.arange(key_span, dtype=jnp.int32)
        return (key_block, value_block, key_pos)

    def stats_step(step_index, running):
        row_max, row_sum = running
        key_block, value_block, key_pos = key_slices(step_index)
        scores = block_scores(query_matrix, key_block, positions, key_pos)
        new_max = jnp.maximum(row_max, jnp.max(scores, axis=-1))
        row_sum = row_sum * jnp.exp(row_max - new_max) + jnp.sum(
            jnp.exp(scores - new_max[..., None]), axis=-1
        )
        return (new_max, row_sum)

    statistics_shape = (query_group_count, KEY_VALUE_HEADS, repeat_heads, local_row_count)
    row_max, row_sum = lax.fori_loop(
        0,
        block_total,
        stats_step,
        (jnp.full(statistics_shape, MASKED, jnp.float32), jnp.zeros(statistics_shape, jnp.float32)),
    )
    log_total = row_max + jnp.log(row_sum)

    def mix_step(step_index, running):
        key_block, value_block, key_pos = key_slices(step_index)
        scores = block_scores(query_matrix, key_block, positions, key_pos)
        probs = jnp.exp(scores - log_total[..., None]).astype(jnp.bfloat16)
        return running + jnp.einsum(
            "ghrqk,gkhd->gqhrd", probs, value_block, preferred_element_type=jnp.float32
        )

    attended_full = lax.fori_loop(
        0,
        block_total,
        mix_step,
        jnp.zeros(
            (query_group_count, local_row_count, KEY_VALUE_HEADS, repeat_heads, head_width),
            jnp.float32,
        ),
    )
    attended = attended_full.astype(jnp.bfloat16).reshape(
        query_group_count, local_row_count, query_width
    )
    branch = jnp.einsum("gse,ed->gsd", attended, wo_full, preferred_element_type=jnp.float32)
    middle = inputs + branch
    scale2 = rms_scale(middle)
    normed2 = (middle * scale2 * gain2f).astype(jnp.bfloat16)
    gate_act = jnp.einsum("gsd,df->gsf", normed2, wg_full, preferred_element_type=jnp.float32)
    up_act = jnp.einsum("gsd,df->gsf", normed2, wu_full, preferred_element_type=jnp.float32)
    gate_sig = jax.nn.sigmoid(gate_act)
    gate_silu = gate_act * gate_sig
    hidden = (gate_silu * up_act).astype(jnp.bfloat16)
    mlp_out = jnp.einsum("gsf,fd->gsd", hidden, wd_full, preferred_element_type=jnp.float32)
    output = (middle + mlp_out).astype(jnp.bfloat16)
    out_float = out_grad.astype(jnp.float32)
    grad_down = jnp.einsum("gsf,gsd->fd", hidden, out_grad, preferred_element_type=jnp.float32)
    hidden_grad = jnp.einsum("gsd,fd->gsf", out_grad, wd_full, preferred_element_type=jnp.float32)
    gate_grad = (hidden_grad * up_act * gate_sig * (1.0 + gate_act * (1.0 - gate_sig))).astype(
        jnp.bfloat16
    )
    up_grad = (hidden_grad * gate_silu).astype(jnp.bfloat16)
    grad_gate = jnp.einsum("gsd,gsf->df", normed2, gate_grad, preferred_element_type=jnp.float32)
    grad_up = jnp.einsum("gsd,gsf->df", normed2, up_grad, preferred_element_type=jnp.float32)
    normed2_grad = jnp.einsum("gsf,df->gsd", gate_grad, wg_full, preferred_element_type=jnp.float32)
    normed2_grad = normed2_grad + jnp.einsum(
        "gsf,df->gsd", up_grad, wu_full, preferred_element_type=jnp.float32
    )
    grad_gain2 = jnp.sum(normed2_grad * middle * scale2, axis=(0, 1))
    scaled2 = gain2f * normed2_grad
    middle_grad = (
        out_float
        + scale2 * scaled2
        - middle * scale2**3 * jnp.mean(scaled2 * middle, axis=-1, keepdims=True)
    )
    branch_grad = middle_grad.astype(jnp.bfloat16)
    grad_out = jnp.einsum("gse,gsd->ed", attended, branch_grad, preferred_element_type=jnp.float32)
    attended_output_gradient = jnp.einsum(
        "gsd,ed->gse", branch_grad, wo_full, preferred_element_type=jnp.float32
    ).astype(jnp.bfloat16)
    attention_gradient = attended_output_gradient.reshape(
        query_group_count, local_row_count, KEY_VALUE_HEADS, repeat_heads, head_width
    )
    delta = jnp.sum(attention_gradient.astype(jnp.float32) * attended_full, axis=-1).transpose(
        0, 2, 3, 1
    )

    def query_grad_step(step_index, running):
        key_block, value_block, key_pos = key_slices(step_index)
        scores = block_scores(query_matrix, key_block, positions, key_pos)
        probs = jnp.exp(scores - log_total[..., None])
        dprob = jnp.einsum(
            "gqhrd,gkhd->ghrqk", attention_gradient, value_block, preferred_element_type=jnp.float32
        )
        score_grad = (probs * (dprob - delta[..., None])).astype(jnp.bfloat16)
        return running + jnp.einsum(
            "ghrqk,gkhd->gqhrd", score_grad, key_block, preferred_element_type=jnp.float32
        )

    query_grad = (
        lax.fori_loop(
            0,
            block_total,
            query_grad_step,
            jnp.zeros(
                (query_group_count, local_row_count, KEY_VALUE_HEADS, repeat_heads, head_width),
                jnp.float32,
            ),
        )
        * 0.125
    )
    row_total = local_row_count * lax.axis_size("ctx")
    term_span = math.gcd(row_total, key_span)

    def key_block_term(step_index):
        first_key = step_index * term_span
        key_block = lax.dynamic_slice_in_dim(every_key_row, first_key, term_span, 1)
        value_block = lax.dynamic_slice_in_dim(every_value_row, first_key, term_span, 1)
        key_pos = first_key + jnp.arange(term_span, dtype=jnp.int32)

        def compute_term(unused):
            scores = block_scores(query_matrix, key_block, positions, key_pos)
            probs = jnp.exp(scores - log_total[..., None])
            dprob = jnp.einsum(
                "gqhrd,gkhd->ghrqk",
                attention_gradient,
                value_block,
                preferred_element_type=jnp.float32,
            )
            score_grad = (probs * (dprob - delta[..., None])).astype(jnp.bfloat16)
            key_term = (
                jnp.einsum(
                    "ghrqk,gqhrd->kghd",
                    score_grad,
                    query_matrix,
                    preferred_element_type=jnp.float32,
                )
                * 0.125
            )
            value_term = jnp.einsum(
                "ghrqk,gqhrd->kghd",
                probs.astype(jnp.bfloat16),
                attention_gradient,
                preferred_element_type=jnp.float32,
            )
            return jnp.concatenate(
                [
                    key_term.reshape(term_span, query_group_count, key_value_width),
                    value_term.reshape(term_span, query_group_count, key_value_width),
                ],
                -1,
            )

        def empty_term(unused):
            return jnp.zeros((term_span, query_group_count, 2 * key_value_width), jnp.float32)

        return lax.cond(first_key <= last_row, compute_term, empty_term, 0)

    terms = lax.map(key_block_term, jnp.arange(row_total // term_span, dtype=jnp.int32))
    paired_gradients = (
        lax.psum_scatter(
            terms.reshape(row_total, query_group_count, 2 * key_value_width).astype(jnp.bfloat16),
            "ctx",
            scatter_dimension=0,
            tiled=True,
        )
        .astype(jnp.float32)
        .transpose(1, 0, 2)
    )
    key_gradient = paired_gradients[..., :key_value_width].reshape(
        query_group_count, local_row_count, KEY_VALUE_HEADS, head_width
    )
    value_gradient = paired_gradients[..., key_value_width:].reshape(
        query_group_count, local_row_count, KEY_VALUE_HEADS, head_width
    )
    query_pre_grad = rotate_back(
        query_grad.reshape(query_group_count, local_row_count, QUERY_HEADS, head_width),
        cosine_table,
        sine_table,
    )
    query_pre_grad = query_pre_grad.astype(jnp.bfloat16).reshape(
        query_group_count, local_row_count, query_width
    )
    key_pre_grad = (
        rotate_back(key_gradient, cosine_table, sine_table)
        .astype(jnp.bfloat16)
        .reshape(query_group_count, local_row_count, key_value_width)
    )
    value_pre_grad = value_gradient.astype(jnp.bfloat16).reshape(
        query_group_count, local_row_count, key_value_width
    )
    grad_query = jnp.einsum(
        "gsd,gse->de", normed1, query_pre_grad, preferred_element_type=jnp.float32
    )
    grad_key = jnp.einsum("gsd,gse->de", normed1, key_pre_grad, preferred_element_type=jnp.float32)
    grad_value = jnp.einsum(
        "gsd,gse->de", normed1, value_pre_grad, preferred_element_type=jnp.float32
    )
    normed1_grad = jnp.einsum(
        "gse,de->gsd", query_pre_grad, wq_full, preferred_element_type=jnp.float32
    )
    normed1_grad = normed1_grad + jnp.einsum(
        "gse,de->gsd", key_pre_grad, wk_full, preferred_element_type=jnp.float32
    )
    normed1_grad = normed1_grad + jnp.einsum(
        "gse,de->gsd", value_pre_grad, wv_full, preferred_element_type=jnp.float32
    )
    grad_gain1 = jnp.sum(normed1_grad * inputs * scale1, axis=(0, 1))
    scaled1 = gain1f * normed1_grad
    input_grad = (
        middle_grad
        + scale1 * scaled1
        - inputs * scale1**3 * jnp.mean(scaled1 * inputs, axis=-1, keepdims=True)
    )
    totals = lax.psum(
        (
            grad_gain1,
            grad_query,
            grad_key,
            grad_value,
            grad_out,
            grad_gain2,
            grad_gate,
            grad_up,
            grad_down,
        ),
        ("dp", "ctx", "fsdp"),
    )
    owner = lax.axis_index("fsdp")
    shards = (norm1_gain, w_query, w_key, w_value, w_out, norm2_gain, w_gate, w_up, w_down)
    shares = tuple(
        (
            lax.dynamic_slice_in_dim(summed, owner * shard.shape[0], shard.shape[0], 0)
            for summed, shard in zip(totals, shards)
        )
    )
    return (
        output,
        input_grad,
        shares[0],
        shares[1],
        shares[2],
        shares[3],
        shares[4],
        shares[5],
        shares[6],
        shares[7],
        shares[8],
    )


WIDTH = 576
QUERY_WIDTH = QUERY_HEADS * HEAD_SIZE
KEY_WIDTH = KEY_VALUE_HEADS * HEAD_SIZE
ROTATED = QUERY_HEADS + KEY_VALUE_HEADS
REPEAT = QUERY_HEADS // KEY_VALUE_HEADS
HALF = HEAD_SIZE // 2
USED = QUERY_WIDTH + 2 * KEY_WIDTH
PACKED = USED + 64
GAIN_ROWS = 16
TILE = 256
WIDE_TILE = 512
MEBI = 1024 * 1024
F32 = jnp.float32
BF16 = jnp.bfloat16


def mm(a, b):
    return jnp.dot(a, b, preferred_element_type=F32)


def mm_nt(a, b):
    return lax.dot_general(a, b, (((1,), (1,)), ((), ())), preferred_element_type=F32)


def flip(tensor):
    return tensor.astype(F32).T.astype(tensor.dtype)


def span(index, size, step=None):
    step = size if step is None else step
    return pl.ds(pl.multiple_of(index * step, step), size)


def flip_blocks(target, source, block):
    def one(step, carry):
        at = span(step, block)
        target[at, :] = flip(source[:, at])
        return carry

    lax.fori_loop(0, source.shape[1] // block, one, 0)


def column_scale(tensor):
    return lax.rsqrt(jnp.mean(tensor * tensor, axis=0, keepdims=True) + EPSILON)


def sigmoid(tensor):
    return 0.5 * jnp.tanh(0.5 * tensor) + 0.5


def causal_last(scores, tile):
    shape = (TILE, REPEAT * TILE)
    visible = lax.broadcasted_iota(jnp.int32, shape, 0) <= (
        lax.broadcasted_iota(jnp.int32, shape, 1) & (TILE - 1)
    )
    last = jnp.where(visible, scores[tile * TILE :, :], MASKED)
    return last if tile == 0 else jnp.concatenate([scores[: tile * TILE, :], last], 0)


def attend_kernel(
    place,
    tokens,
    theirs,
    w_own,
    w_y,
    w_core,
    w_both,
    cosine,
    sine,
    x_seq,
    normed,
    packed,
    gains,
    qkv_t,
    log_total,
    attended_t,
    packed_t,
    key_rows,
):
    me, shard = place[0], place[1]
    half_rows = theirs.shape[1]
    sequence = 2 * half_rows
    x_seq[:, span(me, half_rows)] = tokens[me]
    x_seq[:, span(1 - me, half_rows)] = theirs[...]
    rows = packed.shape[0] // 4
    for bits, piece in ((0, w_own), (2, w_y), (1, w_core), (3, w_both)):
        at = span(shard ^ bits, rows)
        packed[at, :] = piece[:rows, :]
        gains[at, :GAIN_ROWS] = piece[rows:, :TILE].astype(F32).T[:rows, :]
    flip_blocks(packed_t, packed, TILE)
    gain1 = gains[:, :1]

    def project(step, carry):
        at = span(step, WIDE_TILE)
        x = x_seq[:, at].astype(F32)
        normed_tile = (x * column_scale(x) * gain1).astype(BF16)
        normed[:, at] = normed_tile
        turned = mm(packed_t[:USED, :], normed_tile)
        cos, sin = cosine[:, at], sine[:, at]
        for head in range(ROTATED):
            a = turned[head * HEAD_SIZE : head * HEAD_SIZE + HALF, :]
            b = turned[head * HEAD_SIZE + HALF : (head + 1) * HEAD_SIZE, :]
            both = jnp.concatenate([a * cos - b * sin, b * cos + a * sin], 0)
            if head < QUERY_HEADS:
                both = both * 0.125
            else:
                key_rows[head - QUERY_HEADS, at, :] = both.T.astype(BF16)
            qkv_t[head * HEAD_SIZE : (head + 1) * HEAD_SIZE, at] = both.astype(BF16)
        qkv_t[ROTATED * HEAD_SIZE :, at] = turned[ROTATED * HEAD_SIZE :, :].astype(BF16)
        return carry

    lax.fori_loop(0, sequence // WIDE_TILE, project, 0)

    def one_group(group, carry):
        value_rows = span(ROTATED + group, HEAD_SIZE)
        for tile in range(sequence // TILE):
            extent = (tile + 1) * TILE
            cols = slice(tile * TILE, extent)
            queries = jnp.concatenate(
                [qkv_t[span(group * REPEAT + r, HEAD_SIZE), cols] for r in range(REPEAT)], 1
            )
            scores = causal_last(mm(key_rows[group, :extent, :], queries), tile)
            top = jnp.max(scores, axis=0, keepdims=True)
            weights = jnp.exp(scores - top)
            total = jnp.sum(weights, axis=0, keepdims=True)
            mixed = mm(qkv_t[value_rows, :extent], weights.astype(BF16))
            mixed = (mixed * (1.0 / total)).astype(BF16)
            logs = top + jnp.log(total)
            for r in range(REPEAT):
                own = slice(r * TILE, (r + 1) * TILE)
                attended_t[span(group * REPEAT + r, HEAD_SIZE), cols] = mixed[:, own]
                log_total[group, r : r + 1, cols] = logs[:, own]
        return carry

    lax.fori_loop(0, KEY_VALUE_HEADS, one_group, 0)


def places(shard, row_bit, keep, send):
    for y_bit in range(2):
        for x_bit in range(2):
            for core_bit, target in ((0, keep), (1, send)):
                yield target, y_bit, x_bit, shard ^ (2 * y_bit + core_bit), row_bit ^ x_bit


def chunk_step(place, pieces, normed, dy, out_sum, grad_sum, keep, send, scratch):
    w_gate, w_up, w_down_t, w_gate_t, w_up_t, w_down, hidden, gate_grad, up_grad, total = scratch
    row_bit, shard, level = place[3], place[1], place[2]
    rows = pieces[0].shape[0]
    wide = w_gate.shape[1]
    part = wide // 4
    sequence = normed.shape[1]
    for bits, piece in zip((0, 2, 1, 3), pieces):
        at = span(shard ^ bits, rows)
        w_gate[at, :] = piece[:, :wide]
        w_up[at, :] = piece[:, wide : 2 * wide]
        for block in range(4):
            first = 2 * wide + block * part
            w_down_t[block * rows : (block + 1) * rows, span(shard ^ bits, part)] = piece[
                :, first : first + part
            ]
    w_gate_t[...] = flip(w_gate[...])
    w_up_t[...] = flip(w_up[...])
    w_down[...] = flip(w_down_t[...])
    for first in range(0, sequence, 2 * WIDE_TILE):
        at = slice(first, first + 2 * WIDE_TILE)
        gate = mm(w_gate_t[...], normed[:, at])
        up = mm(w_up_t[...], normed[:, at])
        hidden_grad = mm(w_down[...], dy[:, at])
        sig = sigmoid(gate)
        silu = gate * sig
        hidden_tile = (silu * up).astype(BF16)
        gate_tile = (hidden_grad * up * (sig + silu * (1.0 - sig))).astype(BF16)
        up_tile = (hidden_grad * silu).astype(BF16)
        hidden[:, at] = hidden_tile
        gate_grad[:, at] = gate_tile
        up_grad[:, at] = up_tile
        out_sum[:, at] += mm(w_down_t[...], hidden_tile)
        grad_sum[:, at] += mm(w_gate[...], gate_tile) + mm(w_up[...], up_tile)
    half = rows // 2
    middle = wide // 2
    for grads, moves in (
        (gate_grad, ((0, 0, 0, wide),)),
        (up_grad, ((0, 0, wide, middle), (1, middle, 0, middle))),
    ):
        total[...] = mm_nt(normed[...], grads[...])
        for target, y_bit, x_bit, owner, side in places(shard, place[3], keep, send):
            at = span(owner * 2 + side, half)
            for z_half, first, to, count in moves:
                target[y_bit, x_bit, level ^ z_half, :, to : to + count] = total[
                    at, first : first + count
                ].astype(BF16)
    total[...] = mm_nt(dy[...], hidden[...])
    for target, y_bit, x_bit, owner, side in places(shard, place[3], keep, send):
        for block in range(4):
            at = pl.ds(pl.multiple_of(block * rows + side * half, 8), half)
            to = middle + block * part
            target[y_bit, x_bit, level ^ 1, :, to : to + part] = total[
                at, span(owner, part)
            ].astype(BF16)


def first_chunk_kernel(
    place,
    x_seq,
    attended_t,
    out_grad,
    dy_theirs,
    gains,
    p_own,
    p_y,
    p_core,
    p_both,
    middle,
    normed,
    scales,
    dy,
    w_out,
    out_sum,
    grad_sum,
    keep,
    send,
    w_out_t,
    *scratch,
):
    me, shard = place[0], place[1]
    half_rows = dy_theirs.shape[1]
    sequence = 2 * half_rows
    dy[:, span(me, half_rows)] = out_grad[me]
    dy[:, span(1 - me, half_rows)] = dy_theirs[...]
    pieces = (p_own, p_y, p_core, p_both)
    rows = p_own.shape[0]
    packed_width = p_own.shape[1] - QUERY_WIDTH
    for bits, piece in zip((0, 2, 1, 3), pieces):
        w_out[span(shard ^ bits, rows), :] = piece[:, packed_width:]
    w_out_t[...] = flip(w_out[...])
    gain2 = gains[:, 1:2]
    for first in range(0, sequence, WIDE_TILE):
        at = slice(first, first + WIDE_TILE)
        mid = x_seq[:, at].astype(F32) + mm(w_out_t[...], attended_t[:, at])
        middle[:, at] = mid
        out_sum[:, at] = mid
        grad_sum[:, at] = jnp.zeros_like(mid)
        scale = column_scale(mid)
        scales[:, at] = jnp.broadcast_to(scale, (8, WIDE_TILE))
        normed[:, at] = (mid * scale * gain2).astype(BF16)
    chunk_step(place, pieces, normed, dy, out_sum, grad_sum, keep, send, scratch)


def next_chunk_kernel(
    place, normed, dy, out_in, grad_in, p_own, p_y, p_core, p_both, out_sum, grad_sum, keep, send, *scratch
):
    out_sum[...] = out_in[...]
    grad_sum[...] = grad_in[...]
    pieces = (p_own, p_y, p_core, p_both)
    chunk_step(place, pieces, normed, dy, out_sum, grad_sum, keep, send, scratch)


def last_chunk_kernel(
    place,
    normed,
    dy,
    out_in,
    grad_in,
    p_own,
    p_y,
    p_core,
    p_both,
    attended_t,
    gains,
    middle,
    scales,
    w_out,
    out_keep,
    out_send,
    middle_grad,
    attended_grad_t,
    keep,
    send,
    out_sum,
    branch_grad,
    *scratch,
):
    me, shard = place[0], place[1]
    half_rows = out_keep.shape[1]
    sequence = 2 * half_rows
    grad_sum = middle_grad
    out_sum[...] = out_in[...]
    grad_sum[...] = grad_in[...]
    pieces = (p_own, p_y, p_core, p_both)
    chunk_step(place, pieces, normed, dy, out_sum, grad_sum, keep, send, scratch)
    gain2 = gains[:, 1:2]
    for first in range(0, sequence, WIDE_TILE):
        at = slice(first, first + WIDE_TILE)
        output = out_sum[:, at].astype(BF16)
        block, start = divmod(first, half_rows)
        block_cols = slice(start, start + WIDE_TILE)

        @pl.when(me == block)
        def _():
            out_keep[:, block_cols] = output

        @pl.when(me != block)
        def _():
            out_send[:, block_cols] = output

        mid = middle[:, at]
        scale = scales[0:1, at]
        scaled = grad_sum[:, at] * gain2
        back = (
            dy[:, at].astype(F32)
            + scale * scaled
            - mid * (scale * scale * scale) * jnp.mean(scaled * mid, axis=0, keepdims=True)
        )
        middle_grad[:, at] = back
        branch = back.astype(BF16)
        branch_grad[:, at] = branch
        attended_grad_t[:, at] = mm(w_out[...], branch).astype(BF16)
    total = scratch[-1]
    half = p_own.shape[0] // 2
    columns = QUERY_WIDTH // 2
    first_to = keep.shape[4] - columns
    for start in range(0, QUERY_WIDTH, TILE):
        count = min(TILE, QUERY_WIDTH - start)
        total[:, :count] = mm_nt(attended_t[...], branch_grad[start : start + count, :])
        for target, y_bit, x_bit, owner, side in places(shard, place[3], keep, send):
            at = span(owner * 2 + side, half)
            for z_half in range(2):
                low = max(start, z_half * columns)
                high = min(start + count, (z_half + 1) * columns)
                if low < high:
                    to = first_to + low - z_half * columns
                    target[y_bit, x_bit, place[2] ^ z_half, :, to : to + high - low] = total[
                        at, low - start : high - start
                    ].astype(BF16)


def attend_back_kernel(
    queries_t,
    keys_t,
    values_t,
    log_total,
    attended_t,
    grad_t,
    cosine,
    sine,
    dq_out,
    dk_out,
    dv_out,
    keys,
    values,
    dk,
    dv,
):
    sequence = keys_t.shape[1]
    keys[...] = flip(keys_t[...])
    values[...] = flip(values_t[...])
    dk[...] = jnp.zeros_like(dk)
    dv[...] = jnp.zeros_like(dv)

    def back(a, b, cos, sin):
        return (a * cos + b * sin).astype(BF16), (b * cos - a * sin).astype(BF16)

    for tile in range(sequence // TILE):
        extent = (tile + 1) * TILE
        cols = slice(tile * TILE, extent)
        heads = [slice(r * HEAD_SIZE, (r + 1) * HEAD_SIZE) for r in range(REPEAT)]
        q_t = jnp.concatenate([queries_t[head, cols] for head in heads], 1)
        do_t = jnp.concatenate([grad_t[head, cols] for head in heads], 1)
        mixed = jnp.concatenate([attended_t[head, cols] for head in heads], 1)
        logs = jnp.concatenate([log_total[0, r : r + 1, cols] for r in range(REPEAT)], 1)
        delta = jnp.sum(do_t.astype(F32) * mixed.astype(F32), axis=0, keepdims=True)
        scores = causal_last(mm(keys[:extent, :], q_t), tile)
        probs = jnp.exp(scores - logs)
        dprob = mm(values[:extent, :], do_t)
        score_grad = (probs * (dprob - delta)).astype(BF16)
        dv[:extent, :] += mm(probs.astype(BF16), flip(do_t))
        dk[:extent, :] += mm(score_grad, flip(q_t))
        dq = mm(keys_t[:, :extent], score_grad) * 0.125
        cos, sin = cosine[:, cols], sine[:, cols]
        for r, head in enumerate(heads):
            own = slice(r * TILE, (r + 1) * TILE)
            a, b = back(dq[:HALF, own], dq[HALF:, own], cos, sin)
            dq_out[head.start : head.start + HALF, cols] = a
            dq_out[head.start + HALF : head.stop, cols] = b
    turned = dk[...].T
    a, b = back(turned[:HALF, :], turned[HALF:, :], cosine[...], sine[...])
    dk_out[:HALF, :] = a
    dk_out[HALF:, :] = b
    dv_out[...] = dv[...].T.astype(BF16)


def input_kernel(place, normed, x_seq, packed, gains, middle_grad, *rest):
    heads = rest[: 3 * KEY_VALUE_HEADS]
    keep_w, send_w, keep_x, send_x, joined, grad_seq, total = rest[3 * KEY_VALUE_HEADS :]
    me, shard = place[0], place[1]
    group_width = REPEAT * HEAD_SIZE
    for group in range(KEY_VALUE_HEADS):
        dq, dk, dv = heads[3 * group : 3 * group + 3]
        joined[group * group_width : (group + 1) * group_width, :] = dq[...]
        at = QUERY_WIDTH + group * HEAD_SIZE
        joined[at : at + HEAD_SIZE, :] = dk[...]
        at = QUERY_WIDTH + KEY_WIDTH + group * HEAD_SIZE
        joined[at : at + HEAD_SIZE, :] = dv[...]
    half = keep_w.shape[2]
    for first in range(0, USED, 512):
        cols = slice(first, min(first + 512, USED))
        total[:, cols] = mm_nt(normed[...], joined[cols, :])
    for target, y_bit, x_bit, owner, side in places(shard, me, keep_w, send_w):
        target[y_bit, x_bit] = total[span(owner * 2 + side, half), :].astype(BF16)
    half_rows = keep_x.shape[1]
    sequence = 2 * half_rows
    gain1 = gains[:, :1]
    for first in range(0, sequence, WIDE_TILE):
        at = slice(first, first + WIDE_TILE)
        scaled = mm(packed[:, :USED], joined[:, at]) * gain1
        x = x_seq[:, at].astype(F32)
        scale = column_scale(x)
        grad_seq[:, at] = (
            middle_grad[:, at]
            + scale * scaled
            - x * (scale * scale * scale) * jnp.mean(scaled * x, axis=0, keepdims=True)
        )
    keep_x[...] = grad_seq[:, span(me, half_rows)]
    send_x[...] = grad_seq[:, span(1 - me, half_rows)].astype(BF16)


def pack_input_kernel(place, w_query, w_key, w_value, gains, packed):
    rows = w_query.shape[0]
    packed[:rows, :QUERY_WIDTH] = w_query[...]
    packed[:rows, QUERY_WIDTH : QUERY_WIDTH + KEY_WIDTH] = w_key[...]
    packed[:rows, QUERY_WIDTH + KEY_WIDTH :] = jnp.concatenate(
        [w_value[...].astype(F32), jnp.zeros((rows, PACKED - USED), F32)], 1
    ).astype(BF16)
    packed[rows:, :] = jnp.zeros((GAIN_ROWS, PACKED), BF16)
    packed[rows:, :TILE] = gains[...]


def pack_kernel(place, w_gate, w_up, w_down_t, w_out, *chunks):
    rows = w_gate.shape[0]
    down_rows = w_down_t.shape[1]
    part = 128
    for index, chunk in enumerate(chunks):
        at = index * part
        for i in range(4):
            source = slice(i * down_rows + at, i * down_rows + at + part)
            chunk[:, i * part : (i + 1) * part] = w_gate[:, source]
            chunk[:, (4 + i) * part : (5 + i) * part] = w_up[:, source]
            chunk[:, (8 + i) * part : (9 + i) * part] = w_down_t[
                i * rows : (i + 1) * rows, at : at + part
            ]
    chunks[0][:, 12 * part :] = w_out[...]


def combine_kernel(kinds, place, *refs):
    count = sum(4 if kind == "orders" else 2 for kind in kinds)
    sources, targets = list(refs[:count]), list(refs[count:])
    for kind in kinds:
        a, b = sources.pop(0), sources.pop(0)
        if kind == "orders":
            target = targets.pop(0)
            for i, own, other in ((0, a, b), (1, sources.pop(0), sources.pop(0))):
                target[i, place[2]] = own[...]
                target[i, 1 - place[2]] = other[...]
        elif kind == "order":
            target = targets.pop(0)
            target[place[2]] = a[...]
            target[1 - place[2]] = b[...]
        elif kind == "pair":
            for i in range(2):
                targets.pop(0)[...] = (a[i].astype(F32) + b[i].astype(F32)).astype(BF16)
        else:
            targets.pop(0)[...] = (a[...].astype(F32) + b[...].astype(F32)).astype(BF16)


def halves_kernel(place, keep, *rest):
    target = rest[-1]
    target[place[0]] = keep[...]
    first = 0
    for got in rest[:-1]:
        size = got.shape[0]
        target[1 - place[0], first : first + size] = got[...].astype(target.dtype)
        first += size


def gain_row(products, gain):
    column = jnp.sum(products, axis=1, keepdims=True)
    row = jnp.broadcast_to(column, (column.shape[0], 128)).T[:1, :]
    return row / gain.astype(F32)


def unpack_kernel(place, own, other, own2, other2, w_gate, w_up, gain, *out):
    gate_out, up_out, down_out, out_out, gain_out = out
    me = place[0]
    half = own2.shape[1]
    rows = 2 * half
    part = 128
    down_rows = down_out.shape[1]
    last = (own2, other2)
    for index, sources in enumerate(
        ((own.at[0], own.at[1], own2), (other.at[0], other.at[1], other2))
    ):
        for chunk, source in enumerate(sources):
            side = index ^ me
            at = span(side, half)
            for i in range(4):
                to = slice(i * down_rows + chunk * part, i * down_rows + (chunk + 1) * part)
                gate_out[at, to] = source[0, :, i * part : (i + 1) * part].astype(F32)
                z_half, first = (0, (4 + i) * part) if i < 2 else (1, (i - 2) * part)
                up_out[at, to] = source[z_half, :, first : first + part].astype(F32)
                down_at = pl.ds(pl.multiple_of(i * rows + side * half, 8), half)
                first = (2 + i) * part
                down_out[down_at, chunk * part : (chunk + 1) * part] = source[
                    1, :, first : first + part
                ].astype(F32)
        first = 6 * part
        out_out[span(index ^ me, half), :] = jnp.concatenate(
            [last[index][0, :, first:].astype(F32), last[index][1, :, first:].astype(F32)], 1
        )
    products = gate_out[...] * w_gate[...].astype(F32) + up_out[...] * w_up[...].astype(F32)
    gain_out[...] = gain_row(products, gain[...])


def unpack_input_kernel(
    place, own, other, w_query, w_key, w_value, gain, query_out, key_out, value_out, gain_out
):
    me = place[0]
    half = own.shape[0]
    key_at = QUERY_WIDTH + KEY_WIDTH
    for side, source in ((me, own), (1 - me, other)):
        at = span(side, half)
        wide = source[...].astype(F32)
        query_out[at, :] = wide[:, :QUERY_WIDTH]
        key_out[at, :] = wide[:, QUERY_WIDTH:key_at]
        value_out[at, :] = wide[:, key_at:]
    products = jnp.sum(query_out[...] * w_query[...].astype(F32), axis=1, keepdims=True)
    products += jnp.sum(key_out[...] * w_key[...].astype(F32), axis=1, keepdims=True)
    products += jnp.sum(value_out[...] * w_value[...].astype(F32), axis=1, keepdims=True)
    gain_out[...] = gain_row(products, gain[...])


def call(kernel, out, scratch, flops, exps, args, name, limit, aliases=None):
    shapes = [jax.ShapeDtypeStruct(s, d) for s, d in out]
    moved = sum(a.size * a.dtype.itemsize for a in args[1:]) + sum(
        s.size * s.dtype.itemsize for s in shapes
    )
    in_specs = [pl.BlockSpec(memory_space=pltpu.SMEM)] + [
        pl.BlockSpec(memory_space=pltpu.VMEM)
    ] * (len(args) - 1)
    return pl.pallas_call(
        kernel,
        out_shape=shapes,
        in_specs=in_specs,
        out_specs=[pl.BlockSpec(memory_space=pltpu.VMEM)] * len(shapes),
        scratch_shapes=[pltpu.VMEM(s, d) for s, d in scratch],
        input_output_aliases=aliases or {},
        compiler_params=pltpu.CompilerParams(vmem_limit_bytes=limit * MEBI),
        cost_estimate=pl.CostEstimate(
            flops=flops, bytes_accessed=moved if flops else 1024, transcendentals=exps
        ),
        name=name,
    )(*args)


def attend_back(group, qkv_t, log_total, attended_t, grad_t, cosine, sine):
    sequence = qkv_t.shape[1]
    group_width = REPEAT * HEAD_SIZE

    def rows_of(size, index):
        return pl.BlockSpec((size, sequence), lambda step: (index, 0))

    flops = 5 * REPEAT * sequence * sequence * HEAD_SIZE * 2
    return pl.pallas_call(
        attend_back_kernel,
        grid=(1,),
        out_shape=[
            jax.ShapeDtypeStruct((group_width, sequence), BF16),
            jax.ShapeDtypeStruct((HEAD_SIZE, sequence), BF16),
            jax.ShapeDtypeStruct((HEAD_SIZE, sequence), BF16),
        ],
        in_specs=[
            rows_of(group_width, group),
            rows_of(HEAD_SIZE, QUERY_HEADS + group),
            rows_of(HEAD_SIZE, ROTATED + group),
            pl.BlockSpec((1, 8, sequence), lambda step: (group, 0, 0)),
            rows_of(group_width, group),
            rows_of(group_width, group),
            rows_of(HALF, 0),
            rows_of(HALF, 0),
        ],
        out_specs=[rows_of(group_width, 0), rows_of(HEAD_SIZE, 0), rows_of(HEAD_SIZE, 0)],
        scratch_shapes=[
            pltpu.VMEM((sequence, HEAD_SIZE), BF16),
            pltpu.VMEM((sequence, HEAD_SIZE), BF16),
            pltpu.VMEM((sequence, HEAD_SIZE), F32),
            pltpu.VMEM((sequence, HEAD_SIZE), F32),
        ],
        compiler_params=pltpu.CompilerParams(vmem_limit_bytes=16 * MEBI),
        cost_estimate=pl.CostEstimate(
            flops=flops, bytes_accessed=4_000_000, transcendentals=REPEAT * sequence * sequence
        ),
        name="attend_back",
    )(qkv_t, qkv_t, qkv_t, log_total, attended_t, grad_t, cosine, sine)


def across(tensor, bit):
    return lax.ppermute(tensor, "fsdp", [(i, i ^ bit) for i in range(4)])


def over_context(tensor):
    return lax.ppermute(tensor, "ctx", [(0, 1), (1, 0)])


def after(tensor, *done):
    return lax.optimization_barrier((tensor, *done))[0]


def together(*values):
    return lax.optimization_barrier(values)


def along(tensor, bit):
    size = lax.axis_size("dp")
    return lax.ppermute(tensor, "dp", [(i, i ^ bit) for i in range(size)])


def whole_sequences(
    tokens, norm1_gain, w_query, w_key, w_value, w_out, norm2_gain, w_gate, w_up, w_down, out_grad
):
    half_rows, width = tokens.shape[1:]
    sequence = 2 * half_rows
    rows = w_query.shape[0]
    down_rows = w_down.shape[0]
    hidden_width = w_gate.shape[1]
    part = 128
    me = lax.axis_index("ctx")
    line = lax.axis_index("dp")
    shard = lax.axis_index("fsdp")
    place = jnp.stack([me, shard, line & 1, me]).astype(jnp.int32)
    tokens = jnp.swapaxes(tokens, 1, 2)
    out_grad = jnp.swapaxes(out_grad, 1, 2)

    tokens_send = lax.dynamic_index_in_dim(tokens, 1 - me, 0, False)
    tokens_theirs = over_context(tokens_send)
    gain_rows = jnp.stack(together(norm1_gain, norm2_gain, tokens_send)[:2])
    gains_own = jnp.pad(gain_rows, ((0, GAIN_ROWS - 2), (0, TILE - rows)))
    (packed,) = call(
        pack_input_kernel,
        [((rows + GAIN_ROWS, PACKED), BF16)],
        [],
        0,
        0,
        (place, w_query, w_key, w_value, gains_own),
        "pack_input",
        16,
    )
    packed_y = across(packed, 2)
    packed_core = across(packed, 1)
    dy_theirs = over_context(lax.dynamic_index_in_dim(out_grad, 1 - me, 0, False))
    chunks = call(
        pack_kernel,
        [((rows, 12 * part + (0 if index else QUERY_WIDTH)), BF16) for index in range(3)],
        [],
        0,
        0,
        (place, w_gate, w_up, w_down.T, after(w_out, packed)),
        "pack",
        16,
    )
    cosine, sine = rope_tables(jnp.arange(sequence, dtype=jnp.int32), HEAD_SIZE)
    *chunks, _, cosine, sine, place = together(*chunks, packed, cosine.T, sine.T, place)
    packed_y, tokens_theirs = together(packed_y, tokens_theirs)
    packed_both = across(packed_y, 1)
    chunks_y = [across(chunk, 2) for chunk in chunks]
    chunks_core = [across(chunk, 1) for chunk in chunks]

    pairs = sequence * sequence
    x_seq, normed, packed_all, gains, qkv_t, log_total, attended_t = call(
        attend_kernel,
        [
            ((width, sequence), BF16),
            ((width, sequence), BF16),
            ((width, PACKED), BF16),
            ((width, 128), F32),
            ((USED, sequence), BF16),
            ((KEY_VALUE_HEADS, 8, sequence), F32),
            ((QUERY_WIDTH, sequence), BF16),
        ],
        [((PACKED, width), BF16), ((KEY_VALUE_HEADS, sequence, HEAD_SIZE), BF16)],
        2 * sequence * width * PACKED + 4 * QUERY_WIDTH * pairs,
        QUERY_HEADS * pairs,
        (place, tokens, tokens_theirs, packed, packed_y, packed_core, packed_both, cosine, sine),
        "attend",
        20,
    )

    natural, turned = ((width, 4 * part), BF16), ((4 * part, width), BF16)
    row, wide_row = ((width, sequence), BF16), ((4 * part, sequence), BF16)
    row_sum = ((width, sequence), F32)
    share = ((2, 2, 2, rows // 2, 6 * part), BF16)
    last_share = ((2, 2, 2, rows // 2, 6 * part + QUERY_WIDTH // 2), BF16)
    chunk_scratch = [
        natural,
        natural,
        natural,
        turned,
        turned,
        turned,
        wide_row,
        wide_row,
        wide_row,
        ((width, 4 * part), F32),
    ]
    flops = 2 * sequence * width * 9 * 4 * part
    exps = sequence * 4 * part

    first_y, second_y, third_y = chunks_y
    first_y, second_y, attended_t, dy_theirs = together(first_y, second_y, attended_t, dy_theirs)
    pieces = (chunks[0], first_y, chunks_core[0], across(first_y, 1))
    second_both = across(second_y, 1)
    middle, normed2, scales, dy, w_out_all, out_sum, grad_sum, keep0, send0 = call(
        first_chunk_kernel,
        [
            row_sum,
            row,
            ((8, sequence), F32),
            row,
            ((QUERY_WIDTH, width), BF16),
            row_sum,
            row_sum,
            share,
            share,
        ],
        [((width, QUERY_WIDTH), BF16), *chunk_scratch],
        flops + 2 * sequence * width * QUERY_WIDTH,
        exps,
        (place, x_seq, attended_t, out_grad, dy_theirs, gains, *pieces),
        "first_chunk",
        26,
    )

    def combine(*items):
        kinds = tuple(item[0] for item in items)
        args = [tensor for item in items for tensor in item[1:]]
        out = []
        for kind, tensor, *_ in items:
            if kind == "orders":
                out.append(((2, 2, *tensor.shape), BF16))
            elif kind == "order":
                out.append(((2, *tensor.shape), BF16))
            elif kind == "pair":
                out += [(tensor.shape[1:], BF16)] * 2
            else:
                out.append((tensor.shape, BF16))
        kernel = functools.partial(combine_kernel, kinds)
        return call(kernel, out, [], 0, 0, (place, *args), "combine", 16)

    out_sum, send0, third_y, second_both = together(out_sum, send0, third_y, second_both)
    got0 = across(send0, 1)
    pieces = (chunks[1], second_y, chunks_core[1], second_both)
    third_both = across(third_y, 1)
    out_sum, grad_sum, keep1, send1 = call(
        next_chunk_kernel,
        [row_sum, row_sum, share, share],
        chunk_scratch,
        flops,
        exps,
        (place, normed2, dy, out_sum, grad_sum, *pieces),
        "next_chunk",
        20,
        {3: 0, 4: 1},
    )

    got0, out_sum, send1, third_both = together(got0, out_sum, send1, third_both)
    own0, part0 = combine(("pair", keep0, got0))
    part0, send1, out_sum = together(part0, send1, out_sum)
    got0, got1 = across(part0, 2), across(send1, 1)
    pieces = (chunks[2], third_y, chunks_core[2], third_both)
    out_keep, out_send, middle_grad, grad_t, keep2, send2 = call(
        last_chunk_kernel,
        [
            ((width, half_rows), BF16),
            ((width, half_rows), BF16),
            row_sum,
            ((QUERY_WIDTH, sequence), BF16),
            last_share,
            last_share,
        ],
        [row_sum, row, *chunk_scratch],
        flops + 4 * sequence * width * QUERY_WIDTH,
        exps,
        (
            place,
            normed2,
            dy,
            out_sum,
            grad_sum,
            *pieces,
            attended_t,
            gains,
            middle,
            scales,
            w_out_all,
        ),
        "last_chunk",
        24,
    )

    got0, got1, grad_t, send2, out_send = together(got0, got1, grad_t, send2, out_send)
    own0, part0, own1, part1 = combine(("pair", own0, got0), ("pair", keep1, got1))
    part0, part1, grad_t = together(part0, part1, grad_t)
    def place_halves(keep, name, *got):
        (both,) = call(
            halves_kernel, [((2, *keep.shape), keep.dtype)], [], 0, 0, (place, keep, *got), name, 16
        )
        return jnp.swapaxes(both, 1, 2)

    got0, got1, got2 = over_context(part0), across(part1, 2), across(send2, 1)
    out_theirs = over_context(out_send)

    back_args = (log_total, attended_t, grad_t, cosine, sine)
    grads0 = attend_back(0, qkv_t, *back_args)
    got0, got2, *grads0 = together(got0, got2, *grads0)
    own0, part0, own2, part2 = combine(("pair", own0, got0), ("pair", keep2, got2))
    part0, part2, qkv_t = together(part0, part2, qkv_t)

    got0, got2 = along(part0, 1), across(part2, 2)
    grads1 = attend_back(1, qkv_t, *back_args)
    got0, got1, *grads1 = together(got0, got1, *grads1)
    own0, own1, part1 = combine(("one", own0, got0), ("pair", own1, got1))
    own0, part1, qkv_t = together(own0, part1, qkv_t)

    got0, got1 = along(own0, 2), over_context(part1)
    grads2 = attend_back(2, qkv_t, *back_args)
    got0, got1, got2, out_theirs, *grads2 = together(got0, got1, got2, out_theirs, *grads2)
    own0, own1, part1, own2, part2 = combine(
        ("one", own0, got0), ("pair", own1, got1), ("pair", own2, got2)
    )
    own0, part1, part2, *grads2 = together(own0, part1, part2, *grads2)

    got0, got1, got2 = along(own0, 1), along(part1, 1), over_context(part2)
    keep_w, send_w, keep_x, send_x = call(
        input_kernel,
        [
            ((2, 2, rows // 2, USED), BF16),
            ((2, 2, rows // 2, USED), BF16),
            ((width, half_rows), F32),
            ((width, half_rows), BF16),
        ],
        [((USED, sequence), BF16), ((width, sequence), F32), ((width, USED), F32)],
        4 * sequence * width * USED,
        sequence,
        (
            place,
            normed,
            x_seq,
            packed_all,
            gains,
            middle_grad,
            *grads0,
            *grads1,
            *grads2,
        ),
        "input_side",
        24,
    )
    got0, got1, got2, send_w, send_x = together(got0, got1, got2, send_w, send_x)
    got_w = across(send_w, 1)
    own1, own2, part2 = combine(("one", own1, got1), ("pair", own2, got2))
    got_w, own1, part2, send_x = together(got_w, own1, part2, send_x)
    own_w, part_w = combine(("pair", keep_w, got_w))
    got_w, got1, got2 = across(part_w, 2), along(own1, 2), along(part2, 1)
    x_theirs = over_context(send_x)
    output = place_halves(out_keep, "output_halves", out_theirs)

    got_w, got1, got2, output = together(got_w, got1, got2, output)
    own_w, part_w, own1, own2 = combine(
        ("pair", own_w, got_w), ("one", own1, got1), ("one", own2, got2)
    )
    part_w, own1, own2 = together(part_w, own1, own2)
    got_w, got1, got2 = over_context(part_w), along(own1, 1), along(own2, 2)

    got_w, got1, got2, x_theirs = together(got_w, got1, got2, x_theirs)
    own_w, own, own2 = combine(
        ("one", own_w, got_w), ("orders", own0, got0, own1, got1), ("one", own2, got2)
    )
    own_w, own, own2, x_theirs = together(own_w, own, own2, x_theirs)
    got_w, got2, other = along(own_w, 1), along(own2, 1), over_context(own)
    gradient = place_halves(keep_x, "gradient_halves", x_theirs)

    got_w, got2, gradient = together(got_w, got2, gradient)
    own_w, own2 = combine(("one", own_w, got_w), ("order", own2, got2))
    own_w, own2 = together(own_w, own2)
    got_w, other2 = along(own_w, 2), over_context(own2)

    got_w, other = together(got_w, other)
    (own_w,) = combine(("one", own_w, got_w))
    other_w = over_context(own_w)
    own_w, other2 = together(own_w, other2)

    gate_sum, up_sum, down_sum, out_sum, gain2_sum = call(
        unpack_kernel,
        [
            ((rows, hidden_width), F32),
            ((rows, hidden_width), F32),
            ((width, down_rows), F32),
            ((rows, width), F32),
            ((1, rows), F32),
        ],
        [],
        0,
        0,
        (place, own, other, own2, other2, w_gate, w_up, norm2_gain[None, :]),
        "unpack",
        24,
    )
    gate_sum, other_w = together(gate_sum, other_w)
    query_sum, key_sum, value_sum, gain1_sum = call(
        unpack_input_kernel,
        [
            ((rows, QUERY_WIDTH), F32),
            ((rows, KEY_WIDTH), F32),
            ((rows, KEY_WIDTH), F32),
            ((1, rows), F32),
        ],
        [],
        0,
        0,
        (place, own_w, other_w, w_query, w_key, w_value, norm1_gain[None, :]),
        "unpack_input",
        16,
    )
    return (
        output,
        gradient,
        gain1_sum[0],
        query_sum,
        key_sum,
        value_sum,
        out_sum,
        gain2_sum[0],
        gate_sum,
        up_sum,
        down_sum.T,
    )


def layer_step(tokens, *rest):
    whole = (
        lax.axis_size("ctx") == 2
        and lax.axis_size("fsdp") == 4
        and lax.axis_size("dp") == 4
        and tokens.shape[0] == 2
        and tokens.shape[1] % WIDE_TILE == 0
        and rest[8].shape == (384, 576)
    )
    return (whole_sequences if whole else split_context)(tokens, *rest)


def solution(mesh):
    return jax.shard_map(
        layer_step,
        mesh=mesh,
        in_specs=(
            P(("dp", "fsdp"), "ctx", None),
            P("fsdp"),
            P("fsdp", None),
            P("fsdp", None),
            P("fsdp", None),
            P("fsdp", None),
            P("fsdp"),
            P("fsdp", None),
            P("fsdp", None),
            P("fsdp", None),
            P(("dp", "fsdp"), "ctx", None),
        ),
        out_specs=(
            P(("dp", "fsdp"), "ctx", None),
            P(("dp", "fsdp"), "ctx", None),
            P("fsdp"),
            P("fsdp", None),
            P("fsdp", None),
            P("fsdp", None),
            P("fsdp", None),
            P("fsdp"),
            P("fsdp", None),
            P("fsdp", None),
            P("fsdp", None),
        ),
        check_vma=False,
    )
```
